32 devices in a mesh: fsdp: 32 (over z, y, x, core).
Axes of the slice: x: 2, y: 2, z: 4, core: 2. Of those that a mesh axis runs over, the one named last changes fastest.
Arguments:
- tokens: bfloat16 [32, 128, 2048], P(None, 'fsdp'), may hold values from -6 to 6
- lengths: int32 [32], replicated, may hold values from 1 to 128, 2457 in all
- permutation: int32 [32], replicated, may hold values from 0 to 31, each once
- query_weight: bfloat16 [2048, 2048], P('fsdp'), may hold values from -0.015625 to 0.015625
- key_weight: bfloat16 [2048, 2048], P('fsdp'), may hold values from -0.125 to 0.125
- value_weight: bfloat16 [2048, 2048], P('fsdp'), may hold values from -0.125 to 0.125
- out_weight: bfloat16 [2048, 2048], P('fsdp'), may hold values from -1 to 1
- gate_weight: bfloat16 [2048, 5120], P('fsdp'), may hold values from -0.125 to 0.125
- up_weight: bfloat16 [2048, 5120], P('fsdp'), may hold values from -0.125 to 0.125
- down_weight: bfloat16 [5120, 2048], P('fsdp'), may hold values from -0.125 to 0.125
- gain_attention: bfloat16 [2048], P('fsdp'), may hold values from 0.25 to 1.75
- gain_feedforward: bfloat16 [2048], P('fsdp'), may hold values from 0.25 to 1.75
- bias_table: bfloat16 [1024], P('fsdp'), may hold values from -5 to 5
- cotangent: bfloat16 [32, 128, 2048], P('fsdp'), may hold values from -6 to 6
Outputs:
- layer_output: bfloat16 [32, 128, 2048], P('fsdp')
- tokens_grad: bfloat16 [32, 128, 2048], P(None, 'fsdp')
- query_grad: float32 [2048, 2048], P('fsdp')
- key_grad: float32 [2048, 2048], P('fsdp')
- value_grad: float32 [2048, 2048], P('fsdp')
- out_grad: float32 [2048, 2048], P('fsdp')
- gate_grad: float32 [2048, 5120], P('fsdp')
- up_grad: float32 [2048, 5120], P('fsdp')
- down_grad: float32 [5120, 2048], P('fsdp')
- gain_attention_grad: float32 [2048], P('fsdp')
- gain_feedforward_grad: float32 [2048], P('fsdp')
- table_grad: float32 [1024], P('fsdp')
The draws below stay inside these ranges and needn't reach their ends.
Inputs may be any that keep to these rules, and one draw needn't show every extreme that they name: The lengths sum to 2457 and at least one sequence has exactly 128 tokens. `permutation`: every sequence number appears exactly once.
All inputs are finite; a program needn't handle non-finite values.
Results may differ from the reference program's by a relative error of at most 0.015.
Values may be sent and summed in bfloat16 or wider, within the bound.
A program may use at most 768 MiB of HBM per device.

```python
import math
import jax
import jax.numpy as jnp
import numpy as np
from jax import lax

D = 2048
HEADS = 32
HEAD_DIM = 64
FF = 5120
BUCKETS = 32
LMAX = 128
SEQS = 32


def shard_levels(key, dims, split, low, largest):
    def one(axis_at, shards_of):
        heights = jax.random.uniform(jax.random.fold_in(jax.random.fold_in(key, 6), axis_at), (shards_of,), jnp.float32, low / len(split), largest / len(split))
        return jnp.repeat(jnp.exp(heights), dims[axis_at] // shards_of).reshape((-1,) + (1,) * (len(dims) - axis_at - 1))

    factor_of = one(*split[0])
    for cut in split[1:]:
        factor_of = factor_of * one(*cut)
    return factor_of


def length_profile(count, total, most, lean):
    loads = [(1 << 20) // math.isqrt(grade ** lean) + 1 for grade in range(2, count + 1)]
    surplus, counts = total - most - (count - 1), [1] * (count - 1)
    while surplus > 0:
        free = [i for i in range(count - 1) if counts[i] < most]
        whole, left = sum([loads[i] for i in free]), surplus
        for i in free:
            addition = min(most - counts[i], max(1, left * loads[i] // whole), surplus)
            counts[i] = counts[i] + addition
            surplus = surplus - addition
    return np.array([most] + counts)


def ragged_sizes(key, count, total, bound, slope):
    if count == 2:
        one = jax.random.randint(key, (), max(1, total - bound), min(bound, total - 1) + 1)
        return jnp.stack([one, total - one])
    sizes = jnp.asarray(length_profile(count, total, bound, slope), jnp.int32)
    twos = (count - 1) // 2
    source_of, taker = sizes[1:1 + 2 * twos:2], sizes[2:2 + 2 * twos:2]
    room = jnp.minimum(source_of - 1, bound - taker)
    shifted = jax.random.randint(jax.random.fold_in(key, 1), (twos,), 0, 1 << 20) % (room + 1)
    sizes = sizes.at[1:1 + 2 * twos:2].set(source_of - shifted).at[2:2 + 2 * twos:2].set(taker + shifted)
    return sizes[jax.random.permutation(jax.random.fold_in(key, 2), count)]


def normal_values(own_key, extent, width, most, cuts=(), kind=jnp.bfloat16):
    values = width * jax.random.normal(own_key, extent, jnp.float32)
    if cuts:
        values = values * shard_levels(own_key, extent, cuts, -0.22, 0.18)
    return jnp.clip(values, -most, most).astype(kind)


def setup_inputs(seed: int = 0) -> dict:
    key_of = jax.random.split(jax.random.key(seed), 15)
    return {
        "tokens": normal_values(key_of[0], (SEQS, LMAX, D), 1.0, 6.0, ((1, 32),)),
        "lengths": ragged_sizes(key_of[1], SEQS, 3 * SEQS * LMAX // 5, LMAX, 2).astype(jnp.int32),
        "permutation": jax.random.permutation(key_of[2], SEQS).astype(jnp.int32),
        "query_weight": normal_values(key_of[3], (D, D), (D * HEAD_DIM) ** -0.5, 0.015625, ((0, 32),)),
        "key_weight": normal_values(key_of[4], (D, D), D ** -0.5, 0.125, ((0, 32),)),
        "value_weight": normal_values(key_of[5], (D, D), D ** -0.5, 0.125, ((0, 32),)),
        "out_weight": normal_values(key_of[6], (D, D), (D // 64) ** -0.5, 1.0, ((0, 32),)),
        "gate_weight": normal_values(key_of[7], (D, FF), D ** -0.5, 0.125, ((0, 32),)),
        "up_weight": normal_values(key_of[8], (D, FF), D ** -0.5, 0.125, ((0, 32),)),
        "down_weight": normal_values(key_of[9], (FF, D), (FF // 2) ** -0.5, 0.125, ((0, 32),)),
        "gain_attention": jnp.clip(1.0 + 0.15 * jax.random.normal(key_of[10], (D,), jnp.float32), 0.25, 1.75).astype(jnp.bfloat16),
        "gain_feedforward": jnp.clip(1.0 + 0.15 * jax.random.normal(key_of[11], (D,), jnp.float32), 0.25, 1.75).astype(jnp.bfloat16),
        "bias_table": normal_values(key_of[12], (BUCKETS * HEADS,), 1.0, 5.0, ((0, 32),)),
        "cotangent": normal_values(key_of[13], (SEQS, LMAX, D), 1.0, 6.0, ((0, 32),)),
    }


EPSILON = 1e-06
masked_score = -1000000000.0
HIGHEST = lax.Precision.HIGHEST

@jax.custom_vjp
def low(v):
    return lax.optimization_barrier(v.astype(jnp.bfloat16)).astype(jnp.float32)

@jax.custom_vjp
def low_back(v):
    return v

def low_keep(v):
    return (low(v), None)

def low_pass(kept, grad):
    return (grad,)

def back_keep(v):
    return (v, None)

def back_low(kept, grad):
    return (low(grad),)
low.defvjp(low_keep, low_pass)
low_back.defvjp(back_keep, back_low)

def bucket_index(relative):
    half_buckets = BUCKETS // 2
    exact_count = half_buckets // 2
    distance = jnp.abs(relative)
    side_offset = jnp.where(relative > 0, half_buckets, 0).astype(jnp.int32)
    square = distance * distance
    far_bucket = jnp.full_like(distance, exact_count)
    for doubling in range(1, half_buckets - exact_count):
        far_bucket = far_bucket + (square >= exact_count * exact_count * 2 ** doubling).astype(jnp.int32)
    return (side_offset + jnp.where(distance < exact_count, distance, far_bucket)).astype(jnp.int32)

def relative_bias(table_full):
    positions = jnp.arange(LMAX, dtype=jnp.int32)
    buckets = bucket_index(positions[None, :] - positions[:, None])
    return jnp.transpose(table_full[buckets], (2, 0, 1))

def norm_scale(values):
    return lax.rsqrt(lax.optimization_barrier(jnp.mean(values * values, axis=-1, keepdims=True)) + EPSILON)

def attend_sequence(query_heads, key_heads, value_heads, rel_bias, length):
    scores = jnp.einsum('qhd,khd->hqk', query_heads, key_heads, precision=HIGHEST) + rel_bias
    scores = low_back(scores)
    key_valid = jnp.arange(LMAX, dtype=jnp.int32) < length
    scores = jnp.where(key_valid[None, None, :], scores, masked_score)
    weights_soft = low(jax.nn.softmax(scores, axis=-1))
    return jnp.einsum('hqk,khd->qhd', weights_soft, value_heads, precision=HIGHEST)

def block_forward(inputs, block_lengths, parameters):
    query_weight, key_weight, value_weight, out_weight, gate_weight, up_weight, down_weight, gain_attention, gain_feedforward, table_full = parameters
    count_seqs = inputs.shape[0]
    rows_in = inputs.reshape(-1, D)
    normed = low(rows_in * norm_scale(rows_in) * gain_attention)

    def project(matrix):
        product = jnp.dot(normed, matrix, precision=HIGHEST)
        return low(low_back(product)).reshape(count_seqs, LMAX, HEADS, HEAD_DIM)
    attended = jax.vmap(attend_sequence, in_axes=(0, 0, 0, None, 0))(project(query_weight), project(key_weight), project(value_weight), relative_bias(table_full), block_lengths)
    attended = low(low_back(attended.reshape(-1, D)))
    middle = rows_in + low_back(jnp.dot(attended, out_weight, precision=HIGHEST))
    normed_two = low(middle * norm_scale(middle) * gain_feedforward)
    gate_values = low_back(jnp.dot(normed_two, gate_weight, precision=HIGHEST))
    up_values = low_back(jnp.dot(normed_two, up_weight, precision=HIGHEST))
    hidden = low(jax.nn.gelu(gate_values, approximate=True) * up_values)
    result = middle + low_back(jnp.dot(hidden, down_weight, precision=HIGHEST))
    positions = jnp.arange(LMAX, dtype=jnp.int32)
    row_valid = (positions[None, :] < block_lengths[:, None]).astype(jnp.float32).reshape(-1, 1)
    return (result * row_valid).reshape(count_seqs, LMAX, D)

def reference(tokens, lengths, permutation, query_weight, key_weight, value_weight, out_weight, gate_weight, up_weight, down_weight, gain_attention, gain_feedforward, bias_table, cotangent):
    group_size = 1
    while group_size * 2 * LMAX <= 4096 and SEQS % (group_size * 2) == 0:
        group_size = group_size * 2
    blocks = SEQS // group_size
    dealt = tokens[permutation].astype(jnp.float32).reshape(blocks, group_size, LMAX, D)
    dealt_lengths = lengths[permutation].reshape(blocks, group_size)
    upstream = cotangent.astype(jnp.float32).reshape(blocks, group_size, LMAX, D)
    matrices = (query_weight, key_weight, value_weight, out_weight, gate_weight, up_weight, down_weight, gain_attention, gain_feedforward)
    parameters = tuple((matrix.astype(jnp.float32) for matrix in matrices)) + (bias_table.astype(jnp.float32).reshape(BUCKETS, HEADS),)

    def scan_step(running, pieces):
        block_in, block_lengths, block_upstream = pieces

        def forward_fn(inputs, weights_all):
            return block_forward(inputs, block_lengths, weights_all)
        result, pullback = jax.vjp(forward_fn, block_in, parameters)
        input_grad, weight_grads = pullback(block_upstream)
        running = tuple((before + gradient for before, gradient in zip(running, weight_grads)))
        return (running, (result.astype(jnp.bfloat16), input_grad.astype(jnp.bfloat16)))
    zeros_init = tuple((jnp.zeros_like(parameter) for parameter in parameters))
    running, (outputs, input_grads) = lax.scan(scan_step, zeros_init, (dealt, dealt_lengths, upstream))
    layer_output = outputs.reshape(SEQS, LMAX, D)
    tokens_grad = input_grads.reshape(SEQS, LMAX, D)[jnp.argsort(permutation)]
    return (layer_output, tokens_grad, running[0], running[1], running[2], running[3], running[4], running[5], running[6], running[7], running[8], running[9].reshape(BUCKETS * HEADS))
```

```python
import functools

import jax
import jax.numpy as jnp
from jax import lax
from jax.experimental import pallas as pl
from jax.experimental.pallas import tpu as pltpu
from jax.sharding import PartitionSpec as P

HEADS = 32
HEAD_DIM = 64
BUCKETS = 32


EPSILON = 1e-06
masked_score = -1000000000.0
HIGHEST = lax.Precision.HIGHEST


def bucket_index(relative):
    half_buckets = BUCKETS // 2
    exact_count = half_buckets // 2
    distance = jnp.abs(relative)
    side_offset = jnp.where(relative > 0, half_buckets, 0).astype(jnp.int32)
    square = distance * distance
    far_bucket = jnp.full_like(distance, exact_count)
    for doubling in range(1, half_buckets - exact_count):
        far_bucket = far_bucket + (square >= exact_count * exact_count * 2**doubling).astype(
            jnp.int32
        )
    return side_offset + jnp.where(distance < exact_count, distance, far_bucket)


def bucket_onehot(seq_len):
    positions = jnp.arange(seq_len, dtype=jnp.int32)
    relative = (positions[None, :] - positions[:, None]).reshape(-1)
    bucket_ids = jnp.arange(BUCKETS, dtype=jnp.int32)
    return (bucket_index(relative)[None, :] == bucket_ids[:, None]).astype(jnp.float32)


def norm_scale(values):
    return lax.rsqrt(jnp.mean(values * values, axis=-1, keepdims=True) + EPSILON)


def norm_back(values, scale, gain_vec, d_norm):
    weighted = gain_vec * d_norm
    return scale * weighted - values * (scale * scale * scale) * jnp.mean(
        weighted * values, axis=-1, keepdims=True
    )


def rows_product(left, right):
    return lax.dot_general(
        left, right, (((0,), (0,)), ((), ())), preferred_element_type=jnp.float32
    )


def against_rows(left, right):
    return lax.dot_general(
        left, right, (((1,), (1,)), ((), ())), preferred_element_type=jnp.float32
    )


def masked_scores(query_heads, key_heads, rel_bias, length):
    scores = (
        jnp.einsum("qhd,khd->hqk", query_heads, key_heads, preferred_element_type=jnp.float32)
        + rel_bias
    )
    key_valid = jnp.arange(key_heads.shape[0], dtype=jnp.int32) < length
    return jnp.where(key_valid[None, None, :], scores, masked_score)


def unpack_weights(full_weights, onehot, seq_len):
    table_full = full_weights[4].astype(jnp.float32).reshape(BUCKETS, HEADS)
    rel_bias = jnp.dot(table_full.T, onehot, precision=HIGHEST).reshape(HEADS, seq_len, seq_len)
    return (
        full_weights[0],
        full_weights[1],
        full_weights[2].astype(jnp.float32),
        full_weights[3].astype(jnp.float32),
        rel_bias,
    )


def body_any(
    tokens,
    lengths,
    permutation,
    query_weight,
    key_weight,
    value_weight,
    out_weight,
    gate_weight,
    up_weight,
    down_weight,
    gain_attention,
    gain_feedforward,
    bias_table,
    cotangent,
):
    model_width = query_weight.shape[1]
    hidden_width = gate_weight.shape[1]
    packed = jnp.concatenate(
        (query_weight, key_weight, value_weight, out_weight, gate_weight, up_weight), axis=1
    )
    shards = (packed, down_weight, gain_attention, gain_feedforward, bias_table)
    full_weights = (
        lax.all_gather(shards[0], "fsdp", axis=0, tiled=True),
        lax.all_gather(shards[1], "fsdp", axis=0, tiled=True),
        lax.all_gather(shards[2], "fsdp", axis=0, tiled=True),
        lax.all_gather(shards[3], "fsdp", axis=0, tiled=True),
        lax.all_gather(shards[4], "fsdp", axis=0, tiled=True),
    )
    reordered = tokens[permutation]
    dealt = lax.all_to_all(reordered, "fsdp", split_axis=0, concat_axis=1, tiled=True)
    seq_count = dealt.shape[0]
    seq_len = dealt.shape[1]
    local_ids = lax.dynamic_slice_in_dim(permutation, lax.axis_index("fsdp") * seq_count, seq_count)
    seq_lengths = lengths[local_ids]
    positions = jnp.arange(seq_len, dtype=jnp.int32)
    row_valid = (positions[None, :] < seq_lengths[:, None]).astype(jnp.float32).reshape(-1, 1)
    onehot = bucket_onehot(seq_len)
    onehot_low = onehot.astype(jnp.bfloat16)
    full_packed, full_down, gain_one, gain_two, rel_bias = unpack_weights(
        full_weights, onehot, seq_len
    )
    head_shape = (seq_count, seq_len, HEADS, HEAD_DIM)
    rows_in = dealt.reshape(-1, model_width).astype(jnp.float32)
    scale_one = norm_scale(rows_in)
    normed = (rows_in * scale_one * gain_one).astype(jnp.bfloat16)
    projected = jnp.dot(
        normed, full_packed[:, : 3 * model_width], preferred_element_type=jnp.float32
    ).astype(jnp.bfloat16)
    query_heads = projected[:, :model_width].reshape(head_shape)
    key_heads = projected[:, model_width : 2 * model_width].reshape(head_shape)
    value_heads = projected[:, 2 * model_width :].reshape(head_shape)

    def attend_forward(pieces):
        query_one, key_one, value_one, length = pieces
        scores = masked_scores(query_one, key_one, rel_bias, length)
        row_max = jnp.max(scores, axis=-1, keepdims=True)
        exp_total = jnp.sum(jnp.exp(scores - row_max), axis=-1, keepdims=True)
        log_total = row_max + jnp.log(exp_total)
        weights_soft = jnp.exp(scores - log_total).astype(jnp.bfloat16)
        attended_one = jnp.einsum(
            "hqk,khd->qhd", weights_soft, value_one, preferred_element_type=jnp.float32
        )
        return (attended_one.astype(jnp.bfloat16), log_total)

    attended_heads, log_totals = lax.map(
        attend_forward, (query_heads, key_heads, value_heads, seq_lengths)
    )
    attended_rows = attended_heads.reshape(-1, model_width)
    middle = rows_in + jnp.dot(
        attended_rows,
        full_packed[:, 3 * model_width : 4 * model_width],
        preferred_element_type=jnp.float32,
    )
    scale_two = norm_scale(middle)
    normed_two = (middle * scale_two * gain_two).astype(jnp.bfloat16)
    gate_up = jnp.dot(
        normed_two, full_packed[:, 4 * model_width :], preferred_element_type=jnp.float32
    )

    def gelu_product(gate_part, up_part):
        return jax.nn.gelu(gate_part, approximate=True) * up_part

    hidden_full, gelu_pull = jax.vjp(
        gelu_product, gate_up[:, :hidden_width], gate_up[:, hidden_width:]
    )
    hidden = hidden_full.astype(jnp.bfloat16)
    result = middle + jnp.dot(hidden, full_down, preferred_element_type=jnp.float32)
    layer_output = (
        (result * row_valid).astype(jnp.bfloat16).reshape(seq_count, seq_len, model_width)
    )
    full_weights = (
        lax.all_gather(shards[0], "fsdp", axis=0, tiled=True),
        lax.all_gather(shards[1], "fsdp", axis=0, tiled=True),
        lax.all_gather(shards[2], "fsdp", axis=0, tiled=True),
        lax.all_gather(shards[3], "fsdp", axis=0, tiled=True),
        lax.all_gather(shards[4], "fsdp", axis=0, tiled=True),
    )
    full_packed, full_down, gain_one, gain_two, rel_bias = unpack_weights(
        full_weights, onehot, seq_len
    )
    upstream = cotangent.reshape(-1, model_width).astype(jnp.float32) * row_valid
    upstream_low = upstream.astype(jnp.bfloat16)
    d_hidden = against_rows(upstream_low, full_down)
    d_gate, d_up = gelu_pull(d_hidden)
    d_gate_up = jnp.concatenate((d_gate, d_up), axis=1).astype(jnp.bfloat16)
    d_normed_two = against_rows(d_gate_up, full_packed[:, 4 * model_width :])
    gain_two_grad = jnp.sum(d_normed_two * middle * scale_two, axis=0)
    d_middle = upstream + norm_back(middle, scale_two, gain_two, d_normed_two)
    d_branch = d_middle.astype(jnp.bfloat16)
    d_attended = against_rows(d_branch, full_packed[:, 3 * model_width : 4 * model_width]).astype(
        jnp.bfloat16
    )

    def attend_backward(pieces):
        query_one, key_one, value_one, length, log_total, d_attended_one = pieces
        scores = masked_scores(query_one, key_one, rel_bias, length)
        probs = jnp.exp(scores - log_total)
        probs_low = probs.astype(jnp.bfloat16)
        d_value = jnp.einsum(
            "hqk,qhd->khd", probs_low, d_attended_one, preferred_element_type=jnp.float32
        )
        d_probs = jnp.einsum(
            "qhd,khd->hqk", d_attended_one, value_one, preferred_element_type=jnp.float32
        )
        inner = jnp.sum(probs * d_probs, axis=-1, keepdims=True)
        d_scores = (probs * (d_probs - inner)).astype(jnp.bfloat16)
        d_query = jnp.einsum("hqk,khd->qhd", d_scores, key_one, preferred_element_type=jnp.float32)
        d_key = jnp.einsum("hqk,qhd->khd", d_scores, query_one, preferred_element_type=jnp.float32)
        d_bias = against_rows(d_scores.reshape(HEADS, -1), onehot_low)
        return (
            (
                d_query.astype(jnp.bfloat16),
                d_key.astype(jnp.bfloat16),
                d_value.astype(jnp.bfloat16),
            ),
            d_bias,
        )

    (d_query_all, d_key_all, d_value_all), d_bias_all = lax.map(
        attend_backward,
        (
            query_heads,
            key_heads,
            value_heads,
            seq_lengths,
            log_totals,
            d_attended.reshape(head_shape),
        ),
    )
    d_qkv = jnp.concatenate(
        (
            d_query_all.reshape(-1, model_width),
            d_key_all.reshape(-1, model_width),
            d_value_all.reshape(-1, model_width),
        ),
        axis=1,
    )
    d_normed = against_rows(d_qkv, full_packed[:, : 3 * model_width])
    gain_one_grad = jnp.sum(d_normed * rows_in * scale_one, axis=0)
    d_rows = d_middle + norm_back(rows_in, scale_one, gain_one, d_normed)
    d_dealt = d_rows.astype(jnp.bfloat16).reshape(seq_count, seq_len, model_width)
    returned_rows = lax.all_to_all(d_dealt, "fsdp", split_axis=1, concat_axis=0, tiled=True)
    tokens_grad = returned_rows[jnp.argsort(permutation)]
    packed_grad = lax.psum_scatter(
        jnp.concatenate(
            (
                rows_product(normed, d_qkv),
                jnp.concatenate(
                    (rows_product(attended_rows, d_branch), rows_product(normed_two, d_gate_up)),
                    axis=1,
                ),
            ),
            axis=1,
        ),
        "fsdp",
        scatter_dimension=0,
        tiled=True,
    )
    mixer_grad = packed_grad[:, : 3 * model_width]
    branch_grad = packed_grad[:, 3 * model_width :]
    down_grad = lax.psum_scatter(
        rows_product(hidden, upstream_low), "fsdp", scatter_dimension=0, tiled=True
    )
    table_sum = jnp.sum(d_bias_all, axis=0).T.reshape(-1)
    gain_attention_grad, gain_feedforward_grad, table_grad = (
        lax.psum_scatter(gain_one_grad, "fsdp", scatter_dimension=0, tiled=True),
        lax.psum_scatter(gain_two_grad, "fsdp", scatter_dimension=0, tiled=True),
        lax.psum_scatter(table_sum, "fsdp", scatter_dimension=0, tiled=True),
    )
    return (
        layer_output,
        tokens_grad,
        mixer_grad[:, :model_width],
        mixer_grad[:, model_width : 2 * model_width],
        mixer_grad[:, 2 * model_width :],
        branch_grad[:, :model_width],
        branch_grad[:, model_width : model_width + hidden_width],
        branch_grad[:, model_width + hidden_width :],
        down_grad,
        gain_attention_grad,
        gain_feedforward_grad,
        table_grad,
    )


MESH = pl.DeviceIdType.MESH
AXIS = "fsdp"


def place():
    me = lax.axis_index(AXIS)
    c, x, y, z = me % 2, (me // 2) % 2, (me // 4) % 2, me // 8
    return me, c, x, y, z


def greet(nc, nx, ny, n1, n2, mid):
    bar = pltpu.get_barrier_semaphore()
    for peer in (nc, nx, ny, n1):
        pl.semaphore_signal(bar, inc=1, device_id=(peer,), device_id_type=MESH)

    @pl.when(mid)
    def _():
        pl.semaphore_signal(bar, inc=1, device_id=(n2,), device_id_type=MESH)

    pl.semaphore_wait(bar, 4 + mid.astype(jnp.int32))


def gather_kernel(a_ref, o_ref, own_sem, ssem, rsem):
    me, c, x, y, z = place()
    half = a_ref.shape[1] // 2
    mid = (z == 1) | (z == 2)
    z1, z2, z3 = z + 1 - 2 * (z % 2), 2 - z // 2, 3 - 3 * (z // 2)
    nc, nx, ny = me + 1 - 2 * c, me + 2 - 4 * x, me + 4 - 8 * y
    n1, n2 = me + 8 * (z1 - z), me + 8 * (z2 - z)
    greet(nc, nx, ny, n1, n2, mid)
    own = pltpu.make_async_copy(a_ref, o_ref.at[me], own_sem)
    own.start()
    cols = (pl.ds(0, half), pl.ds(half, half))
    sends = []
    count = [0]

    def push(part, block, peer, mine=False, when=None):
        k = count[0]
        count[0] += 1
        src = a_ref.at[:, cols[part]] if mine else o_ref.at[block, :, cols[part]]

        def copy():
            return pltpu.make_async_remote_copy(
                src, o_ref.at[block, :, cols[part]], ssem.at[k], rsem.at[part, block],
                device_id=(peer,), device_id_type=MESH)

        def start():
            copy().start()

        def finish():
            copy().wait_send()
        if when is None:
            start()
        else:
            pl.when(when)(start)
        sends.append((finish, when))

    def arrive(part, block):
        pltpu.make_async_remote_copy(
            o_ref.at[block, :, cols[part]], o_ref.at[block, :, cols[part]], ssem.at[0],
            rsem.at[part, block], device_id=(nc,), device_id_type=MESH).wait_recv()

    for part in (0, 1):
        push(part, me, n1, True)
        push(part, me, n2, True, mid)
        push(part, me, (nx, ny)[part], True)
        push(part, me, (ny, nx)[part], True)
    for part in (0, 1):
        push(part, me, nc, True)

    zs = (z, z1, z2, z3)
    zdel = [8 * (zz - z) for zz in zs]

    def from_z(part, j):
        b = me + zdel[j]
        arrive(part, b)
        push(part, b, n2 if j == 1 else n1, when=mid)
        push(part, b, (nx, ny)[part])
        push(part, b, (ny, nx)[part])
        push(part, b, nc)

    def from_first(part, j):
        b = (nx, ny)[part] + zdel[j]
        arrive(part, b)
        push(part, b, (ny, nx)[part])
        push(part, b, nc)

    def from_last(part, j, diag):
        b = (ny, nx)[part] + zdel[j]
        if diag:
            b = nx + ny - me + zdel[j]
        arrive(part, b)
        push(part, b, nc)

    for j in range(4):
        if j:
            for part in (0, 1):
                from_z(part, j)
        for part in (0, 1):
            from_first(part, j)
        if j:
            for part in (0, 1):
                from_last(part, j - 1, False)
    for part in (0, 1):
        from_last(part, 3, False)
    for j in range(4):
        for part in (0, 1):
            from_last(part, j, True)
    for j in range(4):
        for base in (nc, nc + nx - me, nc + ny - me, nc + nx + ny - 2 * me):
            for part in (0, 1):
                arrive(part, base + zdel[j])
    own.wait()
    for finish, when in sends:
        if when is None:
            finish()
        else:
            pl.when(when)(finish)


def gather(block, cid=0):
    rows, width = block.shape
    n_sends = 10 + 3 * 2 * 4 + 4 * 2 * 2 + 8 * 2
    return pl.pallas_call(
        gather_kernel,
        out_shape=jax.ShapeDtypeStruct((32, rows, width), block.dtype),
        in_specs=[pl.BlockSpec(memory_space=pl.ANY)],
        out_specs=pl.BlockSpec(memory_space=pl.ANY),
        scratch_shapes=[
            pltpu.SemaphoreType.DMA,
            pltpu.SemaphoreType.DMA((n_sends,)),
            pltpu.SemaphoreType.DMA((2, 32)),
        ],
        name="gather_rows",
        compiler_params=pltpu.CompilerParams(collective_id=cid, has_side_effects=True),
    )(block)


def scatter_kernel(p_ref, o_ref, m_ref, s_ref, first_ref, second_ref, za_ref, zb_ref,
                   lsem, ssem, csem, fsem, gsem, zasem, zbsem):
    me, c, x, y, z = place()
    rows, width = o_ref.shape
    half = width // 2
    mid = (z == 1) | (z == 2)
    end = jnp.logical_not(mid)
    z1, z2, z3 = z + 1 - 2 * (z % 2), 2 - z // 2, 3 - 3 * (z // 2)
    nc, nx, ny = me + 1 - 2 * c, me + 2 - 4 * x, me + 4 - 8 * y
    n1, n2 = me + 8 * (z1 - z), me + 8 * (z2 - z)
    diag = nx + ny - me
    greet(nc, nx, ny, n1, n2, mid)
    cols = (pl.ds(0, half), pl.ds(half, half))
    zs = (z, z1, z2, z3)
    sends = []
    count = [0]

    def push(src, dst, rsem, peer, when=None):
        k = count[0]
        count[0] += 1

        def copy():
            return pltpu.make_async_remote_copy(src, dst, ssem.at[k], rsem, device_id=(peer,), device_id_type=MESH)
        if when is None:
            copy().start()
        else:
            pl.when(when)(lambda: copy().start())
        sends.append((lambda: copy().wait_send(), when))

    def arrive(dst, rsem):
        pltpu.make_async_remote_copy(dst, dst, ssem.at[0], rsem, device_id=(nc,), device_id_type=MESH).wait_recv()

    def add_into(dst, src, extra=None):
        def step(i, _):
            r = pl.ds(pl.multiple_of(i * 16, 16), 16)
            v = dst[r, :].astype(jnp.float32) + src[r, :].astype(jnp.float32)
            if extra is not None:
                v = v + extra[r, :].astype(jnp.float32)
            dst[r, :] = v.astype(dst.dtype)
            return _
        lax.fori_loop(0, rows // 16, step, 0)

    plane = (me, nx, ny, diag)
    order = [(q, j) for q in (3, 1, 2, 0) for j in (3, 2, 1, 0)]
    for q, j in order:
        b = plane[q] + 8 * (zs[j] - z)
        slot = q * 4 + zs[j]
        pltpu.make_async_copy(p_ref.at[b], m_ref.at[slot], lsem.at[slot]).start()
        push(p_ref.at[b + nc - me], s_ref.at[slot], csem.at[slot], nc)
    first_peer, second_peer = (ny, nx), (nx, ny)

    def joined(q, j):
        slot = q * 4 + zs[j]
        pltpu.make_async_copy(p_ref.at[0], m_ref.at[slot], lsem.at[slot]).wait()
        arrive(s_ref.at[slot], csem.at[slot])
        add_into(m_ref.at[slot], s_ref.at[slot])

    def to_first(part, q, j):
        far = 4 if q == 3 else 0
        push(m_ref.at[q * 4 + zs[j], :, cols[part]], first_ref.at[part, far + zs[j]],
             fsem.at[part, far + zs[j]], first_peer[part])

    for j in (3, 2, 1, 0):
        joined(3, j)
        to_first(0, 3, j)
        to_first(1, 3, j)
    for j in (3, 2, 1, 0):
        joined(2, j)
        to_first(0, 2, j)
        joined(1, j)
        to_first(1, 1, j)
    for j in (3, 2, 1, 0):
        for part in (0, 1):
            arrive(first_ref.at[part, 4 + zs[j]], fsem.at[part, 4 + zs[j]])
            q = (1, 2)[part]
            m = m_ref.at[q * 4 + zs[j], :, cols[part]]
            add_into(m, first_ref.at[part, 4 + zs[j]])
            push(m, second_ref.at[part, zs[j]], gsem.at[part, zs[j]], second_peer[part])
        joined(0, j)

    def plane_sum(part, j):
        m = m_ref.at[zs[j], :, cols[part]]
        arrive(first_ref.at[part, zs[j]], fsem.at[part, zs[j]])
        arrive(second_ref.at[part, zs[j]], gsem.at[part, zs[j]])
        add_into(m, first_ref.at[part, zs[j]], second_ref.at[part, zs[j]])
        return m
    for part in (0, 1):
        pass
    for j in (3, 2, 1, 0):
        for part in (0, 1):
            m = plane_sum(part, j)
            if j == 3:
                push(m, za_ref.at[part, 0], zasem.at[part, 0], n1, end)

                @pl.when(mid)
                def _():
                    arrive(za_ref.at[part, 0], zasem.at[part, 0])
                    add_into(m, za_ref.at[part, 0])
                push(m, zb_ref.at[part, 0], zbsem.at[part, 0], n2, mid)
            elif j == 2:
                push(m, za_ref.at[part, 1], zasem.at[part, 1], n1, end)

                @pl.when(mid)
                def _():
                    arrive(za_ref.at[part, 1], zasem.at[part, 1])
                    add_into(m, za_ref.at[part, 1])
                push(m, zb_ref.at[part, 1], zbsem.at[part, 1], n2, mid)
            elif j == 1:
                push(m, za_ref.at[part, 2], zasem.at[part, 2], n1, end)

                @pl.when(mid)
                def _():
                    arrive(zb_ref.at[part, 0], zbsem.at[part, 0])
                    add_into(m, zb_ref.at[part, 0])
                push(m, zb_ref.at[part, 0], zbsem.at[part, 0], n1, mid)
    for part in (0, 1):
        m = m_ref.at[zs[0], :, cols[part]]
        o = o_ref.at[:, cols[part]]

        def total(*more):
            def step(i, _):
                r = pl.ds(pl.multiple_of(i * 16, 16), 16)
                v = m[r, :].astype(jnp.float32)
                for e in more:
                    v = v + e[r, :].astype(jnp.float32)
                o[r, :] = v
                return _
            lax.fori_loop(0, rows // 16, step, 0)

        @pl.when(mid)
        def _():
            arrive(za_ref.at[part, 2], zasem.at[part, 2])
            arrive(zb_ref.at[part, 1], zbsem.at[part, 1])
            total(za_ref.at[part, 2], zb_ref.at[part, 1])

        @pl.when(end)
        def _():
            arrive(zb_ref.at[part, 0], zbsem.at[part, 0])
            total(zb_ref.at[part, 0])
    for finish, when in sends:
        if when is None:
            finish()
        else:
            pl.when(when)(finish)


def scatter(parts, cid=1):
    n, rows, width = parts.shape
    dt = parts.dtype
    half = width // 2
    return pl.pallas_call(
        scatter_kernel,
        out_shape=jax.ShapeDtypeStruct((rows, width), jnp.float32),
        in_specs=[pl.BlockSpec(memory_space=pl.ANY)],
        out_specs=pl.BlockSpec(memory_space=pltpu.VMEM),
        scratch_shapes=[
            pltpu.VMEM((16, rows, width), dt),
            pltpu.VMEM((16, rows, width), dt),
            pltpu.VMEM((2, 8, rows, half), dt),
            pltpu.VMEM((2, 4, rows, half), dt),
            pltpu.VMEM((2, 3, rows, half), dt),
            pltpu.VMEM((2, 2, rows, half), dt),
            pltpu.SemaphoreType.DMA((16,)),
            pltpu.SemaphoreType.DMA((16 + 16 + 8 + 12,)),
            pltpu.SemaphoreType.DMA((16,)),
            pltpu.SemaphoreType.DMA((2, 8)),
            pltpu.SemaphoreType.DMA((2, 4)),
            pltpu.SemaphoreType.DMA((2, 3)),
            pltpu.SemaphoreType.DMA((2, 2)),
        ],
        name="scatter_rows",
        compiler_params=pltpu.CompilerParams(collective_id=cid, has_side_effects=True, vmem_limit_bytes=56 * 2**20),
    )(parts)


def exchange(blocks):
    return lax.all_to_all(blocks, AXIS, split_axis=0, concat_axis=0, tiled=True)


def dot(left, right):
    return jnp.dot(left, right, preferred_element_type=jnp.float32)


def select(mask, rows):
    return dot(mask.astype(jnp.bfloat16), rows).astype(jnp.bfloat16)


def natural(rows, count, tiles):
    width = rows.shape[-1]
    return (
        rows.reshape(count, tiles, -1, width).transpose(1, 0, 2, 3).reshape(tiles, -1, width)
    )


def dealt_order(rows, count):
    tiles, length, width = rows.shape
    return (
        rows.reshape(tiles, count, length // count, width)
        .transpose(1, 0, 2, 3)
        .reshape(-1, width)
    )


def windows(tiled):
    edge = jnp.zeros_like(tiled[:1])
    padded = jnp.concatenate((edge, tiled, edge), axis=0)
    return jnp.concatenate((padded[:-2], padded[1:-1], padded[2:]), axis=1)


def unwindow(wide):
    length = wide.shape[1] // 3
    edge = jnp.zeros_like(wide[:1, :length])
    return (
        jnp.concatenate((wide[1:, :length], edge), axis=0)
        + wide[:, length : 2 * length]
        + jnp.concatenate((edge, wide[:-1, 2 * length :]), axis=0)
    )


def batched(left, right, left_dim, right_dim):
    return lax.dot_general(
        left,
        right,
        (((left_dim,), (right_dim,)), ((0,), (0,))),
        preferred_element_type=jnp.float32,
    )


def body(
    tokens,
    lengths,
    permutation,
    query_weight,
    key_weight,
    value_weight,
    out_weight,
    gate_weight,
    up_weight,
    down_weight,
    gain_attention,
    gain_feedforward,
    bias_table,
    cotangent,
):
    me = lax.axis_index(AXIS)
    count = tokens.shape[0]
    grain = tokens.shape[1]
    length = cotangent.shape[1]
    width = tokens.shape[2]
    shard = query_weight.shape[0]
    hidden_width = gate_weight.shape[1] // count
    head = HEAD_DIM
    total = 3 * count * length // 5
    tiles = -(-total // length)
    slots = tiles * grain

    columns = jnp.concatenate(
        (
            query_weight.reshape(shard, count, head),
            key_weight.reshape(shard, count, head),
            value_weight.reshape(shard, count, head),
            gate_weight.reshape(shard, count, hidden_width),
            up_weight.reshape(shard, count, hidden_width),
        ),
        axis=2,
    )
    columns = exchange(columns.transpose(1, 0, 2)).reshape(count * shard, -1)
    qkv_columns, gate_up_columns = columns[:, : 3 * head], columns[:, 3 * head :]

    small = jnp.concatenate((gain_attention, gain_feedforward, bias_table))
    small = jnp.pad(small, (0, width - small.shape[0]))
    small = jnp.broadcast_to(small, (count, 1, width))
    came = exchange(jnp.concatenate((tokens[permutation], small), axis=1))
    dealt = came[:, :grain].reshape(length, width)
    gain_one = came[:, grain, :shard].reshape(-1).astype(jnp.float32)
    gain_two = came[:, grain, shard : 2 * shard].reshape(-1).astype(jnp.float32)
    table = came[:, grain, 2 * shard : 2 * shard + HEADS]

    dealt_lengths = lengths[permutation]
    ends = jnp.cumsum(dealt_lengths)
    starts = ends - dealt_lengths
    my_start, my_length = starts[me], dealt_lengths[me]
    place_in = jnp.arange(length, dtype=jnp.int32)
    turn = (
        (place_in[:, None] - my_start) % length == place_in[None, :]
    ) & (place_in[None, :] < my_length)
    rolled = select(turn, jnp.concatenate((dealt, cotangent[0]), axis=1))
    came = exchange(rolled.reshape(count, grain, 2 * width)).reshape(length, 2 * width)
    slot_ids = jnp.arange(slots, dtype=jnp.int32)
    packed_ids = slot_ids // grain * length + me * grain + slot_ids % grain
    source_seq = jnp.sum((packed_ids[:, None] >= ends[None, :]).astype(jnp.int32), axis=1)
    pick = (source_seq * grain + slot_ids % grain)[:, None] == place_in[None, :]
    blocks = select(pick, came)
    rows_in = blocks[:, :width].astype(jnp.float32)
    upstream_low = blocks[:, width:]
    upstream = upstream_low.astype(jnp.float32)

    all_ids = jnp.arange(tiles * length, dtype=jnp.int32)
    segment = jnp.sum((all_ids[:, None] >= ends[None, :]).astype(jnp.int32), axis=1) + 1
    segment = segment.reshape(tiles, length, 1)
    same = segment == windows(segment).reshape(tiles, 1, 3 * length)
    relative = (
        jnp.arange(3 * length, dtype=jnp.int32)[None, :] - length - place_in[:, None]
    ).reshape(-1)
    onehot = bucket_index(relative)[None, :] == jnp.arange(BUCKETS, dtype=jnp.int32)[:, None]
    head_table = lax.dynamic_slice_in_dim(table, me, 1, axis=1)
    rel_bias = dot(head_table.T, onehot.astype(jnp.bfloat16)).reshape(1, length, 3 * length)

    scale_one = norm_scale(rows_in)
    normed = (rows_in * scale_one * gain_one).astype(jnp.bfloat16)
    normed_all = gather(normed).reshape(-1, width)
    qkv = natural(dot(normed_all, qkv_columns).astype(jnp.bfloat16), count, tiles)
    query, key, value = qkv[:, :, :head], qkv[:, :, head : 2 * head], qkv[:, :, 2 * head :]
    key_window, value_window = windows(key), windows(value)
    scores = jnp.where(same, batched(query, key_window, 2, 2) + rel_bias, masked_score)
    probs = jax.nn.softmax(scores, axis=-1)
    probs_low = probs.astype(jnp.bfloat16)
    attended = dealt_order(batched(probs_low, value_window, 2, 1).astype(jnp.bfloat16), count)
    branch = scatter(dot(attended, out_weight).astype(jnp.bfloat16).reshape(count, slots, width))
    middle = rows_in + branch

    scale_two = norm_scale(middle)
    normed_two = (middle * scale_two * gain_two).astype(jnp.bfloat16)
    normed_two_all = gather(normed_two).reshape(-1, width)
    gate_up = dot(normed_two_all, gate_up_columns)

    def gelu_product(gate_part, up_part):
        return jax.nn.gelu(gate_part, approximate=True) * up_part

    hidden_full, gelu_pull = jax.vjp(
        gelu_product, gate_up[:, :hidden_width], gate_up[:, hidden_width:]
    )
    hidden = hidden_full.astype(jnp.bfloat16)
    down = scatter(dot(hidden, down_weight).astype(jnp.bfloat16).reshape(count, slots, width))
    result = (middle + down).astype(jnp.bfloat16)

    upstream_all = gather(upstream_low).reshape(-1, width)
    d_gate, d_up = gelu_pull(against_rows(upstream_all, down_weight))
    d_gate_up = jnp.concatenate((d_gate, d_up), axis=1).astype(jnp.bfloat16)
    down_grad = rows_product(hidden, upstream_all)
    gate_up_grad = rows_product(normed_two_all, d_gate_up)
    d_normed_two = scatter(
        against_rows(d_gate_up, gate_up_columns)
        .astype(jnp.bfloat16)
        .reshape(count, slots, width)
    )
    gain_two_grad = jnp.sum(d_normed_two * middle * scale_two, axis=0)
    d_middle = upstream + norm_back(middle, scale_two, gain_two, d_normed_two)

    d_branch_all = gather(d_middle.astype(jnp.bfloat16)).reshape(-1, width)
    out_grad = rows_product(attended, d_branch_all)
    d_attended = natural(
        against_rows(d_branch_all, out_weight).astype(jnp.bfloat16), count, tiles
    )
    d_value = unwindow(batched(probs_low, d_attended, 1, 1))
    d_probs = batched(d_attended, value_window, 2, 2)
    inner = jnp.sum(probs * d_probs, axis=-1, keepdims=True)
    d_scores = (probs * (d_probs - inner)).astype(jnp.bfloat16)
    d_query = batched(d_scores, key_window, 2, 1)
    d_key = unwindow(batched(d_scores, query, 1, 1))
    d_bias = jnp.sum(d_scores.astype(jnp.float32), axis=0).reshape(1, -1)
    table_sum = jnp.sum(jnp.where(onehot, d_bias, 0.0), axis=1)
    d_qkv = dealt_order(
        jnp.concatenate((d_query, d_key, d_value), axis=2).astype(jnp.bfloat16), count
    )
    qkv_grad = rows_product(normed_all, d_qkv)
    d_normed = scatter(
        against_rows(d_qkv, qkv_columns).astype(jnp.bfloat16).reshape(count, slots, width)
    )
    gain_one_grad = jnp.sum(d_normed * rows_in * scale_one, axis=0)
    d_dealt = (d_middle + norm_back(rows_in, scale_one, gain_one, d_normed)).astype(jnp.bfloat16)

    turned = starts + (me * grain + jnp.arange(grain, dtype=jnp.int32)[:, None] - starts) % length
    back_slot = (turned // length * grain + jnp.arange(grain, dtype=jnp.int32)[:, None]).T
    spread = back_slot.reshape(-1, 1) == slot_ids[None, :]
    going = select(spread, jnp.concatenate((result, d_dealt), axis=1))
    came = exchange(going.reshape(count, grain, 2 * width)).reshape(length, 2 * width)
    came = select(turn.T, came)
    layer_output = came[None, :, :width]
    tokens_grad = exchange(came[:, width:].reshape(count, grain, width))[jnp.argsort(permutation)]

    going = jnp.concatenate((qkv_grad, gate_up_grad), axis=1).astype(jnp.bfloat16)
    grads = exchange(going.reshape(count, shard, -1)).astype(jnp.float32)

    def owned(first, size):
        return grads[:, :, first : first + size].transpose(1, 0, 2).reshape(shard, -1)

    going = jnp.concatenate(
        (
            gain_one_grad.reshape(count, shard),
            gain_two_grad.reshape(count, shard),
            table_sum.reshape(count, 1),
        ),
        axis=1,
    )
    came = exchange(jnp.pad(going, ((0, 0), (0, 256 - going.shape[1]))))
    return (
        layer_output,
        tokens_grad,
        owned(0, head),
        owned(head, head),
        owned(2 * head, head),
        out_grad,
        owned(3 * head, hidden_width),
        owned(3 * head + hidden_width, hidden_width),
        down_grad,
        jnp.sum(came[:, :shard], axis=0),
        jnp.sum(came[:, shard : 2 * shard], axis=0),
        came[:, 2 * shard],
    )


def solution(mesh):
    placed = (
        P(None, "fsdp", None),
        P(),
        P(),
        P("fsdp", None),
        P("fsdp", None),
        P("fsdp", None),
        P("fsdp", None),
        P("fsdp", None),
        P("fsdp", None),
        P("fsdp", None),
        P("fsdp"),
        P("fsdp"),
        P("fsdp"),
        P("fsdp", None, None),
    )
    return jax.shard_map(
        body if mesh.shape[AXIS] == 32 else body_any,
        mesh=mesh,
        in_specs=placed,
        out_specs=(
            P("fsdp", None, None),
            P(None, "fsdp", None),
            P("fsdp", None),
            P("fsdp", None),
            P("fsdp", None),
            P("fsdp", None),
            P("fsdp", None),
            P("fsdp", None),
            P("fsdp", None),
            P("fsdp"),
            P("fsdp"),
            P("fsdp"),
        ),
        check_vma=False,
    )
```

```python
import functools

import jax
import jax.numpy as jnp
from jax import lax
from jax.experimental import pallas as pl
from jax.experimental.pallas import tpu as pltpu
from jax.sharding import PartitionSpec as P

HEADS = 32
HEAD_DIM = 64
BUCKETS = 32


EPSILON = 1e-06
masked_score = -1000000000.0
HIGHEST = lax.Precision.HIGHEST


def bucket_index(relative):
    half_buckets = BUCKETS // 2
    exact_count = half_buckets // 2
    distance = jnp.abs(relative)
    side_offset = jnp.where(relative > 0, half_buckets, 0).astype(jnp.int32)
    square = distance * distance
    far_bucket = jnp.full_like(distance, exact_count)
    for doubling in range(1, half_buckets - exact_count):
        far_bucket = far_bucket + (square >= exact_count * exact_count * 2**doubling).astype(
            jnp.int32
        )
    return side_offset + jnp.where(distance < exact_count, distance, far_bucket)


def bucket_onehot(seq_len):
    positions = jnp.arange(seq_len, dtype=jnp.int32)
    relative = (positions[None, :] - positions[:, None]).reshape(-1)
    bucket_ids = jnp.arange(BUCKETS, dtype=jnp.int32)
    return (bucket_index(relative)[None, :] == bucket_ids[:, None]).astype(jnp.float32)


def norm_scale(values):
    return lax.rsqrt(jnp.mean(values * values, axis=-1, keepdims=True) + EPSILON)


def norm_back(values, scale, gain_vec, d_norm):
    weighted = gain_vec * d_norm
    return scale * weighted - values * (scale * scale * scale) * jnp.mean(
        weighted * values, axis=-1, keepdims=True
    )


def rows_product(left, right):
    return lax.dot_general(
        left, right, (((0,), (0,)), ((), ())), preferred_element_type=jnp.float32
    )


def against_rows(left, right):
    return lax.dot_general(
        left, right, (((1,), (1,)), ((), ())), preferred_element_type=jnp.float32
    )


def masked_scores(query_heads, key_heads, rel_bias, length):
    scores = (
        jnp.einsum("qhd,khd->hqk", query_heads, key_heads, preferred_element_type=jnp.float32)
        + rel_bias
    )
    key_valid = jnp.arange(key_heads.shape[0], dtype=jnp.int32) < length
    return jnp.where(key_valid[None, None, :], scores, masked_score)


def unpack_weights(full_weights, onehot, seq_len):
    table_full = full_weights[4].astype(jnp.float32).reshape(BUCKETS, HEADS)
    rel_bias = jnp.dot(table_full.T, onehot, precision=HIGHEST).reshape(HEADS, seq_len, seq_len)
    return (
        full_weights[0],
        full_weights[1],
        full_weights[2].astype(jnp.float32),
        full_weights[3].astype(jnp.float32),
        rel_bias,
    )


def body_any(
    tokens,
    lengths,
    permutation,
    query_weight,
    key_weight,
    value_weight,
    out_weight,
    gate_weight,
    up_weight,
    down_weight,
    gain_attention,
    gain_feedforward,
    bias_table,
    cotangent,
):
    model_width = query_weight.shape[1]
    hidden_width = gate_weight.shape[1]
    packed = jnp.concatenate(
        (query_weight, key_weight, value_weight, out_weight, gate_weight, up_weight), axis=1
    )
    shards = (packed, down_weight, gain_attention, gain_feedforward, bias_table)
    full_weights = (
        lax.all_gather(shards[0], "fsdp", axis=0, tiled=True),
        lax.all_gather(shards[1], "fsdp", axis=0, tiled=True),
        lax.all_gather(shards[2], "fsdp", axis=0, tiled=True),
        lax.all_gather(shards[3], "fsdp", axis=0, tiled=True),
        lax.all_gather(shards[4], "fsdp", axis=0, tiled=True),
    )
    reordered = tokens[permutation]
    dealt = lax.all_to_all(reordered, "fsdp", split_axis=0, concat_axis=1, tiled=True)
    seq_count = dealt.shape[0]
    seq_len = dealt.shape[1]
    local_ids = lax.dynamic_slice_in_dim(permutation, lax.axis_index("fsdp") * seq_count, seq_count)
    seq_lengths = lengths[local_ids]
    positions = jnp.arange(seq_len, dtype=jnp.int32)
    row_valid = (positions[None, :] < seq_lengths[:, None]).astype(jnp.float32).reshape(-1, 1)
    onehot = bucket_onehot(seq_len)
    onehot_low = onehot.astype(jnp.bfloat16)
    full_packed, full_down, gain_one, gain_two, rel_bias = unpack_weights(
        full_weights, onehot, seq_len
    )
    head_shape = (seq_count, seq_len, HEADS, HEAD_DIM)
    rows_in = dealt.reshape(-1, model_width).astype(jnp.float32)
    scale_one = norm_scale(rows_in)
    normed = (rows_in * scale_one * gain_one).astype(jnp.bfloat16)
    projected = jnp.dot(
        normed, full_packed[:, : 3 * model_width], preferred_element_type=jnp.float32
    ).astype(jnp.bfloat16)
    query_heads = projected[:, :model_width].reshape(head_shape)
    key_heads = projected[:, model_width : 2 * model_width].reshape(head_shape)
    value_heads = projected[:, 2 * model_width :].reshape(head_shape)

    def attend_forward(pieces):
        query_one, key_one, value_one, length = pieces
        scores = masked_scores(query_one, key_one, rel_bias, length)
        row_max = jnp.max(scores, axis=-1, keepdims=True)
        exp_total = jnp.sum(jnp.exp(scores - row_max), axis=-1, keepdims=True)
        log_total = row_max + jnp.log(exp_total)
        weights_soft = jnp.exp(scores - log_total).astype(jnp.bfloat16)
        attended_one = jnp.einsum(
            "hqk,khd->qhd", weights_soft, value_one, preferred_element_type=jnp.float32
        )
        return (attended_one.astype(jnp.bfloat16), log_total)

    attended_heads, log_totals = lax.map(
        attend_forward, (query_heads, key_heads, value_heads, seq_lengths)
    )
    attended_rows = attended_heads.reshape(-1, model_width)
    middle = rows_in + jnp.dot(
        attended_rows,
        full_packed[:, 3 * model_width : 4 * model_width],
        preferred_element_type=jnp.float32,
    )
    scale_two = norm_scale(middle)
    normed_two = (middle * scale_two * gain_two).astype(jnp.bfloat16)
    gate_up = jnp.dot(
        normed_two, full_packed[:, 4 * model_width :], preferred_element_type=jnp.float32
    )

    def gelu_product(gate_part, up_part):
        return jax.nn.gelu(gate_part, approximate=True) * up_part

    hidden_full, gelu_pull = jax.vjp(
        gelu_product, gate_up[:, :hidden_width], gate_up[:, hidden_width:]
    )
    hidden = hidden_full.astype(jnp.bfloat16)
    result = middle + jnp.dot(hidden, full_down, preferred_element_type=jnp.float32)
    layer_output = (
        (result * row_valid).astype(jnp.bfloat16).reshape(seq_count, seq_len, model_width)
    )
    full_weights = (
        lax.all_gather(shards[0], "fsdp", axis=0, tiled=True),
        lax.all_gather(shards[1], "fsdp", axis=0, tiled=True),
        lax.all_gather(shards[2], "fsdp", axis=0, tiled=True),
        lax.all_gather(shards[3], "fsdp", axis=0, tiled=True),
        lax.all_gather(shards[4], "fsdp", axis=0, tiled=True),
    )
    full_packed, full_down, gain_one, gain_two, rel_bias = unpack_weights(
        full_weights, onehot, seq_len
    )
    upstream = cotangent.reshape(-1, model_width).astype(jnp.float32) * row_valid
    upstream_low = upstream.astype(jnp.bfloat16)
    d_hidden = against_rows(upstream_low, full_down)
    d_gate, d_up = gelu_pull(d_hidden)
    d_gate_up = jnp.concatenate((d_gate, d_up), axis=1).astype(jnp.bfloat16)
    d_normed_two = against_rows(d_gate_up, full_packed[:, 4 * model_width :])
    gain_two_grad = jnp.sum(d_normed_two * middle * scale_two, axis=0)
    d_middle = upstream + norm_back(middle, scale_two, gain_two, d_normed_two)
    d_branch = d_middle.astype(jnp.bfloat16)
    d_attended = against_rows(d_branch, full_packed[:, 3 * model_width : 4 * model_width]).astype(
        jnp.bfloat16
    )

    def attend_backward(pieces):
        query_one, key_one, value_one, length, log_total, d_attended_one = pieces
        scores = masked_scores(query_one, key_one, rel_bias, length)
        probs = jnp.exp(scores - log_total)
        probs_low = probs.astype(jnp.bfloat16)
        d_value = jnp.einsum(
            "hqk,qhd->khd", probs_low, d_attended_one, preferred_element_type=jnp.float32
        )
        d_probs = jnp.einsum(
            "qhd,khd->hqk", d_attended_one, value_one, preferred_element_type=jnp.float32
        )
        inner = jnp.sum(probs * d_probs, axis=-1, keepdims=True)
        d_scores = (probs * (d_probs - inner)).astype(jnp.bfloat16)
        d_query = jnp.einsum("hqk,khd->qhd", d_scores, key_one, preferred_element_type=jnp.float32)
        d_key = jnp.einsum("hqk,qhd->khd", d_scores, query_one, preferred_element_type=jnp.float32)
        d_bias = against_rows(d_scores.reshape(HEADS, -1), onehot_low)
        return (
            (
                d_query.astype(jnp.bfloat16),
                d_key.astype(jnp.bfloat16),
                d_value.astype(jnp.bfloat16),
            ),
            d_bias,
        )

    (d_query_all, d_key_all, d_value_all), d_bias_all = lax.map(
        attend_backward,
        (
            query_heads,
            key_heads,
            value_heads,
            seq_lengths,
            log_totals,
            d_attended.reshape(head_shape),
        ),
    )
    d_qkv = jnp.concatenate(
        (
            d_query_all.reshape(-1, model_width),
            d_key_all.reshape(-1, model_width),
            d_value_all.reshape(-1, model_width),
        ),
        axis=1,
    )
    d_normed = against_rows(d_qkv, full_packed[:, : 3 * model_width])
    gain_one_grad = jnp.sum(d_normed * rows_in * scale_one, axis=0)
    d_rows = d_middle + norm_back(rows_in, scale_one, gain_one, d_normed)
    d_dealt = d_rows.astype(jnp.bfloat16).reshape(seq_count, seq_len, model_width)
    returned_rows = lax.all_to_all(d_dealt, "fsdp", split_axis=1, concat_axis=0, tiled=True)
    tokens_grad = returned_rows[jnp.argsort(permutation)]
    packed_grad = lax.psum_scatter(
        jnp.concatenate(
            (
                rows_product(normed, d_qkv),
                jnp.concatenate(
                    (rows_product(attended_rows, d_branch), rows_product(normed_two, d_gate_up)),
                    axis=1,
                ),
            ),
            axis=1,
        ),
        "fsdp",
        scatter_dimension=0,
        tiled=True,
    )
    mixer_grad = packed_grad[:, : 3 * model_width]
    branch_grad = packed_grad[:, 3 * model_width :]
    down_grad = lax.psum_scatter(
        rows_product(hidden, upstream_low), "fsdp", scatter_dimension=0, tiled=True
    )
    table_sum = jnp.sum(d_bias_all, axis=0).T.reshape(-1)
    gain_attention_grad, gain_feedforward_grad, table_grad = (
        lax.psum_scatter(gain_one_grad, "fsdp", scatter_dimension=0, tiled=True),
        lax.psum_scatter(gain_two_grad, "fsdp", scatter_dimension=0, tiled=True),
        lax.psum_scatter(table_sum, "fsdp", scatter_dimension=0, tiled=True),
    )
    return (
        layer_output,
        tokens_grad,
        mixer_grad[:, :model_width],
        mixer_grad[:, model_width : 2 * model_width],
        mixer_grad[:, 2 * model_width :],
        branch_grad[:, :model_width],
        branch_grad[:, model_width : model_width + hidden_width],
        branch_grad[:, model_width + hidden_width :],
        down_grad,
        gain_attention_grad,
        gain_feedforward_grad,
        table_grad,
    )


MESH = pl.DeviceIdType.MESH
AXIS = "fsdp"


def place():
    me = lax.axis_index(AXIS)
    c, x, y, z = me % 2, (me // 2) % 2, (me // 4) % 2, me // 8
    return me, c, x, y, z


def greet(nc, nx, ny, n1, n2, mid):
    bar = pltpu.get_barrier_semaphore()
    for peer in (nc, nx, ny, n1):
        pl.semaphore_signal(bar, inc=1, device_id=(peer,), device_id_type=MESH)

    @pl.when(mid)
    def _():
        pl.semaphore_signal(bar, inc=1, device_id=(n2,), device_id_type=MESH)

    pl.semaphore_wait(bar, 4 + mid.astype(jnp.int32))


def gather_kernel(a_ref, o_ref, own_sem, ssem, rsem):
    me, c, x, y, z = place()
    half = a_ref.shape[1] // 2
    mid = (z == 1) | (z == 2)
    z1, z2, z3 = z + 1 - 2 * (z % 2), 2 - z // 2, 3 - 3 * (z // 2)
    nc, nx, ny = me + 1 - 2 * c, me + 2 - 4 * x, me + 4 - 8 * y
    n1, n2 = me + 8 * (z1 - z), me + 8 * (z2 - z)
    greet(nc, nx, ny, n1, n2, mid)
    own = pltpu.make_async_copy(a_ref, o_ref.at[me], own_sem)
    own.start()
    cols = (pl.ds(0, half), pl.ds(half, half))
    sends = []
    count = [0]

    def push(part, block, peer, mine=False, when=None):
        k = count[0]
        count[0] += 1
        src = a_ref.at[:, cols[part]] if mine else o_ref.at[block, :, cols[part]]

        def copy():
            return pltpu.make_async_remote_copy(
                src, o_ref.at[block, :, cols[part]], ssem.at[k], rsem.at[part, block],
                device_id=(peer,), device_id_type=MESH)

        def start():
            copy().start()

        def finish():
            copy().wait_send()
        if when is None:
            start()
        else:
            pl.when(when)(start)
        sends.append((finish, when))

    def arrive(part, block):
        pltpu.make_async_remote_copy(
            o_ref.at[block, :, cols[part]], o_ref.at[block, :, cols[part]], ssem.at[0],
            rsem.at[part, block], device_id=(nc,), device_id_type=MESH).wait_recv()

    for part in (0, 1):
        push(part, me, n1, True)
        push(part, me, n2, True, mid)
        push(part, me, (nx, ny)[part], True)
        push(part, me, (ny, nx)[part], True)
    for part in (0, 1):
        push(part, me, nc, True)

    zs = (z, z1, z2, z3)
    zdel = [8 * (zz - z) for zz in zs]

    def from_z(part, j):
        b = me + zdel[j]
        arrive(part, b)
        push(part, b, n2 if j == 1 else n1, when=mid)
        push(part, b, (nx, ny)[part])
        push(part, b, (ny, nx)[part])
        push(part, b, nc)

    def from_first(part, j):
        b = (nx, ny)[part] + zdel[j]
        arrive(part, b)
        push(part, b, (ny, nx)[part])
        push(part, b, nc)

    def from_last(part, j, diag):
        b = (ny, nx)[part] + zdel[j]
        if diag:
            b = nx + ny - me + zdel[j]
        arrive(part, b)
        push(part, b, nc)

    for j in range(4):
        if j:
            for part in (0, 1):
                from_z(part, j)
        for part in (0, 1):
            from_first(part, j)
        if j:
            for part in (0, 1):
                from_last(part, j - 1, False)
    for part in (0, 1):
        from_last(part, 3, False)
    for j in range(4):
        for part in (0, 1):
            from_last(part, j, True)
    for j in range(4):
        for base in (nc, nc + nx - me, nc + ny - me, nc + nx + ny - 2 * me):
            for part in (0, 1):
                arrive(part, base + zdel[j])
    own.wait()
    for finish, when in sends:
        if when is None:
            finish()
        else:
            pl.when(when)(finish)


def gather(block, cid=0):
    rows, width = block.shape
    n_sends = 10 + 3 * 2 * 4 + 4 * 2 * 2 + 8 * 2
    return pl.pallas_call(
        gather_kernel,
        out_shape=jax.ShapeDtypeStruct((32, rows, width), block.dtype),
        in_specs=[pl.BlockSpec(memory_space=pl.ANY)],
        out_specs=pl.BlockSpec(memory_space=pl.ANY),
        scratch_shapes=[
            pltpu.SemaphoreType.DMA,
            pltpu.SemaphoreType.DMA((n_sends,)),
            pltpu.SemaphoreType.DMA((2, 32)),
        ],
        name="gather_rows",
        compiler_params=pltpu.CompilerParams(collective_id=cid, has_side_effects=True),
    )(block)


def scatter_kernel(p_ref, o_ref, m_ref, s_ref, first_ref, second_ref, za_ref, zb_ref,
                   lsem, ssem, csem, fsem, gsem, zasem, zbsem):
    me, c, x, y, z = place()
    rows, width = o_ref.shape
    half = width // 2
    mid = (z == 1) | (z == 2)
    end = jnp.logical_not(mid)
    z1, z2, z3 = z + 1 - 2 * (z % 2), 2 - z // 2, 3 - 3 * (z // 2)
    nc, nx, ny = me + 1 - 2 * c, me + 2 - 4 * x, me + 4 - 8 * y
    n1, n2 = me + 8 * (z1 - z), me + 8 * (z2 - z)
    diag = nx + ny - me
    greet(nc, nx, ny, n1, n2, mid)
    cols = (pl.ds(0, half), pl.ds(half, half))
    zs = (z, z1, z2, z3)
    sends = []
    count = [0]

    def push(src, dst, rsem, peer, when=None):
        k = count[0]
        count[0] += 1

        def copy():
            return pltpu.make_async_remote_copy(src, dst, ssem.at[k], rsem, device_id=(peer,), device_id_type=MESH)
        if when is None:
            copy().start()
        else:
            pl.when(when)(lambda: copy().start())
        sends.append((lambda: copy().wait_send(), when))

    def arrive(dst, rsem):
        pltpu.make_async_remote_copy(dst, dst, ssem.at[0], rsem, device_id=(nc,), device_id_type=MESH).wait_recv()

    def add_into(dst, src, extra=None):
        def step(i, _):
            r = pl.ds(pl.multiple_of(i * 16, 16), 16)
            v = dst[r, :].astype(jnp.float32) + src[r, :].astype(jnp.float32)
            if extra is not None:
                v = v + extra[r, :].astype(jnp.float32)
            dst[r, :] = v.astype(dst.dtype)
            return _
        lax.fori_loop(0, rows // 16, step, 0)

    plane = (me, nx, ny, diag)
    order = [(q, j) for q in (3, 1, 2, 0) for j in (3, 2, 1, 0)]
    for q, j in order:
        b = plane[q] + 8 * (zs[j] - z)
        slot = q * 4 + zs[j]
        pltpu.make_async_copy(p_ref.at[b], m_ref.at[slot], lsem.at[slot]).start()
        push(p_ref.at[b + nc - me], s_ref.at[slot], csem.at[slot], nc)
    first_peer, second_peer = (ny, nx), (nx, ny)

    def joined(q, j):
        slot = q * 4 + zs[j]
        pltpu.make_async_copy(p_ref.at[0], m_ref.at[slot], lsem.at[slot]).wait()
        arrive(s_ref.at[slot], csem.at[slot])
        add_into(m_ref.at[slot], s_ref.at[slot])

    def to_first(part, q, j):
        far = 4 if q == 3 else 0
        push(m_ref.at[q * 4 + zs[j], :, cols[part]], first_ref.at[part, far + zs[j]],
             fsem.at[part, far + zs[j]], first_peer[part])

    for j in (3, 2, 1, 0):
        joined(3, j)
        to_first(0, 3, j)
        to_first(1, 3, j)
    for j in (3, 2, 1, 0):
        joined(2, j)
        to_first(0, 2, j)
        joined(1, j)
        to_first(1, 1, j)
    for j in (3, 2, 1, 0):
        for part in (0, 1):
            arrive(first_ref.at[part, 4 + zs[j]], fsem.at[part, 4 + zs[j]])
            q = (1, 2)[part]
            m = m_ref.at[q * 4 + zs[j], :, cols[part]]
            add_into(m, first_ref.at[part, 4 + zs[j]])
            push(m, second_ref.at[part, zs[j]], gsem.at[part, zs[j]], second_peer[part])
        joined(0, j)

    def plane_sum(part, j):
        m = m_ref.at[zs[j], :, cols[part]]
        arrive(first_ref.at[part, zs[j]], fsem.at[part, zs[j]])
        arrive(second_ref.at[part, zs[j]], gsem.at[part, zs[j]])
        add_into(m, first_ref.at[part, zs[j]], second_ref.at[part, zs[j]])
        return m
    for part in (0, 1):
        pass
    for j in (3, 2, 1, 0):
        for part in (0, 1):
            m = plane_sum(part, j)
            if j == 3:
                push(m, za_ref.at[part, 0], zasem.at[part, 0], n1, end)

                @pl.when(mid)
                def _():
                    arrive(za_ref.at[part, 0], zasem.at[part, 0])
                    add_into(m, za_ref.at[part, 0])
                push(m, zb_ref.at[part, 0], zbsem.at[part, 0], n2, mid)
            elif j == 2:
                push(m, za_ref.at[part, 1], zasem.at[part, 1], n1, end)

                @pl.when(mid)
                def _():
                    arrive(za_ref.at[part, 1], zasem.at[part, 1])
                    add_into(m, za_ref.at[part, 1])
                push(m, zb_ref.at[part, 1], zbsem.at[part, 1], n2, mid)
            elif j == 1:
                push(m, za_ref.at[part, 2], zasem.at[part, 2], n1, end)

                @pl.when(mid)
                def _():
                    arrive(zb_ref.at[part, 0], zbsem.at[part, 0])
                    add_into(m, zb_ref.at[part, 0])
                push(m, zb_ref.at[part, 0], zbsem.at[part, 0], n1, mid)
    for part in (0, 1):
        m = m_ref.at[zs[0], :, cols[part]]
        o = o_ref.at[:, cols[part]]

        def total(*more):
            def step(i, _):
                r = pl.ds(pl.multiple_of(i * 16, 16), 16)
                v = m[r, :].astype(jnp.float32)
                for e in more:
                    v = v + e[r, :].astype(jnp.float32)
                o[r, :] = v
                return _
            lax.fori_loop(0, rows // 16, step, 0)

        @pl.when(mid)
        def _():
            arrive(za_ref.at[part, 2], zasem.at[part, 2])
            arrive(zb_ref.at[part, 1], zbsem.at[part, 1])
            total(za_ref.at[part, 2], zb_ref.at[part, 1])

        @pl.when(end)
        def _():
            arrive(zb_ref.at[part, 0], zbsem.at[part, 0])
            total(zb_ref.at[part, 0])
    for finish, when in sends:
        if when is None:
            finish()
        else:
            pl.when(when)(finish)


def scatter(parts, cid=1):
    n, rows, width = parts.shape
    dt = parts.dtype
    half = width // 2
    return pl.pallas_call(
        scatter_kernel,
        out_shape=jax.ShapeDtypeStruct((rows, width), jnp.float32),
        in_specs=[pl.BlockSpec(memory_space=pl.ANY)],
        out_specs=pl.BlockSpec(memory_space=pltpu.VMEM),
        scratch_shapes=[
            pltpu.VMEM((16, rows, width), dt),
            pltpu.VMEM((16, rows, width), dt),
            pltpu.VMEM((2, 8, rows, half), dt),
            pltpu.VMEM((2, 4, rows, half), dt),
            pltpu.VMEM((2, 3, rows, half), dt),
            pltpu.VMEM((2, 2, rows, half), dt),
            pltpu.SemaphoreType.DMA((16,)),
            pltpu.SemaphoreType.DMA((16 + 16 + 8 + 12,)),
            pltpu.SemaphoreType.DMA((16,)),
            pltpu.SemaphoreType.DMA((2, 8)),
            pltpu.SemaphoreType.DMA((2, 4)),
            pltpu.SemaphoreType.DMA((2, 3)),
            pltpu.SemaphoreType.DMA((2, 2)),
        ],
        name="scatter_rows",
        compiler_params=pltpu.CompilerParams(collective_id=cid, has_side_effects=True, vmem_limit_bytes=56 * 2**20),
    )(parts)


def exchange(blocks):
    return lax.all_to_all(blocks, AXIS, split_axis=0, concat_axis=0, tiled=True)


def dot(left, right):
    return jnp.dot(left, right, preferred_element_type=jnp.float32)


def select(mask, rows):
    return dot(mask.astype(jnp.bfloat16), rows).astype(jnp.bfloat16)


def natural(rows, count, tiles):
    width = rows.shape[-1]
    return (
        rows.reshape(count, tiles, -1, width).transpose(1, 0, 2, 3).reshape(tiles, -1, width)
    )


def dealt_order(rows, count):
    tiles, length, width = rows.shape
    return (
        rows.reshape(tiles, count, length // count, width)
        .transpose(1, 0, 2, 3)
        .reshape(-1, width)
    )


def windows(tiled):
    edge = jnp.zeros_like(tiled[:1])
    padded = jnp.concatenate((edge, tiled, edge), axis=0)
    return jnp.concatenate((padded[:-2], padded[1:-1], padded[2:]), axis=1)


def unwindow(wide):
    length = wide.shape[1] // 3
    edge = jnp.zeros_like(wide[:1, :length])
    return (
        jnp.concatenate((wide[1:, :length], edge), axis=0)
        + wide[:, length : 2 * length]
        + jnp.concatenate((edge, wide[:-1, 2 * length :]), axis=0)
    )


def batched(left, right, left_dim, right_dim):
    return lax.dot_general(
        left,
        right,
        (((left_dim,), (right_dim,)), ((0,), (0,))),
        preferred_element_type=jnp.float32,
    )


def beside(sent, chain, kernel):
    sent, chain = lax.optimization_barrier((sent, chain))
    return lax.optimization_barrier((exchange(sent), kernel(chain)))


def pack_kernel(query_ref, key_ref, value_ref, gate_ref, up_ref, first_ref, second_ref):
    count = first_ref.shape[0]
    head = query_ref.shape[1] // count
    units = gate_ref.shape[1] // count
    for j in range(count):
        for i, ref in enumerate((query_ref, key_ref, value_ref)):
            first_ref[j, :, i * head : (i + 1) * head] = ref[:, j * head : (j + 1) * head]
        first_ref[j, :, 3 * head :] = gate_ref[:, j * units : j * units + head]
        second_ref[j, :, : units - head] = gate_ref[:, j * units + head : (j + 1) * units]
        second_ref[j, :, units - head :] = up_ref[:, j * units : (j + 1) * units]


def pack(shards, count):
    rows, width = shards[0].shape
    head, units = width // count, shards[3].shape[1] // count
    return pl.pallas_call(
        pack_kernel,
        out_shape=[
            jax.ShapeDtypeStruct((count, rows, 4 * head), jnp.bfloat16),
            jax.ShapeDtypeStruct((count, rows, 2 * units - head), jnp.bfloat16),
        ],
        in_specs=[pl.BlockSpec(memory_space=pltpu.VMEM)] * 5,
        out_specs=[pl.BlockSpec(memory_space=pltpu.VMEM)] * 2,
        name="pack_columns",
        compiler_params=pltpu.CompilerParams(vmem_limit_bytes=32 * 2**20),
    )(*shards)


def unpack_kernel(first_ref, second_ref, query_ref, key_ref, value_ref, gate_ref, up_ref):
    count = first_ref.shape[0]
    head = query_ref.shape[1] // count
    units = gate_ref.shape[1] // count
    wide = jnp.float32
    for j in range(count):
        for i, ref in enumerate((query_ref, key_ref, value_ref)):
            ref[:, j * head : (j + 1) * head] = first_ref[j, :, i * head : (i + 1) * head].astype(wide)
        gate_ref[:, j * units : j * units + head] = first_ref[j, :, 3 * head :].astype(wide)
        gate_ref[:, j * units + head : (j + 1) * units] = second_ref[j, :, : units - head].astype(wide)
        up_ref[:, j * units : (j + 1) * units] = second_ref[j, :, units - head :].astype(wide)


def unpack(first, second, width, hidden):
    rows = first.shape[1]
    widths = (width, width, width, hidden, hidden)
    return pl.pallas_call(
        unpack_kernel,
        out_shape=[jax.ShapeDtypeStruct((rows, columns), jnp.float32) for columns in widths],
        in_specs=[pl.BlockSpec(memory_space=pltpu.VMEM)] * 2,
        out_specs=[pl.BlockSpec(memory_space=pltpu.VMEM)] * 5,
        name="unpack_columns",
        compiler_params=pltpu.CompilerParams(vmem_limit_bytes=32 * 2**20),
    )(first, second)


def body(
    tokens,
    lengths,
    permutation,
    query_weight,
    key_weight,
    value_weight,
    out_weight,
    gate_weight,
    up_weight,
    down_weight,
    gain_attention,
    gain_feedforward,
    bias_table,
    cotangent,
):
    me = lax.axis_index(AXIS)
    count = tokens.shape[0]
    grain = tokens.shape[1]
    length = cotangent.shape[1]
    width = tokens.shape[2]
    shard = query_weight.shape[0]
    hidden_width = gate_weight.shape[1] // count
    head = HEAD_DIM
    total = 3 * count * length // 5
    tiles = -(-total // length)
    slots = tiles * grain

    small = jnp.concatenate((gain_attention, gain_feedforward, bias_table))
    small = jnp.pad(small, (0, grain * 128 - small.shape[0])).reshape(1, grain, 128)
    small = jnp.broadcast_to(small, (count, grain, 128))
    came = exchange(jnp.concatenate((tokens[permutation], small), axis=2))
    dealt = came[:, :, :width].reshape(length, width)
    small = came[:, :, width:].reshape(count, -1)
    gain_one = small[:, :shard].reshape(-1).astype(jnp.float32)
    gain_two = small[:, shard : 2 * shard].reshape(-1).astype(jnp.float32)
    table = small[:, 2 * shard : 2 * shard + HEADS]

    dealt_lengths = lengths[permutation]
    ends = jnp.cumsum(dealt_lengths)
    starts = ends - dealt_lengths
    my_start, my_length = starts[me], dealt_lengths[me]
    place_in = jnp.arange(length, dtype=jnp.int32)
    turn = (
        (place_in[:, None] - my_start) % length == place_in[None, :]
    ) & (place_in[None, :] < my_length)
    slot_ids = jnp.arange(slots, dtype=jnp.int32)
    packed_ids = slot_ids // grain * length + me * grain + slot_ids % grain
    source_seq = jnp.sum((packed_ids[:, None] >= ends[None, :]).astype(jnp.int32), axis=1)
    pick = (source_seq * grain + slot_ids % grain)[:, None] == place_in[None, :]

    def spread_out(rows):
        return select(turn, rows).reshape(count, grain, width)

    def packed_block(came):
        return select(pick, came.reshape(length, width))

    rows_low = packed_block(exchange(spread_out(dealt)))
    rows_in = rows_low.astype(jnp.float32)
    first_columns, second_columns = pack(
        (query_weight, key_weight, value_weight, gate_weight, up_weight), count
    )

    all_ids = jnp.arange(tiles * length, dtype=jnp.int32)
    segment = jnp.sum((all_ids[:, None] >= ends[None, :]).astype(jnp.int32), axis=1) + 1
    segment = segment.reshape(tiles, length, 1)
    same = segment == windows(segment).reshape(tiles, 1, 3 * length)
    relative = (
        jnp.arange(3 * length, dtype=jnp.int32)[None, :] - length - place_in[:, None]
    ).reshape(-1)
    onehot = bucket_index(relative)[None, :] == jnp.arange(BUCKETS, dtype=jnp.int32)[:, None]
    head_table = lax.dynamic_slice_in_dim(table, me, 1, axis=1)
    rel_bias = dot(head_table.T, onehot.astype(jnp.bfloat16)).reshape(1, length, 3 * length)

    def owners_share(turned):
        return lax.optimization_barrier(turned).T.reshape(count, shard, -1)

    scale_one = norm_scale(rows_in)
    normed = (rows_in * scale_one * gain_one).astype(jnp.bfloat16)
    cut = (count, -1, 4 * head)
    sent = jnp.concatenate((first_columns, spread_out(cotangent[0]).reshape(cut)), axis=1)
    came, normed_all = beside(sent, normed, gather)
    normed_all = normed_all.reshape(-1, width)
    first_columns = came[:, :shard].reshape(-1, 4 * head)
    upstream_low = packed_block(came[:, shard:])
    upstream = upstream_low.astype(jnp.float32)
    upstream_all = lax.all_gather(upstream_low, AXIS, axis=0, tiled=True)
    qkv_columns = first_columns[:, : 3 * head]
    qkv = natural(dot(normed_all, qkv_columns).astype(jnp.bfloat16), count, tiles)
    query, key, value = qkv[:, :, :head], qkv[:, :, head : 2 * head], qkv[:, :, 2 * head :]
    key_window, value_window = windows(key), windows(value)
    scores = jnp.where(same, batched(query, key_window, 2, 2) + rel_bias, masked_score)
    probs = jax.nn.softmax(scores, axis=-1)
    probs_low = probs.astype(jnp.bfloat16)
    attended = dealt_order(batched(probs_low, value_window, 2, 1).astype(jnp.bfloat16), count)
    partial = dot(attended, out_weight).astype(jnp.bfloat16).reshape(count, slots, width)
    came, branch = beside(second_columns, partial, scatter)
    second_columns = came.reshape(count * shard, -1)
    gate_up_columns = jnp.concatenate((first_columns[:, 3 * head :], second_columns), axis=1)
    middle = rows_in + branch

    scale_two = norm_scale(middle)
    normed_two = (middle * scale_two * gain_two).astype(jnp.bfloat16)
    normed_two, upstream_all = lax.optimization_barrier((normed_two, upstream_all))
    normed_two_all = gather(normed_two).reshape(-1, width)
    gate_up = dot(normed_two_all, gate_up_columns)

    def gelu_product(gate_part, up_part):
        return jax.nn.gelu(gate_part, approximate=True) * up_part

    hidden_full, gelu_pull = jax.vjp(
        gelu_product, gate_up[:, :hidden_width], gate_up[:, hidden_width:]
    )
    hidden = hidden_full.astype(jnp.bfloat16)

    d_gate, d_up = gelu_pull(against_rows(upstream_all, down_weight))
    d_gate_up = jnp.concatenate((d_gate, d_up), axis=1).astype(jnp.bfloat16)
    gate_up_grad = rows_product(d_gate_up, normed_two_all).astype(jnp.bfloat16)
    partial = against_rows(d_gate_up, gate_up_columns).astype(jnp.bfloat16)
    d_normed_two = scatter(partial.reshape(count, slots, width))
    partial = dot(hidden, down_weight).astype(jnp.bfloat16)
    partial, d_normed_two = lax.optimization_barrier((partial, d_normed_two))
    down = scatter(partial.reshape(count, slots, width))
    d_normed_two, down = lax.optimization_barrier((d_normed_two, down))
    result = (middle + down).astype(jnp.bfloat16)
    gain_two_grad = jnp.sum(d_normed_two * middle * scale_two, axis=0)
    d_middle = upstream + norm_back(middle, scale_two, gain_two, d_normed_two)
    turned = starts + (me * grain + jnp.arange(grain, dtype=jnp.int32)[:, None] - starts) % length
    back_slot = (turned // length * grain + jnp.arange(grain, dtype=jnp.int32)[:, None]).T
    spread = back_slot.reshape(-1, 1) == slot_ids[None, :]

    sent = jnp.concatenate(
        (owners_share(gate_up_grad[head:]), select(spread, result).reshape(cut)), axis=1
    )
    came, d_branch_all = beside(sent, d_middle.astype(jnp.bfloat16), gather)
    second_grad = came[:, :shard]
    layer_output = select(turn.T, came[:, shard:].reshape(length, width))[None]
    d_branch_all = d_branch_all.reshape(-1, width)
    d_attended = natural(
        against_rows(d_branch_all, out_weight).astype(jnp.bfloat16), count, tiles
    )
    d_value = unwindow(batched(probs_low, d_attended, 1, 1))
    d_probs = batched(d_attended, value_window, 2, 2)
    inner = jnp.sum(probs * d_probs, axis=-1, keepdims=True)
    d_scores = (probs * (d_probs - inner)).astype(jnp.bfloat16)
    d_query = batched(d_scores, key_window, 2, 1)
    d_key = unwindow(batched(d_scores, query, 1, 1))
    d_bias = jnp.sum(d_scores.astype(jnp.float32), axis=0).reshape(1, -1)
    table_sum = jnp.sum(jnp.where(onehot, d_bias, 0.0), axis=1)
    d_qkv = dealt_order(
        jnp.concatenate((d_query, d_key, d_value), axis=2).astype(jnp.bfloat16), count
    )
    qkv_grad = rows_product(d_qkv, normed_all).astype(jnp.bfloat16)
    sent = owners_share(jnp.concatenate((qkv_grad, gate_up_grad[:head]), axis=0))
    partial = against_rows(d_qkv, qkv_columns).astype(jnp.bfloat16)
    first_grad, d_normed = beside(sent, partial.reshape(count, slots, width), scatter)
    first_grad, second_grad, attended, hidden, d_normed = lax.optimization_barrier(
        (first_grad, second_grad, attended, hidden, d_normed)
    )
    out_grad = rows_product(attended, d_branch_all)
    down_grad = rows_product(hidden, upstream_all)
    gain_one_grad = jnp.sum(d_normed * rows_in * scale_one, axis=0)
    d_dealt = (d_middle + norm_back(rows_in, scale_one, gain_one, d_normed)).astype(jnp.bfloat16)

    sums = jnp.concatenate(
        (
            gain_one_grad.reshape(count, shard),
            gain_two_grad.reshape(count, shard),
            table_sum.reshape(count, 1),
        ),
        axis=1,
    )
    high = lax.reduce_precision(sums, 8, 7)
    sums = jnp.concatenate((high, sums - high), axis=1).astype(jnp.bfloat16)
    sums = jnp.pad(sums, ((0, 0), (0, grain * 128 - sums.shape[1]))).reshape(count, grain, 128)
    going = select(spread, d_dealt).reshape(count, grain, width)
    came = exchange(jnp.concatenate((going, sums), axis=2))
    sums = came[:, :, width:].reshape(count, -1).astype(jnp.float32)
    sums = sums[:, : 2 * shard + 1] + sums[:, 2 * shard + 1 : 4 * shard + 2]
    came = select(turn.T, came[:, :, :width].reshape(length, width))
    tokens_grad = exchange(came.reshape(count, grain, width))[jnp.argsort(permutation)]

    query_grad, key_grad, value_grad, gate_grad, up_grad = unpack(
        first_grad, second_grad, width, hidden_width * count
    )
    return (
        layer_output,
        tokens_grad,
        query_grad,
        key_grad,
        value_grad,
        out_grad,
        gate_grad,
        up_grad,
        down_grad,
        jnp.sum(sums[:, :shard], axis=0),
        jnp.sum(sums[:, shard : 2 * shard], axis=0),
        sums[:, 2 * shard],
    )


def solution(mesh):
    placed = (
        P(None, "fsdp", None),
        P(),
        P(),
        P("fsdp", None),
        P("fsdp", None),
        P("fsdp", None),
        P("fsdp", None),
        P("fsdp", None),
        P("fsdp", None),
        P("fsdp", None),
        P("fsdp"),
        P("fsdp"),
        P("fsdp"),
        P("fsdp", None, None),
    )
    return jax.shard_map(
        body if mesh.shape[AXIS] == 32 else body_any,
        mesh=mesh,
        in_specs=placed,
        out_specs=(
            P("fsdp", None, None),
            P(None, "fsdp", None),
            P("fsdp", None),
            P("fsdp", None),
            P("fsdp", None),
            P("fsdp", None),
            P("fsdp", None),
            P("fsdp", None),
            P("fsdp", None),
            P("fsdp"),
            P("fsdp"),
            P("fsdp"),
        ),
        check_vma=False,
    )
```

```python
import functools

import jax
import jax.numpy as jnp
from jax import lax
from jax.experimental import pallas as pl
from jax.experimental.pallas import tpu as pltpu
from jax.sharding import PartitionSpec as P

HEADS = 32
HEAD_DIM = 64
BUCKETS = 32


EPSILON = 1e-06
masked_score = -1000000000.0
HIGHEST = lax.Precision.HIGHEST


def bucket_index(relative):
    half_buckets = BUCKETS // 2
    exact_count = half_buckets // 2
    distance = jnp.abs(relative)
    side_offset = jnp.where(relative > 0, half_buckets, 0).astype(jnp.int32)
    square = distance * distance
    far_bucket = jnp.full_like(distance, exact_count)
    for doubling in range(1, half_buckets - exact_count):
        far_bucket = far_bucket + (square >= exact_count * exact_count * 2**doubling).astype(
            jnp.int32
        )
    return side_offset + jnp.where(distance < exact_count, distance, far_bucket)


def bucket_onehot(seq_len):
    positions = jnp.arange(seq_len, dtype=jnp.int32)
    relative = (positions[None, :] - positions[:, None]).reshape(-1)
    bucket_ids = jnp.arange(BUCKETS, dtype=jnp.int32)
    return (bucket_index(relative)[None, :] == bucket_ids[:, None]).astype(jnp.float32)


def norm_scale(values):
    return lax.rsqrt(jnp.mean(values * values, axis=-1, keepdims=True) + EPSILON)


def norm_back(values, scale, gain_vec, d_norm):
    weighted = gain_vec * d_norm
    return scale * weighted - values * (scale * scale * scale) * jnp.mean(
        weighted * values, axis=-1, keepdims=True
    )


def rows_product(left, right):
    return lax.dot_general(
        left, right, (((0,), (0,)), ((), ())), preferred_element_type=jnp.float32
    )


def against_rows(left, right):
    return lax.dot_general(
        left, right, (((1,), (1,)), ((), ())), preferred_element_type=jnp.float32
    )


def masked_scores(query_heads, key_heads, rel_bias, length):
    scores = (
        jnp.einsum("qhd,khd->hqk", query_heads, key_heads, preferred_element_type=jnp.float32)
        + rel_bias
    )
    key_valid = jnp.arange(key_heads.shape[0], dtype=jnp.int32) < length
    return jnp.where(key_valid[None, None, :], scores, masked_score)


def unpack_weights(full_weights, onehot, seq_len):
    table_full = full_weights[4].astype(jnp.float32).reshape(BUCKETS, HEADS)
    rel_bias = jnp.dot(table_full.T, onehot, precision=HIGHEST).reshape(HEADS, seq_len, seq_len)
    return (
        full_weights[0],
        full_weights[1],
        full_weights[2].astype(jnp.float32),
        full_weights[3].astype(jnp.float32),
        rel_bias,
    )


def body_any(
    tokens,
    lengths,
    permutation,
    query_weight,
    key_weight,
    value_weight,
    out_weight,
    gate_weight,
    up_weight,
    down_weight,
    gain_attention,
    gain_feedforward,
    bias_table,
    cotangent,
):
    model_width = query_weight.shape[1]
    hidden_width = gate_weight.shape[1]
    packed = jnp.concatenate(
        (query_weight, key_weight, value_weight, out_weight, gate_weight, up_weight), axis=1
    )
    shards = (packed, down_weight, gain_attention, gain_feedforward, bias_table)
    full_weights = (
        lax.all_gather(shards[0], "fsdp", axis=0, tiled=True),
        lax.all_gather(shards[1], "fsdp", axis=0, tiled=True),
        lax.all_gather(shards[2], "fsdp", axis=0, tiled=True),
        lax.all_gather(shards[3], "fsdp", axis=0, tiled=True),
        lax.all_gather(shards[4], "fsdp", axis=0, tiled=True),
    )
    reordered = tokens[permutation]
    dealt = lax.all_to_all(reordered, "fsdp", split_axis=0, concat_axis=1, tiled=True)
    seq_count = dealt.shape[0]
    seq_len = dealt.shape[1]
    local_ids = lax.dynamic_slice_in_dim(permutation, lax.axis_index("fsdp") * seq_count, seq_count)
    seq_lengths = lengths[local_ids]
    positions = jnp.arange(seq_len, dtype=jnp.int32)
    row_valid = (positions[None, :] < seq_lengths[:, None]).astype(jnp.float32).reshape(-1, 1)
    onehot = bucket_onehot(seq_len)
    onehot_low = onehot.astype(jnp.bfloat16)
    full_packed, full_down, gain_one, gain_two, rel_bias = unpack_weights(
        full_weights, onehot, seq_len
    )
    head_shape = (seq_count, seq_len, HEADS, HEAD_DIM)
    rows_in = dealt.reshape(-1, model_width).astype(jnp.float32)
    scale_one = norm_scale(rows_in)
    normed = (rows_in * scale_one * gain_one).astype(jnp.bfloat16)
    projected = jnp.dot(
        normed, full_packed[:, : 3 * model_width], preferred_element_type=jnp.float32
    ).astype(jnp.bfloat16)
    query_heads = projected[:, :model_width].reshape(head_shape)
    key_heads = projected[:, model_width : 2 * model_width].reshape(head_shape)
    value_heads = projected[:, 2 * model_width :].reshape(head_shape)

    def attend_forward(pieces):
        query_one, key_one, value_one, length = pieces
        scores = masked_scores(query_one, key_one, rel_bias, length)
        row_max = jnp.max(scores, axis=-1, keepdims=True)
        exp_total = jnp.sum(jnp.exp(scores - row_max), axis=-1, keepdims=True)
        log_total = row_max + jnp.log(exp_total)
        weights_soft = jnp.exp(scores - log_total).astype(jnp.bfloat16)
        attended_one = jnp.einsum(
            "hqk,khd->qhd", weights_soft, value_one, preferred_element_type=jnp.float32
        )
        return (attended_one.astype(jnp.bfloat16), log_total)

    attended_heads, log_totals = lax.map(
        attend_forward, (query_heads, key_heads, value_heads, seq_lengths)
    )
    attended_rows = attended_heads.reshape(-1, model_width)
    middle = rows_in + jnp.dot(
        attended_rows,
        full_packed[:, 3 * model_width : 4 * model_width],
        preferred_element_type=jnp.float32,
    )
    scale_two = norm_scale(middle)
    normed_two = (middle * scale_two * gain_two).astype(jnp.bfloat16)
    gate_up = jnp.dot(
        normed_two, full_packed[:, 4 * model_width :], preferred_element_type=jnp.float32
    )

    def gelu_product(gate_part, up_part):
        return jax.nn.gelu(gate_part, approximate=True) * up_part

    hidden_full, gelu_pull = jax.vjp(
        gelu_product, gate_up[:, :hidden_width], gate_up[:, hidden_width:]
    )
    hidden = hidden_full.astype(jnp.bfloat16)
    result = middle + jnp.dot(hidden, full_down, preferred_element_type=jnp.float32)
    layer_output = (
        (result * row_valid).astype(jnp.bfloat16).reshape(seq_count, seq_len, model_width)
    )
    full_weights = (
        lax.all_gather(shards[0], "fsdp", axis=0, tiled=True),
        lax.all_gather(shards[1], "fsdp", axis=0, tiled=True),
        lax.all_gather(shards[2], "fsdp", axis=0, tiled=True),
        lax.all_gather(shards[3], "fsdp", axis=0, tiled=True),
        lax.all_gather(shards[4], "fsdp", axis=0, tiled=True),
    )
    full_packed, full_down, gain_one, gain_two, rel_bias = unpack_weights(
        full_weights, onehot, seq_len
    )
    upstream = cotangent.reshape(-1, model_width).astype(jnp.float32) * row_valid
    upstream_low = upstream.astype(jnp.bfloat16)
    d_hidden = against_rows(upstream_low, full_down)
    d_gate, d_up = gelu_pull(d_hidden)
    d_gate_up = jnp.concatenate((d_gate, d_up), axis=1).astype(jnp.bfloat16)
    d_normed_two = against_rows(d_gate_up, full_packed[:, 4 * model_width :])
    gain_two_grad = jnp.sum(d_normed_two * middle * scale_two, axis=0)
    d_middle = upstream + norm_back(middle, scale_two, gain_two, d_normed_two)
    d_branch = d_middle.astype(jnp.bfloat16)
    d_attended = against_rows(d_branch, full_packed[:, 3 * model_width : 4 * model_width]).astype(
        jnp.bfloat16
    )

    def attend_backward(pieces):
        query_one, key_one, value_one, length, log_total, d_attended_one = pieces
        scores = masked_scores(query_one, key_one, rel_bias, length)
        probs = jnp.exp(scores - log_total)
        probs_low = probs.astype(jnp.bfloat16)
        d_value = jnp.einsum(
            "hqk,qhd->khd", probs_low, d_attended_one, preferred_element_type=jnp.float32
        )
        d_probs = jnp.einsum(
            "qhd,khd->hqk", d_attended_one, value_one, preferred_element_type=jnp.float32
        )
        inner = jnp.sum(probs * d_probs, axis=-1, keepdims=True)
        d_scores = (probs * (d_probs - inner)).astype(jnp.bfloat16)
        d_query = jnp.einsum("hqk,khd->qhd", d_scores, key_one, preferred_element_type=jnp.float32)
        d_key = jnp.einsum("hqk,qhd->khd", d_scores, query_one, preferred_element_type=jnp.float32)
        d_bias = against_rows(d_scores.reshape(HEADS, -1), onehot_low)
        return (
            (
                d_query.astype(jnp.bfloat16),
                d_key.astype(jnp.bfloat16),
                d_value.astype(jnp.bfloat16),
            ),
            d_bias,
        )

    (d_query_all, d_key_all, d_value_all), d_bias_all = lax.map(
        attend_backward,
        (
            query_heads,
            key_heads,
            value_heads,
            seq_lengths,
            log_totals,
            d_attended.reshape(head_shape),
        ),
    )
    d_qkv = jnp.concatenate(
        (
            d_query_all.reshape(-1, model_width),
            d_key_all.reshape(-1, model_width),
            d_value_all.reshape(-1, model_width),
        ),
        axis=1,
    )
    d_normed = against_rows(d_qkv, full_packed[:, : 3 * model_width])
    gain_one_grad = jnp.sum(d_normed * rows_in * scale_one, axis=0)
    d_rows = d_middle + norm_back(rows_in, scale_one, gain_one, d_normed)
    d_dealt = d_rows.astype(jnp.bfloat16).reshape(seq_count, seq_len, model_width)
    returned_rows = lax.all_to_all(d_dealt, "fsdp", split_axis=1, concat_axis=0, tiled=True)
    tokens_grad = returned_rows[jnp.argsort(permutation)]
    packed_grad = lax.psum_scatter(
        jnp.concatenate(
            (
                rows_product(normed, d_qkv),
                jnp.concatenate(
                    (rows_product(attended_rows, d_branch), rows_product(normed_two, d_gate_up)),
                    axis=1,
                ),
            ),
            axis=1,
        ),
        "fsdp",
        scatter_dimension=0,
        tiled=True,
    )
    mixer_grad = packed_grad[:, : 3 * model_width]
    branch_grad = packed_grad[:, 3 * model_width :]
    down_grad = lax.psum_scatter(
        rows_product(hidden, upstream_low), "fsdp", scatter_dimension=0, tiled=True
    )
    table_sum = jnp.sum(d_bias_all, axis=0).T.reshape(-1)
    gain_attention_grad, gain_feedforward_grad, table_grad = (
        lax.psum_scatter(gain_one_grad, "fsdp", scatter_dimension=0, tiled=True),
        lax.psum_scatter(gain_two_grad, "fsdp", scatter_dimension=0, tiled=True),
        lax.psum_scatter(table_sum, "fsdp", scatter_dimension=0, tiled=True),
    )
    return (
        layer_output,
        tokens_grad,
        mixer_grad[:, :model_width],
        mixer_grad[:, model_width : 2 * model_width],
        mixer_grad[:, 2 * model_width :],
        branch_grad[:, :model_width],
        branch_grad[:, model_width : model_width + hidden_width],
        branch_grad[:, model_width + hidden_width :],
        down_grad,
        gain_attention_grad,
        gain_feedforward_grad,
        table_grad,
    )


MESH = pl.DeviceIdType.MESH
AXIS = "fsdp"


def place():
    me = lax.axis_index(AXIS)
    c, x, y, z = me % 2, (me // 2) % 2, (me // 4) % 2, me // 8
    return me, c, x, y, z


def greet(nc, nx, ny, n1, n2, mid):
    bar = pltpu.get_barrier_semaphore()
    for peer in (nc, nx, ny, n1):
        pl.semaphore_signal(bar, inc=1, device_id=(peer,), device_id_type=MESH)

    @pl.when(mid)
    def _():
        pl.semaphore_signal(bar, inc=1, device_id=(n2,), device_id_type=MESH)

    pl.semaphore_wait(bar, 4 + mid.astype(jnp.int32))


def gather_kernel(a_ref, o_ref, own_sem, ssem, rsem):
    me, c, x, y, z = place()
    half = a_ref.shape[1] // 2
    mid = (z == 1) | (z == 2)
    z1, z2, z3 = z + 1 - 2 * (z % 2), 2 - z // 2, 3 - 3 * (z // 2)
    nc, nx, ny = me + 1 - 2 * c, me + 2 - 4 * x, me + 4 - 8 * y
    n1, n2 = me + 8 * (z1 - z), me + 8 * (z2 - z)
    greet(nc, nx, ny, n1, n2, mid)
    own = pltpu.make_async_copy(a_ref, o_ref.at[me], own_sem)
    own.start()
    cols = (pl.ds(0, half), pl.ds(half, half))
    sends = []
    count = [0]

    def push(part, block, peer, mine=False, when=None):
        k = count[0]
        count[0] += 1
        src = a_ref.at[:, cols[part]] if mine else o_ref.at[block, :, cols[part]]

        def copy():
            return pltpu.make_async_remote_copy(
                src, o_ref.at[block, :, cols[part]], ssem.at[k], rsem.at[part, block],
                device_id=(peer,), device_id_type=MESH)

        def start():
            copy().start()

        def finish():
            copy().wait_send()
        if when is None:
            start()
        else:
            pl.when(when)(start)
        sends.append((finish, when))

    def arrive(part, block):
        pltpu.make_async_remote_copy(
            o_ref.at[block, :, cols[part]], o_ref.at[block, :, cols[part]], ssem.at[0],
            rsem.at[part, block], device_id=(nc,), device_id_type=MESH).wait_recv()

    for part in (0, 1):
        push(part, me, n1, True)
        push(part, me, n2, True, mid)
        push(part, me, (nx, ny)[part], True)
        push(part, me, (ny, nx)[part], True)
    for part in (0, 1):
        push(part, me, nc, True)

    zs = (z, z1, z2, z3)
    zdel = [8 * (zz - z) for zz in zs]

    def from_z(part, j):
        b = me + zdel[j]
        arrive(part, b)
        push(part, b, n2 if j == 1 else n1, when=mid)
        push(part, b, (nx, ny)[part])
        push(part, b, (ny, nx)[part])
        push(part, b, nc)

    def from_first(part, j):
        b = (nx, ny)[part] + zdel[j]
        arrive(part, b)
        push(part, b, (ny, nx)[part])
        push(part, b, nc)

    def from_last(part, j, diag):
        b = (ny, nx)[part] + zdel[j]
        if diag:
            b = nx + ny - me + zdel[j]
        arrive(part, b)
        push(part, b, nc)

    for j in range(4):
        if j:
            for part in (0, 1):
                from_z(part, j)
        for part in (0, 1):
            from_first(part, j)
        if j:
            for part in (0, 1):
                from_last(part, j - 1, False)
    for part in (0, 1):
        from_last(part, 3, False)
    for j in range(4):
        for part in (0, 1):
            from_last(part, j, True)
    for j in range(4):
        for base in (nc, nc + nx - me, nc + ny - me, nc + nx + ny - 2 * me):
            for part in (0, 1):
                arrive(part, base + zdel[j])
    own.wait()
    for finish, when in sends:
        if when is None:
            finish()
        else:
            pl.when(when)(finish)


def gather(block):
    rows, width = block.shape
    n_sends = 10 + 3 * 2 * 4 + 4 * 2 * 2 + 8 * 2
    return pl.pallas_call(
        gather_kernel,
        out_shape=jax.ShapeDtypeStruct((32, rows, width), block.dtype),
        in_specs=[pl.BlockSpec(memory_space=pl.ANY)],
        out_specs=pl.BlockSpec(memory_space=pl.ANY),
        scratch_shapes=[
            pltpu.SemaphoreType.DMA,
            pltpu.SemaphoreType.DMA((n_sends,)),
            pltpu.SemaphoreType.DMA((2, 32)),
        ],
        name="gather_rows",
        compiler_params=pltpu.CompilerParams(collective_id=0, has_side_effects=True),
    )(block)


def scatter_kernel(given, *refs):
    p_refs, o_refs, refs = refs[:given], refs[given : 2 * given], refs[2 * given :]
    m_ref, s_ref, first_ref, second_ref, za_ref, zb_ref = refs[:6]
    lsem, ssem, csem, fsem, gsem, zasem, zbsem = refs[6:]
    me, c, x, y, z = place()
    rows, width = o_refs[0].shape
    half = given * width // 2
    mid = (z == 1) | (z == 2)
    end = jnp.logical_not(mid)
    z1, z2, z3 = z + 1 - 2 * (z % 2), 2 - z // 2, 3 - 3 * (z // 2)
    nc, nx, ny = me + 1 - 2 * c, me + 2 - 4 * x, me + 4 - 8 * y
    n1, n2 = me + 8 * (z1 - z), me + 8 * (z2 - z)
    diag = nx + ny - me
    greet(nc, nx, ny, n1, n2, mid)
    cols = (pl.ds(0, half), pl.ds(half, half))
    zs = (z, z1, z2, z3)
    sends = []
    count = [0]

    def push(src, dst, rsem, peer, when=None):
        k = count[0]
        count[0] += 1

        def copy():
            return pltpu.make_async_remote_copy(src, dst, ssem.at[k], rsem, device_id=(peer,), device_id_type=MESH)
        if when is None:
            copy().start()
        else:
            pl.when(when)(lambda: copy().start())
        sends.append((lambda: copy().wait_send(), when))

    def arrive(dst, rsem):
        pltpu.make_async_remote_copy(dst, dst, ssem.at[0], rsem, device_id=(nc,), device_id_type=MESH).wait_recv()

    def add_into(dst, src, extra=None):
        def step(i, _):
            r = pl.ds(pl.multiple_of(i * 16, 16), 16)
            v = dst[r, :].astype(jnp.float32) + src[r, :].astype(jnp.float32)
            if extra is not None:
                v = v + extra[r, :].astype(jnp.float32)
            dst[r, :] = v.astype(dst.dtype)
            return _
        lax.fori_loop(0, rows // 16, step, 0)

    plane = (me, nx, ny, diag)
    def pair_exchange(j):
        for q in (3, 2, 1, 0):
            b = plane[q] + 8 * (zs[j] - z)
            slot = q * 4 + zs[j]
            for i, p_ref in enumerate(p_refs):
                own = pl.ds(i * width, width)
                push(p_ref.at[b + nc - me], s_ref.at[slot, :, own], csem.at[i, slot], nc)
                pltpu.make_async_copy(p_ref.at[b], m_ref.at[slot, :, own], lsem.at[i, slot]).start()

    pair_exchange(3)
    first_peer, second_peer = (ny, nx), (nx, ny)

    def joined(q, j):
        slot = q * 4 + zs[j]
        for i, p_ref in enumerate(p_refs):
            own = pl.ds(i * width, width)
            pltpu.make_async_copy(p_ref.at[0], m_ref.at[slot, :, own], lsem.at[i, slot]).wait()
            arrive(s_ref.at[slot, :, own], csem.at[i, slot])
        add_into(m_ref.at[slot], s_ref.at[slot])

    def to_first(part, q, j):
        far = 4 if q == 3 else 0
        push(m_ref.at[q * 4 + zs[j], :, cols[part]], first_ref.at[part, far + zs[j]],
             fsem.at[part, far + zs[j]], first_peer[part])

    def first_stage(j):
        joined(3, j)
        if j:
            pair_exchange(j - 1)
        to_first(0, 3, j)
        to_first(1, 3, j)
        joined(2, j)
        to_first(0, 2, j)
        joined(1, j)
        to_first(1, 1, j)

    def second_stage(j):
        for part in (0, 1):
            arrive(first_ref.at[part, 4 + zs[j]], fsem.at[part, 4 + zs[j]])
            q = (1, 2)[part]
            m = m_ref.at[q * 4 + zs[j], :, cols[part]]
            add_into(m, first_ref.at[part, 4 + zs[j]])
            push(m, second_ref.at[part, zs[j]], gsem.at[part, zs[j]], second_peer[part])
        joined(0, j)

    def plane_sum(part, j):
        m = m_ref.at[zs[j], :, cols[part]]
        arrive(first_ref.at[part, zs[j]], fsem.at[part, zs[j]])
        arrive(second_ref.at[part, zs[j]], gsem.at[part, zs[j]])
        add_into(m, first_ref.at[part, zs[j]], second_ref.at[part, zs[j]])
        return m

    def z_send(j):
        for part in (0, 1):
            m = plane_sum(part, j)
            if j:
                push(m, za_ref.at[part, 3 - j], zasem.at[part, 3 - j], n1, end)

    def z_relay(j):
        for part in (0, 1):
            m = m_ref.at[zs[j], :, cols[part]]
            came, sem = (za_ref, zasem) if j > 1 else (zb_ref, zbsem)
            slot = 3 - j if j > 1 else 0

            @pl.when(mid)
            def _():
                arrive(came.at[part, slot], sem.at[part, slot])
                add_into(m, came.at[part, slot])
            out = 3 - j if j > 1 else 0
            push(m, zb_ref.at[part, out], zbsem.at[part, out], n2 if j > 1 else n1, mid)

    stages = (first_stage, second_stage, z_send, z_relay)
    for step in range(4 + len(stages) - 1):
        for stage, what in enumerate(stages):
            j = 3 - (step - stage)
            if 0 <= j <= 3 and not (what is z_relay and j == 0):
                what(j)
    for part in (0, 1):
        m = m_ref.at[zs[0], :, cols[part]]
        o = o_refs[part] if given == 2 else o_refs[0].at[:, cols[part]]

        def total(*more):
            def step(i, _):
                r = pl.ds(pl.multiple_of(i * 16, 16), 16)
                v = m[r, :].astype(jnp.float32)
                for e in more:
                    v = v + e[r, :].astype(jnp.float32)
                o[r, :] = v
                return _
            lax.fori_loop(0, rows // 16, step, 0)

        @pl.when(mid)
        def _():
            arrive(za_ref.at[part, 2], zasem.at[part, 2])
            arrive(zb_ref.at[part, 1], zbsem.at[part, 1])
            total(za_ref.at[part, 2], zb_ref.at[part, 1])

        @pl.when(end)
        def _():
            arrive(zb_ref.at[part, 0], zbsem.at[part, 0])
            total(zb_ref.at[part, 0])
    for finish, when in sends:
        if when is None:
            finish()
        else:
            pl.when(when)(finish)


def scatter(*partials):
    given = len(partials)
    n, rows, width = partials[0].shape
    kind = partials[0].dtype
    whole, half = given * width, given * width // 2
    sums = pl.pallas_call(
        functools.partial(scatter_kernel, given),
        out_shape=[jax.ShapeDtypeStruct((rows, width), jnp.float32)] * given,
        in_specs=[pl.BlockSpec(memory_space=pl.ANY)] * given,
        out_specs=[pl.BlockSpec(memory_space=pltpu.VMEM)] * given,
        scratch_shapes=[
            pltpu.VMEM((16, rows, whole), kind),
            pltpu.VMEM((16, rows, whole), kind),
            pltpu.VMEM((2, 8, rows, half), kind),
            pltpu.VMEM((2, 4, rows, half), kind),
            pltpu.VMEM((2, 3, rows, half), kind),
            pltpu.VMEM((2, 2, rows, half), kind),
            pltpu.SemaphoreType.DMA((given, 16)),
            pltpu.SemaphoreType.DMA((16 * given + 36,)),
            pltpu.SemaphoreType.DMA((given, 16)),
            pltpu.SemaphoreType.DMA((2, 8)),
            pltpu.SemaphoreType.DMA((2, 4)),
            pltpu.SemaphoreType.DMA((2, 3)),
            pltpu.SemaphoreType.DMA((2, 2)),
        ],
        name="scatter_rows",
        compiler_params=pltpu.CompilerParams(
            collective_id=given, has_side_effects=True, vmem_limit_bytes=56 * 2**20
        ),
    )(*partials)
    return sums if given > 1 else sums[0]


def over(left, right, left_dim=1, right_dim=0):
    return lax.dot_general(
        left, right, (((left_dim,), (right_dim,)), ((), ())), preferred_element_type=jnp.float32
    )


def low(values):
    return values.astype(jnp.bfloat16)


def tile_probs(query, key, bias, same):
    scores = jnp.where(same, over(query, key, 1, 1) + bias, masked_score)
    grown = jnp.exp(scores - jnp.max(scores, axis=-1, keepdims=True))
    return grown / jnp.sum(grown, axis=-1, keepdims=True)


def attend_kernel(
    groups, x_ref, w_ref, wo_ref, perm_ref, bias_ref, col_ref, row_ref, qkv_ref, att_ref, part_ref
):
    step = pl.program_id(0)
    length = bias_ref.shape[0]
    head = wo_ref.shape[0]
    size = perm_ref.shape[0]
    perm = perm_ref[...]

    @pl.when(step == 0)
    def _():
        qkv_ref[:length, :] = jnp.zeros_like(qkv_ref[:length, :])
        qkv_ref[length + groups * size :, :] = jnp.zeros_like(qkv_ref[:length, :])

    @pl.when(step < groups)
    def _():
        rows = low(over(x_ref[...].reshape(size, -1), w_ref[...]))
        at = pl.multiple_of(length + step * size, length)
        qkv_ref[pl.ds(at, size), :] = low(over(perm, rows))

    @pl.when(step > 0)
    def _():
        attended = []
        for tile in range(size // length):
            base = pl.multiple_of((step - 1) * size + tile * length, length)
            query = qkv_ref[pl.ds(base + length, length), :head]
            key = qkv_ref[pl.ds(base, 3 * length), head : 2 * head]
            value = qkv_ref[pl.ds(base, 3 * length), 2 * head :]
            same = col_ref[pl.ds(base, length), :] == row_ref[:, pl.ds(base, 3 * length)]
            probs = tile_probs(query, key, bias_ref[...], same)
            attended.append(low(over(low(probs), value)))
        rows = low(over(perm, jnp.concatenate(attended, axis=0), 0, 0))
        att_ref[...] = rows.reshape(att_ref.shape)
        part_ref[...] = low(over(rows, wo_ref[...])).reshape(part_ref.shape)


def attend(x_all, w, wo, perm, bias, col, row):
    count, slots, width = x_all.shape
    head, length, size = wo.shape[0], bias.shape[0], perm.shape[0]
    grain = size // count
    groups = slots // grain

    def now(i):
        return (0, jnp.minimum(i, groups - 1), 0)

    def late(i):
        return (0, jnp.maximum(i - 1, 0), 0)

    def whole(array):
        return pl.BlockSpec(array.shape, lambda i: (0,) * array.ndim)

    qkv_shape = ((groups * size + 2 * length), 3 * head)
    return pl.pallas_call(
        functools.partial(attend_kernel, groups),
        grid=(groups + 1,),
        out_shape=[
            jax.ShapeDtypeStruct(qkv_shape, jnp.bfloat16),
            jax.ShapeDtypeStruct((count, slots, head), jnp.bfloat16),
            jax.ShapeDtypeStruct((count, slots, width), jnp.bfloat16),
        ],
        in_specs=[pl.BlockSpec((count, grain, width), now)]
        + [whole(array) for array in (w, wo, perm, bias, col, row)],
        out_specs=[
            pl.BlockSpec(qkv_shape, lambda i: (0, 0)),
            pl.BlockSpec((count, grain, head), late),
            pl.BlockSpec((count, grain, width), late),
        ],
        name="attend",
        compiler_params=pltpu.CompilerParams(vmem_limit_bytes=56 * 2**20),
    )(x_all, w, wo, perm, bias, col, row)


def attend_back_kernel(
    groups, d_ref, x_ref, att_ref, qkv_ref, w_ref, wo_ref, perm_ref, bias_ref, col_ref, row_ref,
    part_ref, wo_grad_ref, w_grad_ref, bias_grad_ref, dq_ref, dk_ref, dv_ref,
):
    step = pl.program_id(0)
    length = bias_ref.shape[0]
    head = wo_ref.shape[0]
    size = perm_ref.shape[0]
    perm = perm_ref[...]

    @pl.when(step == 0)
    def _():
        for ref in (wo_grad_ref, w_grad_ref, bias_grad_ref, dk_ref, dv_ref):
            ref[...] = jnp.zeros_like(ref)

    @pl.when(step < groups)
    def _():
        d_branch = d_ref[...].reshape(size, -1)
        wo_grad_ref[...] += over(att_ref[...].reshape(size, head), d_branch, 0, 0)
        d_attended = low(over(perm, low(over(d_branch, wo_ref[...], 1, 1))))
        for tile in range(size // length):
            base = pl.multiple_of(step * size + tile * length, length)
            query = qkv_ref[pl.ds(base + length, length), :head]
            key = qkv_ref[pl.ds(base, 3 * length), head : 2 * head]
            value = qkv_ref[pl.ds(base, 3 * length), 2 * head :]
            same = col_ref[pl.ds(base, length), :] == row_ref[:, pl.ds(base, 3 * length)]
            probs = tile_probs(query, key, bias_ref[...], same)
            d_out = d_attended[tile * length : (tile + 1) * length, :]
            d_probs = over(d_out, value, 1, 1)
            inner = jnp.sum(probs * d_probs, axis=-1, keepdims=True)
            d_scores = low(probs * (d_probs - inner))
            bias_grad_ref[...] += d_scores.astype(jnp.float32)
            dq_ref[pl.ds(base + length, length), :] = over(d_scores, key)
            dk_ref[pl.ds(base, 3 * length), :] += over(d_scores, query, 0, 0)
            dv_ref[pl.ds(base, 3 * length), :] += over(low(probs), d_out, 0, 0)

    @pl.when(step > 0)
    def _():
        at = pl.multiple_of(length + (step - 1) * size, length)
        rows = jnp.concatenate([low(ref[pl.ds(at, size), :]) for ref in (dq_ref, dk_ref, dv_ref)], axis=1)
        rows = low(over(perm, rows, 0, 0))
        w_grad_ref[...] += over(rows, x_ref[...].reshape(size, -1), 0, 0)
        part_ref[...] = low(over(rows, w_ref[...], 1, 1)).reshape(part_ref.shape)


def attend_back(d_all, x_all, att, qkv, w, wo, perm, bias, col, row):
    count, slots, width = x_all.shape
    head, length, size = wo.shape[0], bias.shape[0], perm.shape[0]
    grain = size // count
    groups = slots // grain

    def now(i):
        return (0, jnp.minimum(i, groups - 1), 0)

    def late(i):
        return (0, jnp.maximum(i - 1, 0), 0)

    def whole(shape):
        return pl.BlockSpec(shape, lambda i: (0,) * len(shape))

    grads = [(head, width), (3 * head, width), bias.shape]
    return pl.pallas_call(
        functools.partial(attend_back_kernel, groups),
        grid=(groups + 1,),
        out_shape=[jax.ShapeDtypeStruct((count, slots, width), jnp.bfloat16)]
        + [jax.ShapeDtypeStruct(shape, jnp.float32) for shape in grads],
        in_specs=[
            pl.BlockSpec((count, grain, width), now),
            pl.BlockSpec((count, grain, width), late),
            pl.BlockSpec((count, grain, head), now),
        ]
        + [whole(array.shape) for array in (qkv, w, wo, perm, bias, col, row)],
        out_specs=[pl.BlockSpec((count, grain, width), late)] + [whole(shape) for shape in grads],
        scratch_shapes=[pltpu.VMEM((qkv.shape[0], head), jnp.float32)] * 3,
        name="attend_back",
        compiler_params=pltpu.CompilerParams(vmem_limit_bytes=56 * 2**20),
    )(d_all, x_all, att, qkv, w, wo, perm, bias, col, row)


def feed_kernel(x_ref, up_ref, w_ref, wd_ref, back_ref, down_ref, w_grad_ref, wd_grad_ref):
    units = wd_ref.shape[0]

    @pl.when(pl.program_id(0) == 0)
    def _():
        w_grad_ref[...] = jnp.zeros_like(w_grad_ref)
        wd_grad_ref[...] = jnp.zeros_like(wd_grad_ref)

    x, upstream = x_ref[...], up_ref[...]
    both = over(x, w_ref[...])
    gate, up = both[:, :units], both[:, units:]
    d_hidden = over(upstream, wd_ref[...], 1, 1)
    slope = 0.7978845608028654
    squared = gate * gate
    bent = jnp.tanh(slope * (gate + 0.044715 * gate * squared))
    gelu = 0.5 * gate * (1.0 + bent)
    d_gelu = 0.5 * (1.0 + bent) + 0.5 * gate * (1.0 - bent * bent) * slope * (
        1.0 + 3.0 * 0.044715 * squared
    )
    hidden = low(gelu * up)
    d_both = jnp.concatenate((low(d_hidden * up * d_gelu), low(d_hidden * gelu)), axis=1)
    back_ref[...] = low(over(d_both, w_ref[...], 1, 1))
    down_ref[...] = low(over(hidden, wd_ref[...]))
    w_grad_ref[...] += over(d_both, x, 0, 0)
    wd_grad_ref[...] += over(hidden, upstream, 0, 0)


def feed(x_all, upstream_all, w, wd):
    rows, width = x_all.shape
    step = 512 if rows % 512 == 0 else rows
    block = pl.BlockSpec((step, width), lambda i: (i, 0))

    def whole(shape):
        return pl.BlockSpec(shape, lambda i: (0, 0))

    grads = [(w.shape[1], width), wd.shape]
    return pl.pallas_call(
        feed_kernel,
        grid=(rows // step,),
        out_shape=[jax.ShapeDtypeStruct((rows, width), jnp.bfloat16)] * 2
        + [jax.ShapeDtypeStruct(shape, jnp.float32) for shape in grads],
        in_specs=[block, block, whole(w.shape), whole(wd.shape)],
        out_specs=[block, block] + [whole(shape) for shape in grads],
        name="feed_forward_and_back",
        compiler_params=pltpu.CompilerParams(vmem_limit_bytes=56 * 2**20),
    )(x_all, upstream_all, w, wd)


class Spot:
    def __init__(self):
        me = lax.axis_index(AXIS)
        c, x, y, z = me % 2, (me // 2) % 2, (me // 4) % 2, me // 8
        self.me = me
        self.mid = (z == 1) | (z == 2)
        self.end = jnp.logical_not(self.mid)
        self.zs = (z, z + 1 - 2 * (z % 2), 2 - z // 2, 3 - 3 * (z // 2))
        self.shift = [8 * (zz - z) for zz in self.zs]
        self.core, self.x, self.y = me + 1 - 2 * c, me + 2 - 4 * x, me + 4 - 8 * y
        self.diag = self.x + self.y - me
        self.n1, self.n2 = me + self.shift[1], me + self.shift[2]

    def greet(self):
        bar = pltpu.get_barrier_semaphore()
        for peer in (self.core, self.x, self.y, self.n1):
            pl.semaphore_signal(bar, inc=1, device_id=(peer,), device_id_type=MESH)

        @pl.when(self.mid)
        def _():
            pl.semaphore_signal(bar, inc=1, device_id=(self.n2,), device_id_type=MESH)

        pl.semaphore_wait(bar, 4 + self.mid.astype(jnp.int32))


class Sends:
    def __init__(self, sems):
        self.sems, self.used, self.open = sems, 0, []

    def push(self, src, dst, rsem, peer, when=None):
        ssem = self.sems.at[self.used]
        self.used += 1

        def copy():
            return pltpu.make_async_remote_copy(
                src, dst, ssem, rsem, device_id=(peer,), device_id_type=MESH
            )

        if when is None:
            copy().start()
        else:
            pl.when(when)(lambda: copy().start())
        self.open.append((lambda: copy().wait_send(), when))

    def finish(self):
        for wait, when in self.open:
            if when is None:
                wait()
            else:
                pl.when(when)(wait)
        self.open = []


def arrive(dst, rsem, spot):
    pltpu.make_async_remote_copy(
        dst, dst, rsem, rsem, device_id=(spot.core,), device_id_type=MESH
    ).wait_recv()


def gather_steps(spot, src, dst, rows, sends, rsem, own_sem):
    half = src.shape[1] // 2
    cols = (pl.ds(0, half), pl.ds(half, half))
    me, mid, shift = spot.me, spot.mid, spot.shift
    first, last = (spot.x, spot.y), (spot.y, spot.x)
    own = pltpu.make_async_copy(src.at[rows, :], dst.at[me, rows, :], own_sem)
    own.start()

    def push(part, block, peer, mine=False, when=None):
        there = dst.at[block, rows, cols[part]]
        here = src.at[rows, cols[part]] if mine else there
        sends.push(here, there, rsem.at[part, block], peer, when)

    def landed(part, block):
        arrive(dst.at[block, rows, cols[part]], rsem.at[part, block], spot)

    for part in (0, 1):
        push(part, me, spot.n1, True)
        push(part, me, spot.n2, True, mid)
        push(part, me, first[part], True)
        push(part, me, last[part], True)
    for part in (0, 1):
        push(part, me, spot.core, True)
    yield

    def from_z(part, j):
        b = me + shift[j]
        landed(part, b)
        push(part, b, spot.n2 if j == 1 else spot.n1, when=mid)
        push(part, b, first[part])
        push(part, b, last[part])
        push(part, b, spot.core)

    def from_first(part, j):
        b = first[part] + shift[j]
        landed(part, b)
        push(part, b, last[part])
        push(part, b, spot.core)

    def from_last(part, b):
        landed(part, b)
        push(part, b, spot.core)

    for j in range(4):
        if j:
            for part in (0, 1):
                from_z(part, j)
                yield
        for part in (0, 1):
            from_first(part, j)
        yield
        if j:
            for part in (0, 1):
                from_last(part, last[part] + shift[j - 1])
            yield
    for part in (0, 1):
        from_last(part, last[part] + shift[3])
    yield
    for j in range(4):
        for part in (0, 1):
            from_last(part, spot.diag + shift[j])
        yield
    for j in range(4):
        for base in (me, spot.x, spot.y, spot.diag):
            for part in (0, 1):
                landed(part, base + spot.core - me + shift[j])
    own.wait()
    yield


def scatter_steps(spot, p_refs, o_refs, rows, bufs, sems, sends):
    m_ref, s_ref, first_ref, second_ref, za_ref, zb_ref = bufs
    lsem, csem, fsem, gsem, zasem, zbsem = sems
    given = len(p_refs)
    width = p_refs[0].shape[2]
    half = given * width // 2
    me, mid, end, zs = spot.me, spot.mid, spot.end, spot.zs
    cols, short = (pl.ds(0, half), pl.ds(half, half)), pl.ds(0, half)
    plane = (me, spot.x, spot.y, spot.diag)
    first_peer, second_peer = (spot.y, spot.x), (spot.x, spot.y)
    start, size = rows.start, rows.size

    def mine(q, j, part):
        return m_ref.at[q * 4 + zs[j], rows, cols[part]]

    def held(ref, part, slot):
        return ref.at[part, slot, rows, short]

    def chunks(count, step):
        lax.fori_loop(0, size // 16, lambda i, _: step(pl.ds(pl.multiple_of(start + i * 16, 16), 16)) or _, 0)

    def add(q, j, part, *more):
        def step(r):
            v = m_ref[q * 4 + zs[j], r, cols[part]].astype(jnp.float32)
            for ref, slot in more:
                v = v + ref[part, slot, r, short].astype(jnp.float32)
            m_ref[q * 4 + zs[j], r, cols[part]] = v.astype(m_ref.dtype)

        chunks(size, step)

    def pair_exchange(j):
        for q in (3, 2, 1, 0):
            b = plane[q] + spot.shift[j]
            slot = q * 4 + zs[j]
            for i, p_ref in enumerate(p_refs):
                own = pl.ds(i * width, width)
                sends.push(p_ref.at[b + spot.core - me, rows, :], s_ref.at[slot, rows, own], csem.at[i, slot], spot.core)
                pltpu.make_async_copy(p_ref.at[b, rows, :], m_ref.at[slot, rows, own], lsem.at[i, slot]).start()

    def joined(q, j):
        slot = q * 4 + zs[j]
        for i, p_ref in enumerate(p_refs):
            own = pl.ds(i * width, width)
            pltpu.make_async_copy(p_ref.at[0, rows, :], m_ref.at[slot, rows, own], lsem.at[i, slot]).wait()
            arrive(s_ref.at[slot, rows, own], csem.at[i, slot], spot)
        everything = pl.ds(0, given * width)

        def step(r):
            v = m_ref[slot, r, everything].astype(jnp.float32) + s_ref[slot, r, everything].astype(jnp.float32)
            m_ref[slot, r, everything] = v.astype(m_ref.dtype)

        chunks(size, step)

    def to_first(part, q, j):
        slot = (4 if q == 3 else 0) + zs[j]
        sends.push(mine(q, j, part), held(first_ref, part, slot), fsem.at[part, slot], first_peer[part])

    def first_stage(j):
        joined(3, j)
        if j:
            pair_exchange(j - 1)
        to_first(0, 3, j)
        to_first(1, 3, j)
        joined(2, j)
        to_first(0, 2, j)
        joined(1, j)
        to_first(1, 1, j)

    def second_stage(j):
        for part in (0, 1):
            q, slot = (1, 2)[part], 4 + zs[j]
            arrive(held(first_ref, part, slot), fsem.at[part, slot], spot)
            add(q, j, part, (first_ref, slot))
            sends.push(mine(q, j, part), held(second_ref, part, zs[j]), gsem.at[part, zs[j]], second_peer[part])
        joined(0, j)

    def z_send(j):
        for part in (0, 1):
            arrive(held(first_ref, part, zs[j]), fsem.at[part, zs[j]], spot)
            arrive(held(second_ref, part, zs[j]), gsem.at[part, zs[j]], spot)
            add(0, j, part, (first_ref, zs[j]), (second_ref, zs[j]))
            if j:
                sends.push(mine(0, j, part), held(za_ref, part, 3 - j), zasem.at[part, 3 - j], spot.n1, end)

    def z_relay(j):
        if not j:
            return
        for part in (0, 1):
            came, sem, slot = (za_ref, zasem, 3 - j) if j > 1 else (zb_ref, zbsem, 0)

            @pl.when(mid)
            def _():
                arrive(held(came, part, slot), sem.at[part, slot], spot)
                add(0, j, part, (came, slot))

            slot = 3 - j if j > 1 else 0
            peer = spot.n2 if j > 1 else spot.n1
            sends.push(mine(0, j, part), held(zb_ref, part, slot), zbsem.at[part, slot], peer, mid)

    pair_exchange(3)
    stages = (first_stage, second_stage, z_send, z_relay)
    for step in range(4 + len(stages) - 1):
        for stage, what in enumerate(stages):
            j = 3 - (step - stage)
            if 0 <= j <= 3:
                what(j)
                yield
    for part in (0, 1):
        o_ref, there = (o_refs[part], pl.ds(0, half)) if given == 2 else (o_refs[0], cols[part])

        def total(*more):
            def step(r):
                v = m_ref[zs[0], r, cols[part]].astype(jnp.float32)
                for ref, slot in more:
                    v = v + ref[part, slot, r, short].astype(jnp.float32)
                o_ref[r, there] = v

            chunks(size, step)

        @pl.when(mid)
        def _():
            arrive(held(za_ref, part, 2), zasem.at[part, 2], spot)
            arrive(held(zb_ref, part, 1), zbsem.at[part, 1], spot)
            total((za_ref, 2), (zb_ref, 1))

        @pl.when(end)
        def _():
            arrive(held(zb_ref, part, 0), zbsem.at[part, 0], spot)
            total((zb_ref, 0))

    yield


def weave(tasks):
    ended, clocks, left = {}, {}, dict(tasks)
    while left:
        best = None
        for name, (after, delay, pace, _) in left.items():
            if any(other not in ended for other in after):
                continue
            at = clocks.get(name, max([ended[other] for other in after], default=0.0) + delay)
            if best is None or at < best[0]:
                best = (at, name)
        at, name = best
        _, _, pace, steps = left[name]
        try:
            next(steps)
            clocks[name] = at + pace
        except StopIteration:
            ended[name] = at
            del left[name]


N_GATHER_SENDS = 66
FEED_BLOCKS = 8


def middle_kernel(cuts, *refs):
    part_ref, rows_ref, up_ref, gain_ref, w_ref, wd_ref = refs[:6]
    d_all_ref, result_ref, d_mid_ref, gain_grad_ref, w_grad_ref, wd_grad_ref = refs[6:12]
    up_all_ref, x_all_ref, back_ref, forth_ref = refs[12:16]
    branch_ref, middle_ref, x_ref, dn_ref, down_ref, d_ref = refs[16:22]
    bufs = refs[22:28]
    x_in, up_in, back_out, forth_out = refs[28:32]
    own_sem, g_ssem, g_rsem, feed_sem = refs[32:36]
    one_sems, two_sems = refs[36:43], refs[43:50]
    spot = Spot()
    spot.greet()
    width = rows_ref.shape[1]
    units = wd_ref.shape[0]
    count = part_ref.shape[0]
    ranges = [pl.ds(a, b - a) for a, b in zip(cuts[:-1], cuts[1:])]
    everything = pl.ds(0, cuts[-1])
    w_grad_ref[...] = jnp.zeros_like(w_grad_ref)
    wd_grad_ref[...] = jnp.zeros_like(wd_grad_ref)
    gain_grad_ref[...] = jnp.zeros_like(gain_grad_ref)
    sends = {}

    def rows_of(rows):
        return [pl.ds(rows.start + i, 16) for i in range(0, rows.size, 16)]

    def scale_of(v):
        return lax.rsqrt(jnp.sum(v * v, axis=1, keepdims=True) / width + EPSILON)

    def gathering(name, at, src, dst, rows):
        sends[name] = Sends(g_ssem.at[at])
        yield from gather_steps(spot, src, dst, rows, sends[name], g_rsem.at[at], own_sem.at[at])

    def scattering(name, p_refs, o_refs, rows, sems, at, before=()):
        for other in before:
            sends[other].finish()
        sends[name] = Sends(sems[0].at[at])
        yield from scatter_steps(spot, p_refs, o_refs, rows, bufs, [sem.at[at] for sem in sems[1:]], sends[name])

    def first_norm(rows):
        for r in rows_of(rows):
            v = rows_ref[r, :].astype(jnp.float32) + branch_ref[r, :]
            middle_ref[r, :] = v
            x_ref[r, :] = (v * scale_of(v) * gain_ref[...]).astype(x_ref.dtype)
        yield

    def norm_back_rows(rows):
        for r in rows_of(rows):
            v, d, gain = middle_ref[r, :], dn_ref[r, :], gain_ref[...]
            scale = scale_of(v)
            result_ref[r, :] = (v + down_ref[r, :]).astype(result_ref.dtype)
            gain_grad_ref[...] += jnp.sum(d * v * scale, axis=0, keepdims=True)
            w = gain * d
            mean = jnp.sum(w * v, axis=1, keepdims=True) / width
            d_mid = up_ref[r, :].astype(jnp.float32) + scale * w - v * (scale * scale * scale) * mean
            d_mid_ref[r, :] = d_mid
            d_ref[r, :] = d_mid.astype(d_ref.dtype)
        yield

    def feeding(rows):
        size = rows.size
        steps = count // FEED_BLOCKS
        deep = pl.ds(0, size)

        def fetch(step, slot):
            blocks = pl.ds(step * FEED_BLOCKS, FEED_BLOCKS)
            return [
                pltpu.make_async_copy(ref.at[blocks, rows, :], to.at[slot, :, deep, :], feed_sem.at[i, slot])
                for i, (ref, to) in enumerate(((x_all_ref, x_in), (up_all_ref, up_in)))
            ]

        def store(step):
            blocks = pl.ds(step * FEED_BLOCKS, FEED_BLOCKS)
            return [
                pltpu.make_async_copy(of.at[:, deep, :], ref.at[blocks, rows, :], feed_sem.at[2 + i, 0])
                for i, (ref, of) in enumerate(((back_ref, back_out), (forth_ref, forth_out)))
            ]

        for copy in fetch(0, 0):
            copy.start()
        for step in range(steps):
            slot = step % 2
            if step + 1 < steps:
                for copy in fetch(step + 1, 1 - slot):
                    copy.start()
            for copy in fetch(step, slot):
                copy.wait()
            x = x_in[slot, :, :size, :].reshape(-1, width)
            upstream = up_in[slot, :, :size, :].reshape(-1, width)
            both = over(x, w_ref[...])
            gate, up = both[:, :units], both[:, units:]
            d_hidden = over(upstream, wd_ref[...], 1, 1)
            gelu, d_gelu = gelu_pair(gate)
            hidden = low(gelu * up)
            d_both = jnp.concatenate((low(d_hidden * up * d_gelu), low(d_hidden * gelu)), axis=1)
            if step:
                for copy in store(step - 1):
                    copy.wait()
            shape = (FEED_BLOCKS, size, width)
            back_out[:, :size, :] = low(over(d_both, w_ref[...], 1, 1)).reshape(shape)
            forth_out[:, :size, :] = low(over(hidden, wd_ref[...])).reshape(shape)
            for copy in store(step):
                copy.start()
            w_grad_ref[...] += over(d_both, x, 0, 0)
            wd_grad_ref[...] += over(hidden, upstream, 0, 0)
            yield
        for copy in store(steps - 1):
            copy.wait()
        yield

    tasks = {"up": ([], 12.0, 2.0, gathering("up", 0, up_ref, up_all_ref, everything))}
    for i, rows in enumerate(ranges):
        h, k = str(i), len(ranges)
        earlier = [f"feed{i - 1}"] if i else []
        tasks |= {
            "one" + h: ([], 7.0 * i, 2.0, scattering("one" + h, (part_ref,), (branch_ref,), rows, one_sems, i)),
            "norm" + h: (["one" + h], 0.0, 0.5, first_norm(rows)),
            "x" + h: (["norm" + h], 0.0, 1.2, gathering("x" + h, 1 + i, x_ref, x_all_ref, rows)),
            "feed" + h: (["x" + h, "up"] + earlier, 0.0, 4.0, feeding(rows)),
            "two" + h: (
                ["feed" + h], 0.0, 3.0,
                scattering("two" + h, (back_ref, forth_ref), (dn_ref, down_ref), rows, two_sems, i, ["one" + h]),
            ),
            "back" + h: (["two" + h], 0.0, 0.5, norm_back_rows(rows)),
            "d" + h: (["back" + h], 0.0, 1.2, gathering("d" + h, 1 + k + i, d_ref, d_all_ref, rows)),
        }
    weave(tasks)
    for some in sends.values():
        some.finish()


def gelu_pair(gate):
    slope = 0.7978845608028654
    squared = gate * gate
    bent = jnp.tanh(slope * (gate + 0.044715 * gate * squared))
    gelu = 0.5 * gate * (1.0 + bent)
    return gelu, 0.5 * (1.0 + bent) + 0.5 * gate * (1.0 - bent * bent) * slope * (1.0 + 3.0 * 0.044715 * squared)


def middle_part(partial, rows_low, upstream_low, gain, w, wd):
    count, rows, width = partial.shape
    cuts = (0, 48, 80) if rows == 80 else (0, rows)
    halves = len(cuts) - 1
    deep = max(b - a for a, b in zip(cuts[:-1], cuts[1:]))
    low_rows, all_rows = (rows, width), (count, rows, width)
    bf, wide, dma = jnp.bfloat16, jnp.float32, pltpu.SemaphoreType.DMA

    def scatter_sems(given):
        return [
            dma((halves, 16 * given + 36)), dma((halves, given, 16)), dma((halves, given, 16)), dma((halves, 2, 8)),
            dma((halves, 2, 4)), dma((halves, 2, 3)), dma((halves, 2, 2)),
        ]

    vmem, hbm = pl.BlockSpec(memory_space=pltpu.VMEM), pl.BlockSpec(memory_space=pl.ANY)
    shape = jax.ShapeDtypeStruct
    outs = pl.pallas_call(
        functools.partial(middle_kernel, cuts),
        out_shape=[
            shape(all_rows, bf), shape(low_rows, bf), shape(low_rows, wide), shape((1, width), wide),
            shape((w.shape[1], width), wide), shape(wd.shape, wide),
        ] + [shape(all_rows, bf)] * 4,
        in_specs=[hbm] + [vmem] * 5,
        out_specs=[hbm] + [vmem] * 5 + [hbm] * 4,
        scratch_shapes=[
            pltpu.VMEM(low_rows, wide), pltpu.VMEM(low_rows, wide), pltpu.VMEM(low_rows, bf),
            pltpu.VMEM(low_rows, wide), pltpu.VMEM(low_rows, wide), pltpu.VMEM(low_rows, bf),
            pltpu.VMEM((16, rows, 2 * width), bf), pltpu.VMEM((16, rows, 2 * width), bf),
            pltpu.VMEM((2, 8, rows, width), bf), pltpu.VMEM((2, 4, rows, width), bf),
            pltpu.VMEM((2, 3, rows, width), bf), pltpu.VMEM((2, 2, rows, width), bf),
            pltpu.VMEM((2, FEED_BLOCKS, deep, width), bf), pltpu.VMEM((2, FEED_BLOCKS, deep, width), bf),
            pltpu.VMEM((FEED_BLOCKS, deep, width), bf), pltpu.VMEM((FEED_BLOCKS, deep, width), bf),
            dma((1 + 2 * halves,)), dma((1 + 2 * halves, N_GATHER_SENDS)), dma((1 + 2 * halves, 2, 32)), dma((4, 2)),
        ] + scatter_sems(1) + scatter_sems(2),
        name="middle_part",
        compiler_params=pltpu.CompilerParams(collective_id=3, has_side_effects=True, vmem_limit_bytes=63 * 2**20),
    )(partial, rows_low, upstream_low, gain, w, wd)
    return outs[:6]


def exchange(blocks):
    return lax.all_to_all(blocks, AXIS, split_axis=0, concat_axis=0, tiled=True)


def dot(left, right):
    return jnp.dot(left, right, preferred_element_type=jnp.float32)


def select(mask, rows):
    return dot(mask.astype(jnp.bfloat16), rows).astype(jnp.bfloat16)


def beside(sent, chain, kernel):
    sent, chain = lax.optimization_barrier((sent, chain))
    return lax.optimization_barrier((exchange(sent), kernel(chain)))


def pack_kernel(query_ref, key_ref, value_ref, gate_ref, up_ref, first_ref, second_ref):
    count = first_ref.shape[0]
    head = query_ref.shape[1] // count
    units = gate_ref.shape[1] // count
    for j in range(count):
        for i, ref in enumerate((query_ref, key_ref, value_ref)):
            first_ref[j, :, i * head : (i + 1) * head] = ref[:, j * head : (j + 1) * head]
        first_ref[j, :, 3 * head :] = gate_ref[:, j * units : j * units + head]
        second_ref[j, :, : units - head] = gate_ref[:, j * units + head : (j + 1) * units]
        second_ref[j, :, units - head :] = up_ref[:, j * units : (j + 1) * units]


def pack(shards, count):
    rows, width = shards[0].shape
    head, units = width // count, shards[3].shape[1] // count
    return pl.pallas_call(
        pack_kernel,
        out_shape=[
            jax.ShapeDtypeStruct((count, rows, 4 * head), jnp.bfloat16),
            jax.ShapeDtypeStruct((count, rows, 2 * units - head), jnp.bfloat16),
        ],
        in_specs=[pl.BlockSpec(memory_space=pltpu.VMEM)] * 5,
        out_specs=[pl.BlockSpec(memory_space=pltpu.VMEM)] * 2,
        name="pack_columns",
        compiler_params=pltpu.CompilerParams(vmem_limit_bytes=32 * 2**20),
    )(*shards)


def unpack_kernel(first_ref, second_ref, query_ref, key_ref, value_ref, gate_ref, up_ref):
    count = first_ref.shape[0]
    head = query_ref.shape[1] // count
    units = gate_ref.shape[1] // count
    wide = jnp.float32
    for j in range(count):
        for i, ref in enumerate((query_ref, key_ref, value_ref)):
            ref[:, j * head : (j + 1) * head] = first_ref[j, :, i * head : (i + 1) * head].astype(wide)
        gate_ref[:, j * units : j * units + head] = first_ref[j, :, 3 * head :].astype(wide)
        gate_ref[:, j * units + head : (j + 1) * units] = second_ref[j, :, : units - head].astype(wide)
        up_ref[:, j * units : (j + 1) * units] = second_ref[j, :, units - head :].astype(wide)


def unpack(first, second, width, hidden):
    rows = first.shape[1]
    widths = (width, width, width, hidden, hidden)
    return pl.pallas_call(
        unpack_kernel,
        out_shape=[jax.ShapeDtypeStruct((rows, columns), jnp.float32) for columns in widths],
        in_specs=[pl.BlockSpec(memory_space=pltpu.VMEM)] * 2,
        out_specs=[pl.BlockSpec(memory_space=pltpu.VMEM)] * 5,
        name="unpack_columns",
        compiler_params=pltpu.CompilerParams(vmem_limit_bytes=32 * 2**20),
    )(first, second)


def body(
    tokens,
    lengths,
    permutation,
    query_weight,
    key_weight,
    value_weight,
    out_weight,
    gate_weight,
    up_weight,
    down_weight,
    gain_attention,
    gain_feedforward,
    bias_table,
    cotangent,
):
    me = lax.axis_index(AXIS)
    count = tokens.shape[0]
    grain = tokens.shape[1]
    length = cotangent.shape[1]
    width = tokens.shape[2]
    shard = query_weight.shape[0]
    hidden_width = gate_weight.shape[1] // count
    head = HEAD_DIM
    total = 3 * count * length // 5
    tiles = -(-total // length)
    slots = tiles * grain

    small = jnp.concatenate((gain_attention, gain_feedforward, bias_table))
    small = jnp.pad(small, (0, grain * 128 - small.shape[0])).reshape(1, grain, 128)
    small = jnp.broadcast_to(small, (count, grain, 128))
    came = exchange(jnp.concatenate((tokens[permutation], small), axis=2))
    dealt = came[:, :, :width].reshape(length, width)
    small = came[:, :, width:].reshape(count, -1)
    gain_one = small[:, :shard].reshape(-1).astype(jnp.float32)
    gain_two = small[:, shard : 2 * shard].reshape(-1).astype(jnp.float32)
    table = small[:, 2 * shard : 2 * shard + HEADS]

    dealt_lengths = lengths[permutation]
    ends = jnp.cumsum(dealt_lengths)
    starts = ends - dealt_lengths
    my_start, my_length = starts[me], dealt_lengths[me]
    place_in = jnp.arange(length, dtype=jnp.int32)
    turn = (
        (place_in[:, None] - my_start) % length == place_in[None, :]
    ) & (place_in[None, :] < my_length)
    slot_ids = jnp.arange(slots, dtype=jnp.int32)
    packed_ids = slot_ids // grain * length + me * grain + slot_ids % grain
    source_seq = jnp.sum((packed_ids[:, None] >= ends[None, :]).astype(jnp.int32), axis=1)
    pick = (source_seq * grain + slot_ids % grain)[:, None] == place_in[None, :]

    def spread_out(rows):
        return select(turn, rows).reshape(count, grain, width)

    def packed_block(came):
        return select(pick, came.reshape(length, width))

    rows_low = packed_block(exchange(spread_out(dealt)))
    rows_in = rows_low.astype(jnp.float32)
    first_columns, second_columns = pack(
        (query_weight, key_weight, value_weight, gate_weight, up_weight), count
    )

    all_ids = jnp.arange(tiles * length, dtype=jnp.int32)
    segment = jnp.sum((all_ids[:, None] >= ends[None, :]).astype(jnp.int32), axis=1) + 1
    column, row = segment[:, None], jnp.pad(segment, (length, length))[None, :]
    relative = (
        jnp.arange(3 * length, dtype=jnp.int32)[None, :] - length - place_in[:, None]
    ).reshape(-1)
    onehot = bucket_index(relative)[None, :] == jnp.arange(BUCKETS, dtype=jnp.int32)[:, None]
    head_table = lax.dynamic_slice_in_dim(table, me, 1, axis=1)
    rel_bias = dot(head_table.T, onehot.astype(jnp.bfloat16)).reshape(length, 3 * length)
    few = 16
    ids = jnp.arange(few * count, dtype=jnp.int32)
    ids = ids % length // grain * few + ids // length * grain + ids % grain
    perm = (ids[:, None] == jnp.arange(few * count, dtype=jnp.int32)[None, :]).astype(jnp.bfloat16)

    def owners_share(turned):
        return lax.optimization_barrier(turned).T.reshape(count, shard, -1)

    scale_one = norm_scale(rows_in)
    normed = (rows_in * scale_one * gain_one).astype(jnp.bfloat16)
    cut = (count, -1, 4 * head)
    sent = jnp.concatenate((first_columns, spread_out(cotangent[0]).reshape(cut)), axis=1)
    normed, perm, rel_bias, column, row = lax.optimization_barrier(
        (normed, perm, rel_bias, column, row)
    )
    came, normed_all = beside(sent, normed, gather)
    first_columns = came[:, :shard].reshape(-1, 4 * head)
    upstream_low = packed_block(came[:, shard:])
    qkv_columns = first_columns[:, : 3 * head]
    shared = (qkv_columns, out_weight, perm, rel_bias, column, row)
    came, (qkv, attended, partial) = beside(
        second_columns, (normed_all, *shared), lambda given: attend(*given)
    )
    second_columns = came.reshape(count * shard, -1)
    gate_up_columns = jnp.concatenate((first_columns[:, 3 * head :], second_columns), axis=1)

    d_branch_all, result, d_middle, gain_two_grad, gate_up_grad, down_grad = middle_part(
        partial, rows_low, upstream_low, gain_two[None, :], gate_up_columns, down_weight
    )
    gate_up_grad = gate_up_grad.astype(jnp.bfloat16)
    turned = starts + (me * grain + jnp.arange(grain, dtype=jnp.int32)[:, None] - starts) % length
    back_slot = (turned // length * grain + jnp.arange(grain, dtype=jnp.int32)[:, None]).T
    spread = back_slot.reshape(-1, 1) == slot_ids[None, :]

    sent = jnp.concatenate(
        (owners_share(gate_up_grad[head:]), select(spread, result).reshape(cut)), axis=1
    )
    came, (partial, out_grad, qkv_grad, bias_grad) = beside(
        sent, (d_branch_all, normed_all, attended, qkv, *shared), lambda given: attend_back(*given)
    )
    second_grad = came[:, :shard]
    layer_output = select(turn.T, came[:, shard:].reshape(length, width))[None]
    table_sum = jnp.sum(jnp.where(onehot, bias_grad.reshape(1, -1), 0.0), axis=1)
    qkv_grad = qkv_grad.astype(jnp.bfloat16)
    sent = owners_share(jnp.concatenate((qkv_grad, gate_up_grad[:head]), axis=0))
    first_grad, d_normed = beside(sent, partial, scatter)
    gain_one_grad = jnp.sum(d_normed * rows_in * scale_one, axis=0)
    d_dealt = (d_middle + norm_back(rows_in, scale_one, gain_one, d_normed)).astype(jnp.bfloat16)

    sums = jnp.concatenate(
        (
            gain_one_grad.reshape(count, shard),
            gain_two_grad.reshape(count, shard),
            table_sum.reshape(count, 1),
        ),
        axis=1,
    )
    high = lax.reduce_precision(sums, 8, 7)
    sums = jnp.concatenate((high, sums - high), axis=1).astype(jnp.bfloat16)
    sums = jnp.pad(sums, ((0, 0), (0, grain * 128 - sums.shape[1]))).reshape(count, grain, 128)
    going = select(spread, d_dealt).reshape(count, grain, width)
    came = exchange(jnp.concatenate((going, sums), axis=2))
    sums = came[:, :, width:].reshape(count, -1).astype(jnp.float32)
    sums = sums[:, : 2 * shard + 1] + sums[:, 2 * shard + 1 : 4 * shard + 2]
    came = select(turn.T, came[:, :, :width].reshape(length, width))
    tokens_grad = exchange(came.reshape(count, grain, width))[jnp.argsort(permutation)]

    query_grad, key_grad, value_grad, gate_grad, up_grad = unpack(
        first_grad, second_grad, width, hidden_width * count
    )
    return (
        layer_output,
        tokens_grad,
        query_grad,
        key_grad,
        value_grad,
        out_grad,
        gate_grad,
        up_grad,
        down_grad,
        jnp.sum(sums[:, :shard], axis=0),
        jnp.sum(sums[:, shard : 2 * shard], axis=0),
        sums[:, 2 * shard],
    )


def solution(mesh):
    placed = (
        P(None, "fsdp", None),
        P(),
        P(),
        P("fsdp", None),
        P("fsdp", None),
        P("fsdp", None),
        P("fsdp", None),
        P("fsdp", None),
        P("fsdp", None),
        P("fsdp", None),
        P("fsdp"),
        P("fsdp"),
        P("fsdp"),
        P("fsdp", None, None),
    )
    return jax.shard_map(
        body if mesh.shape[AXIS] == 32 else body_any,
        mesh=mesh,
        in_specs=placed,
        out_specs=(
            P("fsdp", None, None),
            P(None, "fsdp", None),
            P("fsdp", None),
            P("fsdp", None),
            P("fsdp", None),
            P("fsdp", None),
            P("fsdp", None),
            P("fsdp", None),
            P("fsdp", None),
            P("fsdp"),
            P("fsdp"),
            P("fsdp"),
        ),
        check_vma=False,
    )
```

```python
import functools

import jax
import jax.numpy as jnp
from jax import lax
from jax.experimental import pallas as pl
from jax.experimental.pallas import tpu as pltpu
from jax.sharding import PartitionSpec as P

HEADS = 32
HEAD_DIM = 64
BUCKETS = 32


EPSILON = 1e-06
masked_score = -1000000000.0
HIGHEST = lax.Precision.HIGHEST


def bucket_index(relative):
    half_buckets = BUCKETS // 2
    exact_count = half_buckets // 2
    distance = jnp.abs(relative)
    side_offset = jnp.where(relative > 0, half_buckets, 0).astype(jnp.int32)
    square = distance * distance
    far_bucket = jnp.full_like(distance, exact_count)
    for doubling in range(1, half_buckets - exact_count):
        far_bucket = far_bucket + (square >= exact_count * exact_count * 2**doubling).astype(
            jnp.int32
        )
    return side_offset + jnp.where(distance < exact_count, distance, far_bucket)


def bucket_onehot(seq_len):
    positions = jnp.arange(seq_len, dtype=jnp.int32)
    relative = (positions[None, :] - positions[:, None]).reshape(-1)
    bucket_ids = jnp.arange(BUCKETS, dtype=jnp.int32)
    return (bucket_index(relative)[None, :] == bucket_ids[:, None]).astype(jnp.float32)


def norm_scale(values):
    return lax.rsqrt(jnp.mean(values * values, axis=-1, keepdims=True) + EPSILON)


def norm_back(values, scale, gain_vec, d_norm):
    weighted = gain_vec * d_norm
    return scale * weighted - values * (scale * scale * scale) * jnp.mean(
        weighted * values, axis=-1, keepdims=True
    )


def rows_product(left, right):
    return lax.dot_general(
        left, right, (((0,), (0,)), ((), ())), preferred_element_type=jnp.float32
    )


def against_rows(left, right):
    return lax.dot_general(
        left, right, (((1,), (1,)), ((), ())), preferred_element_type=jnp.float32
    )


def masked_scores(query_heads, key_heads, rel_bias, length):
    scores = (
        jnp.einsum("qhd,khd->hqk", query_heads, key_heads, preferred_element_type=jnp.float32)
        + rel_bias
    )
    key_valid = jnp.arange(key_heads.shape[0], dtype=jnp.int32) < length
    return jnp.where(key_valid[None, None, :], scores, masked_score)


def unpack_weights(full_weights, onehot, seq_len):
    table_full = full_weights[4].astype(jnp.float32).reshape(BUCKETS, HEADS)
    rel_bias = jnp.dot(table_full.T, onehot, precision=HIGHEST).reshape(HEADS, seq_len, seq_len)
    return (
        full_weights[0],
        full_weights[1],
        full_weights[2].astype(jnp.float32),
        full_weights[3].astype(jnp.float32),
        rel_bias,
    )


def body_any(
    tokens,
    lengths,
    permutation,
    query_weight,
    key_weight,
    value_weight,
    out_weight,
    gate_weight,
    up_weight,
    down_weight,
    gain_attention,
    gain_feedforward,
    bias_table,
    cotangent,
):
    model_width = query_weight.shape[1]
    hidden_width = gate_weight.shape[1]
    packed = jnp.concatenate(
        (query_weight, key_weight, value_weight, out_weight, gate_weight, up_weight), axis=1
    )
    shards = (packed, down_weight, gain_attention, gain_feedforward, bias_table)
    full_weights = (
        lax.all_gather(shards[0], "fsdp", axis=0, tiled=True),
        lax.all_gather(shards[1], "fsdp", axis=0, tiled=True),
        lax.all_gather(shards[2], "fsdp", axis=0, tiled=True),
        lax.all_gather(shards[3], "fsdp", axis=0, tiled=True),
        lax.all_gather(shards[4], "fsdp", axis=0, tiled=True),
    )
    reordered = tokens[permutation]
    dealt = lax.all_to_all(reordered, "fsdp", split_axis=0, concat_axis=1, tiled=True)
    seq_count = dealt.shape[0]
    seq_len = dealt.shape[1]
    local_ids = lax.dynamic_slice_in_dim(permutation, lax.axis_index("fsdp") * seq_count, seq_count)
    seq_lengths = lengths[local_ids]
    positions = jnp.arange(seq_len, dtype=jnp.int32)
    row_valid = (positions[None, :] < seq_lengths[:, None]).astype(jnp.float32).reshape(-1, 1)
    onehot = bucket_onehot(seq_len)
    onehot_low = onehot.astype(jnp.bfloat16)
    full_packed, full_down, gain_one, gain_two, rel_bias = unpack_weights(
        full_weights, onehot, seq_len
    )
    head_shape = (seq_count, seq_len, HEADS, HEAD_DIM)
    rows_in = dealt.reshape(-1, model_width).astype(jnp.float32)
    scale_one = norm_scale(rows_in)
    normed = (rows_in * scale_one * gain_one).astype(jnp.bfloat16)
    projected = jnp.dot(
        normed, full_packed[:, : 3 * model_width], preferred_element_type=jnp.float32
    ).astype(jnp.bfloat16)
    query_heads = projected[:, :model_width].reshape(head_shape)
    key_heads = projected[:, model_width : 2 * model_width].reshape(head_shape)
    value_heads = projected[:, 2 * model_width :].reshape(head_shape)

    def attend_forward(pieces):
        query_one, key_one, value_one, length = pieces
        scores = masked_scores(query_one, key_one, rel_bias, length)
        row_max = jnp.max(scores, axis=-1, keepdims=True)
        exp_total = jnp.sum(jnp.exp(scores - row_max), axis=-1, keepdims=True)
        log_total = row_max + jnp.log(exp_total)
        weights_soft = jnp.exp(scores - log_total).astype(jnp.bfloat16)
        attended_one = jnp.einsum(
            "hqk,khd->qhd", weights_soft, value_one, preferred_element_type=jnp.float32
        )
        return (attended_one.astype(jnp.bfloat16), log_total)

    attended_heads, log_totals = lax.map(
        attend_forward, (query_heads, key_heads, value_heads, seq_lengths)
    )
    attended_rows = attended_heads.reshape(-1, model_width)
    middle = rows_in + jnp.dot(
        attended_rows,
        full_packed[:, 3 * model_width : 4 * model_width],
        preferred_element_type=jnp.float32,
    )
    scale_two = norm_scale(middle)
    normed_two = (middle * scale_two * gain_two).astype(jnp.bfloat16)
    gate_up = jnp.dot(
        normed_two, full_packed[:, 4 * model_width :], preferred_element_type=jnp.float32
    )

    def gelu_product(gate_part, up_part):
        return jax.nn.gelu(gate_part, approximate=True) * up_part

    hidden_full, gelu_pull = jax.vjp(
        gelu_product, gate_up[:, :hidden_width], gate_up[:, hidden_width:]
    )
    hidden = hidden_full.astype(jnp.bfloat16)
    result = middle + jnp.dot(hidden, full_down, preferred_element_type=jnp.float32)
    layer_output = (
        (result * row_valid).astype(jnp.bfloat16).reshape(seq_count, seq_len, model_width)
    )
    full_weights = (
        lax.all_gather(shards[0], "fsdp", axis=0, tiled=True),
        lax.all_gather(shards[1], "fsdp", axis=0, tiled=True),
        lax.all_gather(shards[2], "fsdp", axis=0, tiled=True),
        lax.all_gather(shards[3], "fsdp", axis=0, tiled=True),
        lax.all_gather(shards[4], "fsdp", axis=0, tiled=True),
    )
    full_packed, full_down, gain_one, gain_two, rel_bias = unpack_weights(
        full_weights, onehot, seq_len
    )
    upstream = cotangent.reshape(-1, model_width).astype(jnp.float32) * row_valid
    upstream_low = upstream.astype(jnp.bfloat16)
    d_hidden = against_rows(upstream_low, full_down)
    d_gate, d_up = gelu_pull(d_hidden)
    d_gate_up = jnp.concatenate((d_gate, d_up), axis=1).astype(jnp.bfloat16)
    d_normed_two = against_rows(d_gate_up, full_packed[:, 4 * model_width :])
    gain_two_grad = jnp.sum(d_normed_two * middle * scale_two, axis=0)
    d_middle = upstream + norm_back(middle, scale_two, gain_two, d_normed_two)
    d_branch = d_middle.astype(jnp.bfloat16)
    d_attended = against_rows(d_branch, full_packed[:, 3 * model_width : 4 * model_width]).astype(
        jnp.bfloat16
    )

    def attend_backward(pieces):
        query_one, key_one, value_one, length, log_total, d_attended_one = pieces
        scores = masked_scores(query_one, key_one, rel_bias, length)
        probs = jnp.exp(scores - log_total)
        probs_low = probs.astype(jnp.bfloat16)
        d_value = jnp.einsum(
            "hqk,qhd->khd", probs_low, d_attended_one, preferred_element_type=jnp.float32
        )
        d_probs = jnp.einsum(
            "qhd,khd->hqk", d_attended_one, value_one, preferred_element_type=jnp.float32
        )
        inner = jnp.sum(probs * d_probs, axis=-1, keepdims=True)
        d_scores = (probs * (d_probs - inner)).astype(jnp.bfloat16)
        d_query = jnp.einsum("hqk,khd->qhd", d_scores, key_one, preferred_element_type=jnp.float32)
        d_key = jnp.einsum("hqk,qhd->khd", d_scores, query_one, preferred_element_type=jnp.float32)
        d_bias = against_rows(d_scores.reshape(HEADS, -1), onehot_low)
        return (
            (
                d_query.astype(jnp.bfloat16),
                d_key.astype(jnp.bfloat16),
                d_value.astype(jnp.bfloat16),
            ),
            d_bias,
        )

    (d_query_all, d_key_all, d_value_all), d_bias_all = lax.map(
        attend_backward,
        (
            query_heads,
            key_heads,
            value_heads,
            seq_lengths,
            log_totals,
            d_attended.reshape(head_shape),
        ),
    )
    d_qkv = jnp.concatenate(
        (
            d_query_all.reshape(-1, model_width),
            d_key_all.reshape(-1, model_width),
            d_value_all.reshape(-1, model_width),
        ),
        axis=1,
    )
    d_normed = against_rows(d_qkv, full_packed[:, : 3 * model_width])
    gain_one_grad = jnp.sum(d_normed * rows_in * scale_one, axis=0)
    d_rows = d_middle + norm_back(rows_in, scale_one, gain_one, d_normed)
    d_dealt = d_rows.astype(jnp.bfloat16).reshape(seq_count, seq_len, model_width)
    returned_rows = lax.all_to_all(d_dealt, "fsdp", split_axis=1, concat_axis=0, tiled=True)
    tokens_grad = returned_rows[jnp.argsort(permutation)]
    packed_grad = lax.psum_scatter(
        jnp.concatenate(
            (
                rows_product(normed, d_qkv),
                jnp.concatenate(
                    (rows_product(attended_rows, d_branch), rows_product(normed_two, d_gate_up)),
                    axis=1,
                ),
            ),
            axis=1,
        ),
        "fsdp",
        scatter_dimension=0,
        tiled=True,
    )
    mixer_grad = packed_grad[:, : 3 * model_width]
    branch_grad = packed_grad[:, 3 * model_width :]
    down_grad = lax.psum_scatter(
        rows_product(hidden, upstream_low), "fsdp", scatter_dimension=0, tiled=True
    )
    table_sum = jnp.sum(d_bias_all, axis=0).T.reshape(-1)
    gain_attention_grad, gain_feedforward_grad, table_grad = (
        lax.psum_scatter(gain_one_grad, "fsdp", scatter_dimension=0, tiled=True),
        lax.psum_scatter(gain_two_grad, "fsdp", scatter_dimension=0, tiled=True),
        lax.psum_scatter(table_sum, "fsdp", scatter_dimension=0, tiled=True),
    )
    return (
        layer_output,
        tokens_grad,
        mixer_grad[:, :model_width],
        mixer_grad[:, model_width : 2 * model_width],
        mixer_grad[:, 2 * model_width :],
        branch_grad[:, :model_width],
        branch_grad[:, model_width : model_width + hidden_width],
        branch_grad[:, model_width + hidden_width :],
        down_grad,
        gain_attention_grad,
        gain_feedforward_grad,
        table_grad,
    )


MESH = pl.DeviceIdType.MESH
AXIS = "fsdp"


def over(left, right, left_dim=1, right_dim=0):
    return lax.dot_general(
        left, right, (((left_dim,), (right_dim,)), ((), ())), preferred_element_type=jnp.float32
    )


def low(values):
    return values.astype(jnp.bfloat16)


def tile_probs(query, key, bias, same):
    scores = jnp.where(same, over(query, key, 1, 1) + bias, masked_score)
    grown = jnp.exp(scores - jnp.max(scores, axis=-1, keepdims=True))
    return grown / jnp.sum(grown, axis=-1, keepdims=True)


class Spot:
    def __init__(self):
        me = lax.axis_index(AXIS)
        c, x, y, z = me % 2, (me // 2) % 2, (me // 4) % 2, me // 8
        self.me = me
        self.mid = (z == 1) | (z == 2)
        self.end = jnp.logical_not(self.mid)
        self.zs = (z, z + 1 - 2 * (z % 2), 2 - z // 2, 3 - 3 * (z // 2))
        self.shift = [8 * (zz - z) for zz in self.zs]
        self.core, self.x, self.y = me + 1 - 2 * c, me + 2 - 4 * x, me + 4 - 8 * y
        self.diag = self.x + self.y - me
        self.n1, self.n2 = me + self.shift[1], me + self.shift[2]

    def greet(self):
        bar = pltpu.get_barrier_semaphore()
        for peer in (self.core, self.x, self.y, self.n1):
            pl.semaphore_signal(bar, inc=1, device_id=(peer,), device_id_type=MESH)

        @pl.when(self.mid)
        def _():
            pl.semaphore_signal(bar, inc=1, device_id=(self.n2,), device_id_type=MESH)

        pl.semaphore_wait(bar, 4 + self.mid.astype(jnp.int32))

    def greet_all(self, count):
        bar = pltpu.get_barrier_semaphore()

        def signal(d, _):
            peer = (self.me + d) % count
            pl.semaphore_signal(bar, inc=1, device_id=(peer,), device_id_type=MESH)
            return _

        lax.fori_loop(1, count, signal, 0)
        pl.semaphore_wait(bar, count - 1)


class Sends:
    def __init__(self, sems):
        self.sems, self.used, self.open = sems, 0, []

    def push(self, src, dst, rsem, peer, when=None):
        ssem = self.sems.at[self.used]
        self.used += 1

        def copy():
            return pltpu.make_async_remote_copy(
                src, dst, ssem, rsem, device_id=(peer,), device_id_type=MESH
            )

        if when is None:
            copy().start()
        else:
            pl.when(when)(lambda: copy().start())
        self.open.append((lambda: copy().wait_send(), when))

    def finish(self):
        for wait, when in self.open:
            if when is None:
                wait()
            else:
                pl.when(when)(wait)
        self.open = []


def arrive(dst, rsem, spot):
    pltpu.make_async_remote_copy(
        dst, dst, rsem, rsem, device_id=(spot.core,), device_id_type=MESH
    ).wait_recv()


def gather_steps(spot, src, dst, rows, sends, rsem, own_sem):
    half = src.shape[1] // 2
    cols = (pl.ds(0, half), pl.ds(half, half))
    me, mid, shift = spot.me, spot.mid, spot.shift
    first, last = (spot.x, spot.y), (spot.y, spot.x)
    own = pltpu.make_async_copy(src.at[rows, :], dst.at[me, rows, :], own_sem)
    own.start()

    def push(part, block, peer, mine=False, when=None):
        there = dst.at[block, rows, cols[part]]
        here = src.at[rows, cols[part]] if mine else there
        sends.push(here, there, rsem.at[part, block], peer, when)

    def landed(part, block):
        arrive(dst.at[block, rows, cols[part]], rsem.at[part, block], spot)

    for part in (0, 1):
        push(part, me, spot.n1, True)
        push(part, me, spot.n2, True, mid)
        push(part, me, first[part], True)
        push(part, me, last[part], True)
    for part in (0, 1):
        push(part, me, spot.core, True)
    yield

    def from_z(part, j):
        b = me + shift[j]
        landed(part, b)
        push(part, b, spot.n2 if j == 1 else spot.n1, when=mid)
        push(part, b, first[part])
        push(part, b, last[part])
        push(part, b, spot.core)

    def from_first(part, j):
        b = first[part] + shift[j]
        landed(part, b)
        push(part, b, last[part])
        push(part, b, spot.core)

    def from_last(part, b):
        landed(part, b)
        push(part, b, spot.core)

    for j in range(4):
        if j:
            for part in (0, 1):
                from_z(part, j)
                yield
        for part in (0, 1):
            from_first(part, j)
            yield
        if j:
            for part in (0, 1):
                from_last(part, last[part] + shift[j - 1])
                yield
    for part in (0, 1):
        from_last(part, last[part] + shift[3])
        yield
    for j in range(4):
        for part in (0, 1):
            from_last(part, spot.diag + shift[j])
            yield
    for j in range(4):
        for base in (me, spot.x, spot.y, spot.diag):
            for part in (0, 1):
                landed(part, base + spot.core - me + shift[j])
    own.wait()
    yield


def scatter_steps(spot, p_refs, o_refs, rows, bufs, sems, sends):
    ring_ref, s_ref, first_ref, second_ref, za_ref, zb_ref = bufs
    lsem, csem, fsem, gsem, zasem, zbsem = sems
    given = len(p_refs)
    width = p_refs[0].shape[2]
    half = given * width // 2
    me, mid, end, zs = spot.me, spot.mid, spot.end, spot.zs
    cols, short = (pl.ds(0, half), pl.ds(half, half)), pl.ds(0, half)
    plane = (me, spot.x, spot.y, spot.diag)
    first_peer, second_peer = (spot.y, spot.x), (spot.x, spot.y)
    start, size = rows.start, rows.size

    def mine(q, j, part):
        return s_ref.at[q * 4 + zs[j], rows, cols[part]]

    def held(ref, part, slot):
        return ref.at[part, slot, rows, short]

    def chunks(count, step):
        lax.fori_loop(0, size // 16, lambda i, _: step(pl.ds(pl.multiple_of(start + i * 16, 16), 16)) or _, 0)

    def add(q, j, part, *more):
        def step(r):
            v = s_ref[q * 4 + zs[j], r, cols[part]].astype(jnp.float32)
            for ref, slot in more:
                v = v + ref[part, slot, r, short].astype(jnp.float32)
            s_ref[q * 4 + zs[j], r, cols[part]] = v.astype(s_ref.dtype)

        chunks(size, step)

    def pair_exchange(j):
        for q in (3, 2, 1, 0):
            b = plane[q] + spot.shift[j]
            slot = q * 4 + zs[j]
            for i, p_ref in enumerate(p_refs):
                own = pl.ds(i * width, width)
                sends.push(p_ref.at[b + spot.core - me, rows, :], s_ref.at[slot, rows, own], csem.at[i, slot], spot.core)
                here = ring_ref.at[j % 2 * 4 + q, rows, own]
                pltpu.make_async_copy(p_ref.at[b, rows, :], here, lsem.at[i, j % 2 * 4 + q]).start()

    def joined(q, j):
        slot, near = q * 4 + zs[j], j % 2 * 4 + q
        for i, p_ref in enumerate(p_refs):
            own = pl.ds(i * width, width)
            pltpu.make_async_copy(p_ref.at[0, rows, :], ring_ref.at[near, rows, own], lsem.at[i, near]).wait()
            arrive(s_ref.at[slot, rows, own], csem.at[i, slot], spot)
        everything = pl.ds(0, given * width)

        def step(r):
            v = ring_ref[near, r, everything].astype(jnp.float32) + s_ref[slot, r, everything].astype(jnp.float32)
            s_ref[slot, r, everything] = v.astype(s_ref.dtype)

        chunks(size, step)

    def to_first(part, q, j):
        slot = (4 if q == 3 else 0) + zs[j]
        sends.push(mine(q, j, part), held(first_ref, part, slot), fsem.at[part, slot], first_peer[part])

    def first_stage(j):
        joined(3, j)
        if j:
            pair_exchange(j - 1)
        to_first(0, 3, j)
        to_first(1, 3, j)
        yield
        joined(2, j)
        to_first(0, 2, j)
        yield
        joined(1, j)
        to_first(1, 1, j)
        joined(0, j)
        yield

    def second_stage(j):
        for part in (0, 1):
            q, slot = (1, 2)[part], 4 + zs[j]
            arrive(held(first_ref, part, slot), fsem.at[part, slot], spot)
            add(q, j, part, (first_ref, slot))
            sends.push(mine(q, j, part), held(second_ref, part, zs[j]), gsem.at[part, zs[j]], second_peer[part])
            yield

    def z_send(j):
        for part in (0, 1):
            arrive(held(first_ref, part, zs[j]), fsem.at[part, zs[j]], spot)
            arrive(held(second_ref, part, zs[j]), gsem.at[part, zs[j]], spot)
            add(0, j, part, (first_ref, zs[j]), (second_ref, zs[j]))
            if j:
                sends.push(mine(0, j, part), held(za_ref, part, 3 - j), zasem.at[part, 3 - j], spot.n1, end)
            yield

    def z_relay(j):
        if not j:
            return
        for part in (0, 1):
            came, sem, slot = (za_ref, zasem, 3 - j) if j > 1 else (zb_ref, zbsem, 0)

            @pl.when(mid)
            def _():
                arrive(held(came, part, slot), sem.at[part, slot], spot)
                add(0, j, part, (came, slot))

            slot = 3 - j if j > 1 else 0
            peer = spot.n2 if j > 1 else spot.n1
            sends.push(mine(0, j, part), held(zb_ref, part, slot), zbsem.at[part, slot], peer, mid)
            yield

    pair_exchange(3)
    yield
    stages = (first_stage, second_stage, z_send, z_relay)
    for step in range(4 + len(stages) - 1):
        for stage, what in enumerate(stages):
            j = 3 - (step - stage)
            if 0 <= j <= 3:
                yield from what(j)
    for part in (0, 1):
        o_ref, there = (o_refs[part], pl.ds(0, half)) if given == 2 else (o_refs[0], cols[part])

        def total(*more):
            def step(r):
                v = s_ref[zs[0], r, cols[part]].astype(jnp.float32)
                for ref, slot in more:
                    v = v + ref[part, slot, r, short].astype(jnp.float32)
                o_ref[r, there] = v

            chunks(size, step)

        @pl.when(mid)
        def _():
            arrive(held(za_ref, part, 2), zasem.at[part, 2], spot)
            arrive(held(zb_ref, part, 1), zbsem.at[part, 1], spot)
            total((za_ref, 2), (zb_ref, 1))

        @pl.when(end)
        def _():
            arrive(held(zb_ref, part, 0), zbsem.at[part, 0], spot)
            total((zb_ref, 0))

        yield


def gather_kernel(a_ref, o_ref, own_sem, ssem, rsem):
    spot = Spot()
    spot.greet()
    sends = Sends(ssem)
    for _ in gather_steps(spot, a_ref, o_ref, pl.ds(0, a_ref.shape[0]), sends, rsem, own_sem):
        pass
    sends.finish()


def gather(block):
    rows, width = block.shape
    dma = pltpu.SemaphoreType.DMA
    return pl.pallas_call(
        gather_kernel,
        out_shape=jax.ShapeDtypeStruct((32, rows, width), block.dtype),
        in_specs=[pl.BlockSpec(memory_space=pl.ANY)],
        out_specs=pl.BlockSpec(memory_space=pl.ANY),
        scratch_shapes=[dma, dma((N_GATHER_SENDS,)), dma((2, 32))],
        name="gather_rows",
        compiler_params=pltpu.CompilerParams(collective_id=0, has_side_effects=True),
    )(block)


def weave(tasks, order):
    names = list(tasks)
    left = {name: steps for name, (_, steps) in tasks.items()}

    def advance(name):
        for other in tasks[name][0]:
            if other in left:
                advance(other)
                assert other not in left, name
        if name in left and next(left[name], left) is left:
            del left[name]

    for number, times in order:
        for _ in range(times):
            advance(names[number])
    while left:
        name = next(n for n in left if not any(other in left for other in tasks[n][0]))
        while name in left:
            advance(name)


FRONT_ORDER = (
    (0, 1), (2, 1), (1, 1), (2, 9), (1, 1), (2, 3), (1, 1), (2, 1), (1, 2), (3, 8), (1, 1), (3, 4), (1, 1),
    (9, 8), (10, 1), (3, 1), (1, 1), (3, 1), (10, 1), (1, 1), (3, 1), (10, 2), (3, 1), (10, 1), (3, 1), (10,
    2), (1, 2), (3, 4), (10, 1), (3, 4), (10, 5), (0, 1), (1, 1), (10, 2), (3, 1), (1, 3), (3, 2), (1, 1), (3,
    1), (1, 1), (3, 4), (10, 4), (3, 1), (10, 1), (3, 1), (10, 5), (1, 4), (3, 1), (1, 2), (3, 1), (1, 6),
    (10, 3), (4, 1), (5, 1), (10, 4), (1, 3), (10, 3), (5, 1), (10, 1), (5, 1), (10, 1), (11, 1), (5, 26),
    (12, 1), (5, 3), (12, 1), (6, 1), (12, 3), (6, 1), (12, 4), (6, 1), (12, 2), (6, 1), (12, 6), (6, 1), (12,
    1), (6, 1), (12, 12), (6, 1), (12, 2), (7, 12), (13, 2), (7, 2), (13, 1), (7, 6), (13, 1), (7, 3), (13,
    1), (14, 1), (7, 4), (14, 1), (7, 1), (14, 9), (7, 9), (8, 1), (14, 26), (15, 1),
)
REAR_ORDER = (
    (0, 15), (1, 1), (0, 17), (4, 1), (1, 1), (4, 1), (1, 1), (4, 1), (1, 1), (4, 2), (1, 1), (4, 1), (1, 1),
    (4, 1), (1, 1), (4, 1), (1, 1), (4, 1), (1, 1), (4, 1), (1, 1), (4, 1), (1, 1), (4, 2), (1, 1), (4, 1),
    (1, 1), (4, 1), (1, 2), (4, 2), (1, 1), (4, 1), (1, 1), (4, 1), (1, 1), (4, 1), (1, 1), (4, 2), (1, 2),
    (4, 1), (1, 1), (5, 1), (6, 1), (5, 1), (1, 3), (5, 1), (1, 2), (5, 1), (1, 1), (5, 1), (6, 1), (1, 1),
    (6, 1), (5, 1), (6, 1), (1, 1), (6, 1), (5, 1), (1, 1), (6, 1), (1, 1), (5, 1), (1, 1), (6, 1), (1, 1),
    (5, 1), (6, 1), (1, 1), (5, 1), (1, 1), (6, 1), (5, 1), (1, 1), (5, 3), (7, 1), (5, 1), (7, 1), (5, 2),
    (3, 1), (7, 1), (5, 7), (7, 6), (5, 1), (7, 1), (5, 1), (7, 1), (5, 1), (7, 1), (5, 1), (7, 1), (5, 1),
    (7, 3), (5, 2), (7, 3), (5, 1), (7, 1), (2, 1), (7, 1), (5, 1), (7, 3), (5, 1), (7, 2), (5, 1), (7, 2),
    (5, 1), (7, 1), (5, 1), (7, 8), (8, 1), (3, 1), (2, 1), (8, 2),
)
N_GATHER_SENDS = 66
FEW = 16


def gelu_pair(gate):
    slope = 0.7978845608028654
    squared = gate * gate
    bent = jnp.tanh(slope * (gate + 0.044715 * gate * squared))
    gelu = 0.5 * gate * (1.0 + bent)
    return gelu, 0.5 * (1.0 + bent) + 0.5 * gate * (1.0 - bent * bent) * slope * (1.0 + 3.0 * 0.044715 * squared)


def scatter_sems(halves, given):
    dma = pltpu.SemaphoreType.DMA
    return [
        dma((halves, 16 * given + 36)), dma((halves, given, 8)), dma((halves, given, 16)), dma((halves, 2, 8)),
        dma((halves, 2, 4)), dma((halves, 2, 3)), dma((halves, 2, 2)),
    ]


def scatter_bufs(rows, width, given):
    half = given * width // 2
    shapes = ((8, rows, given * width), (16, rows, given * width), (2, 8, rows, half), (2, 4, rows, half))
    return [pltpu.VMEM(shape, jnp.bfloat16) for shape in shapes + ((2, 3, rows, half), (2, 2, rows, half))]


class Stage:
    def __init__(self, count, cuts, in_refs, out_refs, in_sems, out_sems):
        self.spot = Spot()
        self.count = count
        self.ranges = [pl.ds(a, b - a) for a, b in zip(cuts[:-1], cuts[1:])]
        self.cuts = cuts
        self.sends = {}
        self.in_refs, self.out_refs, self.in_sems, self.out_sems = in_refs, out_refs, in_sems, out_sems

    def gathering(self, name, at, src, dst, rows, sems):
        own_sem, ssem, rsem = sems
        self.sends[name] = Sends(ssem.at[at])
        yield from gather_steps(self.spot, src, dst, rows, self.sends[name], rsem.at[at], own_sem.at[at])

    def scattering(self, name, p_refs, o_refs, rows, bufs, sems, at):
        self.sends[name] = Sends(sems[0].at[at])
        yield from scatter_steps(
            self.spot, p_refs, o_refs, rows, bufs, [sem.at[at] for sem in sems[1:]], self.sends[name]
        )

    def fetch(self, group, sources, streams=None):
        streams = range(len(sources)) if streams is None else streams
        for i, source in zip(streams, sources):
            there = self.in_refs[i].at[group % 2]
            yield pltpu.make_async_copy(source.at[:, pl.ds(group * FEW, FEW), :], there, self.in_sems.at[i, group % 2])

    def store(self, group, targets):
        for i, target in enumerate(targets):
            there = target.at[:, pl.ds(group * FEW, FEW), :]
            yield pltpu.make_async_copy(self.out_refs[i], there, self.out_sems.at[i])

    def finish(self):
        for some in self.sends.values():
            some.finish()


def start_all(copies):
    for copy in copies:
        copy.start()


def wait_all(copies):
    for copy in copies:
        copy.wait()


def tile_inputs(qkv_ref, col_ref, row_ref, base, length, head):
    query = qkv_ref[pl.ds(base + length, length), :head]
    key = qkv_ref[pl.ds(base, 3 * length), head : 2 * head]
    value = qkv_ref[pl.ds(base, 3 * length), 2 * head :]
    return query, key, value, col_ref[pl.ds(base, length), :] == row_ref[:, pl.ds(base, 3 * length)]


def front_kernel(cuts, *refs):
    (nx_all_ref, rows_ref, up_ref, gain_ref, qkv_w_ref, gate_w_ref, mine_ref, wd_ref, wo_ref, perm_ref, bias_ref, col_ref,
     row_ref) = refs[:13]
    (qkv_ref, att_ref, middle_ref, d_mid_ref, d_ref, gain_grad_ref, near_grad_ref, far_grad_ref, wd_grad_ref,
     forth_ref) = refs[13:23]
    part_ref, up_all_ref, x_all_ref, back_ref = refs[23:27]
    branch_ref, x_ref, dn_ref, w_ref = refs[27:31]
    bufs, two_ref, in_refs, out_refs = refs[31:37], refs[37], refs[38:40], refs[40:42]
    in_sems, out_sems, w_ssem, w_rsem, w_own = refs[42:47]
    g_sems, one_sems, two_sems = refs[47:50], refs[50:57], refs[57:64]
    two_bufs = (bufs[0], two_ref, *bufs[2:])
    count = part_ref.shape[0]
    stage = Stage(count, cuts, in_refs, out_refs, in_sems, out_sems)
    spot, ranges = stage.spot, stage.ranges
    spot.greet_all(count)
    width, units, head, length = rows_ref.shape[1], wd_ref.shape[0], wo_ref.shape[0], bias_ref.shape[0]
    size = perm_ref.shape[0]
    groups = cuts[-1] // FEW
    shard = mine_ref.shape[1]
    near = units - head

    def column_blocks(what):
        def one(d, _):
            peer = (spot.me + d) % count
            source = (spot.me + count - d) % count
            if what == "send":
                pltpu.make_async_remote_copy(
                    mine_ref.at[peer], w_ref.at[pl.ds(pl.multiple_of(spot.me * shard, shard), shard), :], w_ssem.at[peer],
                    w_rsem.at[spot.me], device_id=(peer,), device_id_type=MESH,
                ).start()
            else:
                there = w_ref.at[pl.ds(pl.multiple_of(source * shard, shard), shard), :]
                copy = pltpu.make_async_remote_copy(
                    there, there, w_ssem.at[peer], w_rsem.at[source], device_id=(peer,), device_id_type=MESH,
                )
                copy.wait_recv()
                copy.wait_send()
            return _

        lax.fori_loop(1, count, one, 0)

    def columns():
        own = pltpu.make_async_copy(
            mine_ref.at[spot.me], w_ref.at[pl.ds(pl.multiple_of(spot.me * shard, shard), shard), :], w_own
        )
        own.start()
        column_blocks("send")
        yield
        column_blocks("wait")
        own.wait()
        yield

    def attending(first, last):
        perm = perm_ref[...]
        if first == 0:
            start_all(stage.fetch(0, (nx_all_ref,)))
            qkv_ref[:length, :] = jnp.zeros((length, 3 * head), qkv_ref.dtype)
            qkv_ref[length + groups * size :, :] = jnp.zeros((length, 3 * head), qkv_ref.dtype)
        for step in range(first, last):
            if step < groups:
                if step + 1 < groups:
                    start_all(stage.fetch(step + 1, (nx_all_ref,)))
                wait_all(stage.fetch(step, (nx_all_ref,)))
                rows = low(over(in_refs[0][step % 2].reshape(size, -1), qkv_w_ref[...]))
                qkv_ref[length + step * size : length + (step + 1) * size, :] = low(over(perm, rows))
                yield
            if step > 0:
                attended = []
                for tile in range(size // length):
                    base = (step - 1) * size + tile * length
                    query, key, value, same = tile_inputs(qkv_ref, col_ref, row_ref, base, length, head)
                    attended.append(low(over(low(tile_probs(query, key, bias_ref[...], same)), value)))
                    if tile % 2:
                        yield
                rows = low(over(perm, jnp.concatenate(attended, axis=0), 0, 0))
                att_ref[:, (step - 1) * FEW : step * FEW, :] = rows.reshape(count, FEW, head)
                if step > max(first, 1):
                    wait_all(stage.store(step - 2, (part_ref,)))
                for i in range(2):
                    there = pl.ds(i * count // 2, count // 2)
                    piece = over(rows[i * size // 2 : (i + 1) * size // 2], wo_ref[...])
                    out_refs[0][there] = low(piece).reshape(count // 2, FEW, width)
                start_all(stage.store(step - 1, (part_ref,)))
                yield
        if last > max(first, 1):
            wait_all(stage.store(last - 2, (part_ref,)))
        yield

    def rows_of(rows):
        return [pl.ds(rows.start + i, 16) for i in range(0, rows.size, 16)]

    def scale_of(v):
        return lax.rsqrt(jnp.sum(v * v, axis=1, keepdims=True) / width + EPSILON)

    def first_norm(rows):
        for r in rows_of(rows):
            v = rows_ref[r, :].astype(jnp.float32) + branch_ref[r, :]
            middle_ref[r, :] = v
            x_ref[r, :] = (v * scale_of(v) * gain_ref[...]).astype(x_ref.dtype)
        yield

    def norm_back_rows(rows):
        for r in rows_of(rows):
            v, d, gain = middle_ref[r, :], dn_ref[r, :], gain_ref[...]
            scale = scale_of(v)
            gain_grad_ref[...] += jnp.sum(d * v * scale, axis=0, keepdims=True)
            w = gain * d
            mean = jnp.sum(w * v, axis=1, keepdims=True) / width
            d_mid = up_ref[r, :].astype(jnp.float32) + scale * w - v * (scale * scale * scale) * mean
            d_mid_ref[r, :] = d_mid
            d_ref[r, :] = d_mid.astype(d_ref.dtype)
        yield

    def feeding(first, last):
        sources, targets = (x_all_ref, up_all_ref), (back_ref, forth_ref)
        start_all(stage.fetch(first, sources))
        for group in range(first, last):
            if group + 1 < last:
                start_all(stage.fetch(group + 1, sources))
            wait_all(stage.fetch(group, sources))
            for i in range(2):
                blocks = slice(i * count // 2, (i + 1) * count // 2)
                x = in_refs[0][group % 2, blocks].reshape(size // 2, width)
                upstream = in_refs[1][group % 2, blocks].reshape(size // 2, width)
                both = over(x, w_ref[...])
                gate = jnp.concatenate((over(x, gate_w_ref[...]), both[:, :near]), axis=1)
                up = both[:, near:]
                d_hidden = over(upstream, wd_ref[...], 1, 1)
                gelu, d_gelu = gelu_pair(gate)
                hidden = low(gelu * up)
                d_gate, d_up = low(d_hidden * up * d_gelu), low(d_hidden * gelu)
                d_first, d_both = d_gate[:, :head], jnp.concatenate((d_gate[:, head:], d_up), axis=1)
                if i == 0 and group > first:
                    wait_all(stage.store(group - 1, targets))
                shape = (count // 2, FEW, width)
                back = over(d_both, w_ref[...], 1, 1) + over(d_first, gate_w_ref[...], 1, 1)
                out_refs[0][blocks] = low(back).reshape(shape)
                out_refs[1][blocks] = low(over(hidden, wd_ref[...])).reshape(shape)
                if i:
                    start_all(stage.store(group, targets))
                near_grad_ref[...] += over(d_first, x, 0, 0)
                far_grad_ref[...] += over(d_both, x, 0, 0)
                wd_grad_ref[...] += over(hidden, upstream, 0, 0)
                yield
        wait_all(stage.store(last - 1, targets))
        yield

    for ref in (near_grad_ref, far_grad_ref, wd_grad_ref, gain_grad_ref):
        ref[...] = jnp.zeros_like(ref)
    halves = len(ranges)
    tasks = {
        "columns": ([], columns()),
        "up": ([], stage.gathering("up", 0, up_ref, up_all_ref, pl.ds(0, cuts[-1]), g_sems)),
    }
    for i, rows in enumerate(ranges):
        h = str(i)
        last_step = groups + 1 if i == halves - 1 else cuts[i + 1] // FEW + 1
        first_step = cuts[i] // FEW + 1 if i else 0
        tasks |= {
            "attend" + h: ([f"attend{i - 1}"] if i else [], attending(first_step, last_step)),
            "one" + h: (
                ["attend" + h], stage.scattering("one" + h, (part_ref,), (branch_ref,), rows, bufs, one_sems, i),
            ),
            "norm" + h: (["one" + h], first_norm(rows)),
            "x" + h: (["norm" + h], stage.gathering("x" + h, 1 + i, x_ref, x_all_ref, rows, g_sems)),
            "feed" + h: (
                ["x" + h, "up", "columns", f"feed{i - 1}" if i else f"attend{halves - 1}"],
                feeding(cuts[i] // FEW, cuts[i + 1] // FEW),
            ),
            "two" + h: (
                ["feed" + h],
                stage.scattering("two" + h, (back_ref,), (dn_ref,), rows, two_bufs, two_sems, i),
            ),
            "back" + h: (["two" + h], norm_back_rows(rows)),
        }
    weave(tasks, FRONT_ORDER)
    stage.finish()


def halves_of(rows):
    return (0, 48, 80) if rows == 80 else (0, rows)


def front(normed_all, rows_low, upstream_low, gain, qkv_w, gate_w, mine, wd, wo, perm, bias, col, row):
    count, rows, width = normed_all.shape
    cuts = halves_of(rows)
    halves = len(cuts) - 1
    head, length, size = wo.shape[0], bias.shape[0], perm.shape[0]
    low_rows, all_rows, group = (rows, width), (count, rows, width), (count, FEW, width)
    bf, wide, dma = jnp.bfloat16, jnp.float32, pltpu.SemaphoreType.DMA
    vmem, hbm = pl.BlockSpec(memory_space=pltpu.VMEM), pl.BlockSpec(memory_space=pl.ANY)
    shape = jax.ShapeDtypeStruct
    outs = pl.pallas_call(
        functools.partial(front_kernel, cuts),
        out_shape=[
            shape((rows // FEW * size + 2 * length, 3 * head), bf), shape((count, rows, head), bf), shape(low_rows, wide),
            shape(low_rows, wide), shape(low_rows, bf), shape((1, width), wide), shape((head, width), wide),
            shape((mine.shape[2], width), wide), shape(wd.shape, wide),
        ] + [shape(all_rows, bf)] * 5,
        in_specs=[hbm] + [vmem] * 5 + [hbm] + [vmem] * 6,
        out_specs=[vmem] * 9 + [hbm] * 5,
        scratch_shapes=[
            pltpu.VMEM(low_rows, wide), pltpu.VMEM(low_rows, bf), pltpu.VMEM(low_rows, wide),
            pltpu.VMEM((width, mine.shape[2]), bf),
        ] + scatter_bufs(rows, width, 1) + [
            pltpu.VMEM((16, rows, width), bf),
            pltpu.VMEM((2,) + group, bf), pltpu.VMEM((2,) + group, bf), pltpu.VMEM(group, bf), pltpu.VMEM(group, bf),
            dma((2, 2)), dma((2,)), dma((count,)), dma((count,)), dma,
            dma((1 + halves,)), dma((1 + halves, N_GATHER_SENDS)), dma((1 + halves, 2, 32)),
        ] + scatter_sems(halves, 1) * 2,
        name="front",
        compiler_params=pltpu.CompilerParams(collective_id=3, has_side_effects=True, vmem_limit_bytes=63 * 2**20),
    )(normed_all, rows_low, upstream_low, gain, qkv_w, gate_w, mine, wd, wo, perm, bias, col, row)
    return outs[:10]


def swap(spot, count, src, dst, sems, what):
    send_sem, recv_sem, own_sem = sems
    share = src.shape[0] // count

    def part(ref, index):
        return ref.at[pl.ds(pl.multiple_of(index * share, share), share), :]

    own = pltpu.make_async_copy(part(src, spot.me), part(dst, spot.me), own_sem)

    def one(d, _):
        peer, source = (spot.me + d) % count, (spot.me + count - d) % count
        if what == "send":
            pltpu.make_async_remote_copy(
                part(src, peer), part(dst, spot.me), send_sem.at[peer], recv_sem.at[spot.me], device_id=(peer,),
                device_id_type=MESH,
            ).start()
        else:
            copy = pltpu.make_async_remote_copy(
                part(src, peer), part(dst, source), send_sem.at[peer], recv_sem.at[source], device_id=(peer,),
                device_id_type=MESH,
            )
            copy.wait_recv()
            copy.wait_send()
        return _

    if what == "send":
        own.start()
    lax.fori_loop(1, count, one, 0)
    if what == "wait":
        own.wait()


def rear_kernel(cuts, *refs):
    (d_ref, x_all_ref, att_ref, qkv_ref, w_ref, wo_ref, perm_ref, bias_ref, col_ref, row_ref, near_ref, forth_ref, middle_ref,
     rows_ref, d_mid_ref, gain_ref, spread_ref, turn_ref, bucket_ref) = refs[:19]
    wo_grad_ref, owned_ref, out_rows_ref, sums_ref, token_rows_ref = refs[19:24]
    d_all_ref, part_ref = refs[24:26]
    dn_ref, down_ref, bias_grad_ref, dq_ref, dkv_ref, w_grad_ref, turned_ref, result_ref, going_ref, came_ref, last_ref = refs[26:37]
    bufs, other_bufs, in_refs, out_refs = refs[37:43], refs[43:49], refs[49:51], refs[51:52]
    in_sems, out_sems = refs[52:54]
    w_sems, r_sems, t_sems, l_sems = refs[54:57], refs[57:60], refs[60:63], refs[63:66]
    g_sems, one_sems, down_sems = refs[66:69], refs[69:76], refs[76:83]
    count, width = part_ref.shape[0], part_ref.shape[2]
    stage = Stage(count, cuts, in_refs, out_refs, in_sems, out_sems)
    spot, ranges = stage.spot, stage.ranges
    spot.greet_all(count)
    head, length, size = wo_ref.shape[0], bias_ref.shape[0], perm_ref.shape[0]
    groups = cuts[-1] // FEW
    folds, piece = spread_ref.shape[0], result_ref.shape[1]

    def owners():
        merged = jnp.concatenate((low(w_grad_ref[...]), low(near_ref[...])), axis=0)
        for i in range(0, width, 512):
            turned_ref[i : i + 512, :] = merged[:, i : i + 512].T
        swap(spot, count, turned_ref, owned_ref, w_sems, "send")
        yield
        swap(spot, count, turned_ref, owned_ref, w_sems, "wait")
        yield

    def dealt_out(rows):
        return sum(
            over(spread_ref[i], rows[:, i * piece : (i + 1) * piece]) for i in range(folds)
        )

    def output():
        rows = low(middle_ref[...] + down_ref[...])
        result_ref[...] = low(dealt_out(rows))
        swap(spot, count, result_ref, out_rows_ref, r_sems, "send")
        yield
        swap(spot, count, result_ref, out_rows_ref, r_sems, "wait")
        yield

    def scale_of(v):
        return lax.rsqrt(jnp.sum(v * v, axis=1, keepdims=True) / width + EPSILON)

    def shares(v):
        shape = (going_ref.shape[0], width)
        at, to = lax.broadcasted_iota(jnp.int32, shape, 0), lax.broadcasted_iota(jnp.int32, shape, 1)
        spread = jnp.where(at == to // (width // count) * 16, v, 0.0)
        fold = lax.broadcasted_iota(jnp.int32, (width, width // count), 0) % (width // count)
        fold = fold == lax.broadcasted_iota(jnp.int32, (width, width // count), 1)
        high = low(spread)
        rest = low(spread - high.astype(jnp.float32))
        return jnp.concatenate([over(p, low(fold.astype(jnp.float32))) for p in (high, rest)], axis=1)

    def finals():
        v, d, gain = rows_ref[...].astype(jnp.float32), dn_ref[...], gain_ref[...]
        scale = scale_of(v)
        w = gain * d
        mean = jnp.sum(w * v, axis=1, keepdims=True) / width
        rows = low(d_mid_ref[...] + scale * w - v * (scale * scale * scale) * mean)
        going_ref[:, :piece] = low(dealt_out(rows))
        sums = shares(jnp.sum(d * v * scale, axis=0, keepdims=True))
        at, to = lax.broadcasted_iota(jnp.int32, sums.shape, 0), lax.broadcasted_iota(jnp.int32, sums.shape, 1)
        for b in range(BUCKETS):
            total = jnp.sum(jnp.where(bucket_ref[...] == b, bias_grad_ref[...], 0.0), axis=(0, 1), keepdims=True)
            high = low(total).astype(jnp.float32)
            sums = sums + jnp.where((at == 16 * b + 1) & (to == 0), high, 0.0)
            sums = sums + jnp.where((at == 16 * b + 1) & (to == 1), total - high, 0.0)
        going_ref[:, piece:] = low(sums)
        swap(spot, count, going_ref, came_ref, t_sems, "send")
        yield
        swap(spot, count, going_ref, came_ref, t_sems, "wait")
        sums_ref[...] = came_ref[:, piece:]
        last_ref[...] = low(over(turn_ref[...], came_ref[:, :piece]))
        swap(spot, count, last_ref, token_rows_ref, l_sems, "send")
        yield
        swap(spot, count, last_ref, token_rows_ref, l_sems, "wait")
        yield

    def backing(first, last):
        perm = perm_ref[...]
        for step in range(first, last):
            if step < groups:
                start_all(stage.fetch(step, (d_all_ref,)))
                start_all(stage.fetch(step, (x_all_ref,), (1,)))
                wait_all(stage.fetch(step, (d_all_ref,)))
                d_branch = in_refs[0][step % 2].reshape(size, width)
                attended = att_ref[:, step * FEW : (step + 1) * FEW, :].reshape(size, head)
                wo_grad_ref[...] += over(attended, d_branch, 0, 0)
                yield
                d_attended = low(over(perm, low(over(d_branch, wo_ref[...], 1, 1))))
                yield
                for tile in range(size // length):
                    base = step * size + tile * length
                    query, key, value, same = tile_inputs(qkv_ref, col_ref, row_ref, base, length, head)
                    probs = tile_probs(query, key, bias_ref[...], same)
                    d_out = d_attended[tile * length : (tile + 1) * length, :]
                    d_probs = over(d_out, value, 1, 1)
                    inner = jnp.sum(probs * d_probs, axis=-1, keepdims=True)
                    d_scores = low(probs * (d_probs - inner))
                    bias_grad_ref[...] += d_scores.astype(jnp.float32)
                    dq_ref[base + length : base + 2 * length, :] = low(over(d_scores, key))
                    both = jnp.concatenate((over(d_scores, query, 0, 0), over(low(probs), d_out, 0, 0)), axis=1)
                    dkv_ref[base : base + 3 * length, :] += both
                    if tile % 2:
                        yield
            if step > 0:
                at = slice(length + (step - 1) * size, length + step * size)
                rows = low(over(perm, jnp.concatenate((dq_ref[at, :], low(dkv_ref[at, :])), axis=1), 0, 0))
                wait_all(stage.fetch(step - 1, (x_all_ref,), (1,)))
                w_grad_ref[...] += over(rows, in_refs[1][(step - 1) % 2].reshape(size, width), 0, 0)
                yield
                if step > max(first, 1):
                    wait_all(stage.store(step - 2, (part_ref,)))
                for i in range(2):
                    there = pl.ds(i * count // 2, count // 2)
                    block = over(rows[i * size // 2 : (i + 1) * size // 2], w_ref[...], 1, 1)
                    out_refs[0][there] = low(block).reshape(count // 2, FEW, width)
                start_all(stage.store(step - 1, (part_ref,)))
                yield
        if last > max(first, 1):
            wait_all(stage.store(last - 2, (part_ref,)))
        yield

    for ref in (wo_grad_ref, bias_grad_ref, dkv_ref, w_grad_ref):
        ref[...] = jnp.zeros_like(ref)
    halves = len(ranges)
    everything = pl.ds(0, cuts[-1])
    tasks = {
        "d": ([], stage.gathering("d", 0, d_ref, d_all_ref, everything, g_sems)),
        "down": ([], stage.scattering("down", (forth_ref,), (down_ref,), everything, other_bufs, down_sems, 0)),
        "output": (["down"], output()),
        "owners": ([f"back{halves - 1}"], owners()),
    }
    for i, rows in enumerate(ranges):
        h = str(i)
        first_step = cuts[i] // FEW + 1 if i else 0
        tasks |= {
            "back" + h: ([f"back{i - 1}"] if i else ["d"], backing(first_step, cuts[i + 1] // FEW + 1)),
            "one" + h: (["back" + h], stage.scattering("one" + h, (part_ref,), (dn_ref,), rows, bufs, one_sems, i)),
        }
    tasks["finals"] = ([f"one{i}" for i in range(halves)], finals())
    weave(tasks, REAR_ORDER)
    stage.finish()


def rear(d_rows, normed_all, attended, qkv, qkv_w, wo, perm, bias, col, row, near_grad, forth, middle, rows_low, d_mid, gain,
         spread, turn, buckets):
    count, rows, width = normed_all.shape
    cuts = halves_of(rows)
    halves = len(cuts) - 1
    head = wo.shape[0]
    columns = 4 * head
    size, piece = perm.shape[0], width // spread.shape[0]
    all_rows, group = (count, rows, width), (count, FEW, width)
    bf, wide, dma = jnp.bfloat16, jnp.float32, pltpu.SemaphoreType.DMA
    vmem, hbm = pl.BlockSpec(memory_space=pltpu.VMEM), pl.BlockSpec(memory_space=pl.ANY)
    shape = jax.ShapeDtypeStruct
    outs = pl.pallas_call(
        functools.partial(rear_kernel, cuts),
        out_shape=[
            shape((head, width), wide), shape((width, columns), bf), shape((size, piece), bf), shape((size, 128), bf),
            shape((size, piece), bf),
        ] + [shape(all_rows, bf)] * 2,
        in_specs=[vmem, hbm] + [vmem] * 9 + [hbm] + [vmem] * 7,
        out_specs=[vmem, hbm, hbm, vmem, hbm] + [hbm] * 2,
        scratch_shapes=[
            pltpu.VMEM((rows, width), wide), pltpu.VMEM((rows, width), wide), pltpu.VMEM(bias.shape, wide),
            pltpu.VMEM((qkv.shape[0], head), bf), pltpu.VMEM((qkv.shape[0], 2 * head), wide),
            pltpu.VMEM((3 * head, width), wide), pltpu.VMEM((width, columns), bf),
            pltpu.VMEM((size, piece), bf), pltpu.VMEM((size, piece + 128), bf), pltpu.VMEM((size, piece + 128), bf),
            pltpu.VMEM((size, piece), bf),
        ] + scatter_bufs(rows, width, 1) * 2 + [
            pltpu.VMEM((2,) + group, bf), pltpu.VMEM((2,) + group, bf), pltpu.VMEM(group, bf),
            dma((2, 2)), dma((1,)),
        ] + [dma((count,)), dma((count,)), dma] * 4 + [
            dma((1,)), dma((1, N_GATHER_SENDS)), dma((1, 2, 32)),
        ] + scatter_sems(halves, 1) + scatter_sems(1, 1),
        name="rear",
        compiler_params=pltpu.CompilerParams(collective_id=4, has_side_effects=True, vmem_limit_bytes=63 * 2**20),
    )(d_rows, normed_all, attended, qkv, qkv_w, wo, perm, bias, col, row, near_grad, forth, middle, rows_low, d_mid, gain,
      spread, turn, buckets)
    return outs[:5]


def exchange(blocks):
    return lax.all_to_all(blocks, AXIS, split_axis=0, concat_axis=0, tiled=True)


def dot(left, right):
    return jnp.dot(left, right, preferred_element_type=jnp.float32)


def select(mask, rows):
    return dot(mask.astype(jnp.bfloat16), rows).astype(jnp.bfloat16)


def beside(sent, chain, kernel):
    sent, chain = lax.optimization_barrier((sent, chain))
    return lax.optimization_barrier((exchange(sent), kernel(chain)))


def pack_kernel(query_ref, key_ref, value_ref, gate_ref, up_ref, first_ref, second_ref):
    count = first_ref.shape[0]
    head = query_ref.shape[1] // count
    units = gate_ref.shape[1] // count
    for j in range(count):
        for i, ref in enumerate((query_ref, key_ref, value_ref)):
            first_ref[j, :, i * head : (i + 1) * head] = ref[:, j * head : (j + 1) * head]
        first_ref[j, :, 3 * head :] = gate_ref[:, j * units : j * units + head]
        second_ref[j, :, : units - head] = gate_ref[:, j * units + head : (j + 1) * units]
        second_ref[j, :, units - head :] = up_ref[:, j * units : (j + 1) * units]


def pack(shards, count):
    rows, width = shards[0].shape
    head, units = width // count, shards[3].shape[1] // count
    return pl.pallas_call(
        pack_kernel,
        out_shape=[
            jax.ShapeDtypeStruct((count, rows, 4 * head), jnp.bfloat16),
            jax.ShapeDtypeStruct((count, rows, 2 * units - head), jnp.bfloat16),
        ],
        in_specs=[pl.BlockSpec(memory_space=pltpu.VMEM)] * 5,
        out_specs=[pl.BlockSpec(memory_space=pltpu.VMEM)] * 2,
        name="pack_columns",
        compiler_params=pltpu.CompilerParams(vmem_limit_bytes=32 * 2**20),
    )(*shards)


def unpack_kernel(first_ref, second_ref, query_ref, key_ref, value_ref, gate_ref, up_ref):
    count = first_ref.shape[0]
    head = query_ref.shape[1] // count
    units = gate_ref.shape[1] // count
    wide = jnp.float32
    for j in range(count):
        for i, ref in enumerate((query_ref, key_ref, value_ref)):
            ref[:, j * head : (j + 1) * head] = first_ref[j, :, i * head : (i + 1) * head].astype(wide)
        gate_ref[:, j * units : j * units + head] = first_ref[j, :, 3 * head :].astype(wide)
        gate_ref[:, j * units + head : (j + 1) * units] = second_ref[j, :, : units - head].astype(wide)
        up_ref[:, j * units : (j + 1) * units] = second_ref[j, :, units - head :].astype(wide)


def unpack(first, second, width, hidden):
    rows = first.shape[1]
    widths = (width, width, width, hidden, hidden)
    return pl.pallas_call(
        unpack_kernel,
        out_shape=[jax.ShapeDtypeStruct((rows, columns), jnp.float32) for columns in widths],
        in_specs=[pl.BlockSpec(memory_space=pltpu.VMEM)] * 2,
        out_specs=[pl.BlockSpec(memory_space=pltpu.VMEM)] * 5,
        name="unpack_columns",
        compiler_params=pltpu.CompilerParams(vmem_limit_bytes=32 * 2**20),
    )(first, second)


def body(
    tokens,
    lengths,
    permutation,
    query_weight,
    key_weight,
    value_weight,
    out_weight,
    gate_weight,
    up_weight,
    down_weight,
    gain_attention,
    gain_feedforward,
    bias_table,
    cotangent,
):
    me = lax.axis_index(AXIS)
    count = tokens.shape[0]
    grain = tokens.shape[1]
    length = cotangent.shape[1]
    width = tokens.shape[2]
    shard = query_weight.shape[0]
    hidden_width = gate_weight.shape[1] // count
    head = HEAD_DIM
    total = 3 * count * length // 5
    tiles = -(-total // length)
    slots = tiles * grain

    small = jnp.concatenate((gain_attention, gain_feedforward, bias_table))
    small = jnp.pad(small, (0, grain * 128 - small.shape[0])).reshape(1, grain, 128)
    small = jnp.broadcast_to(small, (count, grain, 128))
    came = exchange(jnp.concatenate((tokens[permutation], small), axis=2))
    dealt = came[:, :, :width].reshape(length, width)
    small = came[:, :, width:].reshape(count, -1)
    gain_one = small[:, :shard].reshape(-1).astype(jnp.float32)
    gain_two = small[:, shard : 2 * shard].reshape(-1).astype(jnp.float32)
    table = small[:, 2 * shard : 2 * shard + HEADS]

    dealt_lengths = lengths[permutation]
    ends = jnp.cumsum(dealt_lengths)
    starts = ends - dealt_lengths
    my_start, my_length = starts[me], dealt_lengths[me]
    place_in = jnp.arange(length, dtype=jnp.int32)
    turn = (
        (place_in[:, None] - my_start) % length == place_in[None, :]
    ) & (place_in[None, :] < my_length)
    slot_ids = jnp.arange(slots, dtype=jnp.int32)
    packed_ids = slot_ids // grain * length + me * grain + slot_ids % grain
    source_seq = jnp.sum((packed_ids[:, None] >= ends[None, :]).astype(jnp.int32), axis=1)
    pick = (source_seq * grain + slot_ids % grain)[:, None] == place_in[None, :]

    def spread_out(rows):
        return select(turn, rows).reshape(count, grain, width)

    def packed_block(came):
        return select(pick, came.reshape(length, width))

    rows_low = packed_block(exchange(spread_out(dealt)))
    rows_in = rows_low.astype(jnp.float32)
    first_columns, second_columns = pack(
        (query_weight, key_weight, value_weight, gate_weight, up_weight), count
    )

    all_ids = jnp.arange(tiles * length, dtype=jnp.int32)
    segment = jnp.sum((all_ids[:, None] >= ends[None, :]).astype(jnp.int32), axis=1) + 1
    column, row = segment[:, None], jnp.pad(segment, (length, length))[None, :]
    relative = (
        jnp.arange(3 * length, dtype=jnp.int32)[None, :] - length - place_in[:, None]
    ).reshape(-1)
    onehot = bucket_index(relative)[None, :] == jnp.arange(BUCKETS, dtype=jnp.int32)[:, None]
    head_table = lax.dynamic_slice_in_dim(table, me, 1, axis=1)
    rel_bias = dot(head_table.T, onehot.astype(jnp.bfloat16)).reshape(length, 3 * length)
    few = 16
    ids = jnp.arange(few * count, dtype=jnp.int32)
    ids = ids % length // grain * few + ids // length * grain + ids % grain
    perm = (ids[:, None] == jnp.arange(few * count, dtype=jnp.int32)[None, :]).astype(jnp.bfloat16)

    scale_one = norm_scale(rows_in)
    normed = (rows_in * scale_one * gain_one).astype(jnp.bfloat16)
    cut = (count, -1, 4 * head)
    sent = jnp.concatenate((first_columns, spread_out(cotangent[0]).reshape(cut)), axis=1)
    normed, perm, rel_bias, column, row = lax.optimization_barrier(
        (normed, perm, rel_bias, column, row)
    )
    came, normed_all = beside(sent, normed, gather)
    first_columns = came[:, :shard].reshape(-1, 4 * head)
    upstream_low = packed_block(came[:, shard:])
    qkv_columns, gate_columns = first_columns[:, : 3 * head], first_columns[:, 3 * head :]
    shared = (out_weight, perm, rel_bias, column, row)
    (qkv, attended, middle, d_middle, d_low, gain_two_grad, near_grad, far_grad, down_grad, forth) = front(
        normed_all, rows_low, upstream_low, gain_two[None, :], qkv_columns, gate_columns, second_columns, down_weight, *shared
    )

    folds = few // grain
    piece = width // folds
    share = jnp.arange(few * count, dtype=jnp.int32)
    share_row, share_fold = share // few * grain + share % grain, share % few // grain
    turned = (starts[None, :] + (me * grain + jnp.arange(grain, dtype=jnp.int32)[:, None] - starts[None, :]) % length).T
    back_slot = (turned // length * grain + jnp.arange(grain, dtype=jnp.int32)[None, :]).reshape(-1)
    spread = (back_slot[share_row][:, None] == slot_ids[None, :])[None] & (
        share_fold[None, :, None] == jnp.arange(folds, dtype=jnp.int32)[:, None, None]
    )
    back_turn = (
        ((share_row[None, :] - my_start) % length == share_row[:, None])
        & (share_row[:, None] < my_length)
        & (share_fold[:, None] == share_fold[None, :])
    )

    high = lax.reduce_precision(gain_two_grad, 8, 7)
    sums = jnp.stack((high, gain_two_grad - high)).astype(jnp.bfloat16).reshape(2, count, shard)
    sums = jnp.pad(sums.transpose(1, 0, 2).reshape(count, 1, -1), ((0, 0), (0, few - 1), (0, 4 * head - 2 * shard)))
    sent = jnp.concatenate((far_grad.astype(jnp.bfloat16).T.reshape(count, shard, -1), sums), axis=1)
    given = (
        d_low, normed_all, attended, qkv, qkv_columns, *shared, near_grad, forth, middle, rows_low, d_middle, gain_one[None, :],
        spread.astype(jnp.bfloat16), back_turn.astype(jnp.bfloat16), bucket_index(relative).reshape(length, -1),
    )
    came, (out_grad, first_grad, out_rows, other_sums, token_rows) = beside(sent, given, lambda given: rear(*given))
    second_grad, sums = came[:, :shard], came[:, shard].astype(jnp.float32)
    first_grad = first_grad.reshape(count, shard, -1)
    other_sums = other_sums.reshape(count, few, -1).astype(jnp.float32)
    gain_attention_grad = jnp.sum(other_sums[:, 0, :shard] + other_sums[:, 0, shard : 2 * shard], axis=0)
    gain_feedforward_grad = jnp.sum(sums[:, :shard] + sums[:, shard : 2 * shard], axis=0)
    table_grad = other_sums[:, 1, 0] + other_sums[:, 1, 1]

    def whole_rows(shares):
        return shares.reshape(count, folds, grain, piece).transpose(0, 2, 1, 3).reshape(count, grain, width)

    layer_output = select(turn.T, whole_rows(out_rows).reshape(length, width))[None]
    tokens_grad = whole_rows(token_rows)[jnp.argsort(permutation)]
    query_grad, key_grad, value_grad, gate_grad, up_grad = unpack(
        first_grad, second_grad, width, hidden_width * count
    )
    return (
        layer_output,
        tokens_grad,
        query_grad,
        key_grad,
        value_grad,
        out_grad,
        gate_grad,
        up_grad,
        down_grad,
        gain_attention_grad,
        gain_feedforward_grad,
        table_grad,
    )


def solution(mesh):
    placed = (
        P(None, "fsdp", None),
        P(),
        P(),
        P("fsdp", None),
        P("fsdp", None),
        P("fsdp", None),
        P("fsdp", None),
        P("fsdp", None),
        P("fsdp", None),
        P("fsdp", None),
        P("fsdp"),
        P("fsdp"),
        P("fsdp"),
        P("fsdp", None, None),
    )
    return jax.shard_map(
        body if mesh.shape[AXIS] == 32 else body_any,
        mesh=mesh,
        in_specs=placed,
        out_specs=(
            P("fsdp", None, None),
            P(None, "fsdp", None),
            P("fsdp", None),
            P("fsdp", None),
            P("fsdp", None),
            P("fsdp", None),
            P("fsdp", None),
            P("fsdp", None),
            P("fsdp", None),
            P("fsdp"),
            P("fsdp"),
            P("fsdp"),
        ),
        check_vma=False,
    )
```

```python
import functools

import jax
import jax.numpy as jnp
from jax import lax
from jax.experimental import pallas as pl
from jax.experimental.pallas import tpu as pltpu
from jax.sharding import PartitionSpec as P

HEADS = 32
HEAD_DIM = 64
BUCKETS = 32


EPSILON = 1e-06
masked_score = -1000000000.0
HIGHEST = lax.Precision.HIGHEST


def bucket_index(relative):
    half_buckets = BUCKETS // 2
    exact_count = half_buckets // 2
    distance = jnp.abs(relative)
    side_offset = jnp.where(relative > 0, half_buckets, 0).astype(jnp.int32)
    square = distance * distance
    far_bucket = jnp.full_like(distance, exact_count)
    for doubling in range(1, half_buckets - exact_count):
        far_bucket = far_bucket + (square >= exact_count * exact_count * 2**doubling).astype(
            jnp.int32
        )
    return side_offset + jnp.where(distance < exact_count, distance, far_bucket)


def bucket_onehot(seq_len):
    positions = jnp.arange(seq_len, dtype=jnp.int32)
    relative = (positions[None, :] - positions[:, None]).reshape(-1)
    bucket_ids = jnp.arange(BUCKETS, dtype=jnp.int32)
    return (bucket_index(relative)[None, :] == bucket_ids[:, None]).astype(jnp.float32)


def norm_scale(values):
    return lax.rsqrt(jnp.mean(values * values, axis=-1, keepdims=True) + EPSILON)


def norm_back(values, scale, gain_vec, d_norm):
    weighted = gain_vec * d_norm
    return scale * weighted - values * (scale * scale * scale) * jnp.mean(
        weighted * values, axis=-1, keepdims=True
    )


def rows_product(left, right):
    return lax.dot_general(
        left, right, (((0,), (0,)), ((), ())), preferred_element_type=jnp.float32
    )


def against_rows(left, right):
    return lax.dot_general(
        left, right, (((1,), (1,)), ((), ())), preferred_element_type=jnp.float32
    )


def masked_scores(query_heads, key_heads, rel_bias, length):
    scores = (
        jnp.einsum("qhd,khd->hqk", query_heads, key_heads, preferred_element_type=jnp.float32)
        + rel_bias
    )
    key_valid = jnp.arange(key_heads.shape[0], dtype=jnp.int32) < length
    return jnp.where(key_valid[None, None, :], scores, masked_score)


def unpack_weights(full_weights, onehot, seq_len):
    table_full = full_weights[4].astype(jnp.float32).reshape(BUCKETS, HEADS)
    rel_bias = jnp.dot(table_full.T, onehot, precision=HIGHEST).reshape(HEADS, seq_len, seq_len)
    return (
        full_weights[0],
        full_weights[1],
        full_weights[2].astype(jnp.float32),
        full_weights[3].astype(jnp.float32),
        rel_bias,
    )


def body_any(
    tokens,
    lengths,
    permutation,
    query_weight,
    key_weight,
    value_weight,
    out_weight,
    gate_weight,
    up_weight,
    down_weight,
    gain_attention,
    gain_feedforward,
    bias_table,
    cotangent,
):
    model_width = query_weight.shape[1]
    hidden_width = gate_weight.shape[1]
    packed = jnp.concatenate(
        (query_weight, key_weight, value_weight, out_weight, gate_weight, up_weight), axis=1
    )
    shards = (packed, down_weight, gain_attention, gain_feedforward, bias_table)
    full_weights = (
        lax.all_gather(shards[0], "fsdp", axis=0, tiled=True),
        lax.all_gather(shards[1], "fsdp", axis=0, tiled=True),
        lax.all_gather(shards[2], "fsdp", axis=0, tiled=True),
        lax.all_gather(shards[3], "fsdp", axis=0, tiled=True),
        lax.all_gather(shards[4], "fsdp", axis=0, tiled=True),
    )
    reordered = tokens[permutation]
    dealt = lax.all_to_all(reordered, "fsdp", split_axis=0, concat_axis=1, tiled=True)
    seq_count = dealt.shape[0]
    seq_len = dealt.shape[1]
    local_ids = lax.dynamic_slice_in_dim(permutation, lax.axis_index("fsdp") * seq_count, seq_count)
    seq_lengths = lengths[local_ids]
    positions = jnp.arange(seq_len, dtype=jnp.int32)
    row_valid = (positions[None, :] < seq_lengths[:, None]).astype(jnp.float32).reshape(-1, 1)
    onehot = bucket_onehot(seq_len)
    onehot_low = onehot.astype(jnp.bfloat16)
    full_packed, full_down, gain_one, gain_two, rel_bias = unpack_weights(
        full_weights, onehot, seq_len
    )
    head_shape = (seq_count, seq_len, HEADS, HEAD_DIM)
    rows_in = dealt.reshape(-1, model_width).astype(jnp.float32)
    scale_one = norm_scale(rows_in)
    normed = (rows_in * scale_one * gain_one).astype(jnp.bfloat16)
    projected = jnp.dot(
        normed, full_packed[:, : 3 * model_width], preferred_element_type=jnp.float32
    ).astype(jnp.bfloat16)
    query_heads = projected[:, :model_width].reshape(head_shape)
    key_heads = projected[:, model_width : 2 * model_width].reshape(head_shape)
    value_heads = projected[:, 2 * model_width :].reshape(head_shape)

    def attend_forward(pieces):
        query_one, key_one, value_one, length = pieces
        scores = masked_scores(query_one, key_one, rel_bias, length)
        row_max = jnp.max(scores, axis=-1, keepdims=True)
        exp_total = jnp.sum(jnp.exp(scores - row_max), axis=-1, keepdims=True)
        log_total = row_max + jnp.log(exp_total)
        weights_soft = jnp.exp(scores - log_total).astype(jnp.bfloat16)
        attended_one = jnp.einsum(
            "hqk,khd->qhd", weights_soft, value_one, preferred_element_type=jnp.float32
        )
        return (attended_one.astype(jnp.bfloat16), log_total)

    attended_heads, log_totals = lax.map(
        attend_forward, (query_heads, key_heads, value_heads, seq_lengths)
    )
    attended_rows = attended_heads.reshape(-1, model_width)
    middle = rows_in + jnp.dot(
        attended_rows,
        full_packed[:, 3 * model_width : 4 * model_width],
        preferred_element_type=jnp.float32,
    )
    scale_two = norm_scale(middle)
    normed_two = (middle * scale_two * gain_two).astype(jnp.bfloat16)
    gate_up = jnp.dot(
        normed_two, full_packed[:, 4 * model_width :], preferred_element_type=jnp.float32
    )

    def gelu_product(gate_part, up_part):
        return jax.nn.gelu(gate_part, approximate=True) * up_part

    hidden_full, gelu_pull = jax.vjp(
        gelu_product, gate_up[:, :hidden_width], gate_up[:, hidden_width:]
    )
    hidden = hidden_full.astype(jnp.bfloat16)
    result = middle + jnp.dot(hidden, full_down, preferred_element_type=jnp.float32)
    layer_output = (
        (result * row_valid).astype(jnp.bfloat16).reshape(seq_count, seq_len, model_width)
    )
    full_weights = (
        lax.all_gather(shards[0], "fsdp", axis=0, tiled=True),
        lax.all_gather(shards[1], "fsdp", axis=0, tiled=True),
        lax.all_gather(shards[2], "fsdp", axis=0, tiled=True),
        lax.all_gather(shards[3], "fsdp", axis=0, tiled=True),
        lax.all_gather(shards[4], "fsdp", axis=0, tiled=True),
    )
    full_packed, full_down, gain_one, gain_two, rel_bias = unpack_weights(
        full_weights, onehot, seq_len
    )
    upstream = cotangent.reshape(-1, model_width).astype(jnp.float32) * row_valid
    upstream_low = upstream.astype(jnp.bfloat16)
    d_hidden = against_rows(upstream_low, full_down)
    d_gate, d_up = gelu_pull(d_hidden)
    d_gate_up = jnp.concatenate((d_gate, d_up), axis=1).astype(jnp.bfloat16)
    d_normed_two = against_rows(d_gate_up, full_packed[:, 4 * model_width :])
    gain_two_grad = jnp.sum(d_normed_two * middle * scale_two, axis=0)
    d_middle = upstream + norm_back(middle, scale_two, gain_two, d_normed_two)
    d_branch = d_middle.astype(jnp.bfloat16)
    d_attended = against_rows(d_branch, full_packed[:, 3 * model_width : 4 * model_width]).astype(
        jnp.bfloat16
    )

    def attend_backward(pieces):
        query_one, key_one, value_one, length, log_total, d_attended_one = pieces
        scores = masked_scores(query_one, key_one, rel_bias, length)
        probs = jnp.exp(scores - log_total)
        probs_low = probs.astype(jnp.bfloat16)
        d_value = jnp.einsum(
            "hqk,qhd->khd", probs_low, d_attended_one, preferred_element_type=jnp.float32
        )
        d_probs = jnp.einsum(
            "qhd,khd->hqk", d_attended_one, value_one, preferred_element_type=jnp.float32
        )
        inner = jnp.sum(probs * d_probs, axis=-1, keepdims=True)
        d_scores = (probs * (d_probs - inner)).astype(jnp.bfloat16)
        d_query = jnp.einsum("hqk,khd->qhd", d_scores, key_one, preferred_element_type=jnp.float32)
        d_key = jnp.einsum("hqk,qhd->khd", d_scores, query_one, preferred_element_type=jnp.float32)
        d_bias = against_rows(d_scores.reshape(HEADS, -1), onehot_low)
        return (
            (
                d_query.astype(jnp.bfloat16),
                d_key.astype(jnp.bfloat16),
                d_value.astype(jnp.bfloat16),
            ),
            d_bias,
        )

    (d_query_all, d_key_all, d_value_all), d_bias_all = lax.map(
        attend_backward,
        (
            query_heads,
            key_heads,
            value_heads,
            seq_lengths,
            log_totals,
            d_attended.reshape(head_shape),
        ),
    )
    d_qkv = jnp.concatenate(
        (
            d_query_all.reshape(-1, model_width),
            d_key_all.reshape(-1, model_width),
            d_value_all.reshape(-1, model_width),
        ),
        axis=1,
    )
    d_normed = against_rows(d_qkv, full_packed[:, : 3 * model_width])
    gain_one_grad = jnp.sum(d_normed * rows_in * scale_one, axis=0)
    d_rows = d_middle + norm_back(rows_in, scale_one, gain_one, d_normed)
    d_dealt = d_rows.astype(jnp.bfloat16).reshape(seq_count, seq_len, model_width)
    returned_rows = lax.all_to_all(d_dealt, "fsdp", split_axis=1, concat_axis=0, tiled=True)
    tokens_grad = returned_rows[jnp.argsort(permutation)]
    packed_grad = lax.psum_scatter(
        jnp.concatenate(
            (
                rows_product(normed, d_qkv),
                jnp.concatenate(
                    (rows_product(attended_rows, d_branch), rows_product(normed_two, d_gate_up)),
                    axis=1,
                ),
            ),
            axis=1,
        ),
        "fsdp",
        scatter_dimension=0,
        tiled=True,
    )
    mixer_grad = packed_grad[:, : 3 * model_width]
    branch_grad = packed_grad[:, 3 * model_width :]
    down_grad = lax.psum_scatter(
        rows_product(hidden, upstream_low), "fsdp", scatter_dimension=0, tiled=True
    )
    table_sum = jnp.sum(d_bias_all, axis=0).T.reshape(-1)
    gain_attention_grad, gain_feedforward_grad, table_grad = (
        lax.psum_scatter(gain_one_grad, "fsdp", scatter_dimension=0, tiled=True),
        lax.psum_scatter(gain_two_grad, "fsdp", scatter_dimension=0, tiled=True),
        lax.psum_scatter(table_sum, "fsdp", scatter_dimension=0, tiled=True),
    )
    return (
        layer_output,
        tokens_grad,
        mixer_grad[:, :model_width],
        mixer_grad[:, model_width : 2 * model_width],
        mixer_grad[:, 2 * model_width :],
        branch_grad[:, :model_width],
        branch_grad[:, model_width : model_width + hidden_width],
        branch_grad[:, model_width + hidden_width :],
        down_grad,
        gain_attention_grad,
        gain_feedforward_grad,
        table_grad,
    )


MESH = pl.DeviceIdType.MESH
AXIS = "fsdp"


def over(left, right, left_dim=1, right_dim=0):
    return lax.dot_general(
        left, right, (((left_dim,), (right_dim,)), ((), ())), preferred_element_type=jnp.float32
    )


def low(values):
    return values.astype(jnp.bfloat16)


def tile_probs(query, key, bias, same):
    scores = jnp.where(same, over(query, key, 1, 1) + bias, masked_score)
    grown = jnp.exp(scores - jnp.max(scores, axis=-1, keepdims=True))
    return grown / jnp.sum(grown, axis=-1, keepdims=True)


class Spot:
    def __init__(self):
        me = lax.axis_index(AXIS)
        c, x, y, z = me % 2, (me // 2) % 2, (me // 4) % 2, me // 8
        self.me = me
        self.mid = (z == 1) | (z == 2)
        self.end = jnp.logical_not(self.mid)
        self.zs = (z, z + 1 - 2 * (z % 2), 2 - z // 2, 3 - 3 * (z // 2))
        self.shift = [8 * (zz - z) for zz in self.zs]
        self.core, self.x, self.y = me + 1 - 2 * c, me + 2 - 4 * x, me + 4 - 8 * y
        self.diag = self.x + self.y - me
        self.n1, self.n2 = me + self.shift[1], me + self.shift[2]

    def greet(self):
        bar = pltpu.get_barrier_semaphore()
        for peer in (self.core, self.x, self.y, self.n1):
            pl.semaphore_signal(bar, inc=1, device_id=(peer,), device_id_type=MESH)

        @pl.when(self.mid)
        def _():
            pl.semaphore_signal(bar, inc=1, device_id=(self.n2,), device_id_type=MESH)

        pl.semaphore_wait(bar, 4 + self.mid.astype(jnp.int32))

    def greet_all(self, count):
        bar = pltpu.get_barrier_semaphore()

        def signal(d, _):
            peer = (self.me + d) % count
            pl.semaphore_signal(bar, inc=1, device_id=(peer,), device_id_type=MESH)
            return _

        lax.fori_loop(1, count, signal, 0)
        pl.semaphore_wait(bar, count - 1)


class Sends:
    def __init__(self, sems):
        self.sems, self.used, self.open = sems, 0, []

    def push(self, src, dst, rsem, peer, when=None):
        ssem = self.sems.at[self.used]
        self.used += 1

        def copy():
            return pltpu.make_async_remote_copy(
                src, dst, ssem, rsem, device_id=(peer,), device_id_type=MESH
            )

        if when is None:
            copy().start()
        else:
            pl.when(when)(lambda: copy().start())
        self.open.append((lambda: copy().wait_send(), when))

    def finish(self):
        for wait, when in self.open:
            if when is None:
                wait()
            else:
                pl.when(when)(wait)
        self.open = []


def arrive(dst, rsem, spot):
    pltpu.make_async_remote_copy(
        dst, dst, rsem, rsem, device_id=(spot.core,), device_id_type=MESH
    ).wait_recv()


def gather_steps(spot, src, dst, rows, sends, rsem, own_sem):
    half = src.shape[1] // 2
    cols = (pl.ds(0, half), pl.ds(half, half))
    me, mid, shift = spot.me, spot.mid, spot.shift
    first, last = (spot.x, spot.y), (spot.y, spot.x)
    own = pltpu.make_async_copy(src.at[rows, :], dst.at[me, rows, :], own_sem)
    own.start()

    def push(part, block, peer, mine=False, when=None):
        there = dst.at[block, rows, cols[part]]
        here = src.at[rows, cols[part]] if mine else there
        sends.push(here, there, rsem.at[part, block], peer, when)

    def landed(part, block):
        arrive(dst.at[block, rows, cols[part]], rsem.at[part, block], spot)

    for part in (0, 1):
        push(part, me, spot.n1, True)
        push(part, me, spot.n2, True, mid)
        push(part, me, first[part], True)
        push(part, me, last[part], True)
    for part in (0, 1):
        push(part, me, spot.core, True)
    yield

    def from_z(part, j):
        b = me + shift[j]
        landed(part, b)
        push(part, b, spot.n2 if j == 1 else spot.n1, when=mid)
        push(part, b, first[part])
        push(part, b, last[part])
        push(part, b, spot.core)

    def from_first(part, j):
        b = first[part] + shift[j]
        landed(part, b)
        push(part, b, last[part])
        push(part, b, spot.core)

    def from_last(part, b):
        landed(part, b)
        push(part, b, spot.core)

    for j in range(4):
        if j:
            for part in (0, 1):
                from_z(part, j)
                yield
        for part in (0, 1):
            from_first(part, j)
            yield
        if j:
            for part in (0, 1):
                from_last(part, last[part] + shift[j - 1])
                yield
    for part in (0, 1):
        from_last(part, last[part] + shift[3])
        yield
    for j in range(4):
        for part in (0, 1):
            from_last(part, spot.diag + shift[j])
            yield
    for j in range(4):
        for base in (me, spot.x, spot.y, spot.diag):
            for part in (0, 1):
                landed(part, base + spot.core - me + shift[j])
    own.wait()
    yield


def scatter_steps(spot, p_refs, o_refs, rows, bufs, sems, sends):
    ring_ref, s_ref, first_ref, second_ref, za_ref, zb_ref = bufs
    lsem, csem, fsem, gsem, zasem, zbsem = sems
    given = len(p_refs)
    width = p_refs[0].shape[2]
    half = given * width // 2
    me, mid, end, zs = spot.me, spot.mid, spot.end, spot.zs
    cols, short = (pl.ds(0, half), pl.ds(half, half)), pl.ds(0, half)
    plane = (me, spot.x, spot.y, spot.diag)
    first_peer, second_peer = (spot.y, spot.x), (spot.x, spot.y)
    start, size = rows.start, rows.size

    def mine(q, j, part):
        return s_ref.at[q * 4 + zs[j], rows, cols[part]]

    def held(ref, part, slot):
        return ref.at[part, slot, rows, short]

    def chunks(count, step):
        lax.fori_loop(0, size // 16, lambda i, _: step(pl.ds(pl.multiple_of(start + i * 16, 16), 16)) or _, 0)

    def add(q, j, part, *more):
        def step(r):
            v = s_ref[q * 4 + zs[j], r, cols[part]].astype(jnp.float32)
            for ref, slot in more:
                v = v + ref[part, slot, r, short].astype(jnp.float32)
            s_ref[q * 4 + zs[j], r, cols[part]] = v.astype(s_ref.dtype)

        chunks(size, step)

    def pair_exchange(j):
        for q in (3, 2, 1, 0):
            b = plane[q] + spot.shift[j]
            slot = q * 4 + zs[j]
            for i, p_ref in enumerate(p_refs):
                own = pl.ds(i * width, width)
                sends.push(p_ref.at[b + spot.core - me, rows, :], s_ref.at[slot, rows, own], csem.at[i, slot], spot.core)
                here = ring_ref.at[j % 2 * 4 + q, rows, own]
                pltpu.make_async_copy(p_ref.at[b, rows, :], here, lsem.at[i, j % 2 * 4 + q]).start()

    def joined(q, j):
        slot, near = q * 4 + zs[j], j % 2 * 4 + q
        for i, p_ref in enumerate(p_refs):
            own = pl.ds(i * width, width)
            pltpu.make_async_copy(p_ref.at[0, rows, :], ring_ref.at[near, rows, own], lsem.at[i, near]).wait()
            arrive(s_ref.at[slot, rows, own], csem.at[i, slot], spot)
        everything = pl.ds(0, given * width)

        def step(r):
            v = ring_ref[near, r, everything].astype(jnp.float32) + s_ref[slot, r, everything].astype(jnp.float32)
            s_ref[slot, r, everything] = v.astype(s_ref.dtype)

        chunks(size, step)

    def to_first(part, q, j):
        slot = (4 if q == 3 else 0) + zs[j]
        sends.push(mine(q, j, part), held(first_ref, part, slot), fsem.at[part, slot], first_peer[part])

    def first_stage(j):
        joined(3, j)
        if j:
            pair_exchange(j - 1)
        to_first(0, 3, j)
        to_first(1, 3, j)
        yield
        joined(2, j)
        to_first(0, 2, j)
        yield
        joined(1, j)
        to_first(1, 1, j)
        joined(0, j)
        yield

    def second_stage(j):
        for part in (0, 1):
            q, slot = (1, 2)[part], 4 + zs[j]
            arrive(held(first_ref, part, slot), fsem.at[part, slot], spot)
            add(q, j, part, (first_ref, slot))
            sends.push(mine(q, j, part), held(second_ref, part, zs[j]), gsem.at[part, zs[j]], second_peer[part])
            yield

    def z_send(j):
        for part in (0, 1):
            arrive(held(first_ref, part, zs[j]), fsem.at[part, zs[j]], spot)
            arrive(held(second_ref, part, zs[j]), gsem.at[part, zs[j]], spot)
            add(0, j, part, (first_ref, zs[j]), (second_ref, zs[j]))
            if j:
                sends.push(mine(0, j, part), held(za_ref, part, 3 - j), zasem.at[part, 3 - j], spot.n1, end)
            yield

    def z_relay(j):
        if not j:
            return
        for part in (0, 1):
            came, sem, slot = (za_ref, zasem, 3 - j) if j > 1 else (zb_ref, zbsem, 0)

            @pl.when(mid)
            def _():
                arrive(held(came, part, slot), sem.at[part, slot], spot)
                add(0, j, part, (came, slot))

            slot = 3 - j if j > 1 else 0
            peer = spot.n2 if j > 1 else spot.n1
            sends.push(mine(0, j, part), held(zb_ref, part, slot), zbsem.at[part, slot], peer, mid)
            yield

    pair_exchange(3)
    yield
    stages = (first_stage, second_stage, z_send, z_relay)
    for step in range(4 + len(stages) - 1):
        for stage, what in enumerate(stages):
            j = 3 - (step - stage)
            if 0 <= j <= 3:
                yield from what(j)
    for part in (0, 1):
        o_ref, there = (o_refs[part], pl.ds(0, half)) if given == 2 else (o_refs[0], cols[part])

        def total(*more):
            def step(r):
                v = s_ref[zs[0], r, cols[part]].astype(jnp.float32)
                for ref, slot in more:
                    v = v + ref[part, slot, r, short].astype(jnp.float32)
                o_ref[r, there] = v

            chunks(size, step)

        @pl.when(mid)
        def _():
            arrive(held(za_ref, part, 2), zasem.at[part, 2], spot)
            arrive(held(zb_ref, part, 1), zbsem.at[part, 1], spot)
            total((za_ref, 2), (zb_ref, 1))

        @pl.when(end)
        def _():
            arrive(held(zb_ref, part, 0), zbsem.at[part, 0], spot)
            total((zb_ref, 0))

        yield


def swap(spot, count, src, dst, sems, what, some=None):
    begin, end = some or (1, count)
    send_sem, recv_sem, own_sem = sems
    share = src.shape[0] // count

    def part(ref, index):
        return ref.at[pl.ds(pl.multiple_of(index * share, share), share), :]

    def own():
        return pltpu.make_async_copy(part(src, spot.me), part(dst, spot.me), own_sem)

    def one(d, _):
        peer, source = (spot.me + d) % count, (spot.me + count - d) % count
        if what == "send":
            pltpu.make_async_remote_copy(
                part(src, peer), part(dst, spot.me), send_sem.at[peer], recv_sem.at[spot.me], device_id=(peer,),
                device_id_type=MESH,
            ).start()
        else:
            copy = pltpu.make_async_remote_copy(
                part(src, peer), part(dst, source), send_sem.at[peer], recv_sem.at[source], device_id=(peer,),
                device_id_type=MESH,
            )
            copy.wait_recv()
            copy.wait_send()
        return _

    if what == "send" and begin == 1:
        own().start()
    lax.fori_loop(begin, end, one, 0)
    if what == "wait" and end == count:
        own().wait()


def pack(weights, first_ref, second_ref):
    query_ref, key_ref, value_ref, gate_ref, up_ref = weights
    rows = query_ref.shape[0]
    count = first_ref.shape[0] // rows
    head, units = query_ref.shape[1] // count, gate_ref.shape[1] // count
    for j in range(count):
        there = pl.ds(j * rows, rows)
        for i, ref in enumerate((query_ref, key_ref, value_ref)):
            first_ref[there, i * head : (i + 1) * head] = ref[:, j * head : (j + 1) * head]
        first_ref[there, 3 * head :] = gate_ref[:, j * units : j * units + head]
        second_ref[there, : units - head] = gate_ref[:, j * units + head : (j + 1) * units]
        second_ref[there, units - head :] = up_ref[:, j * units : (j + 1) * units]


def weave(tasks, order):
    names = list(tasks)
    left = {name: steps for name, (_, steps) in tasks.items()}

    def advance(name):
        for other in tasks[name][0]:
            if other in left:
                advance(other)
                assert other not in left, name
        if name in left and next(left[name], left) is left:
            del left[name]

    for number, times in order:
        for _ in range(times):
            advance(names[number])
    while left:
        name = next(n for n in left if not any(other in left for other in tasks[n][0]))
        while name in left:
            advance(name)


FRONT_ORDER = (
    (0, 1), (2, 1), (0, 1), (2, 4), (0, 2), (4, 5), (2, 1), (3, 1), (4, 16), (1, 1), (4, 11), (6, 1), (1, 1),
    (5, 1), (6, 8), (5, 1), (6, 2), (5, 1), (6, 2), (5, 1), (6, 1), (5, 1), (7, 5), (13, 1), (7, 1), (13, 1),
    (7, 2), (13, 1), (5, 1), (13, 2), (7, 4), (5, 1), (13, 3), (14, 1), (7, 1), (5, 1), (7, 1), (14, 1), (3,
    1), (5, 1), (7, 1), (14, 2), (7, 1), (14, 1), (7, 1), (14, 7), (5, 1), (14, 1), (5, 1), (7, 2), (14, 1),
    (7, 6), (5, 1), (14, 1), (7, 1), (5, 5), (14, 4), (7, 4), (14, 1), (7, 2), (14, 1), (7, 1), (14, 4), (5,
    1), (7, 1), (5, 2), (7, 1), (5, 6), (7, 1), (5, 2), (14, 1), (5, 1), (14, 1), (7, 1), (14, 1), (8, 1), (9,
    1), (14, 2), (5, 1), (14, 1), (3, 1), (5, 2), (14, 1), (3, 1), (14, 3), (9, 1), (14, 1), (9, 1), (14, 1),
    (15, 1), (9, 18), (3, 1), (9, 8), (16, 1), (9, 3), (16, 1), (10, 1), (16, 3), (10, 1), (16, 4), (10, 1),
    (16, 2), (10, 1), (16, 5), (10, 1), (16, 1), (10, 1), (16, 11), (10, 1), (16, 2), (11, 1), (16, 1), (11,
    1), (16, 1), (11, 6), (17, 1), (11, 1), (17, 1), (11, 3), (17, 1), (11, 9), (17, 1), (11, 2), (17, 1),
    (18, 1), (11, 4), (18, 1), (11, 1), (18, 8), (11, 1), (18, 1), (11, 8), (12, 1), (18, 26), (19, 1),
)
REAR_ORDER = (
    (0, 4), (1, 1), (0, 28), (4, 1), (1, 1), (4, 1), (1, 1), (4, 1), (1, 1), (4, 2), (1, 1), (4, 1), (1, 1),
    (4, 1), (1, 1), (4, 1), (1, 1), (4, 1), (1, 1), (4, 1), (1, 1), (4, 1), (1, 1), (4, 2), (1, 1), (4, 1),
    (1, 1), (4, 1), (1, 2), (4, 2), (1, 1), (4, 1), (1, 1), (4, 1), (1, 1), (4, 1), (1, 1), (4, 2), (1, 3),
    (4, 1), (5, 1), (6, 1), (5, 1), (1, 3), (5, 1), (1, 2), (5, 1), (1, 1), (5, 1), (6, 1), (1, 1), (5, 1),
    (1, 1), (5, 1), (6, 3), (1, 1), (5, 1), (1, 1), (6, 1), (1, 1), (5, 1), (1, 1), (6, 1), (5, 1), (1, 1),
    (6, 2), (3, 1), (1, 1), (5, 1), (1, 1), (5, 12), (7, 1), (5, 1), (7, 2), (5, 4), (7, 2), (5, 1), (3, 1),
    (7, 4), (5, 2), (7, 2), (5, 1), (7, 1), (2, 1), (7, 1), (5, 1), (7, 3), (5, 1), (7, 2), (5, 1), (7, 2),
    (5, 1), (7, 1), (5, 1), (7, 4), (2, 1), (7, 12), (8, 3),
)
N_GATHER_SENDS = 66
FEW = 16


def gelu_pair(gate):
    slope = 0.7978845608028654
    squared = gate * gate
    bent = jnp.tanh(slope * (gate + 0.044715 * gate * squared))
    gelu = 0.5 * gate * (1.0 + bent)
    return gelu, 0.5 * (1.0 + bent) + 0.5 * gate * (1.0 - bent * bent) * slope * (1.0 + 3.0 * 0.044715 * squared)


def scatter_sems(halves, given):
    dma = pltpu.SemaphoreType.DMA
    return [
        dma((halves, 16 * given + 36)), dma((halves, given, 8)), dma((halves, given, 16)), dma((halves, 2, 8)),
        dma((halves, 2, 4)), dma((halves, 2, 3)), dma((halves, 2, 2)),
    ]


def scatter_bufs(rows, width, given):
    half = given * width // 2
    shapes = ((8, rows, given * width), (16, rows, given * width), (2, 8, rows, half), (2, 4, rows, half))
    return [pltpu.VMEM(shape, jnp.bfloat16) for shape in shapes + ((2, 3, rows, half), (2, 2, rows, half))]


class Stage:
    def __init__(self, count, cuts, in_refs, out_refs, in_sems, out_sems):
        self.spot = Spot()
        self.count = count
        self.ranges = [pl.ds(a, b - a) for a, b in zip(cuts[:-1], cuts[1:])]
        self.cuts = cuts
        self.sends = {}
        self.in_refs, self.out_refs, self.in_sems, self.out_sems = in_refs, out_refs, in_sems, out_sems

    def gathering(self, name, at, src, dst, rows, sems):
        own_sem, ssem, rsem = sems
        self.sends[name] = Sends(ssem.at[at])
        yield from gather_steps(self.spot, src, dst, rows, self.sends[name], rsem.at[at], own_sem.at[at])

    def scattering(self, name, p_refs, o_refs, rows, bufs, sems, at):
        self.sends[name] = Sends(sems[0].at[at])
        yield from scatter_steps(
            self.spot, p_refs, o_refs, rows, bufs, [sem.at[at] for sem in sems[1:]], self.sends[name]
        )

    def fetch(self, group, sources, streams=None):
        streams = range(len(sources)) if streams is None else streams
        for i, source in zip(streams, sources):
            there = self.in_refs[i].at[group % 2]
            yield pltpu.make_async_copy(source.at[:, pl.ds(group * FEW, FEW), :], there, self.in_sems.at[i, group % 2])

    def store(self, group, targets):
        for i, target in enumerate(targets):
            there = target.at[:, pl.ds(group * FEW, FEW), :]
            yield pltpu.make_async_copy(self.out_refs[i], there, self.out_sems.at[i])

    def finish(self):
        for some in self.sends.values():
            some.finish()


def start_all(copies):
    for copy in copies:
        copy.start()


def wait_all(copies):
    for copy in copies:
        copy.wait()


def tile_inputs(qkv_ref, col_ref, row_ref, base, length, head):
    query = qkv_ref[pl.ds(base + length, length), :head]
    key = qkv_ref[pl.ds(base, 3 * length), head : 2 * head]
    value = qkv_ref[pl.ds(base, 3 * length), 2 * head :]
    return query, key, value, col_ref[pl.ds(base, length), :] == row_ref[:, pl.ds(base, 3 * length)]


def front_kernel(cuts, *refs):
    tok_ref, cot_ref, index_ref, small_ref = refs[:4]
    weights = refs[4:9]
    wd_ref, wo_ref, perm_ref, bucket_ref, col_ref, row_ref = refs[9:15]
    (rows_ref, gain_one_ref, bias_ref, first_w_ref, qkv_ref, att_ref, middle_ref, d_mid_ref, d_ref, gain_grad_ref, near_grad_ref,
     far_grad_ref, wd_grad_ref, nx_all_ref, forth_ref) = refs[15:30]
    part_ref, up_all_ref, x_all_ref, back_ref = refs[30:34]
    branch_ref, x_ref, dn_ref, w_ref, nx_ref, up_ref, gain_ref, gate_w_ref = refs[34:42]
    one_ref, two_ref, cot_out_ref, one_in_ref, two_in_ref, cot_in_ref = refs[42:48]
    small_out_ref, all_small_ref, first_ref, second_ref = refs[48:52]
    bufs, two_total_ref, in_refs, out_refs = refs[52:58], refs[58], refs[59:61], refs[61:63]
    in_sems, out_sems = refs[63:65]
    exchanges = refs[65:83]
    one_x, two_x, cot_x, small_x, first_x, second_x = [exchanges[i : i + 3] for i in range(0, 18, 3)]
    g_sems, one_sems, two_sems = refs[83:86], refs[86:93], refs[93:100]
    two_bufs = (bufs[0], two_total_ref, *bufs[2:])
    count, slots, width = x_all_ref.shape
    stage = Stage(count, cuts, in_refs, out_refs, in_sems, out_sems)
    spot, ranges = stage.spot, stage.ranges
    units, head, length = wd_ref.shape[0], wo_ref.shape[0], bias_ref.shape[0]
    size, piece = one_ref.shape
    folds, share = width // piece, size // count
    grain = share // folds
    groups = cuts[-1] // FEW
    near = units - head
    spot.greet_all(count)

    def at(shape, axis):
        return lax.broadcasted_iota(jnp.int32, shape, axis)

    def marked(mask):
        return low(jnp.where(mask, 1.0, 0.0))

    def folded(rows, sources):
        shape = (length, size)
        return low(
            sum(
                over(
                    marked((at(shape, 0) == sources) & (at(shape, 1) % share // grain == i)),
                    rows[:, i * piece : (i + 1) * piece], 0, 0,
                )
                for i in range(folds)
            )
        )

    def pick(shares, to_ref):
        source = index_ref[2:3, :slots]
        for i in range(folds):
            mask = at((size, slots), 0) == source + i * grain
            to_ref[:, i * piece : (i + 1) * piece] = low(over(marked(mask), shares, 0, 0))

    def tokens():
        for i in range(count):
            small_out_ref[i * share : (i + 1) * share, :] = small_ref[...]
        one_ref[...] = folded(tok_ref[...], index_ref[0:1, :])
        swap(spot, count, one_ref, one_in_ref, one_x, "send")
        swap(spot, count, small_out_ref, all_small_ref, small_x, "send")
        yield
        swap(spot, count, one_ref, one_in_ref, one_x, "wait")
        place = index_ref[1:2, :]
        place = jnp.where(place < 0, -1, place // grain * share + place % grain + at((1, size), 1) % share // grain * grain)
        two_ref[...] = low(over(marked(at((size, size), 0) == place), one_in_ref[...], 0, 0))
        swap(spot, count, two_ref, two_in_ref, two_x, "send")
        yield
        swap(spot, count, small_out_ref, all_small_ref, small_x, "wait")
        each = width // count
        shape = (2 * each, width)
        mine = at((size, width), 0) == at((size, width), 1) // each * share
        for i, ref in enumerate((gain_one_ref, gain_ref)):
            fold = marked(at(shape, 0) == at(shape, 1) % each + i * each)
            ref[...] = jnp.sum(jnp.where(mine, over(all_small_ref[...], fold), 0.0), axis=0, keepdims=True)
        table = jnp.where(at(all_small_ref.shape, 1) == spot.me, all_small_ref[...].astype(jnp.float32), 0.0)
        table = jnp.sum(table, axis=1, keepdims=True)
        bias_ref[...] = sum(
            jnp.where(bucket_ref[...] == b, table[b * share + 1 : b * share + 2, :], 0.0) for b in range(BUCKETS)
        )
        yield
        swap(spot, count, two_ref, two_in_ref, two_x, "wait")
        pick(two_in_ref[...], rows_ref)
        v = rows_ref[...].astype(jnp.float32)
        nx_ref[...] = (v * scale_of(v) * gain_one_ref[...]).astype(nx_ref.dtype)
        yield

    def cotangent():
        cot_out_ref[...] = folded(cot_ref[...], index_ref[1:2, :])
        swap(spot, count, cot_out_ref, cot_in_ref, cot_x, "send")
        yield
        swap(spot, count, cot_out_ref, cot_in_ref, cot_x, "wait")
        pick(cot_in_ref[...], up_ref)
        yield

    def columns(src, dst, sems, packs):
        if packs:
            pack(weights, first_ref, second_ref)
            yield
        for i in range(0, count, 8):
            swap(spot, count, src, dst, sems, "send", (max(i, 1), i + 8))
            yield
        swap(spot, count, src, dst, sems, "wait")
        if packs:
            gate_w_ref[...] = dst[:, 3 * head :]
        yield

    def attending(first, last):
        perm = perm_ref[...]
        if first == 0:
            start_all(stage.fetch(0, (nx_all_ref,)))
            qkv_ref[:length, :] = jnp.zeros((length, 3 * head), qkv_ref.dtype)
            qkv_ref[length + groups * size :, :] = jnp.zeros((length, 3 * head), qkv_ref.dtype)
        for step in range(first, last):
            if step < groups:
                if step + 1 < groups:
                    start_all(stage.fetch(step + 1, (nx_all_ref,)))
                wait_all(stage.fetch(step, (nx_all_ref,)))
                rows = low(over(in_refs[0][step % 2].reshape(size, -1), first_w_ref[:, : 3 * head]))
                qkv_ref[length + step * size : length + (step + 1) * size, :] = low(over(perm, rows))
                yield
            if step > 0:
                attended = []
                for tile in range(size // length):
                    base = (step - 1) * size + tile * length
                    query, key, value, same = tile_inputs(qkv_ref, col_ref, row_ref, base, length, head)
                    attended.append(low(over(low(tile_probs(query, key, bias_ref[...], same)), value)))
                    if tile % 2:
                        yield
                rows = low(over(perm, jnp.concatenate(attended, axis=0), 0, 0))
                att_ref[:, (step - 1) * FEW : step * FEW, :] = rows.reshape(count, FEW, head)
                if step > max(first, 1):
                    wait_all(stage.store(step - 2, (part_ref,)))
                for i in range(2):
                    there = pl.ds(i * count // 2, count // 2)
                    piece = over(rows[i * size // 2 : (i + 1) * size // 2], wo_ref[...])
                    out_refs[0][there] = low(piece).reshape(count // 2, FEW, width)
                start_all(stage.store(step - 1, (part_ref,)))
                yield
        if last > max(first, 1):
            wait_all(stage.store(last - 2, (part_ref,)))
        yield

    def rows_of(rows):
        return [pl.ds(rows.start + i, 16) for i in range(0, rows.size, 16)]

    def scale_of(v):
        return lax.rsqrt(jnp.sum(v * v, axis=1, keepdims=True) / width + EPSILON)

    def first_norm(rows):
        for r in rows_of(rows):
            v = rows_ref[r, :].astype(jnp.float32) + branch_ref[r, :]
            middle_ref[r, :] = v
            x_ref[r, :] = (v * scale_of(v) * gain_ref[...]).astype(x_ref.dtype)
        yield

    def norm_back_rows(rows):
        for r in rows_of(rows):
            v, d, gain = middle_ref[r, :], dn_ref[r, :], gain_ref[...]
            scale = scale_of(v)
            gain_grad_ref[...] += jnp.sum(d * v * scale, axis=0, keepdims=True)
            w = gain * d
            mean = jnp.sum(w * v, axis=1, keepdims=True) / width
            d_mid = up_ref[r, :].astype(jnp.float32) + scale * w - v * (scale * scale * scale) * mean
            d_mid_ref[r, :] = d_mid
            d_ref[r, :] = d_mid.astype(d_ref.dtype)
        yield

    def feeding(first, last):
        sources, targets = (x_all_ref, up_all_ref), (back_ref, forth_ref)
        start_all(stage.fetch(first, sources))
        for group in range(first, last):
            if group + 1 < last:
                start_all(stage.fetch(group + 1, sources))
            wait_all(stage.fetch(group, sources))
            for i in range(2):
                blocks = slice(i * count // 2, (i + 1) * count // 2)
                x = in_refs[0][group % 2, blocks].reshape(size // 2, width)
                upstream = in_refs[1][group % 2, blocks].reshape(size // 2, width)
                both = over(x, w_ref[...])
                gate = jnp.concatenate((over(x, gate_w_ref[...]), both[:, :near]), axis=1)
                up = both[:, near:]
                d_hidden = over(upstream, wd_ref[...], 1, 1)
                gelu, d_gelu = gelu_pair(gate)
                hidden = low(gelu * up)
                d_gate, d_up = low(d_hidden * up * d_gelu), low(d_hidden * gelu)
                d_first, d_both = d_gate[:, :head], jnp.concatenate((d_gate[:, head:], d_up), axis=1)
                if i == 0 and group > first:
                    wait_all(stage.store(group - 1, targets))
                shape = (count // 2, FEW, width)
                back = over(d_both, w_ref[...], 1, 1) + over(d_first, gate_w_ref[...], 1, 1)
                out_refs[0][blocks] = low(back).reshape(shape)
                out_refs[1][blocks] = low(over(hidden, wd_ref[...])).reshape(shape)
                if i:
                    start_all(stage.store(group, targets))
                near_grad_ref[...] += over(d_first, x, 0, 0)
                far_grad_ref[...] += over(d_both, x, 0, 0)
                wd_grad_ref[...] += over(hidden, upstream, 0, 0)
                yield
        wait_all(stage.store(last - 1, targets))
        yield

    for ref in (near_grad_ref, far_grad_ref, wd_grad_ref, gain_grad_ref):
        ref[...] = jnp.zeros_like(ref)
    halves = len(ranges)
    everything = pl.ds(0, slots)
    tasks = {
        "tokens": ([], tokens()),
        "cot": ([], cotangent()),
        "first": ([], columns(first_ref, first_w_ref, first_x, True)),
        "second": (["first"], columns(second_ref, w_ref, second_x, False)),
        "gather": (["tokens"], stage.gathering("gather", 0, nx_ref, nx_all_ref, everything, g_sems)),
        "up": (["cot"], stage.gathering("up", 1, up_ref, up_all_ref, everything, g_sems)),
    }
    for i, rows in enumerate(ranges):
        h = str(i)
        last_step = groups + 1 if i == halves - 1 else cuts[i + 1] // FEW + 1
        first_step = cuts[i] // FEW + 1 if i else 0
        tasks |= {
            "attend" + h: ([f"attend{i - 1}"] if i else ["gather", "first"], attending(first_step, last_step)),
            "one" + h: (
                ["attend" + h], stage.scattering("one" + h, (part_ref,), (branch_ref,), rows, bufs, one_sems, i),
            ),
            "norm" + h: (["one" + h], first_norm(rows)),
            "x" + h: (["norm" + h], stage.gathering("x" + h, 2 + i, x_ref, x_all_ref, rows, g_sems)),
            "feed" + h: (
                ["x" + h, "up", "second", f"feed{i - 1}" if i else f"attend{halves - 1}"],
                feeding(cuts[i] // FEW, cuts[i + 1] // FEW),
            ),
            "two" + h: (
                ["feed" + h],
                stage.scattering("two" + h, (back_ref,), (dn_ref,), rows, two_bufs, two_sems, i),
            ),
            "back" + h: (["two" + h], norm_back_rows(rows)),
        }
    weave(tasks, FRONT_ORDER)
    stage.finish()


def halves_of(rows):
    return (0, 48, 80) if rows == 80 else (0, rows)


def front(tok, cot, index, small, weights, wd, wo, perm, buckets, col, row, slots):
    size, (length, width) = index.shape[1], tok.shape
    shard = weights[0].shape[0]
    count, piece = width // shard, length * width // size
    cuts = halves_of(slots)
    halves = len(cuts) - 1
    head, units = wo.shape[0], wd.shape[0]
    low_rows, all_rows, group, share = (slots, width), (count, slots, width), (count, FEW, width), (size, piece)
    first, second = (width, 4 * head), (width, 2 * units - head)
    bf, wide, dma = jnp.bfloat16, jnp.float32, pltpu.SemaphoreType.DMA
    vmem, hbm = pl.BlockSpec(memory_space=pltpu.VMEM), pl.BlockSpec(memory_space=pl.ANY)
    shape = jax.ShapeDtypeStruct
    outs = pl.pallas_call(
        functools.partial(front_kernel, cuts),
        out_shape=[
            shape(low_rows, bf), shape((1, width), wide), shape(buckets.shape, wide), shape(first, bf),
            shape((slots // FEW * size + 2 * length, 3 * head), bf), shape((count, slots, head), bf), shape(low_rows, wide),
            shape(low_rows, wide), shape(low_rows, bf), shape((1, width), wide), shape((head, width), wide),
            shape((second[1], width), wide), shape(wd.shape, wide),
        ] + [shape(all_rows, bf)] * 6,
        in_specs=[vmem] * 15,
        out_specs=[vmem] * 13 + [hbm] * 6,
        scratch_shapes=[
            pltpu.VMEM(low_rows, wide), pltpu.VMEM(low_rows, bf), pltpu.VMEM(low_rows, wide), pltpu.VMEM(second, bf),
            pltpu.VMEM(low_rows, bf), pltpu.VMEM(low_rows, bf), pltpu.VMEM((1, width), wide), pltpu.VMEM((width, head), bf),
        ] + [pltpu.VMEM(share, bf)] * 6 + [
            pltpu.VMEM((size, 128), bf), pltpu.VMEM((size, 128), bf), pltpu.VMEM(first, bf), pltpu.VMEM(second, bf),
        ] + scatter_bufs(slots, width, 1) + [
            pltpu.VMEM((16, slots, width), bf),
            pltpu.VMEM((2,) + group, bf), pltpu.VMEM((2,) + group, bf), pltpu.VMEM(group, bf), pltpu.VMEM(group, bf),
            dma((2, 2)), dma((2,)),
        ] + [dma((count,)), dma((count,)), dma] * 6 + [
            dma((2 + halves,)), dma((2 + halves, N_GATHER_SENDS)), dma((2 + halves, 2, 32)),
        ] + scatter_sems(halves, 1) * 2,
        name="front",
        compiler_params=pltpu.CompilerParams(collective_id=3, has_side_effects=True, vmem_limit_bytes=63 * 2**20),
    )(tok, cot, index, small, *weights, wd, wo, perm, buckets, col, row)
    return outs[:15]


def rear_kernel(cuts, *refs):
    (d_ref, x_all_ref, att_ref, qkv_ref, w_ref, wo_ref, perm_ref, bias_ref, col_ref, row_ref, near_ref, forth_ref, middle_ref,
     rows_ref, d_mid_ref, gain_ref, spread_ref, turn_ref, bucket_ref) = refs[:19]
    wo_grad_ref, owned_ref, out_rows_ref, sums_ref, token_rows_ref = refs[19:24]
    d_all_ref, part_ref = refs[24:26]
    dn_ref, down_ref, bias_grad_ref, dq_ref, dkv_ref, w_grad_ref, turned_ref, result_ref, going_ref, came_ref, last_ref = refs[26:37]
    bufs, other_bufs, in_refs, out_refs = refs[37:43], refs[43:49], refs[49:51], refs[51:52]
    in_sems, out_sems = refs[52:54]
    w_sems, r_sems, t_sems, l_sems = refs[54:57], refs[57:60], refs[60:63], refs[63:66]
    g_sems, one_sems, down_sems = refs[66:69], refs[69:76], refs[76:83]
    count, width = part_ref.shape[0], part_ref.shape[2]
    stage = Stage(count, cuts, in_refs, out_refs, in_sems, out_sems)
    spot, ranges = stage.spot, stage.ranges
    spot.greet_all(count)
    head, length, size = wo_ref.shape[0], bias_ref.shape[0], perm_ref.shape[0]
    groups = cuts[-1] // FEW
    folds, piece = spread_ref.shape[0], result_ref.shape[1]

    def owners():
        merged = jnp.concatenate((low(w_grad_ref[...]), low(near_ref[...])), axis=0)
        for i in range(0, width, 512):
            turned_ref[i : i + 512, :] = merged[:, i : i + 512].T
        swap(spot, count, turned_ref, owned_ref, w_sems, "send")
        yield
        swap(spot, count, turned_ref, owned_ref, w_sems, "wait")
        yield

    def dealt_out(rows):
        return sum(
            over(spread_ref[i], rows[:, i * piece : (i + 1) * piece]) for i in range(folds)
        )

    def output():
        rows = low(middle_ref[...] + down_ref[...])
        result_ref[...] = low(dealt_out(rows))
        swap(spot, count, result_ref, out_rows_ref, r_sems, "send")
        yield
        swap(spot, count, result_ref, out_rows_ref, r_sems, "wait")
        yield

    def scale_of(v):
        return lax.rsqrt(jnp.sum(v * v, axis=1, keepdims=True) / width + EPSILON)

    def shares(v):
        shape = (going_ref.shape[0], width)
        at, to = lax.broadcasted_iota(jnp.int32, shape, 0), lax.broadcasted_iota(jnp.int32, shape, 1)
        spread = jnp.where(at == to // (width // count) * 16, v, 0.0)
        fold = lax.broadcasted_iota(jnp.int32, (width, width // count), 0) % (width // count)
        fold = fold == lax.broadcasted_iota(jnp.int32, (width, width // count), 1)
        high = low(spread)
        rest = low(spread - high.astype(jnp.float32))
        return jnp.concatenate([over(p, low(fold.astype(jnp.float32))) for p in (high, rest)], axis=1)

    def finals():
        v, d, gain = rows_ref[...].astype(jnp.float32), dn_ref[...], gain_ref[...]
        scale = scale_of(v)
        w = gain * d
        mean = jnp.sum(w * v, axis=1, keepdims=True) / width
        rows = low(d_mid_ref[...] + scale * w - v * (scale * scale * scale) * mean)
        going_ref[:, :piece] = low(dealt_out(rows))
        sums = shares(jnp.sum(d * v * scale, axis=0, keepdims=True))
        at, to = lax.broadcasted_iota(jnp.int32, sums.shape, 0), lax.broadcasted_iota(jnp.int32, sums.shape, 1)
        for b in range(BUCKETS):
            total = jnp.sum(jnp.where(bucket_ref[...] == b, bias_grad_ref[...], 0.0), axis=(0, 1), keepdims=True)
            high = low(total).astype(jnp.float32)
            sums = sums + jnp.where((at == 16 * b + 1) & (to == 0), high, 0.0)
            sums = sums + jnp.where((at == 16 * b + 1) & (to == 1), total - high, 0.0)
        going_ref[:, piece:] = low(sums)
        swap(spot, count, going_ref, came_ref, t_sems, "send")
        yield
        swap(spot, count, going_ref, came_ref, t_sems, "wait")
        sums_ref[...] = came_ref[:, piece:]
        last_ref[...] = low(over(turn_ref[...], came_ref[:, :piece]))
        swap(spot, count, last_ref, token_rows_ref, l_sems, "send")
        yield
        swap(spot, count, last_ref, token_rows_ref, l_sems, "wait")
        yield

    def backing(first, last):
        perm = perm_ref[...]
        for step in range(first, last):
            if step < groups:
                start_all(stage.fetch(step, (d_all_ref,)))
                start_all(stage.fetch(step, (x_all_ref,), (1,)))
                wait_all(stage.fetch(step, (d_all_ref,)))
                d_branch = in_refs[0][step % 2].reshape(size, width)
                attended = att_ref[:, step * FEW : (step + 1) * FEW, :].reshape(size, head)
                wo_grad_ref[...] += over(attended, d_branch, 0, 0)
                yield
                d_attended = low(over(perm, low(over(d_branch, wo_ref[...], 1, 1))))
                yield
                for tile in range(size // length):
                    base = step * size + tile * length
                    query, key, value, same = tile_inputs(qkv_ref, col_ref, row_ref, base, length, head)
                    probs = tile_probs(query, key, bias_ref[...], same)
                    d_out = d_attended[tile * length : (tile + 1) * length, :]
                    d_probs = over(d_out, value, 1, 1)
                    inner = jnp.sum(probs * d_probs, axis=-1, keepdims=True)
                    d_scores = low(probs * (d_probs - inner))
                    bias_grad_ref[...] += d_scores.astype(jnp.float32)
                    dq_ref[base + length : base + 2 * length, :] = low(over(d_scores, key))
                    both = jnp.concatenate((over(d_scores, query, 0, 0), over(low(probs), d_out, 0, 0)), axis=1)
                    dkv_ref[base : base + 3 * length, :] += both
                    if tile % 2:
                        yield
            if step > 0:
                at = slice(length + (step - 1) * size, length + step * size)
                rows = low(over(perm, jnp.concatenate((dq_ref[at, :], low(dkv_ref[at, :])), axis=1), 0, 0))
                wait_all(stage.fetch(step - 1, (x_all_ref,), (1,)))
                w_grad_ref[...] += over(rows, in_refs[1][(step - 1) % 2].reshape(size, width), 0, 0)
                yield
                if step > max(first, 1):
                    wait_all(stage.store(step - 2, (part_ref,)))
                for i in range(2):
                    there = pl.ds(i * count // 2, count // 2)
                    block = over(rows[i * size // 2 : (i + 1) * size // 2], w_ref[:, : 3 * head], 1, 1)
                    out_refs[0][there] = low(block).reshape(count // 2, FEW, width)
                start_all(stage.store(step - 1, (part_ref,)))
                yield
        if last > max(first, 1):
            wait_all(stage.store(last - 2, (part_ref,)))
        yield

    for ref in (wo_grad_ref, bias_grad_ref, dkv_ref, w_grad_ref):
        ref[...] = jnp.zeros_like(ref)
    halves = len(ranges)
    everything = pl.ds(0, cuts[-1])
    tasks = {
        "d": ([], stage.gathering("d", 0, d_ref, d_all_ref, everything, g_sems)),
        "down": ([], stage.scattering("down", (forth_ref,), (down_ref,), everything, other_bufs, down_sems, 0)),
        "output": (["down"], output()),
        "owners": ([f"back{halves - 1}"], owners()),
    }
    for i, rows in enumerate(ranges):
        h = str(i)
        first_step = cuts[i] // FEW + 1 if i else 0
        tasks |= {
            "back" + h: ([f"back{i - 1}"] if i else ["d"], backing(first_step, cuts[i + 1] // FEW + 1)),
            "one" + h: (["back" + h], stage.scattering("one" + h, (part_ref,), (dn_ref,), rows, bufs, one_sems, i)),
        }
    tasks["finals"] = ([f"one{i}" for i in range(halves)], finals())
    weave(tasks, REAR_ORDER)
    stage.finish()


def rear(d_rows, normed_all, attended, qkv, qkv_w, wo, perm, bias, col, row, near_grad, forth, middle, rows_low, d_mid, gain,
         spread, turn, buckets):
    count, rows, width = normed_all.shape
    cuts = halves_of(rows)
    halves = len(cuts) - 1
    head = wo.shape[0]
    columns = 4 * head
    size, piece = perm.shape[0], width // spread.shape[0]
    all_rows, group = (count, rows, width), (count, FEW, width)
    bf, wide, dma = jnp.bfloat16, jnp.float32, pltpu.SemaphoreType.DMA
    vmem, hbm = pl.BlockSpec(memory_space=pltpu.VMEM), pl.BlockSpec(memory_space=pl.ANY)
    shape = jax.ShapeDtypeStruct
    outs = pl.pallas_call(
        functools.partial(rear_kernel, cuts),
        out_shape=[
            shape((head, width), wide), shape((width, columns), bf), shape((size, piece), bf), shape((size, 128), bf),
            shape((size, piece), bf),
        ] + [shape(all_rows, bf)] * 2,
        in_specs=[vmem, hbm] + [vmem] * 9 + [hbm] + [vmem] * 7,
        out_specs=[vmem, hbm, hbm, vmem, hbm] + [hbm] * 2,
        scratch_shapes=[
            pltpu.VMEM((rows, width), wide), pltpu.VMEM((rows, width), wide), pltpu.VMEM(bias.shape, wide),
            pltpu.VMEM((qkv.shape[0], head), bf), pltpu.VMEM((qkv.shape[0], 2 * head), wide),
            pltpu.VMEM((3 * head, width), wide), pltpu.VMEM((width, columns), bf),
            pltpu.VMEM((size, piece), bf), pltpu.VMEM((size, piece + 128), bf), pltpu.VMEM((size, piece + 128), bf),
            pltpu.VMEM((size, piece), bf),
        ] + scatter_bufs(rows, width, 1) * 2 + [
            pltpu.VMEM((2,) + group, bf), pltpu.VMEM((2,) + group, bf), pltpu.VMEM(group, bf),
            dma((2, 2)), dma((1,)),
        ] + [dma((count,)), dma((count,)), dma] * 4 + [
            dma((1,)), dma((1, N_GATHER_SENDS)), dma((1, 2, 32)),
        ] + scatter_sems(halves, 1) + scatter_sems(1, 1),
        name="rear",
        compiler_params=pltpu.CompilerParams(collective_id=4, has_side_effects=True, vmem_limit_bytes=63 * 2**20),
    )(d_rows, normed_all, attended, qkv, qkv_w, wo, perm, bias, col, row, near_grad, forth, middle, rows_low, d_mid, gain,
      spread, turn, buckets)
    return outs[:5]


def exchange(blocks):
    return lax.all_to_all(blocks, AXIS, split_axis=0, concat_axis=0, tiled=True)


def dot(left, right):
    return jnp.dot(left, right, preferred_element_type=jnp.float32)


def select(mask, rows):
    return dot(mask.astype(jnp.bfloat16), rows).astype(jnp.bfloat16)


def beside(sent, chain, kernel):
    sent, chain = lax.optimization_barrier((sent, chain))
    return lax.optimization_barrier((exchange(sent), kernel(chain)))


def unpack_kernel(first_ref, second_ref, query_ref, key_ref, value_ref, gate_ref, up_ref):
    count = first_ref.shape[0]
    head = query_ref.shape[1] // count
    units = gate_ref.shape[1] // count
    wide = jnp.float32
    for j in range(count):
        for i, ref in enumerate((query_ref, key_ref, value_ref)):
            ref[:, j * head : (j + 1) * head] = first_ref[j, :, i * head : (i + 1) * head].astype(wide)
        gate_ref[:, j * units : j * units + head] = first_ref[j, :, 3 * head :].astype(wide)
        gate_ref[:, j * units + head : (j + 1) * units] = second_ref[j, :, : units - head].astype(wide)
        up_ref[:, j * units : (j + 1) * units] = second_ref[j, :, units - head :].astype(wide)


def unpack(first, second, width, hidden):
    rows = first.shape[1]
    widths = (width, width, width, hidden, hidden)
    return pl.pallas_call(
        unpack_kernel,
        out_shape=[jax.ShapeDtypeStruct((rows, columns), jnp.float32) for columns in widths],
        in_specs=[pl.BlockSpec(memory_space=pltpu.VMEM)] * 2,
        out_specs=[pl.BlockSpec(memory_space=pltpu.VMEM)] * 5,
        name="unpack_columns",
        compiler_params=pltpu.CompilerParams(vmem_limit_bytes=32 * 2**20),
    )(first, second)


def body(
    tokens,
    lengths,
    permutation,
    query_weight,
    key_weight,
    value_weight,
    out_weight,
    gate_weight,
    up_weight,
    down_weight,
    gain_attention,
    gain_feedforward,
    bias_table,
    cotangent,
):
    me = lax.axis_index(AXIS)
    count = tokens.shape[0]
    grain = tokens.shape[1]
    length = cotangent.shape[1]
    width = tokens.shape[2]
    shard = query_weight.shape[0]
    hidden_width = gate_weight.shape[1] // count
    head = HEAD_DIM
    total = 3 * count * length // 5
    tiles = -(-total // length)
    slots = tiles * grain

    dealt_lengths = lengths[permutation]
    ends = jnp.cumsum(dealt_lengths)
    starts = ends - dealt_lengths
    my_start, my_length = starts[me], dealt_lengths[me]
    place_in = jnp.arange(length, dtype=jnp.int32)
    slot_ids = jnp.arange(slots, dtype=jnp.int32)
    packed_ids = slot_ids // grain * length + me * grain + slot_ids % grain
    source_seq = jnp.sum((packed_ids[:, None] >= ends[None, :]).astype(jnp.int32), axis=1)

    few = 16
    folds = few // grain
    piece = width // folds
    share = jnp.arange(few * count, dtype=jnp.int32)
    share_row, share_fold = share // few * grain + share % grain, share % few // grain
    position = share_row - my_start % length
    position = jnp.where(position < 0, position + length, position)
    in_share = jnp.arange(few, dtype=jnp.int32)[None, :] % grain
    index = jnp.stack(
        (
            (permutation[:, None] * grain + in_share).reshape(-1),
            jnp.where(position < my_length, position, -1),
            jnp.pad(jnp.where(source_seq < count, source_seq * few + slot_ids % grain, -few), (0, few * count - slots)),
        )
    )
    small = jnp.concatenate((gain_attention, gain_feedforward, bias_table))
    small = jnp.pad(small, (0, few * 128 - small.shape[0])).reshape(few, 128)
    all_ids = jnp.arange(tiles * length, dtype=jnp.int32)
    segment = jnp.sum((all_ids[:, None] >= ends[None, :]).astype(jnp.int32), axis=1) + 1
    column, row = segment[:, None], jnp.pad(segment, (length, length))[None, :]
    relative = (
        jnp.arange(3 * length, dtype=jnp.int32)[None, :] - length - place_in[:, None]
    ).reshape(-1)
    onehot = bucket_index(relative)[None, :] == jnp.arange(BUCKETS, dtype=jnp.int32)[:, None]
    ids = jnp.arange(few * count, dtype=jnp.int32)
    ids = ids % length // grain * few + ids // length * grain + ids % grain
    perm = (ids[:, None] == jnp.arange(few * count, dtype=jnp.int32)[None, :]).astype(jnp.bfloat16)

    buckets = bucket_index(relative).reshape(length, -1)
    (rows_low, gain_one, rel_bias, first_columns, qkv, attended, middle, d_middle, d_low, gain_two_grad, near_grad, far_grad,
     down_grad, normed_all, forth) = front(
        tokens.reshape(length, width), cotangent[0], index, small,
        (query_weight, key_weight, value_weight, gate_weight, up_weight), down_weight, out_weight, perm, buckets, column, row,
        slots,
    )
    shared = (out_weight, perm, rel_bias, column, row)

    turned = me * grain + in_share - starts[:, None] % length
    turned = starts[:, None] + jnp.where(turned < 0, turned + length, turned)
    back_slot = (turned // length * grain + in_share).reshape(-1)
    spread = (back_slot[:, None] == slot_ids[None, :])[None] & (
        share_fold[None, :, None] == jnp.arange(folds, dtype=jnp.int32)[:, None, None]
    )
    back_turn = (
        (position[None, :] == share_row[:, None])
        & (share_row[:, None] < my_length)
        & (share_fold[:, None] == share_fold[None, :])
    )

    high = lax.reduce_precision(gain_two_grad, 8, 7)
    sums = jnp.stack((high, gain_two_grad - high)).astype(jnp.bfloat16).reshape(2, count, shard)
    sums = jnp.pad(sums.transpose(1, 0, 2).reshape(count, 1, -1), ((0, 0), (0, few - 1), (0, 4 * head - 2 * shard)))
    sent = jnp.concatenate((far_grad.astype(jnp.bfloat16).T.reshape(count, shard, -1), sums), axis=1)
    given = (
        d_low, normed_all, attended, qkv, first_columns, *shared, near_grad, forth, middle, rows_low, d_middle, gain_one,
        spread.astype(jnp.bfloat16), back_turn.astype(jnp.bfloat16), buckets,
    )
    came, (out_grad, first_grad, out_rows, other_sums, token_rows) = beside(sent, given, lambda given: rear(*given))
    second_grad, sums = came[:, :shard], came[:, shard].astype(jnp.float32)
    first_grad = first_grad.reshape(count, shard, -1)
    other_sums = other_sums.reshape(count, few, -1).astype(jnp.float32)
    gain_attention_grad = jnp.sum(other_sums[:, 0, :shard] + other_sums[:, 0, shard : 2 * shard], axis=0)
    gain_feedforward_grad = jnp.sum(sums[:, :shard] + sums[:, shard : 2 * shard], axis=0)
    table_grad = other_sums[:, 1, 0] + other_sums[:, 1, 1]

    def whole_rows(shares):
        return shares.reshape(count, folds, grain, piece).transpose(0, 2, 1, 3).reshape(count, grain, width)

    place = place_in - my_start % length
    place = jnp.where(place < 0, place + length, place)
    turned_back = (place[None, :] == place_in[:, None]) & (place_in[:, None] < my_length)
    layer_output = select(turned_back, whole_rows(out_rows).reshape(length, width))[None]
    tokens_grad = whole_rows(token_rows)[jnp.argsort(permutation)]
    query_grad, key_grad, value_grad, gate_grad, up_grad = unpack(
        first_grad, second_grad, width, hidden_width * count
    )
    return (
        layer_output,
        tokens_grad,
        query_grad,
        key_grad,
        value_grad,
        out_grad,
        gate_grad,
        up_grad,
        down_grad,
        gain_attention_grad,
        gain_feedforward_grad,
        table_grad,
    )


def solution(mesh):
    placed = (
        P(None, "fsdp", None),
        P(),
        P(),
        P("fsdp", None),
        P("fsdp", None),
        P("fsdp", None),
        P("fsdp", None),
        P("fsdp", None),
        P("fsdp", None),
        P("fsdp", None),
        P("fsdp"),
        P("fsdp"),
        P("fsdp"),
        P("fsdp", None, None),
    )
    return jax.shard_map(
        body if mesh.shape[AXIS] == 32 else body_any,
        mesh=mesh,
        in_specs=placed,
        out_specs=(
            P("fsdp", None, None),
            P(None, "fsdp", None),
            P("fsdp", None),
            P("fsdp", None),
            P("fsdp", None),
            P("fsdp", None),
            P("fsdp", None),
            P("fsdp", None),
            P("fsdp", None),
            P("fsdp"),
            P("fsdp"),
            P("fsdp"),
        ),
        check_vma=False,
    )
```

```python
import functools

import jax
import jax.numpy as jnp
from jax import lax
from jax.experimental import pallas as pl
from jax.experimental.pallas import tpu as pltpu
from jax.sharding import PartitionSpec as P

HEADS = 32
HEAD_DIM = 64
BUCKETS = 32


EPSILON = 1e-06
masked_score = -1000000000.0
HIGHEST = lax.Precision.HIGHEST


def bucket_index(relative):
    half_buckets = BUCKETS // 2
    exact_count = half_buckets // 2
    distance = jnp.abs(relative)
    side_offset = jnp.where(relative > 0, half_buckets, 0).astype(jnp.int32)
    square = distance * distance
    far_bucket = jnp.full_like(distance, exact_count)
    for doubling in range(1, half_buckets - exact_count):
        far_bucket = far_bucket + (square >= exact_count * exact_count * 2**doubling).astype(
            jnp.int32
        )
    return side_offset + jnp.where(distance < exact_count, distance, far_bucket)


def bucket_onehot(seq_len):
    positions = jnp.arange(seq_len, dtype=jnp.int32)
    relative = (positions[None, :] - positions[:, None]).reshape(-1)
    bucket_ids = jnp.arange(BUCKETS, dtype=jnp.int32)
    return (bucket_index(relative)[None, :] == bucket_ids[:, None]).astype(jnp.float32)


def norm_scale(values):
    return lax.rsqrt(jnp.mean(values * values, axis=-1, keepdims=True) + EPSILON)


def norm_back(values, scale, gain_vec, d_norm):
    weighted = gain_vec * d_norm
    return scale * weighted - values * (scale * scale * scale) * jnp.mean(
        weighted * values, axis=-1, keepdims=True
    )


def rows_product(left, right):
    return lax.dot_general(
        left, right, (((0,), (0,)), ((), ())), preferred_element_type=jnp.float32
    )


def against_rows(left, right):
    return lax.dot_general(
        left, right, (((1,), (1,)), ((), ())), preferred_element_type=jnp.float32
    )


def masked_scores(query_heads, key_heads, rel_bias, length):
    scores = (
        jnp.einsum("qhd,khd->hqk", query_heads, key_heads, preferred_element_type=jnp.float32)
        + rel_bias
    )
    key_valid = jnp.arange(key_heads.shape[0], dtype=jnp.int32) < length
    return jnp.where(key_valid[None, None, :], scores, masked_score)


def unpack_weights(full_weights, onehot, seq_len):
    table_full = full_weights[4].astype(jnp.float32).reshape(BUCKETS, HEADS)
    rel_bias = jnp.dot(table_full.T, onehot, precision=HIGHEST).reshape(HEADS, seq_len, seq_len)
    return (
        full_weights[0],
        full_weights[1],
        full_weights[2].astype(jnp.float32),
        full_weights[3].astype(jnp.float32),
        rel_bias,
    )


def body_any(
    tokens,
    lengths,
    permutation,
    query_weight,
    key_weight,
    value_weight,
    out_weight,
    gate_weight,
    up_weight,
    down_weight,
    gain_attention,
    gain_feedforward,
    bias_table,
    cotangent,
):
    model_width = query_weight.shape[1]
    hidden_width = gate_weight.shape[1]
    packed = jnp.concatenate(
        (query_weight, key_weight, value_weight, out_weight, gate_weight, up_weight), axis=1
    )
    shards = (packed, down_weight, gain_attention, gain_feedforward, bias_table)
    full_weights = (
        lax.all_gather(shards[0], "fsdp", axis=0, tiled=True),
        lax.all_gather(shards[1], "fsdp", axis=0, tiled=True),
        lax.all_gather(shards[2], "fsdp", axis=0, tiled=True),
        lax.all_gather(shards[3], "fsdp", axis=0, tiled=True),
        lax.all_gather(shards[4], "fsdp", axis=0, tiled=True),
    )
    reordered = tokens[permutation]
    dealt = lax.all_to_all(reordered, "fsdp", split_axis=0, concat_axis=1, tiled=True)
    seq_count = dealt.shape[0]
    seq_len = dealt.shape[1]
    local_ids = lax.dynamic_slice_in_dim(permutation, lax.axis_index("fsdp") * seq_count, seq_count)
    seq_lengths = lengths[local_ids]
    positions = jnp.arange(seq_len, dtype=jnp.int32)
    row_valid = (positions[None, :] < seq_lengths[:, None]).astype(jnp.float32).reshape(-1, 1)
    onehot = bucket_onehot(seq_len)
    onehot_low = onehot.astype(jnp.bfloat16)
    full_packed, full_down, gain_one, gain_two, rel_bias = unpack_weights(
        full_weights, onehot, seq_len
    )
    head_shape = (seq_count, seq_len, HEADS, HEAD_DIM)
    rows_in = dealt.reshape(-1, model_width).astype(jnp.float32)
    scale_one = norm_scale(rows_in)
    normed = (rows_in * scale_one * gain_one).astype(jnp.bfloat16)
    projected = jnp.dot(
        normed, full_packed[:, : 3 * model_width], preferred_element_type=jnp.float32
    ).astype(jnp.bfloat16)
    query_heads = projected[:, :model_width].reshape(head_shape)
    key_heads = projected[:, model_width : 2 * model_width].reshape(head_shape)
    value_heads = projected[:, 2 * model_width :].reshape(head_shape)

    def attend_forward(pieces):
        query_one, key_one, value_one, length = pieces
        scores = masked_scores(query_one, key_one, rel_bias, length)
        row_max = jnp.max(scores, axis=-1, keepdims=True)
        exp_total = jnp.sum(jnp.exp(scores - row_max), axis=-1, keepdims=True)
        log_total = row_max + jnp.log(exp_total)
        weights_soft = jnp.exp(scores - log_total).astype(jnp.bfloat16)
        attended_one = jnp.einsum(
            "hqk,khd->qhd", weights_soft, value_one, preferred_element_type=jnp.float32
        )
        return (attended_one.astype(jnp.bfloat16), log_total)

    attended_heads, log_totals = lax.map(
        attend_forward, (query_heads, key_heads, value_heads, seq_lengths)
    )
    attended_rows = attended_heads.reshape(-1, model_width)
    middle = rows_in + jnp.dot(
        attended_rows,
        full_packed[:, 3 * model_width : 4 * model_width],
        preferred_element_type=jnp.float32,
    )
    scale_two = norm_scale(middle)
    normed_two = (middle * scale_two * gain_two).astype(jnp.bfloat16)
    gate_up = jnp.dot(
        normed_two, full_packed[:, 4 * model_width :], preferred_element_type=jnp.float32
    )

    def gelu_product(gate_part, up_part):
        return jax.nn.gelu(gate_part, approximate=True) * up_part

    hidden_full, gelu_pull = jax.vjp(
        gelu_product, gate_up[:, :hidden_width], gate_up[:, hidden_width:]
    )
    hidden = hidden_full.astype(jnp.bfloat16)
    result = middle + jnp.dot(hidden, full_down, preferred_element_type=jnp.float32)
    layer_output = (
        (result * row_valid).astype(jnp.bfloat16).reshape(seq_count, seq_len, model_width)
    )
    full_weights = (
        lax.all_gather(shards[0], "fsdp", axis=0, tiled=True),
        lax.all_gather(shards[1], "fsdp", axis=0, tiled=True),
        lax.all_gather(shards[2], "fsdp", axis=0, tiled=True),
        lax.all_gather(shards[3], "fsdp", axis=0, tiled=True),
        lax.all_gather(shards[4], "fsdp", axis=0, tiled=True),
    )
    full_packed, full_down, gain_one, gain_two, rel_bias = unpack_weights(
        full_weights, onehot, seq_len
    )
    upstream = cotangent.reshape(-1, model_width).astype(jnp.float32) * row_valid
    upstream_low = upstream.astype(jnp.bfloat16)
    d_hidden = against_rows(upstream_low, full_down)
    d_gate, d_up = gelu_pull(d_hidden)
    d_gate_up = jnp.concatenate((d_gate, d_up), axis=1).astype(jnp.bfloat16)
    d_normed_two = against_rows(d_gate_up, full_packed[:, 4 * model_width :])
    gain_two_grad = jnp.sum(d_normed_two * middle * scale_two, axis=0)
    d_middle = upstream + norm_back(middle, scale_two, gain_two, d_normed_two)
    d_branch = d_middle.astype(jnp.bfloat16)
    d_attended = against_rows(d_branch, full_packed[:, 3 * model_width : 4 * model_width]).astype(
        jnp.bfloat16
    )

    def attend_backward(pieces):
        query_one, key_one, value_one, length, log_total, d_attended_one = pieces
        scores = masked_scores(query_one, key_one, rel_bias, length)
        probs = jnp.exp(scores - log_total)
        probs_low = probs.astype(jnp.bfloat16)
        d_value = jnp.einsum(
            "hqk,qhd->khd", probs_low, d_attended_one, preferred_element_type=jnp.float32
        )
        d_probs = jnp.einsum(
            "qhd,khd->hqk", d_attended_one, value_one, preferred_element_type=jnp.float32
        )
        inner = jnp.sum(probs * d_probs, axis=-1, keepdims=True)
        d_scores = (probs * (d_probs - inner)).astype(jnp.bfloat16)
        d_query = jnp.einsum("hqk,khd->qhd", d_scores, key_one, preferred_element_type=jnp.float32)
        d_key = jnp.einsum("hqk,qhd->khd", d_scores, query_one, preferred_element_type=jnp.float32)
        d_bias = against_rows(d_scores.reshape(HEADS, -1), onehot_low)
        return (
            (
                d_query.astype(jnp.bfloat16),
                d_key.astype(jnp.bfloat16),
                d_value.astype(jnp.bfloat16),
            ),
            d_bias,
        )

    (d_query_all, d_key_all, d_value_all), d_bias_all = lax.map(
        attend_backward,
        (
            query_heads,
            key_heads,
            value_heads,
            seq_lengths,
            log_totals,
            d_attended.reshape(head_shape),
        ),
    )
    d_qkv = jnp.concatenate(
        (
            d_query_all.reshape(-1, model_width),
            d_key_all.reshape(-1, model_width),
            d_value_all.reshape(-1, model_width),
        ),
        axis=1,
    )
    d_normed = against_rows(d_qkv, full_packed[:, : 3 * model_width])
    gain_one_grad = jnp.sum(d_normed * rows_in * scale_one, axis=0)
    d_rows = d_middle + norm_back(rows_in, scale_one, gain_one, d_normed)
    d_dealt = d_rows.astype(jnp.bfloat16).reshape(seq_count, seq_len, model_width)
    returned_rows = lax.all_to_all(d_dealt, "fsdp", split_axis=1, concat_axis=0, tiled=True)
    tokens_grad = returned_rows[jnp.argsort(permutation)]
    packed_grad = lax.psum_scatter(
        jnp.concatenate(
            (
                rows_product(normed, d_qkv),
                jnp.concatenate(
                    (rows_product(attended_rows, d_branch), rows_product(normed_two, d_gate_up)),
                    axis=1,
                ),
            ),
            axis=1,
        ),
        "fsdp",
        scatter_dimension=0,
        tiled=True,
    )
    mixer_grad = packed_grad[:, : 3 * model_width]
    branch_grad = packed_grad[:, 3 * model_width :]
    down_grad = lax.psum_scatter(
        rows_product(hidden, upstream_low), "fsdp", scatter_dimension=0, tiled=True
    )
    table_sum = jnp.sum(d_bias_all, axis=0).T.reshape(-1)
    gain_attention_grad, gain_feedforward_grad, table_grad = (
        lax.psum_scatter(gain_one_grad, "fsdp", scatter_dimension=0, tiled=True),
        lax.psum_scatter(gain_two_grad, "fsdp", scatter_dimension=0, tiled=True),
        lax.psum_scatter(table_sum, "fsdp", scatter_dimension=0, tiled=True),
    )
    return (
        layer_output,
        tokens_grad,
        mixer_grad[:, :model_width],
        mixer_grad[:, model_width : 2 * model_width],
        mixer_grad[:, 2 * model_width :],
        branch_grad[:, :model_width],
        branch_grad[:, model_width : model_width + hidden_width],
        branch_grad[:, model_width + hidden_width :],
        down_grad,
        gain_attention_grad,
        gain_feedforward_grad,
        table_grad,
    )


MESH = pl.DeviceIdType.MESH
AXIS = "fsdp"


def over(left, right, left_dim=1, right_dim=0):
    return lax.dot_general(
        left, right, (((left_dim,), (right_dim,)), ((), ())), preferred_element_type=jnp.float32
    )


def low(values):
    return values.astype(jnp.bfloat16)


def tile_probs(query, key, bias, same):
    scores = jnp.where(same, over(query, key, 1, 1) + bias, masked_score)
    grown = jnp.exp(scores - jnp.max(scores, axis=-1, keepdims=True))
    return grown / jnp.sum(grown, axis=-1, keepdims=True)


class Spot:
    def __init__(self):
        me = lax.axis_index(AXIS)
        c, x, y, z = me % 2, (me // 2) % 2, (me // 4) % 2, me // 8
        self.me = me
        self.mid = (z == 1) | (z == 2)
        self.end = jnp.logical_not(self.mid)
        self.zs = (z, z + 1 - 2 * (z % 2), 2 - z // 2, 3 - 3 * (z // 2))
        self.shift = [8 * (zz - z) for zz in self.zs]
        self.core, self.x, self.y = me + 1 - 2 * c, me + 2 - 4 * x, me + 4 - 8 * y
        self.diag = self.x + self.y - me
        self.n1, self.n2 = me + self.shift[1], me + self.shift[2]

    def greet(self):
        bar = pltpu.get_barrier_semaphore()
        for peer in (self.core, self.x, self.y, self.n1):
            pl.semaphore_signal(bar, inc=1, device_id=(peer,), device_id_type=MESH)

        @pl.when(self.mid)
        def _():
            pl.semaphore_signal(bar, inc=1, device_id=(self.n2,), device_id_type=MESH)

        pl.semaphore_wait(bar, 4 + self.mid.astype(jnp.int32))

    def greet_all(self, count):
        bar = pltpu.get_barrier_semaphore()

        def signal(d, _):
            peer = (self.me + d) % count
            pl.semaphore_signal(bar, inc=1, device_id=(peer,), device_id_type=MESH)
            return _

        lax.fori_loop(1, count, signal, 0)
        pl.semaphore_wait(bar, count - 1)


class Sends:
    def __init__(self, sems):
        self.sems, self.used, self.open = sems, 0, []

    def push(self, src, dst, rsem, peer, when=None):
        ssem = self.sems.at[self.used]
        self.used += 1

        def copy():
            return pltpu.make_async_remote_copy(
                src, dst, ssem, rsem, device_id=(peer,), device_id_type=MESH
            )

        if when is None:
            copy().start()
        else:
            pl.when(when)(lambda: copy().start())
        self.open.append((lambda: copy().wait_send(), when))

    def finish(self):
        for wait, when in self.open:
            if when is None:
                wait()
            else:
                pl.when(when)(wait)
        self.open = []


def arrive(dst, rsem, spot):
    pltpu.make_async_remote_copy(
        dst, dst, rsem, rsem, device_id=(spot.core,), device_id_type=MESH
    ).wait_recv()


def gather_steps(spot, src, dst, rows, sends, rsem, own_sem, between=False):
    half = src.shape[1] // 2
    cols = (pl.ds(0, half), pl.ds(half, half))
    me, mid, shift = spot.me, spot.mid, spot.shift
    first, last = (spot.x, spot.y), (spot.y, spot.x)
    own = pltpu.make_async_copy(src.at[rows, :], dst.at[me, rows, :], own_sem)
    own.start()

    def push(part, block, peer, mine=False, when=None):
        there = dst.at[block, rows, cols[part]]
        here = src.at[rows, cols[part]] if mine else there
        sends.push(here, there, rsem.at[part, block], peer, when)

    def landed(part, block):
        arrive(dst.at[block, rows, cols[part]], rsem.at[part, block], spot)

    for part in (0, 1):
        push(part, me, spot.n1, True)
        push(part, me, spot.n2, True, mid)
        push(part, me, first[part], True)
        push(part, me, last[part], True)
    for part in (0, 1):
        push(part, me, spot.core, True)
    yield

    def from_z(part, j):
        b = me + shift[j]
        landed(part, b)
        push(part, b, spot.n2 if j == 1 else spot.n1, when=mid)
        push(part, b, first[part])
        push(part, b, last[part])
        push(part, b, spot.core)

    def from_first(part, j):
        b = first[part] + shift[j]
        landed(part, b)
        push(part, b, last[part])
        push(part, b, spot.core)

    def from_last(part, b):
        landed(part, b)
        push(part, b, spot.core)

    def from_side(part):
        b = first[part]
        landed(part, b)
        push(part, b, spot.n1)
        push(part, b, spot.n2, when=mid)
        push(part, b, last[part])
        push(part, b, spot.core)

    def along_z(part, base, j):
        b = base + shift[j]
        landed(part, b)
        push(part, b, spot.n2 if j == 1 else spot.n1, when=mid)
        push(part, b, last[part])
        push(part, b, spot.core)

    if between:
        for part in (0, 1):
            from_side(part)
            yield
        for j in range(1, 5):
            if j < 4:
                for part in (0, 1):
                    along_z(part, me, j)
                    yield
                for part in (0, 1):
                    along_z(part, first[part], j)
                    yield
            for part in (0, 1):
                from_last(part, last[part] + shift[j - 1])
                from_last(part, spot.diag + shift[j - 1])
                yield
    else:
        for j in range(4):
            if j:
                for part in (0, 1):
                    from_z(part, j)
                    yield
            for part in (0, 1):
                from_first(part, j)
                yield
            if j:
                for part in (0, 1):
                    from_last(part, last[part] + shift[j - 1])
                    yield
        for part in (0, 1):
            from_last(part, last[part] + shift[3])
            yield
        for j in range(4):
            for part in (0, 1):
                from_last(part, spot.diag + shift[j])
                yield
    for j in range(4):
        for base in (me, spot.x, spot.y, spot.diag):
            for part in (0, 1):
                landed(part, base + spot.core - me + shift[j])
    own.wait()
    yield


def scatter_steps(spot, p_refs, o_refs, rows, bufs, sems, sends):
    ring_ref, s_ref, first_ref, second_ref, za_ref, zb_ref = bufs
    lsem, csem, fsem, gsem, zasem, zbsem = sems
    given = len(p_refs)
    width = p_refs[0].shape[2]
    half = given * width // 2
    me, mid, end, zs = spot.me, spot.mid, spot.end, spot.zs
    cols, short = (pl.ds(0, half), pl.ds(half, half)), pl.ds(0, half)
    plane = (me, spot.x, spot.y, spot.diag)
    first_peer, second_peer = (spot.y, spot.x), (spot.x, spot.y)
    start, size = rows.start, rows.size

    def mine(q, j, part):
        return s_ref.at[q * 4 + zs[j], rows, cols[part]]

    def held(ref, part, slot):
        return ref.at[part, slot, rows, short]

    def chunks(count, step):
        lax.fori_loop(0, size // 16, lambda i, _: step(pl.ds(pl.multiple_of(start + i * 16, 16), 16)) or _, 0)

    def add(q, j, part, *more):
        def step(r):
            v = s_ref[q * 4 + zs[j], r, cols[part]].astype(jnp.float32)
            for ref, slot in more:
                v = v + ref[part, slot, r, short].astype(jnp.float32)
            s_ref[q * 4 + zs[j], r, cols[part]] = v.astype(s_ref.dtype)

        chunks(size, step)

    def pair_exchange(j):
        for q in (3, 2, 1, 0):
            b = plane[q] + spot.shift[j]
            slot = q * 4 + zs[j]
            for i, p_ref in enumerate(p_refs):
                own = pl.ds(i * width, width)
                sends.push(p_ref.at[b + spot.core - me, rows, :], s_ref.at[slot, rows, own], csem.at[i, slot], spot.core)
                here = ring_ref.at[j % 2 * 4 + q, rows, own]
                pltpu.make_async_copy(p_ref.at[b, rows, :], here, lsem.at[i, j % 2 * 4 + q]).start()

    def joined(q, j):
        slot, near = q * 4 + zs[j], j % 2 * 4 + q
        for i, p_ref in enumerate(p_refs):
            own = pl.ds(i * width, width)
            pltpu.make_async_copy(p_ref.at[0, rows, :], ring_ref.at[near, rows, own], lsem.at[i, near]).wait()
            arrive(s_ref.at[slot, rows, own], csem.at[i, slot], spot)
        everything = pl.ds(0, given * width)

        def step(r):
            v = ring_ref[near, r, everything].astype(jnp.float32) + s_ref[slot, r, everything].astype(jnp.float32)
            s_ref[slot, r, everything] = v.astype(s_ref.dtype)

        chunks(size, step)

    def to_first(part, q, j):
        slot = (4 if q == 3 else 0) + zs[j]
        sends.push(mine(q, j, part), held(first_ref, part, slot), fsem.at[part, slot], first_peer[part])

    def first_stage(j):
        joined(3, j)
        if j:
            pair_exchange(j - 1)
        to_first(0, 3, j)
        to_first(1, 3, j)
        yield
        joined(2, j)
        to_first(0, 2, j)
        yield
        joined(1, j)
        to_first(1, 1, j)
        joined(0, j)
        yield

    def second_stage(j):
        for part in (0, 1):
            q, slot = (1, 2)[part], 4 + zs[j]
            arrive(held(first_ref, part, slot), fsem.at[part, slot], spot)
            add(q, j, part, (first_ref, slot))
            sends.push(mine(q, j, part), held(second_ref, part, zs[j]), gsem.at[part, zs[j]], second_peer[part])
            yield

    def z_send(j):
        for part in (0, 1):
            arrive(held(first_ref, part, zs[j]), fsem.at[part, zs[j]], spot)
            arrive(held(second_ref, part, zs[j]), gsem.at[part, zs[j]], spot)
            add(0, j, part, (first_ref, zs[j]), (second_ref, zs[j]))
            if j:
                sends.push(mine(0, j, part), held(za_ref, part, 3 - j), zasem.at[part, 3 - j], spot.n1, end)
            yield

    def z_relay(j):
        if not j:
            return
        for part in (0, 1):
            came, sem, slot = (za_ref, zasem, 3 - j) if j > 1 else (zb_ref, zbsem, 0)

            @pl.when(mid)
            def _():
                arrive(held(came, part, slot), sem.at[part, slot], spot)
                add(0, j, part, (came, slot))

            slot = 3 - j if j > 1 else 0
            peer = spot.n2 if j > 1 else spot.n1
            sends.push(mine(0, j, part), held(zb_ref, part, slot), zbsem.at[part, slot], peer, mid)
            yield

    pair_exchange(3)
    yield
    stages = (first_stage, second_stage, z_send, z_relay)
    for step in range(4 + len(stages) - 1):
        for stage, what in enumerate(stages):
            j = 3 - (step - stage)
            if 0 <= j <= 3:
                yield from what(j)
    for part in (0, 1):
        o_ref, there = (o_refs[part], pl.ds(0, half)) if given == 2 else (o_refs[0], cols[part])

        def total(*more):
            def step(r):
                v = s_ref[zs[0], r, cols[part]].astype(jnp.float32)
                for ref, slot in more:
                    v = v + ref[part, slot, r, short].astype(jnp.float32)
                o_ref[r, there] = v

            chunks(size, step)

        @pl.when(mid)
        def _():
            arrive(held(za_ref, part, 2), zasem.at[part, 2], spot)
            arrive(held(zb_ref, part, 1), zbsem.at[part, 1], spot)
            total((za_ref, 2), (zb_ref, 1))

        @pl.when(end)
        def _():
            arrive(held(zb_ref, part, 0), zbsem.at[part, 0], spot)
            total((zb_ref, 0))

        yield


def swap(spot, count, src, dst, sems, what, some=None):
    begin, end = some or (1, count)
    send_sem, recv_sem, own_sem = sems
    share = src.shape[0] // count

    def part(ref, index):
        return ref.at[pl.ds(pl.multiple_of(index * share, share), share), :]

    def own():
        return pltpu.make_async_copy(part(src, spot.me), part(dst, spot.me), own_sem)

    def one(d, _):
        peer, source = (spot.me + d) % count, (spot.me + count - d) % count
        if what == "send":
            pltpu.make_async_remote_copy(
                part(src, peer), part(dst, spot.me), send_sem.at[peer], recv_sem.at[spot.me], device_id=(peer,),
                device_id_type=MESH,
            ).start()
        else:
            copy = pltpu.make_async_remote_copy(
                part(src, peer), part(dst, source), send_sem.at[peer], recv_sem.at[source], device_id=(peer,),
                device_id_type=MESH,
            )
            copy.wait_recv()
            copy.wait_send()
        return _

    if what == "send" and begin == 1:
        own().start()
    lax.fori_loop(begin, end, one, 0)
    if what == "wait" and end == count:
        own().wait()


def pack(weights, first_ref, second_ref):
    query_ref, key_ref, value_ref, gate_ref, up_ref = weights
    rows = query_ref.shape[0]
    count = first_ref.shape[0] // rows
    head, units = query_ref.shape[1] // count, gate_ref.shape[1] // count
    for j in range(count):
        there = pl.ds(j * rows, rows)
        for i, ref in enumerate((query_ref, key_ref, value_ref)):
            first_ref[there, i * head : (i + 1) * head] = ref[:, j * head : (j + 1) * head]
        first_ref[there, 3 * head :] = gate_ref[:, j * units : j * units + head]
        second_ref[there, : units - head] = gate_ref[:, j * units + head : (j + 1) * units]
        second_ref[there, units - head :] = up_ref[:, j * units : (j + 1) * units]


def weave(tasks, order):
    names = list(tasks)
    left = {name: steps for name, (_, steps) in tasks.items()}

    def advance(name):
        for other in tasks[name][0]:
            if other in left:
                advance(other)
                assert other not in left, name
        if name in left and next(left[name], left) is left:
            del left[name]

    for number, times in order:
        for _ in range(times):
            advance(names[number])
    while left:
        name = next(n for n in left if not any(other in left for other in tasks[n][0]))
        while name in left:
            advance(name)


FRONT_ORDER = (
    (0, 2), (2, 3), (0, 1), (2, 2), (0, 1), (4, 12), (2, 1), (4, 15), (1, 1), (4, 5), (6, 1), (3, 1), (6, 8),
    (1, 1), (5, 1), (6, 5), (5, 2), (7, 6), (13, 1), (7, 1), (13, 1), (7, 1), (13, 1), (5, 1), (13, 2), (7,
    4), (13, 3), (5, 1), (14, 1), (7, 1), (5, 2), (7, 1), (14, 6), (5, 1), (7, 1), (5, 1), (7, 2), (5, 1),
    (14, 1), (5, 1), (14, 1), (5, 1), (14, 3), (5, 1), (14, 1), (3, 1), (7, 1), (14, 1), (7, 4), (5, 1), (7,
    1), (5, 1), (7, 2), (5, 1), (14, 1), (5, 3), (7, 1), (5, 2), (14, 2), (5, 1), (14, 2), (5, 1), (7, 2),
    (14, 1), (7, 2), (5, 1), (14, 1), (7, 2), (14, 2), (7, 1), (14, 2), (7, 2), (14, 1), (7, 1), (14, 2), (7,
    1), (8, 1), (9, 1), (14, 6), (9, 1), (14, 1), (9, 6), (14, 1), (9, 2), (14, 1), (9, 2), (3, 1), (9, 1),
    (15, 1), (9, 15), (3, 1), (9, 4), (16, 2), (3, 1), (10, 1), (16, 3), (10, 1), (16, 4), (10, 1), (16, 2),
    (10, 1), (16, 5), (10, 1), (16, 1), (10, 1), (16, 11), (10, 1), (16, 2), (11, 1), (16, 1), (11, 1), (16,
    1), (11, 6), (17, 1), (11, 1), (17, 1), (11, 3), (17, 1), (11, 9), (17, 1), (11, 2), (17, 1), (11, 1),
    (18, 1), (11, 3), (18, 1), (11, 1), (18, 9), (11, 9), (12, 1), (18, 26), (19, 1),
)
REAR_ORDER = (
    (0, 4), (1, 1), (0, 28), (4, 1), (5, 1), (1, 1), (5, 1), (1, 1), (5, 1), (1, 1), (5, 2), (1, 1), (5, 1),
    (1, 1), (5, 1), (1, 1), (5, 1), (1, 1), (5, 1), (1, 1), (5, 1), (1, 1), (5, 1), (1, 1), (5, 2), (1, 1),
    (5, 1), (1, 1), (5, 1), (1, 2), (5, 2), (1, 1), (5, 1), (1, 1), (5, 1), (1, 1), (5, 1), (1, 1), (5, 2),
    (1, 3), (5, 1), (6, 1), (7, 1), (6, 1), (1, 3), (6, 1), (1, 2), (6, 1), (1, 1), (6, 1), (7, 1), (1, 1),
    (6, 1), (1, 1), (6, 1), (7, 3), (1, 1), (6, 1), (1, 1), (7, 1), (1, 1), (6, 1), (1, 1), (7, 1), (6, 1),
    (1, 1), (7, 2), (3, 1), (1, 1), (6, 1), (1, 1), (6, 12), (8, 1), (6, 1), (8, 2), (6, 4), (8, 2), (6, 1),
    (3, 1), (8, 4), (6, 2), (8, 2), (6, 1), (8, 1), (2, 1), (8, 1), (6, 1), (8, 3), (6, 1), (8, 2), (6, 1),
    (8, 2), (6, 1), (8, 1), (6, 1), (8, 4), (2, 1), (8, 12), (9, 3),
)
N_GATHER_SENDS = 70
FEW = 16


def gelu_pair(gate):
    slope = 0.7978845608028654
    squared = gate * gate
    bent = jnp.tanh(slope * (gate + 0.044715 * gate * squared))
    gelu = 0.5 * gate * (1.0 + bent)
    return gelu, 0.5 * (1.0 + bent) + 0.5 * gate * (1.0 - bent * bent) * slope * (1.0 + 3.0 * 0.044715 * squared)


def scatter_sems(halves, given):
    dma = pltpu.SemaphoreType.DMA
    return [
        dma((halves, 16 * given + 36)), dma((halves, given, 8)), dma((halves, given, 16)), dma((halves, 2, 8)),
        dma((halves, 2, 4)), dma((halves, 2, 3)), dma((halves, 2, 2)),
    ]


def scatter_bufs(rows, width, given):
    half = given * width // 2
    shapes = ((8, rows, given * width), (16, rows, given * width), (2, 8, rows, half), (2, 4, rows, half))
    return [pltpu.VMEM(shape, jnp.bfloat16) for shape in shapes + ((2, 3, rows, half), (2, 2, rows, half))]


class Stage:
    def __init__(self, count, cuts, in_refs, out_refs, in_sems, out_sems):
        self.spot = Spot()
        self.count = count
        self.ranges = [pl.ds(a, b - a) for a, b in zip(cuts[:-1], cuts[1:])]
        self.cuts = cuts
        self.sends = {}
        self.in_refs, self.out_refs, self.in_sems, self.out_sems = in_refs, out_refs, in_sems, out_sems

    def gathering(self, name, at, src, dst, rows, sems, between=False):
        own_sem, ssem, rsem = sems
        self.sends[name] = Sends(ssem.at[at])
        yield from gather_steps(self.spot, src, dst, rows, self.sends[name], rsem.at[at], own_sem.at[at], between)

    def scattering(self, name, p_refs, o_refs, rows, bufs, sems, at):
        self.sends[name] = Sends(sems[0].at[at])
        yield from scatter_steps(
            self.spot, p_refs, o_refs, rows, bufs, [sem.at[at] for sem in sems[1:]], self.sends[name]
        )

    def fetch(self, group, sources, streams=None):
        streams = range(len(sources)) if streams is None else streams
        for i, source in zip(streams, sources):
            there = self.in_refs[i].at[group % 2]
            yield pltpu.make_async_copy(source.at[:, pl.ds(group * FEW, FEW), :], there, self.in_sems.at[i, group % 2])

    def store(self, group, targets):
        for i, target in enumerate(targets):
            there = target.at[:, pl.ds(group * FEW, FEW), :]
            yield pltpu.make_async_copy(self.out_refs[i], there, self.out_sems.at[i])

    def finish(self):
        for some in self.sends.values():
            some.finish()


def start_all(copies):
    for copy in copies:
        copy.start()


def wait_all(copies):
    for copy in copies:
        copy.wait()


def tile_inputs(qkv_ref, col_ref, row_ref, base, length, head):
    query = qkv_ref[pl.ds(base + length, length), :head]
    key = qkv_ref[pl.ds(base, 3 * length), head : 2 * head]
    value = qkv_ref[pl.ds(base, 3 * length), 2 * head :]
    tile = base // length
    return query, key, value, col_ref[:, tile : tile + 1] == row_ref[:, pl.ds(base, 3 * length)]


def at(shape, axis):
    return lax.broadcasted_iota(jnp.int32, shape, axis)


def marked(mask):
    return low(jnp.where(mask, 1.0, 0.0))


def packed_order(size, length, grain):
    shape = (size, size)
    row = at((size, 1), 0)
    return marked(at(shape, 1) == row % length // grain * FEW + row // length * grain + row % grain)


def front_kernel(cuts, *refs):
    tok_ref, cot_ref, index_ref, small_ref = refs[:4]
    weights = refs[4:9]
    wd_ref, wo_ref, bucket_ref, col_ref, row_ref, perm_ref = refs[9:14] + refs[-1:]
    refs = (None,) + refs[:-1]
    (rows_ref, gain_one_ref, bias_ref, first_w_ref, qkv_ref, att_ref, middle_ref, d_mid_ref, d_ref, gain_grad_ref, near_grad_ref,
     far_grad_ref, wd_grad_ref, nx_all_ref, forth_ref) = refs[15:30]
    part_ref, up_all_ref, x_all_ref, back_ref = refs[30:34]
    branch_ref, x_ref, dn_ref, w_ref, nx_ref, up_ref, gain_ref, gate_w_ref = refs[34:42]
    one_ref, two_ref, cot_out_ref, one_in_ref, two_in_ref, cot_in_ref = refs[42:48]
    small_out_ref, all_small_ref, first_ref, second_ref = refs[48:52]
    bufs, two_total_ref, in_refs, out_refs = refs[52:58], refs[58], refs[59:61], refs[61:63]
    in_sems, out_sems = refs[63:65]
    exchanges = refs[65:83]
    one_x, two_x, cot_x, small_x, first_x, second_x = [exchanges[i : i + 3] for i in range(0, 18, 3)]
    g_sems, one_sems, two_sems = refs[83:86], refs[86:93], refs[93:100]
    two_bufs = (bufs[0], two_total_ref, *bufs[2:])
    count, slots, width = x_all_ref.shape
    stage = Stage(count, cuts, in_refs, out_refs, in_sems, out_sems)
    spot, ranges = stage.spot, stage.ranges
    units, head, length = wd_ref.shape[0], wo_ref.shape[0], bias_ref.shape[0]
    size, piece = one_ref.shape
    folds, share = width // piece, size // count
    grain = share // folds
    groups = cuts[-1] // FEW
    near = units - head
    spot.greet_all(count)
    perm_ref[...] = packed_order(size, length, grain)

    def folded(rows, sources):
        shape = (length, size)
        return low(
            sum(
                over(
                    marked((at(shape, 0) == sources) & (at(shape, 1) % share // grain == i)),
                    rows[:, i * piece : (i + 1) * piece], 0, 0,
                )
                for i in range(folds)
            )
        )

    def pick(shares, to_ref):
        source = index_ref[2:3, :slots]
        for i in range(folds):
            mask = at((size, slots), 0) == source + i * grain
            to_ref[:, i * piece : (i + 1) * piece] = low(over(marked(mask), shares, 0, 0))

    def tokens():
        for i in range(count):
            small_out_ref[i * share : (i + 1) * share, :] = small_ref[...]
        one_ref[...] = folded(tok_ref[...], index_ref[0:1, :])
        swap(spot, count, one_ref, one_in_ref, one_x, "send")
        swap(spot, count, small_out_ref, all_small_ref, small_x, "send")
        yield
        swap(spot, count, one_ref, one_in_ref, one_x, "wait")
        place = index_ref[1:2, :]
        place = jnp.where(place < 0, -1, place // grain * share + place % grain + at((1, size), 1) % share // grain * grain)
        two_ref[...] = low(over(marked(at((size, size), 0) == place), one_in_ref[...], 0, 0))
        swap(spot, count, two_ref, two_in_ref, two_x, "send")
        yield
        swap(spot, count, small_out_ref, all_small_ref, small_x, "wait")
        each = width // count
        shape = (2 * each, width)
        mine = at((size, width), 0) == at((size, width), 1) // each * share
        for i, ref in enumerate((gain_one_ref, gain_ref)):
            fold = marked(at(shape, 0) == at(shape, 1) % each + i * each)
            ref[...] = jnp.sum(jnp.where(mine, over(all_small_ref[...], fold), 0.0), axis=0, keepdims=True)
        table = jnp.where(at(all_small_ref.shape, 1) == spot.me, all_small_ref[...].astype(jnp.float32), 0.0)
        table = jnp.sum(table, axis=1, keepdims=True)
        bias_ref[...] = sum(
            jnp.where(bucket_ref[...] == b, table[b * share + 1 : b * share + 2, :], 0.0) for b in range(BUCKETS)
        )
        yield
        swap(spot, count, two_ref, two_in_ref, two_x, "wait")
        pick(two_in_ref[...], rows_ref)
        v = rows_ref[...].astype(jnp.float32)
        nx_ref[...] = (v * scale_of(v) * gain_one_ref[...]).astype(nx_ref.dtype)
        yield

    def cotangent():
        cot_out_ref[...] = folded(cot_ref[...], index_ref[1:2, :])
        swap(spot, count, cot_out_ref, cot_in_ref, cot_x, "send")
        yield
        swap(spot, count, cot_out_ref, cot_in_ref, cot_x, "wait")
        pick(cot_in_ref[...], up_ref)
        yield

    def columns(src, dst, sems, packs):
        if packs:
            pack(weights, first_ref, second_ref)
            yield
        for i in range(0, count, 8):
            swap(spot, count, src, dst, sems, "send", (max(i, 1), i + 8))
            yield
        swap(spot, count, src, dst, sems, "wait")
        if packs:
            gate_w_ref[...] = dst[:, 3 * head :]
        yield

    def attending(first, last):
        perm = perm_ref[...]
        if first == 0:
            start_all(stage.fetch(0, (nx_all_ref,)))
            qkv_ref[:length, :] = jnp.zeros((length, 3 * head), qkv_ref.dtype)
            qkv_ref[length + groups * size :, :] = jnp.zeros((length, 3 * head), qkv_ref.dtype)
        for step in range(first, last):
            if step < groups:
                if step + 1 < groups:
                    start_all(stage.fetch(step + 1, (nx_all_ref,)))
                wait_all(stage.fetch(step, (nx_all_ref,)))
                rows = low(over(in_refs[0][step % 2].reshape(size, -1), first_w_ref[:, : 3 * head]))
                qkv_ref[length + step * size : length + (step + 1) * size, :] = low(over(perm, rows))
                yield
            if step > 0:
                attended = []
                for tile in range(size // length):
                    base = (step - 1) * size + tile * length
                    query, key, value, same = tile_inputs(qkv_ref, col_ref, row_ref, base, length, head)
                    attended.append(low(over(low(tile_probs(query, key, bias_ref[...], same)), value)))
                    if tile % 2:
                        yield
                rows = low(over(perm, jnp.concatenate(attended, axis=0), 0, 0))
                att_ref[:, (step - 1) * FEW : step * FEW, :] = rows.reshape(count, FEW, head)
                if step > max(first, 1):
                    wait_all(stage.store(step - 2, (part_ref,)))
                for i in range(2):
                    there = pl.ds(i * count // 2, count // 2)
                    piece = over(rows[i * size // 2 : (i + 1) * size // 2], wo_ref[...])
                    out_refs[0][there] = low(piece).reshape(count // 2, FEW, width)
                start_all(stage.store(step - 1, (part_ref,)))
                yield
        if last > max(first, 1):
            wait_all(stage.store(last - 2, (part_ref,)))
        yield

    def rows_of(rows):
        return [pl.ds(rows.start + i, 16) for i in range(0, rows.size, 16)]

    def scale_of(v):
        return lax.rsqrt(jnp.sum(v * v, axis=1, keepdims=True) / width + EPSILON)

    def first_norm(rows):
        for r in rows_of(rows):
            v = rows_ref[r, :].astype(jnp.float32) + branch_ref[r, :]
            middle_ref[r, :] = v
            x_ref[r, :] = (v * scale_of(v) * gain_ref[...]).astype(x_ref.dtype)
        yield

    def norm_back_rows(rows):
        for r in rows_of(rows):
            v, d, gain = middle_ref[r, :], dn_ref[r, :], gain_ref[...]
            scale = scale_of(v)
            gain_grad_ref[...] += jnp.sum(d * v * scale, axis=0, keepdims=True)
            w = gain * d
            mean = jnp.sum(w * v, axis=1, keepdims=True) / width
            d_mid = up_ref[r, :].astype(jnp.float32) + scale * w - v * (scale * scale * scale) * mean
            d_mid_ref[r, :] = d_mid
            d_ref[r, :] = d_mid.astype(d_ref.dtype)
        yield

    def feeding(first, last):
        sources, targets = (x_all_ref, up_all_ref), (back_ref, forth_ref)
        start_all(stage.fetch(first, sources))
        for group in range(first, last):
            if group + 1 < last:
                start_all(stage.fetch(group + 1, sources))
            wait_all(stage.fetch(group, sources))
            for i in range(2):
                blocks = slice(i * count // 2, (i + 1) * count // 2)
                x = in_refs[0][group % 2, blocks].reshape(size // 2, width)
                upstream = in_refs[1][group % 2, blocks].reshape(size // 2, width)
                both = over(x, w_ref[...])
                gate = jnp.concatenate((over(x, gate_w_ref[...]), both[:, :near]), axis=1)
                up = both[:, near:]
                d_hidden = over(upstream, wd_ref[...], 1, 1)
                gelu, d_gelu = gelu_pair(gate)
                hidden = low(gelu * up)
                d_gate, d_up = low(d_hidden * up * d_gelu), low(d_hidden * gelu)
                d_first, d_both = d_gate[:, :head], jnp.concatenate((d_gate[:, head:], d_up), axis=1)
                if i == 0 and group > first:
                    wait_all(stage.store(group - 1, targets))
                shape = (count // 2, FEW, width)
                back = over(d_both, w_ref[...], 1, 1) + over(d_first, gate_w_ref[...], 1, 1)
                out_refs[0][blocks] = low(back).reshape(shape)
                out_refs[1][blocks] = low(over(hidden, wd_ref[...])).reshape(shape)
                if i:
                    start_all(stage.store(group, targets))
                near_grad_ref[...] += over(d_first, x, 0, 0)
                far_grad_ref[...] += over(d_both, x, 0, 0)
                wd_grad_ref[...] += over(hidden, upstream, 0, 0)
                yield
        wait_all(stage.store(last - 1, targets))
        yield

    for ref in (near_grad_ref, far_grad_ref, wd_grad_ref, gain_grad_ref):
        ref[...] = jnp.zeros_like(ref)
    halves = len(ranges)
    everything = pl.ds(0, slots)
    tasks = {
        "tokens": ([], tokens()),
        "cot": ([], cotangent()),
        "first": ([], columns(first_ref, first_w_ref, first_x, True)),
        "second": (["first"], columns(second_ref, w_ref, second_x, False)),
        "gather": (["tokens"], stage.gathering("gather", 0, nx_ref, nx_all_ref, everything, g_sems)),
        "up": (["cot"], stage.gathering("up", 1, up_ref, up_all_ref, everything, g_sems, True)),
    }
    for i, rows in enumerate(ranges):
        h = str(i)
        last_step = groups + 1 if i == halves - 1 else cuts[i + 1] // FEW + 1
        first_step = cuts[i] // FEW + 1 if i else 0
        tasks |= {
            "attend" + h: ([f"attend{i - 1}"] if i else ["gather", "first"], attending(first_step, last_step)),
            "one" + h: (
                ["attend" + h], stage.scattering("one" + h, (part_ref,), (branch_ref,), rows, bufs, one_sems, i),
            ),
            "norm" + h: (["one" + h], first_norm(rows)),
            "x" + h: (["norm" + h], stage.gathering("x" + h, 2 + i, x_ref, x_all_ref, rows, g_sems)),
            "feed" + h: (
                ["x" + h, "up", "second", f"feed{i - 1}" if i else f"attend{halves - 1}"],
                feeding(cuts[i] // FEW, cuts[i + 1] // FEW),
            ),
            "two" + h: (
                ["feed" + h],
                stage.scattering("two" + h, (back_ref,), (dn_ref,), rows, two_bufs, two_sems, i),
            ),
            "back" + h: (["two" + h], norm_back_rows(rows)),
        }
    weave(tasks, FRONT_ORDER)
    stage.finish()


def halves_of(rows):
    return (0, 48, 80) if rows == 80 else (0, rows)


def front(tok, cot, index, small, weights, wd, wo, buckets, col, row, slots):
    size, (length, width) = index.shape[1], tok.shape
    shard = weights[0].shape[0]
    count, piece = width // shard, length * width // size
    cuts = halves_of(slots)
    halves = len(cuts) - 1
    head, units = wo.shape[0], wd.shape[0]
    low_rows, all_rows, group, share = (slots, width), (count, slots, width), (count, FEW, width), (size, piece)
    first, second = (width, 4 * head), (width, 2 * units - head)
    bf, wide, dma = jnp.bfloat16, jnp.float32, pltpu.SemaphoreType.DMA
    vmem, hbm = pl.BlockSpec(memory_space=pltpu.VMEM), pl.BlockSpec(memory_space=pl.ANY)
    shape = jax.ShapeDtypeStruct
    outs = pl.pallas_call(
        functools.partial(front_kernel, cuts),
        out_shape=[
            shape(low_rows, bf), shape((1, width), wide), shape(buckets.shape, wide), shape(first, bf),
            shape((slots // FEW * size + 2 * length, 3 * head), bf), shape((count, slots, head), bf), shape(low_rows, wide),
            shape(low_rows, wide), shape(low_rows, bf), shape((1, width), wide), shape((head, width), wide),
            shape((second[1], width), wide), shape(wd.shape, wide),
        ] + [shape(all_rows, bf)] * 6,
        in_specs=[vmem] * 14,
        out_specs=[vmem] * 13 + [hbm] * 6,
        scratch_shapes=[
            pltpu.VMEM(low_rows, wide), pltpu.VMEM(low_rows, bf), pltpu.VMEM(low_rows, wide), pltpu.VMEM(second, bf),
            pltpu.VMEM(low_rows, bf), pltpu.VMEM(low_rows, bf), pltpu.VMEM((1, width), wide), pltpu.VMEM((width, head), bf),
        ] + [pltpu.VMEM(share, bf)] * 6 + [
            pltpu.VMEM((size, 128), bf), pltpu.VMEM((size, 128), bf), pltpu.VMEM(first, bf), pltpu.VMEM(second, bf),
        ] + scatter_bufs(slots, width, 1) + [
            pltpu.VMEM((16, slots, width), bf),
            pltpu.VMEM((2,) + group, bf), pltpu.VMEM((2,) + group, bf), pltpu.VMEM(group, bf), pltpu.VMEM(group, bf),
            dma((2, 2)), dma((2,)),
        ] + [dma((count,)), dma((count,)), dma] * 6 + [
            dma((2 + halves,)), dma((2 + halves, N_GATHER_SENDS)), dma((2 + halves, 2, 32)),
        ] + scatter_sems(halves, 1) * 2 + [pltpu.VMEM((size, size), bf)],
        name="front",
        compiler_params=pltpu.CompilerParams(collective_id=3, has_side_effects=True, vmem_limit_bytes=63 * 2**20),
    )(tok, cot, index, small, *weights, wd, wo, buckets, col, row)
    return outs[:15]


def rear_kernel(cuts, *refs):
    (d_ref, x_all_ref, att_ref, qkv_ref, w_ref, wo_ref, bias_ref, col_ref, row_ref, near_ref, far_ref, forth_ref, middle_ref,
     rows_ref, d_mid_ref, gain_ref, gain_two_ref, index_ref, bucket_ref) = refs[:19]
    wo_grad_ref, owned_ref, far_owned_ref, out_rows_ref, sums_ref, token_rows_ref = refs[19:25]
    d_all_ref, part_ref = refs[25:27]
    dn_ref, down_ref, bias_grad_ref, dq_ref, dkv_ref, w_grad_ref, turned_ref, far_turned_ref = refs[27:35]
    result_ref, going_ref, came_ref, last_ref, perm_ref = refs[35:40]
    bufs, other_bufs, in_refs, out_refs = refs[40:46], refs[46:52], refs[52:54], refs[54:55]
    in_sems, out_sems = refs[55:57]
    w_sems, f_sems, r_sems, t_sems, l_sems = [refs[i : i + 3] for i in range(57, 72, 3)]
    g_sems, one_sems, down_sems = refs[72:75], refs[75:82], refs[82:89]
    count, width = part_ref.shape[0], part_ref.shape[2]
    stage = Stage(count, cuts, in_refs, out_refs, in_sems, out_sems)
    spot, ranges = stage.spot, stage.ranges
    spot.greet_all(count)
    head, length, size = wo_ref.shape[0], bias_ref.shape[0], perm_ref.shape[0]
    groups = cuts[-1] // FEW
    piece, share = result_ref.shape[1], size // count
    folds = width // piece
    grain = share // folds
    perm_ref[...] = packed_order(size, length, grain)

    def owners(sources, to_ref, owner_ref, sems):
        merged = jnp.concatenate([low(ref[...]) for ref in sources], axis=0)
        for i in range(0, width, 512):
            to_ref[i : i + 512, :] = merged[:, i : i + 512].T
        swap(spot, count, to_ref, owner_ref, sems, "send")
        yield
        swap(spot, count, to_ref, owner_ref, sems, "wait")
        yield

    def dealt_out(rows):
        shape = (rows.shape[0], size)
        return sum(
            over(
                marked((at(shape, 0) == index_ref[0:1, :]) & (at(shape, 1) % share // grain == i)),
                rows[:, i * piece : (i + 1) * piece], 0, 0,
            )
            for i in range(folds)
        )

    def output():
        rows = low(middle_ref[...] + down_ref[...])
        result_ref[...] = low(dealt_out(rows))
        swap(spot, count, result_ref, out_rows_ref, r_sems, "send")
        yield
        swap(spot, count, result_ref, out_rows_ref, r_sems, "wait")
        yield

    def scale_of(v):
        return lax.rsqrt(jnp.sum(v * v, axis=1, keepdims=True) / width + EPSILON)

    def shares(*values):
        shape, each = (size, width), width // count
        spread = 0.0
        for i, v in enumerate(values):
            spread += jnp.where(at(shape, 0) == at(shape, 1) // each * share + 2 * i, v, 0.0)
        fold = marked(at((width, each), 0) % each == at((width, each), 1))
        high = low(spread)
        rest = low(spread - high.astype(jnp.float32))
        return jnp.concatenate([over(p, fold) for p in (high, rest)], axis=1)

    def finals():
        v, d, gain = rows_ref[...].astype(jnp.float32), dn_ref[...], gain_ref[...]
        scale = scale_of(v)
        w = gain * d
        mean = jnp.sum(w * v, axis=1, keepdims=True) / width
        rows = low(d_mid_ref[...] + scale * w - v * (scale * scale * scale) * mean)
        going_ref[:, :piece] = low(dealt_out(rows))
        sums = shares(jnp.sum(d * v * scale, axis=0, keepdims=True), gain_two_ref[...])
        row, lane = at(sums.shape, 0), at(sums.shape, 1)
        for b in range(BUCKETS):
            total = jnp.sum(jnp.where(bucket_ref[...] == b, bias_grad_ref[...], 0.0), axis=(0, 1), keepdims=True)
            high = low(total).astype(jnp.float32)
            sums = sums + jnp.where((row == share * b + 1) & (lane == 0), high, 0.0)
            sums = sums + jnp.where((row == share * b + 1) & (lane == 1), total - high, 0.0)
        going_ref[:, piece:] = low(sums)
        swap(spot, count, going_ref, came_ref, t_sems, "send")
        yield
        swap(spot, count, going_ref, came_ref, t_sems, "wait")
        sums_ref[...] = came_ref[:, piece:]
        shape, row, lane = (size, size), at((size, 1), 0), at((1, size), 1)
        turn = (index_ref[1:2, :] == row // share * grain + row % grain) & (row % share // grain == lane % share // grain)
        last_ref[...] = low(over(marked(turn), came_ref[:, :piece]))
        swap(spot, count, last_ref, token_rows_ref, l_sems, "send")
        yield
        swap(spot, count, last_ref, token_rows_ref, l_sems, "wait")
        yield

    def backing(first, last):
        perm = perm_ref[...]
        for step in range(first, last):
            if step < groups:
                start_all(stage.fetch(step, (d_all_ref,)))
                start_all(stage.fetch(step, (x_all_ref,), (1,)))
                wait_all(stage.fetch(step, (d_all_ref,)))
                d_branch = in_refs[0][step % 2].reshape(size, width)
                attended = att_ref[:, step * FEW : (step + 1) * FEW, :].reshape(size, head)
                wo_grad_ref[...] += over(attended, d_branch, 0, 0)
                yield
                d_attended = low(over(perm, low(over(d_branch, wo_ref[...], 1, 1))))
                yield
                for tile in range(size // length):
                    base = step * size + tile * length
                    query, key, value, same = tile_inputs(qkv_ref, col_ref, row_ref, base, length, head)
                    probs = tile_probs(query, key, bias_ref[...], same)
                    d_out = d_attended[tile * length : (tile + 1) * length, :]
                    d_probs = over(d_out, value, 1, 1)
                    inner = jnp.sum(probs * d_probs, axis=-1, keepdims=True)
                    d_scores = low(probs * (d_probs - inner))
                    bias_grad_ref[...] += d_scores.astype(jnp.float32)
                    dq_ref[base + length : base + 2 * length, :] = low(over(d_scores, key))
                    both = jnp.concatenate((over(d_scores, query, 0, 0), over(low(probs), d_out, 0, 0)), axis=1)
                    dkv_ref[base : base + 3 * length, :] += both
                    if tile % 2:
                        yield
            if step > 0:
                at = slice(length + (step - 1) * size, length + step * size)
                rows = low(over(perm, jnp.concatenate((dq_ref[at, :], low(dkv_ref[at, :])), axis=1), 0, 0))
                wait_all(stage.fetch(step - 1, (x_all_ref,), (1,)))
                w_grad_ref[...] += over(rows, in_refs[1][(step - 1) % 2].reshape(size, width), 0, 0)
                yield
                if step > max(first, 1):
                    wait_all(stage.store(step - 2, (part_ref,)))
                for i in range(2):
                    there = pl.ds(i * count // 2, count // 2)
                    block = over(rows[i * size // 2 : (i + 1) * size // 2], w_ref[:, : 3 * head], 1, 1)
                    out_refs[0][there] = low(block).reshape(count // 2, FEW, width)
                start_all(stage.store(step - 1, (part_ref,)))
                yield
        if last > max(first, 1):
            wait_all(stage.store(last - 2, (part_ref,)))
        yield

    for ref in (wo_grad_ref, bias_grad_ref, dkv_ref, w_grad_ref):
        ref[...] = jnp.zeros_like(ref)
    halves = len(ranges)
    everything = pl.ds(0, cuts[-1])
    tasks = {
        "d": ([], stage.gathering("d", 0, d_ref, d_all_ref, everything, g_sems)),
        "down": ([], stage.scattering("down", (forth_ref,), (down_ref,), everything, other_bufs, down_sems, 0)),
        "output": (["down"], output()),
        "owners": ([f"back{halves - 1}"], owners((w_grad_ref, near_ref), turned_ref, owned_ref, w_sems)),
        "far": ([], owners((far_ref,), far_turned_ref, far_owned_ref, f_sems)),
    }
    for i, rows in enumerate(ranges):
        h = str(i)
        first_step = cuts[i] // FEW + 1 if i else 0
        tasks |= {
            "back" + h: ([f"back{i - 1}"] if i else ["d"], backing(first_step, cuts[i + 1] // FEW + 1)),
            "one" + h: (["back" + h], stage.scattering("one" + h, (part_ref,), (dn_ref,), rows, bufs, one_sems, i)),
        }
    tasks["finals"] = ([f"one{i}" for i in range(halves)], finals())
    weave(tasks, REAR_ORDER)
    stage.finish()


def rear(d_rows, normed_all, attended, qkv, w, wo, bias, col, row, near_grad, far_grad, forth, middle, rows_low, d_mid, gain,
         gain_two_grad, index, buckets):
    count, rows, width = normed_all.shape
    cuts = halves_of(rows)
    halves = len(cuts) - 1
    head, size = wo.shape[0], index.shape[1]
    piece, owned, far = bias.shape[0] * width // size, (width, w.shape[1]), (width, far_grad.shape[0])
    all_rows, group, share = (count, rows, width), (count, FEW, width), (size, piece)
    bf, wide, dma = jnp.bfloat16, jnp.float32, pltpu.SemaphoreType.DMA
    vmem, hbm = pl.BlockSpec(memory_space=pltpu.VMEM), pl.BlockSpec(memory_space=pl.ANY)
    shape = jax.ShapeDtypeStruct
    outs = pl.pallas_call(
        functools.partial(rear_kernel, cuts),
        out_shape=[
            shape((head, width), wide), shape(owned, bf), shape(far, bf), shape(share, bf), shape((size, 128), bf),
            shape(share, bf),
        ] + [shape(all_rows, bf)] * 2,
        in_specs=[vmem, hbm] + [vmem] * 9 + [hbm] + [vmem] * 7,
        out_specs=[vmem, hbm, hbm, hbm, vmem, hbm] + [hbm] * 2,
        scratch_shapes=[
            pltpu.VMEM((rows, width), wide), pltpu.VMEM((rows, width), wide), pltpu.VMEM(bias.shape, wide),
            pltpu.VMEM((qkv.shape[0], head), bf), pltpu.VMEM((qkv.shape[0], 2 * head), wide),
            pltpu.VMEM((3 * head, width), wide), pltpu.VMEM(owned, bf), pltpu.VMEM(far, bf),
            pltpu.VMEM(share, bf), pltpu.VMEM((size, piece + 128), bf), pltpu.VMEM((size, piece + 128), bf),
            pltpu.VMEM(share, bf), pltpu.VMEM((size, size), bf),
        ] + scatter_bufs(rows, width, 1) * 2 + [
            pltpu.VMEM((2,) + group, bf), pltpu.VMEM((2,) + group, bf), pltpu.VMEM(group, bf),
            dma((2, 2)), dma((1,)),
        ] + [dma((count,)), dma((count,)), dma] * 5 + [
            dma((1,)), dma((1, N_GATHER_SENDS)), dma((1, 2, 32)),
        ] + scatter_sems(halves, 1) + scatter_sems(1, 1),
        name="rear",
        compiler_params=pltpu.CompilerParams(collective_id=4, has_side_effects=True, vmem_limit_bytes=63 * 2**20),
    )(d_rows, normed_all, attended, qkv, w, wo, bias, col, row, near_grad, far_grad, forth, middle, rows_low, d_mid, gain,
      gain_two_grad, index, buckets)
    return outs[:6]


def dot(left, right):
    return jnp.dot(left, right, preferred_element_type=jnp.float32)


def select(mask, rows):
    return dot(mask.astype(jnp.bfloat16), rows).astype(jnp.bfloat16)


def unpack_kernel(first_ref, second_ref, query_ref, key_ref, value_ref, gate_ref, up_ref):
    count = first_ref.shape[0]
    head = query_ref.shape[1] // count
    units = gate_ref.shape[1] // count
    wide = jnp.float32
    for j in range(count):
        for i, ref in enumerate((query_ref, key_ref, value_ref)):
            ref[:, j * head : (j + 1) * head] = first_ref[j, :, i * head : (i + 1) * head].astype(wide)
        gate_ref[:, j * units : j * units + head] = first_ref[j, :, 3 * head :].astype(wide)
        gate_ref[:, j * units + head : (j + 1) * units] = second_ref[j, :, : units - head].astype(wide)
        up_ref[:, j * units : (j + 1) * units] = second_ref[j, :, units - head :].astype(wide)


def unpack(first, second, width, hidden):
    rows = first.shape[1]
    widths = (width, width, width, hidden, hidden)
    return pl.pallas_call(
        unpack_kernel,
        out_shape=[jax.ShapeDtypeStruct((rows, columns), jnp.float32) for columns in widths],
        in_specs=[pl.BlockSpec(memory_space=pltpu.VMEM)] * 2,
        out_specs=[pl.BlockSpec(memory_space=pltpu.VMEM)] * 5,
        name="unpack_columns",
        compiler_params=pltpu.CompilerParams(vmem_limit_bytes=32 * 2**20),
    )(first, second)


def body(
    tokens,
    lengths,
    permutation,
    query_weight,
    key_weight,
    value_weight,
    out_weight,
    gate_weight,
    up_weight,
    down_weight,
    gain_attention,
    gain_feedforward,
    bias_table,
    cotangent,
):
    me = lax.axis_index(AXIS)
    count = tokens.shape[0]
    grain = tokens.shape[1]
    length = cotangent.shape[1]
    width = tokens.shape[2]
    shard = query_weight.shape[0]
    hidden_width = gate_weight.shape[1] // count
    head = HEAD_DIM
    total = 3 * count * length // 5
    tiles = -(-total // length)
    slots = tiles * grain

    dealt_lengths = lengths[permutation]
    ends = jnp.cumsum(dealt_lengths)
    starts = ends - dealt_lengths
    this = jnp.arange(count, dtype=jnp.int32) == me
    my_start, my_length = jnp.sum(jnp.where(this, starts, 0)), jnp.sum(jnp.where(this, dealt_lengths, 0))
    place_in = jnp.arange(length, dtype=jnp.int32)
    slot_ids = jnp.arange(slots, dtype=jnp.int32)
    packed_ids = slot_ids // grain * length + me * grain + slot_ids % grain
    source_seq = jnp.sum((packed_ids[:, None] >= ends[None, :]).astype(jnp.int32), axis=1)

    few = 16
    folds = few // grain
    piece = width // folds
    share = jnp.arange(few * count, dtype=jnp.int32)
    share_row, share_fold = share // few * grain + share % grain, share % few // grain
    position = share_row - my_start % length
    position = jnp.where(position < 0, position + length, position)
    in_share = jnp.arange(few, dtype=jnp.int32)[None, :] % grain
    index = jnp.stack(
        (
            (permutation[:, None] * grain + in_share).reshape(-1),
            jnp.where(position < my_length, position, -1),
            jnp.pad(jnp.where(source_seq < count, source_seq * few + slot_ids % grain, -few), (0, few * count - slots)),
        )
    )
    small = jnp.concatenate((gain_attention, gain_feedforward, bias_table))
    small = jnp.pad(small, (0, few * 128 - small.shape[0])).reshape(few, 128)
    all_ids = jnp.arange(tiles * length, dtype=jnp.int32)
    segment = jnp.sum((all_ids[:, None] >= ends[None, :]).astype(jnp.int32), axis=1) + 1
    column, row = segment.reshape(tiles, length).T, jnp.pad(segment, (length, length))[None, :]
    relative = (
        jnp.arange(3 * length, dtype=jnp.int32)[None, :] - length - place_in[:, None]
    ).reshape(-1)
    onehot = bucket_index(relative)[None, :] == jnp.arange(BUCKETS, dtype=jnp.int32)[:, None]
    buckets = bucket_index(relative).reshape(length, -1)
    (rows_low, gain_one, rel_bias, first_columns, qkv, attended, middle, d_middle, d_low, gain_two_grad, near_grad, far_grad,
     down_grad, normed_all, forth) = front(
        tokens.reshape(length, width), cotangent[0], index, small,
        (query_weight, key_weight, value_weight, gate_weight, up_weight), down_weight, out_weight, buckets, column, row, slots,
    )
    turned = me * grain + in_share - starts[:, None] % length
    turned = starts[:, None] + jnp.where(turned < 0, turned + length, turned)
    back_slot = (turned // length * grain + in_share).reshape(-1)

    out_grad, first_grad, second_grad, out_rows, sums, token_rows = rear(
        d_low, normed_all, attended, qkv, first_columns, out_weight, rel_bias, column, row, near_grad, far_grad, forth, middle,
        rows_low, d_middle, gain_one, gain_two_grad, jnp.stack((back_slot, index[1])), buckets,
    )
    first_grad, second_grad = first_grad.reshape(count, shard, -1), second_grad.reshape(count, shard, -1)
    sums = sums.reshape(count, few, -1).astype(jnp.float32)
    gain_sums = jnp.sum(sums, axis=0)
    gain_attention_grad = gain_sums[0, :shard] + gain_sums[0, shard : 2 * shard]
    gain_feedforward_grad = gain_sums[2, :shard] + gain_sums[2, shard : 2 * shard]
    table_grad = sums[:, 1, 0] + sums[:, 1, 1]

    def whole_rows(shares):
        return shares.reshape(count, folds, grain, piece).transpose(0, 2, 1, 3).reshape(count, grain, width)

    place = place_in - my_start % length
    place = jnp.where(place < 0, place + length, place)
    turned_back = (place[None, :] == place_in[:, None]) & (place_in[:, None] < my_length)
    layer_output = select(turned_back, whole_rows(out_rows).reshape(length, width))[None]
    ids = jnp.arange(count, dtype=jnp.int32)
    dealt_slot = jnp.sum(jnp.where(permutation[None, :] == ids[:, None], ids[None, :], 0), axis=1)
    tokens_grad = whole_rows(token_rows)[dealt_slot]
    query_grad, key_grad, value_grad, gate_grad, up_grad = unpack(
        first_grad, second_grad, width, hidden_width * count
    )
    return (
        layer_output,
        tokens_grad,
        query_grad,
        key_grad,
        value_grad,
        out_grad,
        gate_grad,
        up_grad,
        down_grad,
        gain_attention_grad,
        gain_feedforward_grad,
        table_grad,
    )


def solution(mesh):
    placed = (
        P(None, "fsdp", None),
        P(),
        P(),
        P("fsdp", None),
        P("fsdp", None),
        P("fsdp", None),
        P("fsdp", None),
        P("fsdp", None),
        P("fsdp", None),
        P("fsdp", None),
        P("fsdp"),
        P("fsdp"),
        P("fsdp"),
        P("fsdp", None, None),
    )
    return jax.shard_map(
        body if mesh.shape[AXIS] == 32 else body_any,
        mesh=mesh,
        in_specs=placed,
        out_specs=(
            P("fsdp", None, None),
            P(None, "fsdp", None),
            P("fsdp", None),
            P("fsdp", None),
            P("fsdp", None),
            P("fsdp", None),
            P("fsdp", None),
            P("fsdp", None),
            P("fsdp", None),
            P("fsdp"),
            P("fsdp"),
            P("fsdp"),
        ),
        check_vma=False,
    )
```

```python
import functools

import jax
import jax.numpy as jnp
from jax import lax
from jax.experimental import pallas as pl
from jax.experimental.pallas import tpu as pltpu
from jax.sharding import PartitionSpec as P

HEADS = 32
HEAD_DIM = 64
BUCKETS = 32


EPSILON = 1e-06
masked_score = -1000000000.0
HIGHEST = lax.Precision.HIGHEST


def bucket_index(relative):
    half_buckets = BUCKETS // 2
    exact_count = half_buckets // 2
    distance = jnp.abs(relative)
    side_offset = jnp.where(relative > 0, half_buckets, 0).astype(jnp.int32)
    square = distance * distance
    far_bucket = jnp.full_like(distance, exact_count)
    for doubling in range(1, half_buckets - exact_count):
        far_bucket = far_bucket + (square >= exact_count * exact_count * 2**doubling).astype(
            jnp.int32
        )
    return side_offset + jnp.where(distance < exact_count, distance, far_bucket)


def bucket_onehot(seq_len):
    positions = jnp.arange(seq_len, dtype=jnp.int32)
    relative = (positions[None, :] - positions[:, None]).reshape(-1)
    bucket_ids = jnp.arange(BUCKETS, dtype=jnp.int32)
    return (bucket_index(relative)[None, :] == bucket_ids[:, None]).astype(jnp.float32)


def norm_scale(values):
    return lax.rsqrt(jnp.mean(values * values, axis=-1, keepdims=True) + EPSILON)


def norm_back(values, scale, gain_vec, d_norm):
    weighted = gain_vec * d_norm
    return scale * weighted - values * (scale * scale * scale) * jnp.mean(
        weighted * values, axis=-1, keepdims=True
    )


def rows_product(left, right):
    return lax.dot_general(
        left, right, (((0,), (0,)), ((), ())), preferred_element_type=jnp.float32
    )


def against_rows(left, right):
    return lax.dot_general(
        left, right, (((1,), (1,)), ((), ())), preferred_element_type=jnp.float32
    )


def masked_scores(query_heads, key_heads, rel_bias, length):
    scores = (
        jnp.einsum("qhd,khd->hqk", query_heads, key_heads, preferred_element_type=jnp.float32)
        + rel_bias
    )
    key_valid = jnp.arange(key_heads.shape[0], dtype=jnp.int32) < length
    return jnp.where(key_valid[None, None, :], scores, masked_score)


def unpack_weights(full_weights, onehot, seq_len):
    table_full = full_weights[4].astype(jnp.float32).reshape(BUCKETS, HEADS)
    rel_bias = jnp.dot(table_full.T, onehot, precision=HIGHEST).reshape(HEADS, seq_len, seq_len)
    return (
        full_weights[0],
        full_weights[1],
        full_weights[2].astype(jnp.float32),
        full_weights[3].astype(jnp.float32),
        rel_bias,
    )


def body_any(
    tokens,
    lengths,
    permutation,
    query_weight,
    key_weight,
    value_weight,
    out_weight,
    gate_weight,
    up_weight,
    down_weight,
    gain_attention,
    gain_feedforward,
    bias_table,
    cotangent,
):
    model_width = query_weight.shape[1]
    hidden_width = gate_weight.shape[1]
    packed = jnp.concatenate(
        (query_weight, key_weight, value_weight, out_weight, gate_weight, up_weight), axis=1
    )
    shards = (packed, down_weight, gain_attention, gain_feedforward, bias_table)
    full_weights = (
        lax.all_gather(shards[0], "fsdp", axis=0, tiled=True),
        lax.all_gather(shards[1], "fsdp", axis=0, tiled=True),
        lax.all_gather(shards[2], "fsdp", axis=0, tiled=True),
        lax.all_gather(shards[3], "fsdp", axis=0, tiled=True),
        lax.all_gather(shards[4], "fsdp", axis=0, tiled=True),
    )
    reordered = tokens[permutation]
    dealt = lax.all_to_all(reordered, "fsdp", split_axis=0, concat_axis=1, tiled=True)
    seq_count = dealt.shape[0]
    seq_len = dealt.shape[1]
    local_ids = lax.dynamic_slice_in_dim(permutation, lax.axis_index("fsdp") * seq_count, seq_count)
    seq_lengths = lengths[local_ids]
    positions = jnp.arange(seq_len, dtype=jnp.int32)
    row_valid = (positions[None, :] < seq_lengths[:, None]).astype(jnp.float32).reshape(-1, 1)
    onehot = bucket_onehot(seq_len)
    onehot_low = onehot.astype(jnp.bfloat16)
    full_packed, full_down, gain_one, gain_two, rel_bias = unpack_weights(
        full_weights, onehot, seq_len
    )
    head_shape = (seq_count, seq_len, HEADS, HEAD_DIM)
    rows_in = dealt.reshape(-1, model_width).astype(jnp.float32)
    scale_one = norm_scale(rows_in)
    normed = (rows_in * scale_one * gain_one).astype(jnp.bfloat16)
    projected = jnp.dot(
        normed, full_packed[:, : 3 * model_width], preferred_element_type=jnp.float32
    ).astype(jnp.bfloat16)
    query_heads = projected[:, :model_width].reshape(head_shape)
    key_heads = projected[:, model_width : 2 * model_width].reshape(head_shape)
    value_heads = projected[:, 2 * model_width :].reshape(head_shape)

    def attend_forward(pieces):
        query_one, key_one, value_one, length = pieces
        scores = masked_scores(query_one, key_one, rel_bias, length)
        row_max = jnp.max(scores, axis=-1, keepdims=True)
        exp_total = jnp.sum(jnp.exp(scores - row_max), axis=-1, keepdims=True)
        log_total = row_max + jnp.log(exp_total)
        weights_soft = jnp.exp(scores - log_total).astype(jnp.bfloat16)
        attended_one = jnp.einsum(
            "hqk,khd->qhd", weights_soft, value_one, preferred_element_type=jnp.float32
        )
        return (attended_one.astype(jnp.bfloat16), log_total)

    attended_heads, log_totals = lax.map(
        attend_forward, (query_heads, key_heads, value_heads, seq_lengths)
    )
    attended_rows = attended_heads.reshape(-1, model_width)
    middle = rows_in + jnp.dot(
        attended_rows,
        full_packed[:, 3 * model_width : 4 * model_width],
        preferred_element_type=jnp.float32,
    )
    scale_two = norm_scale(middle)
    normed_two = (middle * scale_two * gain_two).astype(jnp.bfloat16)
    gate_up = jnp.dot(
        normed_two, full_packed[:, 4 * model_width :], preferred_element_type=jnp.float32
    )

    def gelu_product(gate_part, up_part):
        return jax.nn.gelu(gate_part, approximate=True) * up_part

    hidden_full, gelu_pull = jax.vjp(
        gelu_product, gate_up[:, :hidden_width], gate_up[:, hidden_width:]
    )
    hidden = hidden_full.astype(jnp.bfloat16)
    result = middle + jnp.dot(hidden, full_down, preferred_element_type=jnp.float32)
    layer_output = (
        (result * row_valid).astype(jnp.bfloat16).reshape(seq_count, seq_len, model_width)
    )
    full_weights = (
        lax.all_gather(shards[0], "fsdp", axis=0, tiled=True),
        lax.all_gather(shards[1], "fsdp", axis=0, tiled=True),
        lax.all_gather(shards[2], "fsdp", axis=0, tiled=True),
        lax.all_gather(shards[3], "fsdp", axis=0, tiled=True),
        lax.all_gather(shards[4], "fsdp", axis=0, tiled=True),
    )
    full_packed, full_down, gain_one, gain_two, rel_bias = unpack_weights(
        full_weights, onehot, seq_len
    )
    upstream = cotangent.reshape(-1, model_width).astype(jnp.float32) * row_valid
    upstream_low = upstream.astype(jnp.bfloat16)
    d_hidden = against_rows(upstream_low, full_down)
    d_gate, d_up = gelu_pull(d_hidden)
    d_gate_up = jnp.concatenate((d_gate, d_up), axis=1).astype(jnp.bfloat16)
    d_normed_two = against_rows(d_gate_up, full_packed[:, 4 * model_width :])
    gain_two_grad = jnp.sum(d_normed_two * middle * scale_two, axis=0)
    d_middle = upstream + norm_back(middle, scale_two, gain_two, d_normed_two)
    d_branch = d_middle.astype(jnp.bfloat16)
    d_attended = against_rows(d_branch, full_packed[:, 3 * model_width : 4 * model_width]).astype(
        jnp.bfloat16
    )

    def attend_backward(pieces):
        query_one, key_one, value_one, length, log_total, d_attended_one = pieces
        scores = masked_scores(query_one, key_one, rel_bias, length)
        probs = jnp.exp(scores - log_total)
        probs_low = probs.astype(jnp.bfloat16)
        d_value = jnp.einsum(
            "hqk,qhd->khd", probs_low, d_attended_one, preferred_element_type=jnp.float32
        )
        d_probs = jnp.einsum(
            "qhd,khd->hqk", d_attended_one, value_one, preferred_element_type=jnp.float32
        )
        inner = jnp.sum(probs * d_probs, axis=-1, keepdims=True)
        d_scores = (probs * (d_probs - inner)).astype(jnp.bfloat16)
        d_query = jnp.einsum("hqk,khd->qhd", d_scores, key_one, preferred_element_type=jnp.float32)
        d_key = jnp.einsum("hqk,qhd->khd", d_scores, query_one, preferred_element_type=jnp.float32)
        d_bias = against_rows(d_scores.reshape(HEADS, -1), onehot_low)
        return (
            (
                d_query.astype(jnp.bfloat16),
                d_key.astype(jnp.bfloat16),
                d_value.astype(jnp.bfloat16),
            ),
            d_bias,
        )

    (d_query_all, d_key_all, d_value_all), d_bias_all = lax.map(
        attend_backward,
        (
            query_heads,
            key_heads,
            value_heads,
            seq_lengths,
            log_totals,
            d_attended.reshape(head_shape),
        ),
    )
    d_qkv = jnp.concatenate(
        (
            d_query_all.reshape(-1, model_width),
            d_key_all.reshape(-1, model_width),
            d_value_all.reshape(-1, model_width),
        ),
        axis=1,
    )
    d_normed = against_rows(d_qkv, full_packed[:, : 3 * model_width])
    gain_one_grad = jnp.sum(d_normed * rows_in * scale_one, axis=0)
    d_rows = d_middle + norm_back(rows_in, scale_one, gain_one, d_normed)
    d_dealt = d_rows.astype(jnp.bfloat16).reshape(seq_count, seq_len, model_width)
    returned_rows = lax.all_to_all(d_dealt, "fsdp", split_axis=1, concat_axis=0, tiled=True)
    tokens_grad = returned_rows[jnp.argsort(permutation)]
    packed_grad = lax.psum_scatter(
        jnp.concatenate(
            (
                rows_product(normed, d_qkv),
                jnp.concatenate(
                    (rows_product(attended_rows, d_branch), rows_product(normed_two, d_gate_up)),
                    axis=1,
                ),
            ),
            axis=1,
        ),
        "fsdp",
        scatter_dimension=0,
        tiled=True,
    )
    mixer_grad = packed_grad[:, : 3 * model_width]
    branch_grad = packed_grad[:, 3 * model_width :]
    down_grad = lax.psum_scatter(
        rows_product(hidden, upstream_low), "fsdp", scatter_dimension=0, tiled=True
    )
    table_sum = jnp.sum(d_bias_all, axis=0).T.reshape(-1)
    gain_attention_grad, gain_feedforward_grad, table_grad = (
        lax.psum_scatter(gain_one_grad, "fsdp", scatter_dimension=0, tiled=True),
        lax.psum_scatter(gain_two_grad, "fsdp", scatter_dimension=0, tiled=True),
        lax.psum_scatter(table_sum, "fsdp", scatter_dimension=0, tiled=True),
    )
    return (
        layer_output,
        tokens_grad,
        mixer_grad[:, :model_width],
        mixer_grad[:, model_width : 2 * model_width],
        mixer_grad[:, 2 * model_width :],
        branch_grad[:, :model_width],
        branch_grad[:, model_width : model_width + hidden_width],
        branch_grad[:, model_width + hidden_width :],
        down_grad,
        gain_attention_grad,
        gain_feedforward_grad,
        table_grad,
    )


MESH = pl.DeviceIdType.MESH
AXIS = "fsdp"


def over(left, right, left_dim=1, right_dim=0):
    return lax.dot_general(
        left, right, (((left_dim,), (right_dim,)), ((), ())), preferred_element_type=jnp.float32
    )


def low(values):
    return values.astype(jnp.bfloat16)


def tile_probs(query, key, bias, same):
    scores = jnp.where(same, over(query, key, 1, 1) + bias, masked_score)
    grown = jnp.exp(scores - jnp.max(scores, axis=-1, keepdims=True))
    return grown / jnp.sum(grown, axis=-1, keepdims=True)


class Spot:
    def __init__(self):
        me = lax.axis_index(AXIS)
        c, x, y, z = me % 2, (me // 2) % 2, (me // 4) % 2, me // 8
        self.me = me
        self.mid = (z == 1) | (z == 2)
        self.end = jnp.logical_not(self.mid)
        self.zs = (z, z + 1 - 2 * (z % 2), 2 - z // 2, 3 - 3 * (z // 2))
        self.shift = [8 * (zz - z) for zz in self.zs]
        self.core, self.x, self.y = me + 1 - 2 * c, me + 2 - 4 * x, me + 4 - 8 * y
        self.diag = self.x + self.y - me
        self.n1, self.n2 = me + self.shift[1], me + self.shift[2]

    def greet(self):
        bar = pltpu.get_barrier_semaphore()
        for peer in (self.core, self.x, self.y, self.n1):
            pl.semaphore_signal(bar, inc=1, device_id=(peer,), device_id_type=MESH)

        @pl.when(self.mid)
        def _():
            pl.semaphore_signal(bar, inc=1, device_id=(self.n2,), device_id_type=MESH)

        pl.semaphore_wait(bar, 4 + self.mid.astype(jnp.int32))

    def greet_all(self, count):
        bar = pltpu.get_barrier_semaphore()

        def signal(d, _):
            peer = (self.me + d) % count
            pl.semaphore_signal(bar, inc=1, device_id=(peer,), device_id_type=MESH)
            return _

        lax.fori_loop(1, count, signal, 0)
        pl.semaphore_wait(bar, count - 1)


class Sends:
    def __init__(self, sems):
        self.sems, self.used, self.open = sems, 0, []

    def push(self, src, dst, rsem, peer, when=None):
        ssem = self.sems.at[self.used]
        self.used += 1

        def copy():
            return pltpu.make_async_remote_copy(
                src, dst, ssem, rsem, device_id=(peer,), device_id_type=MESH
            )

        if when is None:
            copy().start()
        else:
            pl.when(when)(lambda: copy().start())
        self.open.append((lambda: copy().wait_send(), when))

    def finish(self):
        for wait, when in self.open:
            if when is None:
                wait()
            else:
                pl.when(when)(wait)
        self.open = []


def arrive(dst, rsem, spot):
    pltpu.make_async_remote_copy(
        dst, dst, rsem, rsem, device_id=(spot.core,), device_id_type=MESH
    ).wait_recv()


def gather_steps(spot, src, dst, rows, sends, rsem, own_sem, between=False):
    half = src.shape[1] // 2
    cols = (pl.ds(0, half), pl.ds(half, half))
    me, mid, shift = spot.me, spot.mid, spot.shift
    first, last = (spot.x, spot.y), (spot.y, spot.x)
    own = pltpu.make_async_copy(src.at[rows, :], dst.at[me, rows, :], own_sem)
    own.start()

    def push(part, block, peer, mine=False, when=None):
        there = dst.at[block, rows, cols[part]]
        here = src.at[rows, cols[part]] if mine else there
        sends.push(here, there, rsem.at[part, block], peer, when)

    def landed(part, block):
        arrive(dst.at[block, rows, cols[part]], rsem.at[part, block], spot)

    for part in (0, 1):
        push(part, me, spot.n1, True)
        push(part, me, spot.n2, True, mid)
        push(part, me, first[part], True)
        push(part, me, last[part], True)
    for part in (0, 1):
        push(part, me, spot.core, True)
    yield

    def from_z(part, j):
        b = me + shift[j]
        landed(part, b)
        push(part, b, spot.n2 if j == 1 else spot.n1, when=mid)
        push(part, b, first[part])
        push(part, b, last[part])
        push(part, b, spot.core)

    def from_first(part, j):
        b = first[part] + shift[j]
        landed(part, b)
        push(part, b, last[part])
        push(part, b, spot.core)

    def from_last(part, b):
        landed(part, b)
        push(part, b, spot.core)

    def from_side(part):
        b = first[part]
        landed(part, b)
        push(part, b, spot.n1)
        push(part, b, spot.n2, when=mid)
        push(part, b, last[part])
        push(part, b, spot.core)

    def along_z(part, base, j):
        b = base + shift[j]
        landed(part, b)
        push(part, b, spot.n2 if j == 1 else spot.n1, when=mid)
        push(part, b, last[part])
        push(part, b, spot.core)

    if between:
        for part in (0, 1):
            from_side(part)
            yield
        for j in range(1, 5):
            if j < 4:
                for part in (0, 1):
                    along_z(part, me, j)
                    yield
                for part in (0, 1):
                    along_z(part, first[part], j)
                    yield
            for part in (0, 1):
                from_last(part, last[part] + shift[j - 1])
                from_last(part, spot.diag + shift[j - 1])
                yield
    else:
        for j in range(4):
            if j:
                for part in (0, 1):
                    from_z(part, j)
                    yield
            for part in (0, 1):
                from_first(part, j)
                yield
            if j:
                for part in (0, 1):
                    from_last(part, last[part] + shift[j - 1])
                    yield
        for part in (0, 1):
            from_last(part, last[part] + shift[3])
            yield
        for j in range(4):
            for part in (0, 1):
                from_last(part, spot.diag + shift[j])
                yield
    for j in range(4):
        for base in (me, spot.x, spot.y, spot.diag):
            for part in (0, 1):
                landed(part, base + spot.core - me + shift[j])
    own.wait()
    yield


def scatter_steps(spot, p_refs, o_refs, rows, bufs, sems, sends):
    ring_ref, s_ref, first_ref, second_ref, za_ref, zb_ref = bufs
    lsem, csem, fsem, gsem, zasem, zbsem = sems
    given = len(p_refs)
    width = p_refs[0].shape[2]
    half = given * width // 2
    me, mid, end, zs = spot.me, spot.mid, spot.end, spot.zs
    cols, short = (pl.ds(0, half), pl.ds(half, half)), pl.ds(0, half)
    plane = (me, spot.x, spot.y, spot.diag)
    first_peer, second_peer = (spot.y, spot.x), (spot.x, spot.y)
    start, size = rows.start, rows.size

    def mine(q, j, part):
        return s_ref.at[q * 4 + zs[j], rows, cols[part]]

    def held(ref, part, slot):
        return ref.at[part, slot, rows, short]

    def chunks(count, step):
        lax.fori_loop(0, size // 16, lambda i, _: step(pl.ds(pl.multiple_of(start + i * 16, 16), 16)) or _, 0)

    def add(q, j, part, *more):
        def step(r):
            v = s_ref[q * 4 + zs[j], r, cols[part]].astype(jnp.float32)
            for ref, slot in more:
                v = v + ref[part, slot, r, short].astype(jnp.float32)
            s_ref[q * 4 + zs[j], r, cols[part]] = v.astype(s_ref.dtype)

        chunks(size, step)

    def pair_exchange(j):
        for q in (3, 2, 1, 0):
            b = plane[q] + spot.shift[j]
            slot = q * 4 + zs[j]
            for i, p_ref in enumerate(p_refs):
                own = pl.ds(i * width, width)
                sends.push(p_ref.at[b + spot.core - me, rows, :], s_ref.at[slot, rows, own], csem.at[i, slot], spot.core)
                here = ring_ref.at[j % 2 * 4 + q, rows, own]
                pltpu.make_async_copy(p_ref.at[b, rows, :], here, lsem.at[i, j % 2 * 4 + q]).start()

    def joined(q, j):
        slot, near = q * 4 + zs[j], j % 2 * 4 + q
        for i, p_ref in enumerate(p_refs):
            own = pl.ds(i * width, width)
            pltpu.make_async_copy(p_ref.at[0, rows, :], ring_ref.at[near, rows, own], lsem.at[i, near]).wait()
            arrive(s_ref.at[slot, rows, own], csem.at[i, slot], spot)
        everything = pl.ds(0, given * width)

        def step(r):
            v = ring_ref[near, r, everything].astype(jnp.float32) + s_ref[slot, r, everything].astype(jnp.float32)
            s_ref[slot, r, everything] = v.astype(s_ref.dtype)

        chunks(size, step)

    def to_first(part, q, j):
        slot = (4 if q == 3 else 0) + zs[j]
        sends.push(mine(q, j, part), held(first_ref, part, slot), fsem.at[part, slot], first_peer[part])

    def first_stage(j):
        joined(3, j)
        if j:
            pair_exchange(j - 1)
        to_first(0, 3, j)
        to_first(1, 3, j)
        yield
        joined(2, j)
        to_first(0, 2, j)
        yield
        joined(1, j)
        to_first(1, 1, j)
        joined(0, j)
        yield

    def second_stage(j):
        for part in (0, 1):
            q, slot = (1, 2)[part], 4 + zs[j]
            arrive(held(first_ref, part, slot), fsem.at[part, slot], spot)
            add(q, j, part, (first_ref, slot))
            sends.push(mine(q, j, part), held(second_ref, part, zs[j]), gsem.at[part, zs[j]], second_peer[part])
            yield

    def z_send(j):
        for part in (0, 1):
            arrive(held(first_ref, part, zs[j]), fsem.at[part, zs[j]], spot)
            arrive(held(second_ref, part, zs[j]), gsem.at[part, zs[j]], spot)
            add(0, j, part, (first_ref, zs[j]), (second_ref, zs[j]))
            if j:
                sends.push(mine(0, j, part), held(za_ref, part, 3 - j), zasem.at[part, 3 - j], spot.n1, end)
            yield

    def z_relay(j):
        if not j:
            return
        for part in (0, 1):
            came, sem, slot = (za_ref, zasem, 3 - j) if j > 1 else (zb_ref, zbsem, 0)

            @pl.when(mid)
            def _():
                arrive(held(came, part, slot), sem.at[part, slot], spot)
                add(0, j, part, (came, slot))

            slot = 3 - j if j > 1 else 0
            peer = spot.n2 if j > 1 else spot.n1
            sends.push(mine(0, j, part), held(zb_ref, part, slot), zbsem.at[part, slot], peer, mid)
            yield

    pair_exchange(3)
    yield
    stages = (first_stage, second_stage, z_send, z_relay)
    for step in range(4 + len(stages) - 1):
        for stage, what in enumerate(stages):
            j = 3 - (step - stage)
            if 0 <= j <= 3:
                yield from what(j)
    for part in (0, 1):
        o_ref, there = (o_refs[part], pl.ds(0, half)) if given == 2 else (o_refs[0], cols[part])

        def total(*more):
            def step(r):
                v = s_ref[zs[0], r, cols[part]].astype(jnp.float32)
                for ref, slot in more:
                    v = v + ref[part, slot, r, short].astype(jnp.float32)
                o_ref[r, there] = v

            chunks(size, step)

        @pl.when(mid)
        def _():
            arrive(held(za_ref, part, 2), zasem.at[part, 2], spot)
            arrive(held(zb_ref, part, 1), zbsem.at[part, 1], spot)
            total((za_ref, 2), (zb_ref, 1))

        @pl.when(end)
        def _():
            arrive(held(zb_ref, part, 0), zbsem.at[part, 0], spot)
            total((zb_ref, 0))

        yield


def swap(spot, count, src, dst, sems, what, some=None):
    begin, end = some or (1, count)
    send_sem, recv_sem, own_sem = sems
    share = src.shape[0] // count

    def part(ref, index):
        return ref.at[pl.ds(pl.multiple_of(index * share, share), share), :]

    def own():
        return pltpu.make_async_copy(part(src, spot.me), part(dst, spot.me), own_sem)

    def one(d, _):
        peer, source = (spot.me + d) % count, (spot.me + count - d) % count
        if what == "send":
            pltpu.make_async_remote_copy(
                part(src, peer), part(dst, spot.me), send_sem.at[peer], recv_sem.at[spot.me], device_id=(peer,),
                device_id_type=MESH,
            ).start()
        else:
            copy = pltpu.make_async_remote_copy(
                part(src, peer), part(dst, source), send_sem.at[peer], recv_sem.at[source], device_id=(peer,),
                device_id_type=MESH,
            )
            copy.wait_recv()
            copy.wait_send()
        return _

    if what == "send" and begin == 1:
        own().start()
    lax.fori_loop(begin, end, one, 0)
    if what == "wait" and end == count:
        own().wait()


def pack(weights, first_ref, second_ref):
    query_ref, key_ref, value_ref, gate_ref, up_ref = weights
    rows = query_ref.shape[0]
    count = first_ref.shape[0] // rows
    head, units = query_ref.shape[1] // count, gate_ref.shape[1] // count
    for j in range(count):
        there = pl.ds(j * rows, rows)
        for i, ref in enumerate((query_ref, key_ref, value_ref)):
            first_ref[there, i * head : (i + 1) * head] = ref[:, j * head : (j + 1) * head]
        first_ref[there, 3 * head :] = gate_ref[:, j * units : j * units + head]
        second_ref[there, : units - head] = gate_ref[:, j * units + head : (j + 1) * units]
        second_ref[there, units - head :] = up_ref[:, j * units : (j + 1) * units]


def weave(tasks, order):
    names = list(tasks)
    left = {name: steps for name, (_, steps) in tasks.items()}

    def advance(name):
        for other in tasks[name][0]:
            if other in left:
                advance(other)
                assert other not in left, name
        if name in left and next(left[name], left) is left:
            del left[name]

    for number, times in order:
        for _ in range(times):
            advance(names[number])
    while left:
        name = next(n for n in left if not any(other in left for other in tasks[n][0]))
        while name in left:
            advance(name)


FRONT_ORDER = (
    (0, 2), (2, 3), (0, 1), (2, 2), (0, 1), (4, 5), (2, 1), (4, 20), (1, 1), (4, 7), (6, 1), (3, 1), (6, 8),
    (1, 1), (5, 1), (6, 5), (5, 2), (7, 6), (13, 1), (7, 1), (13, 1), (7, 1), (13, 1), (5, 1), (13, 2), (7,
    4), (13, 3), (5, 1), (14, 1), (7, 1), (5, 2), (7, 1), (14, 6), (5, 1), (7, 1), (5, 1), (7, 2), (5, 1),
    (14, 1), (5, 1), (14, 1), (5, 1), (14, 3), (5, 1), (14, 1), (3, 1), (7, 1), (14, 1), (7, 4), (5, 1), (7,
    1), (5, 1), (7, 2), (5, 1), (14, 1), (5, 3), (7, 1), (5, 2), (14, 2), (5, 1), (14, 2), (5, 1), (7, 2),
    (14, 1), (7, 2), (5, 1), (14, 1), (7, 2), (14, 2), (7, 1), (14, 2), (7, 2), (14, 1), (7, 1), (14, 2), (7,
    1), (8, 1), (9, 1), (14, 6), (9, 1), (14, 1), (9, 6), (14, 1), (9, 2), (14, 1), (9, 2), (3, 1), (9, 1),
    (15, 1), (9, 15), (3, 1), (9, 4), (16, 2), (3, 1), (10, 1), (16, 3), (10, 1), (16, 4), (10, 1), (16, 2),
    (10, 1), (16, 5), (10, 1), (16, 1), (10, 1), (16, 11), (10, 1), (16, 2), (11, 1), (16, 1), (11, 1), (16,
    1), (11, 6), (17, 1), (11, 1), (17, 1), (11, 3), (17, 1), (11, 9), (17, 1), (11, 2), (17, 1), (11, 1),
    (18, 1), (11, 3), (18, 1), (11, 1), (18, 9), (11, 8), (18, 3), (11, 1), (18, 13), (12, 1), (18, 10), (19,
    1),
)
REAR_ORDER = (
    (0, 3), (1, 1), (0, 23), (4, 1), (0, 1), (1, 1), (0, 1), (1, 1), (0, 4), (5, 1), (1, 1), (5, 2), (1, 1),
    (5, 1), (1, 1), (5, 1), (1, 1), (5, 1), (1, 1), (5, 1), (1, 1), (5, 1), (1, 1), (5, 1), (1, 1), (5, 2),
    (1, 1), (5, 1), (1, 1), (5, 1), (1, 1), (5, 1), (1, 1), (5, 1), (1, 1), (5, 1), (1, 1), (5, 1), (1, 1),
    (5, 1), (1, 1), (5, 5), (1, 3), (6, 1), (7, 1), (6, 1), (1, 1), (4, 1), (1, 2), (6, 1), (1, 2), (6, 1),
    (1, 1), (6, 3), (7, 1), (6, 1), (1, 2), (6, 1), (7, 3), (1, 2), (7, 1), (1, 2), (7, 1), (1, 1), (7, 2),
    (3, 1), (1, 2), (6, 18), (8, 1), (6, 1), (8, 1), (6, 1), (8, 1), (2, 1), (8, 1), (6, 2), (8, 1), (3, 1),
    (6, 1), (8, 5), (6, 1), (8, 2), (6, 1), (8, 2), (6, 1), (8, 2), (6, 1), (2, 1), (8, 3), (6, 1), (8, 18),
    (9, 3),
)
N_GATHER_SENDS = 70
FEW = 16


def gelu_pair(gate):
    slope = 0.7978845608028654
    squared = gate * gate
    bent = jnp.tanh(slope * (gate + 0.044715 * gate * squared))
    gelu = 0.5 * gate * (1.0 + bent)
    return gelu, 0.5 * (1.0 + bent) + 0.5 * gate * (1.0 - bent * bent) * slope * (1.0 + 3.0 * 0.044715 * squared)


def scatter_sems(halves, given):
    dma = pltpu.SemaphoreType.DMA
    return [
        dma((halves, 16 * given + 36)), dma((halves, given, 8)), dma((halves, given, 16)), dma((halves, 2, 8)),
        dma((halves, 2, 4)), dma((halves, 2, 3)), dma((halves, 2, 2)),
    ]


def scatter_bufs(rows, width, given):
    half = given * width // 2
    shapes = ((8, rows, given * width), (16, rows, given * width), (2, 8, rows, half), (2, 4, rows, half))
    return [pltpu.VMEM(shape, jnp.bfloat16) for shape in shapes + ((2, 3, rows, half), (2, 2, rows, half))]


class Stage:
    def __init__(self, count, cuts, in_refs, out_refs, in_sems, out_sems):
        self.spot = Spot()
        self.count = count
        self.ranges = [pl.ds(a, b - a) for a, b in zip(cuts[:-1], cuts[1:])]
        self.cuts = cuts
        self.sends = {}
        self.in_refs, self.out_refs, self.in_sems, self.out_sems = in_refs, out_refs, in_sems, out_sems

    def gathering(self, name, at, src, dst, rows, sems, between=False):
        own_sem, ssem, rsem = sems
        self.sends[name] = Sends(ssem.at[at])
        yield from gather_steps(self.spot, src, dst, rows, self.sends[name], rsem.at[at], own_sem.at[at], between)

    def scattering(self, name, p_refs, o_refs, rows, bufs, sems, at):
        self.sends[name] = Sends(sems[0].at[at])
        yield from scatter_steps(
            self.spot, p_refs, o_refs, rows, bufs, [sem.at[at] for sem in sems[1:]], self.sends[name]
        )

    def fetch(self, group, sources, streams=None):
        streams = range(len(sources)) if streams is None else streams
        for i, source in zip(streams, sources):
            there = self.in_refs[i].at[group % 2]
            yield pltpu.make_async_copy(source.at[:, pl.ds(group * FEW, FEW), :], there, self.in_sems.at[i, group % 2])

    def store(self, group, targets):
        for i, target in enumerate(targets):
            there = target.at[:, pl.ds(group * FEW, FEW), :]
            yield pltpu.make_async_copy(self.out_refs[i], there, self.out_sems.at[i])

    def finish(self):
        for some in self.sends.values():
            some.finish()


def start_all(copies):
    for copy in copies:
        copy.start()


def wait_all(copies):
    for copy in copies:
        copy.wait()


def tile_inputs(qkv_ref, col_ref, row_ref, base, length, head):
    query = qkv_ref[pl.ds(base + length, length), :head]
    key = qkv_ref[pl.ds(base, 3 * length), head : 2 * head]
    value = qkv_ref[pl.ds(base, 3 * length), 2 * head :]
    tile = base // length
    return query, key, value, col_ref[:, tile : tile + 1] == row_ref[:, pl.ds(base, 3 * length)]


def at(shape, axis):
    return lax.broadcasted_iota(jnp.int32, shape, axis)


def marked(mask):
    return low(jnp.where(mask, 1.0, 0.0))


def packed_order(size, length, grain):
    shape = (size, size)
    row = at((size, 1), 0)
    return marked(at(shape, 1) == row % length // grain * FEW + row // length * grain + row % grain)


def front_kernel(cuts, *refs):
    tok_ref, cot_ref, index_ref, small_ref = refs[:4]
    weights = refs[4:9]
    wd_ref, wo_ref, bucket_ref, col_ref, row_ref, perm_ref = refs[9:14] + refs[-1:]
    *kept, keep_sems = refs[-17:-1]
    refs = (None,) + refs[:-17]
    (rows_ref, gain_one_ref, bias_ref, first_w_ref, qkv_ref, att_ref, middle_ref, d_mid_ref, d_ref, gain_grad_ref, near_grad_ref,
     far_grad_ref, wd_grad_ref, nx_all_ref, forth_ref) = refs[15:30]
    part_ref, up_all_ref, x_all_ref, back_ref = refs[30:34]
    branch_ref, x_ref, dn_ref, w_ref, nx_ref, up_ref, gain_ref, gate_w_ref = refs[34:42]
    one_ref, two_ref, cot_out_ref, one_in_ref, two_in_ref, cot_in_ref = refs[42:48]
    small_out_ref, all_small_ref, first_ref, second_ref = refs[48:52]
    bufs, two_total_ref, in_refs, out_refs = refs[52:58], refs[58], refs[59:61], refs[61:63]
    in_sems, out_sems = refs[63:65]
    exchanges = refs[65:83]
    one_x, two_x, cot_x, small_x, first_x, second_x = [exchanges[i : i + 3] for i in range(0, 18, 3)]
    g_sems, one_sems, two_sems = refs[83:86], refs[86:93], refs[93:100]
    loads = [
        pltpu.make_async_copy(of, to, keep_sems.at[i])
        for i, (of, to) in enumerate(zip((*weights, cot_ref, wd_ref, wo_ref), kept[:8]))
    ]
    start_all(loads)
    weights, cot_ref, wd_ref, wo_ref = kept[:5], kept[5], kept[6], kept[7]
    results = (first_w_ref, qkv_ref, att_ref, middle_ref, near_grad_ref, far_grad_ref, wd_grad_ref)
    first_w_ref, qkv_ref, att_ref, middle_ref, near_grad_ref, far_grad_ref, wd_grad_ref = kept[8:15]
    saves = [pltpu.make_async_copy(of, to, keep_sems.at[8 + i]) for i, (of, to) in enumerate(zip(kept[8:15], results))]
    two_bufs = (bufs[0], two_total_ref, *bufs[2:])
    count, slots, width = x_all_ref.shape
    stage = Stage(count, cuts, in_refs, out_refs, in_sems, out_sems)
    spot, ranges = stage.spot, stage.ranges
    units, head, length = wd_ref.shape[0], wo_ref.shape[0], bias_ref.shape[0]
    size, piece = one_ref.shape
    folds, share = width // piece, size // count
    grain = share // folds
    groups = cuts[-1] // FEW
    near = units - head
    spot.greet_all(count)
    perm_ref[...] = packed_order(size, length, grain)

    def folded(rows, sources):
        shape = (length, size)
        return low(
            sum(
                over(
                    marked((at(shape, 0) == sources) & (at(shape, 1) % share // grain == i)),
                    rows[:, i * piece : (i + 1) * piece], 0, 0,
                )
                for i in range(folds)
            )
        )

    def pick(shares, to_ref):
        source = index_ref[2:3, :slots]
        for i in range(folds):
            mask = at((size, slots), 0) == source + i * grain
            to_ref[:, i * piece : (i + 1) * piece] = low(over(marked(mask), shares, 0, 0))

    def tokens():
        for i in range(count):
            small_out_ref[i * share : (i + 1) * share, :] = small_ref[...]
        one_ref[...] = folded(tok_ref[...], index_ref[0:1, :])
        swap(spot, count, one_ref, one_in_ref, one_x, "send")
        swap(spot, count, small_out_ref, all_small_ref, small_x, "send")
        yield
        swap(spot, count, one_ref, one_in_ref, one_x, "wait")
        place = index_ref[1:2, :]
        place = jnp.where(place < 0, -1, place // grain * share + place % grain + at((1, size), 1) % share // grain * grain)
        two_ref[...] = low(over(marked(at((size, size), 0) == place), one_in_ref[...], 0, 0))
        swap(spot, count, two_ref, two_in_ref, two_x, "send")
        yield
        swap(spot, count, small_out_ref, all_small_ref, small_x, "wait")
        each = width // count
        shape = (2 * each, width)
        mine = at((size, width), 0) == at((size, width), 1) // each * share
        for i, ref in enumerate((gain_one_ref, gain_ref)):
            fold = marked(at(shape, 0) == at(shape, 1) % each + i * each)
            ref[...] = jnp.sum(jnp.where(mine, over(all_small_ref[...], fold), 0.0), axis=0, keepdims=True)
        table = jnp.where(at(all_small_ref.shape, 1) == spot.me, all_small_ref[...].astype(jnp.float32), 0.0)
        table = jnp.sum(table, axis=1, keepdims=True)
        bias_ref[...] = sum(
            jnp.where(bucket_ref[...] == b, table[b * share + 1 : b * share + 2, :], 0.0) for b in range(BUCKETS)
        )
        yield
        swap(spot, count, two_ref, two_in_ref, two_x, "wait")
        pick(two_in_ref[...], rows_ref)
        v = rows_ref[...].astype(jnp.float32)
        nx_ref[...] = (v * scale_of(v) * gain_one_ref[...]).astype(nx_ref.dtype)
        yield

    def cotangent():
        loads[5].wait()
        cot_out_ref[...] = folded(cot_ref[...], index_ref[1:2, :])
        swap(spot, count, cot_out_ref, cot_in_ref, cot_x, "send")
        yield
        swap(spot, count, cot_out_ref, cot_in_ref, cot_x, "wait")
        pick(cot_in_ref[...], up_ref)
        yield

    def columns(src, dst, sems, packs):
        if packs:
            wait_all(loads[:5])
            pack(weights, first_ref, second_ref)
            yield
        for i in range(0, count, 8):
            swap(spot, count, src, dst, sems, "send", (max(i, 1), i + 8))
            yield
        swap(spot, count, src, dst, sems, "wait")
        if packs:
            gate_w_ref[...] = dst[:, 3 * head :]
            saves[0].start()
            wait_all(loads[6:])
        yield

    def attending(first, last):
        perm = perm_ref[...]
        if first == 0:
            start_all(stage.fetch(0, (nx_all_ref,)))
            qkv_ref[:length, :] = jnp.zeros((length, 3 * head), qkv_ref.dtype)
            qkv_ref[length + groups * size :, :] = jnp.zeros((length, 3 * head), qkv_ref.dtype)
        for step in range(first, last):
            if step < groups:
                if step + 1 < groups:
                    start_all(stage.fetch(step + 1, (nx_all_ref,)))
                wait_all(stage.fetch(step, (nx_all_ref,)))
                rows = low(over(in_refs[0][step % 2].reshape(size, -1), first_w_ref[:, : 3 * head]))
                qkv_ref[length + step * size : length + (step + 1) * size, :] = low(over(perm, rows))
                yield
            if step > 0:
                attended = []
                for tile in range(size // length):
                    base = (step - 1) * size + tile * length
                    query, key, value, same = tile_inputs(qkv_ref, col_ref, row_ref, base, length, head)
                    attended.append(low(over(low(tile_probs(query, key, bias_ref[...], same)), value)))
                    if tile % 2:
                        yield
                rows = low(over(perm, jnp.concatenate(attended, axis=0), 0, 0))
                att_ref[:, (step - 1) * FEW : step * FEW, :] = rows.reshape(count, FEW, head)
                if step > max(first, 1):
                    wait_all(stage.store(step - 2, (part_ref,)))
                for i in range(2):
                    there = pl.ds(i * count // 2, count // 2)
                    piece = over(rows[i * size // 2 : (i + 1) * size // 2], wo_ref[...])
                    out_refs[0][there] = low(piece).reshape(count // 2, FEW, width)
                start_all(stage.store(step - 1, (part_ref,)))
                yield
        if last > max(first, 1):
            wait_all(stage.store(last - 2, (part_ref,)))
        if last > groups:
            start_all(saves[1:3])
        yield

    def rows_of(rows):
        return [pl.ds(rows.start + i, 16) for i in range(0, rows.size, 16)]

    def scale_of(v):
        return lax.rsqrt(jnp.sum(v * v, axis=1, keepdims=True) / width + EPSILON)

    def first_norm(rows):
        for r in rows_of(rows):
            v = rows_ref[r, :].astype(jnp.float32) + branch_ref[r, :]
            middle_ref[r, :] = v
            x_ref[r, :] = (v * scale_of(v) * gain_ref[...]).astype(x_ref.dtype)
        if rows.start + rows.size == slots:
            saves[3].start()
        yield

    def norm_back_rows(rows):
        for r in rows_of(rows):
            v, d, gain = middle_ref[r, :], dn_ref[r, :], gain_ref[...]
            scale = scale_of(v)
            gain_grad_ref[...] += jnp.sum(d * v * scale, axis=0, keepdims=True)
            w = gain * d
            mean = jnp.sum(w * v, axis=1, keepdims=True) / width
            d_mid = up_ref[r, :].astype(jnp.float32) + scale * w - v * (scale * scale * scale) * mean
            d_mid_ref[r, :] = d_mid
            d_ref[r, :] = d_mid.astype(d_ref.dtype)
        yield

    def feeding(first, last):
        sources, targets = (x_all_ref, up_all_ref), (back_ref, forth_ref)
        start_all(stage.fetch(first, sources))
        for group in range(first, last):
            if group + 1 < last:
                start_all(stage.fetch(group + 1, sources))
            wait_all(stage.fetch(group, sources))
            for i in range(2):
                blocks = slice(i * count // 2, (i + 1) * count // 2)
                x = in_refs[0][group % 2, blocks].reshape(size // 2, width)
                upstream = in_refs[1][group % 2, blocks].reshape(size // 2, width)
                both = over(x, w_ref[...])
                gate = jnp.concatenate((over(x, gate_w_ref[...]), both[:, :near]), axis=1)
                up = both[:, near:]
                d_hidden = over(upstream, wd_ref[...], 1, 1)
                gelu, d_gelu = gelu_pair(gate)
                hidden = low(gelu * up)
                d_gate, d_up = low(d_hidden * up * d_gelu), low(d_hidden * gelu)
                d_first, d_both = d_gate[:, :head], jnp.concatenate((d_gate[:, head:], d_up), axis=1)
                if i == 0 and group > first:
                    wait_all(stage.store(group - 1, targets))
                shape = (count // 2, FEW, width)
                back = over(d_both, w_ref[...], 1, 1) + over(d_first, gate_w_ref[...], 1, 1)
                out_refs[0][blocks] = low(back).reshape(shape)
                out_refs[1][blocks] = low(over(hidden, wd_ref[...])).reshape(shape)
                if i:
                    start_all(stage.store(group, targets))
                near_grad_ref[...] += over(d_first, x, 0, 0)
                far_grad_ref[...] += over(d_both, x, 0, 0)
                wd_grad_ref[...] += over(hidden, upstream, 0, 0)
                yield
        wait_all(stage.store(last - 1, targets))
        if last == groups:
            start_all(saves[4:])
        yield

    for ref in (near_grad_ref, far_grad_ref, wd_grad_ref, gain_grad_ref):
        ref[...] = jnp.zeros_like(ref)
    halves = len(ranges)
    everything = pl.ds(0, slots)
    tasks = {
        "tokens": ([], tokens()),
        "cot": ([], cotangent()),
        "first": ([], columns(first_ref, first_w_ref, first_x, True)),
        "second": (["first"], columns(second_ref, w_ref, second_x, False)),
        "gather": (["tokens"], stage.gathering("gather", 0, nx_ref, nx_all_ref, everything, g_sems)),
        "up": (["cot"], stage.gathering("up", 1, up_ref, up_all_ref, everything, g_sems, True)),
    }
    for i, rows in enumerate(ranges):
        h = str(i)
        last_step = groups + 1 if i == halves - 1 else cuts[i + 1] // FEW + 1
        first_step = cuts[i] // FEW + 1 if i else 0
        tasks |= {
            "attend" + h: ([f"attend{i - 1}"] if i else ["gather", "first"], attending(first_step, last_step)),
            "one" + h: (
                ["attend" + h], stage.scattering("one" + h, (part_ref,), (branch_ref,), rows, bufs, one_sems, i),
            ),
            "norm" + h: (["one" + h], first_norm(rows)),
            "x" + h: (["norm" + h], stage.gathering("x" + h, 2 + i, x_ref, x_all_ref, rows, g_sems)),
            "feed" + h: (
                ["x" + h, "up", "second", f"feed{i - 1}" if i else f"attend{halves - 1}"],
                feeding(cuts[i] // FEW, cuts[i + 1] // FEW),
            ),
            "two" + h: (
                ["feed" + h],
                stage.scattering("two" + h, (back_ref,), (dn_ref,), rows, two_bufs, two_sems, i),
            ),
            "back" + h: (["two" + h], norm_back_rows(rows)),
        }
    weave(tasks, FRONT_ORDER)
    wait_all(saves)
    stage.finish()


def halves_of(rows):
    return (0, 48, 80) if rows == 80 else (0, rows)


def front(tok, cot, index, small, weights, wd, wo, buckets, col, row, slots):
    size, (length, width) = index.shape[1], tok.shape
    shard = weights[0].shape[0]
    count, piece = width // shard, length * width // size
    cuts = halves_of(slots)
    halves = len(cuts) - 1
    head, units = wo.shape[0], wd.shape[0]
    low_rows, all_rows, group, share = (slots, width), (count, slots, width), (count, FEW, width), (size, piece)
    first, second = (width, 4 * head), (width, 2 * units - head)
    bf, wide, dma = jnp.bfloat16, jnp.float32, pltpu.SemaphoreType.DMA
    vmem, hbm = pl.BlockSpec(memory_space=pltpu.VMEM), pl.BlockSpec(memory_space=pl.ANY)
    shape = jax.ShapeDtypeStruct
    qkv, attended = (slots // FEW * size + 2 * length, 3 * head), (count, slots, head)
    kept = [pltpu.VMEM(array.shape, bf) for array in (*weights, cot, wd, wo)]
    kept += [pltpu.VMEM(first, bf), pltpu.VMEM(qkv, bf), pltpu.VMEM(attended, bf), pltpu.VMEM(low_rows, wide)]
    kept += [pltpu.VMEM((n, width), wide) for n in (head, second[1], units)]
    outs = pl.pallas_call(
        functools.partial(front_kernel, cuts),
        out_shape=[
            shape(low_rows, bf), shape((1, width), wide), shape(buckets.shape, wide), shape(first, bf),
            shape(qkv, bf), shape(attended, bf), shape(low_rows, wide),
            shape(low_rows, wide), shape(low_rows, bf), shape((1, width), wide), shape((head, width), wide),
            shape((second[1], width), wide), shape(wd.shape, wide),
        ] + [shape(all_rows, bf)] * 6,
        in_specs=[vmem, hbm, vmem, vmem] + [hbm] * 7 + [vmem] * 3,
        out_specs=[vmem] * 3 + [hbm] * 4 + [vmem] * 3 + [hbm] * 9,
        scratch_shapes=[
            pltpu.VMEM(low_rows, wide), pltpu.VMEM(low_rows, bf), pltpu.VMEM(low_rows, wide), pltpu.VMEM(second, bf),
            pltpu.VMEM(low_rows, bf), pltpu.VMEM(low_rows, bf), pltpu.VMEM((1, width), wide), pltpu.VMEM((width, head), bf),
        ] + [pltpu.VMEM(share, bf)] * 6 + [
            pltpu.VMEM((size, 128), bf), pltpu.VMEM((size, 128), bf), pltpu.VMEM(first, bf), pltpu.VMEM(second, bf),
        ] + scatter_bufs(slots, width, 1) + [
            pltpu.VMEM((16, slots, width), bf),
            pltpu.VMEM((2,) + group, bf), pltpu.VMEM((2,) + group, bf), pltpu.VMEM(group, bf), pltpu.VMEM(group, bf),
            dma((2, 2)), dma((2,)),
        ] + [dma((count,)), dma((count,)), dma] * 6 + [
            dma((2 + halves,)), dma((2 + halves, N_GATHER_SENDS)), dma((2 + halves, 2, 32)),
        ] + scatter_sems(halves, 1) * 2 + kept + [dma((15,)), pltpu.VMEM((size, size), bf)],
        name="front",
        compiler_params=pltpu.CompilerParams(collective_id=3, has_side_effects=True, vmem_limit_bytes=63 * 2**20),
    )(tok, cot, index, small, *weights, wd, wo, buckets, col, row)
    return outs[:15]


def rear_kernel(cuts, *refs):
    (d_ref, x_all_ref, att_ref, qkv_ref, w_ref, wo_ref, bias_ref, col_ref, row_ref, near_ref, far_ref, forth_ref, middle_ref,
     rows_ref, d_mid_ref, gain_ref, gain_two_ref, index_ref, bucket_ref) = refs[:19]
    wo_grad_ref, owned_ref, far_owned_ref, out_rows_ref, sums_ref, token_rows_ref = refs[19:25]
    d_all_ref, part_ref = refs[25:27]
    dn_ref, down_ref, bias_grad_ref, dq_ref, dkv_ref, w_grad_ref, turned_ref, far_turned_ref = refs[27:35]
    result_ref, going_ref, came_ref, last_ref, perm_ref = refs[35:40]
    sums_out_ref, *s_sems = refs[-14:-10]
    refs = refs[:-14] + refs[-10:]
    *kept, keep_sems = refs[-10:]
    large = (att_ref, qkv_ref, w_ref, wo_ref, near_ref, far_ref, middle_ref, rows_ref, d_mid_ref)
    loads = [pltpu.make_async_copy(of, to, keep_sems.at[i]) for i, (of, to) in enumerate(zip(large, kept))]
    start_all(loads)
    att_ref, qkv_ref, w_ref, wo_ref, near_ref, far_ref, middle_ref, rows_ref, d_mid_ref = kept
    bufs, other_bufs, in_refs, out_refs = refs[40:46], refs[46:52], refs[52:54], refs[54:55]
    in_sems, out_sems = refs[55:57]
    w_sems, f_sems, r_sems, t_sems, l_sems = [refs[i : i + 3] for i in range(57, 72, 3)]
    g_sems, one_sems, down_sems = refs[72:75], refs[75:82], refs[82:89]
    count, width = part_ref.shape[0], part_ref.shape[2]
    stage = Stage(count, cuts, in_refs, out_refs, in_sems, out_sems)
    spot, ranges = stage.spot, stage.ranges
    spot.greet_all(count)
    head, length, size = wo_ref.shape[0], bias_ref.shape[0], perm_ref.shape[0]
    groups = cuts[-1] // FEW
    piece, share = result_ref.shape[1], size // count
    folds = width // piece
    grain = share // folds
    perm_ref[...] = packed_order(size, length, grain)

    def owners(sources, to_ref, owner_ref, sems, load):
        load.wait()
        merged = jnp.concatenate([low(ref[...]) for ref in sources], axis=0)
        for i in range(0, width, 512):
            to_ref[i : i + 512, :] = merged[:, i : i + 512].T
        swap(spot, count, to_ref, owner_ref, sems, "send")
        yield
        swap(spot, count, to_ref, owner_ref, sems, "wait")
        yield

    def dealt_out(rows):
        shape = (rows.shape[0], size)
        return sum(
            over(
                marked((at(shape, 0) == index_ref[0:1, :]) & (at(shape, 1) % share // grain == i)),
                rows[:, i * piece : (i + 1) * piece], 0, 0,
            )
            for i in range(folds)
        )

    def output():
        loads[6].wait()
        rows = low(middle_ref[...] + down_ref[...])
        result_ref[...] = low(dealt_out(rows))
        swap(spot, count, result_ref, out_rows_ref, r_sems, "send")
        yield
        swap(spot, count, result_ref, out_rows_ref, r_sems, "wait")
        yield

    def scale_of(v):
        return lax.rsqrt(jnp.sum(v * v, axis=1, keepdims=True) / width + EPSILON)

    def shares(*values):
        shape, each = (size, width), width // count
        spread = 0.0
        for i, v in enumerate(values):
            spread += jnp.where(at(shape, 0) == at(shape, 1) // each * share + 2 * i, v, 0.0)
        fold = marked(at((width, each), 0) % each == at((width, each), 1))
        high = low(spread)
        rest = low(spread - high.astype(jnp.float32))
        return jnp.concatenate([over(p, fold) for p in (high, rest)], axis=1)

    def finals():
        wait_all(loads[7:])
        v, d, gain = rows_ref[...].astype(jnp.float32), dn_ref[...], gain_ref[...]
        scale = scale_of(v)
        w = gain * d
        mean = jnp.sum(w * v, axis=1, keepdims=True) / width
        rows = low(d_mid_ref[...] + scale * w - v * (scale * scale * scale) * mean)
        going_ref[...] = low(dealt_out(rows))
        swap(spot, count, going_ref, came_ref, t_sems, "send")
        sums = shares(jnp.sum(d * v * scale, axis=0, keepdims=True), gain_two_ref[...])
        row, lane = at(sums.shape, 0), at(sums.shape, 1)
        for b in range(BUCKETS):
            total = jnp.sum(jnp.where(bucket_ref[...] == b, bias_grad_ref[...], 0.0), axis=(0, 1), keepdims=True)
            high = low(total).astype(jnp.float32)
            sums = sums + jnp.where((row == share * b + 1) & (lane < 2), jnp.where(lane == 0, high, total - high), 0.0)
        sums_out_ref[...] = low(sums)
        swap(spot, count, sums_out_ref, sums_ref, s_sems, "send")
        shape, row, lane = (size, size), at((size, 1), 0), at((1, size), 1)
        turn = (index_ref[1:2, :] == row // share * grain + row % grain) & (row % share // grain == lane % share // grain)
        turn = marked(turn)
        yield
        swap(spot, count, going_ref, came_ref, t_sems, "wait")
        last_ref[...] = low(over(turn, came_ref[...]))
        swap(spot, count, last_ref, token_rows_ref, l_sems, "send")
        yield
        swap(spot, count, sums_out_ref, sums_ref, s_sems, "wait")
        swap(spot, count, last_ref, token_rows_ref, l_sems, "wait")
        yield

    def backing(first, last):
        perm = perm_ref[...]
        if not first:
            wait_all(loads[:4])
        for step in range(first, last):
            if step < groups:
                start_all(stage.fetch(step, (d_all_ref,)))
                start_all(stage.fetch(step, (x_all_ref,), (1,)))
                wait_all(stage.fetch(step, (d_all_ref,)))
                d_branch = in_refs[0][step % 2].reshape(size, width)
                attended = att_ref[:, step * FEW : (step + 1) * FEW, :].reshape(size, head)
                wo_grad_ref[...] += over(attended, d_branch, 0, 0)
                yield
                d_attended = low(over(perm, low(over(d_branch, wo_ref[...], 1, 1))))
                yield
                for tile in range(size // length):
                    base = step * size + tile * length
                    query, key, value, same = tile_inputs(qkv_ref, col_ref, row_ref, base, length, head)
                    probs = tile_probs(query, key, bias_ref[...], same)
                    d_out = d_attended[tile * length : (tile + 1) * length, :]
                    d_probs = over(d_out, value, 1, 1)
                    inner = jnp.sum(probs * d_probs, axis=-1, keepdims=True)
                    d_scores = low(probs * (d_probs - inner))
                    bias_grad_ref[...] += d_scores.astype(jnp.float32)
                    dq_ref[base + length : base + 2 * length, :] = low(over(d_scores, key))
                    both = jnp.concatenate((over(d_scores, query, 0, 0), over(low(probs), d_out, 0, 0)), axis=1)
                    dkv_ref[base : base + 3 * length, :] += both
                    if tile % 2:
                        yield
            if step > 0:
                at = slice(length + (step - 1) * size, length + step * size)
                rows = low(over(perm, jnp.concatenate((dq_ref[at, :], low(dkv_ref[at, :])), axis=1), 0, 0))
                wait_all(stage.fetch(step - 1, (x_all_ref,), (1,)))
                w_grad_ref[...] += over(rows, in_refs[1][(step - 1) % 2].reshape(size, width), 0, 0)
                yield
                if step > max(first, 1):
                    wait_all(stage.store(step - 2, (part_ref,)))
                for i in range(2):
                    there = pl.ds(i * count // 2, count // 2)
                    block = over(rows[i * size // 2 : (i + 1) * size // 2], w_ref[:, : 3 * head], 1, 1)
                    out_refs[0][there] = low(block).reshape(count // 2, FEW, width)
                start_all(stage.store(step - 1, (part_ref,)))
                yield
        if last > max(first, 1):
            wait_all(stage.store(last - 2, (part_ref,)))
        yield

    for ref in (wo_grad_ref, bias_grad_ref, dkv_ref, w_grad_ref):
        ref[...] = jnp.zeros_like(ref)
    halves = len(ranges)
    everything = pl.ds(0, cuts[-1])
    tasks = {
        "d": ([], stage.gathering("d", 0, d_ref, d_all_ref, everything, g_sems)),
        "down": ([], stage.scattering("down", (forth_ref,), (down_ref,), everything, other_bufs, down_sems, 0)),
        "output": (["down"], output()),
        "owners": ([f"back{halves - 1}"], owners((w_grad_ref, near_ref), turned_ref, owned_ref, w_sems, loads[4])),
        "far": ([], owners((far_ref,), far_turned_ref, far_owned_ref, f_sems, loads[5])),
    }
    for i, rows in enumerate(ranges):
        h = str(i)
        first_step = cuts[i] // FEW + 1 if i else 0
        tasks |= {
            "back" + h: ([f"back{i - 1}"] if i else ["d"], backing(first_step, cuts[i + 1] // FEW + 1)),
            "one" + h: (["back" + h], stage.scattering("one" + h, (part_ref,), (dn_ref,), rows, bufs, one_sems, i)),
        }
    tasks["finals"] = ([f"one{i}" for i in range(halves)], finals())
    weave(tasks, REAR_ORDER)
    stage.finish()


def rear(d_rows, normed_all, attended, qkv, w, wo, bias, col, row, near_grad, far_grad, forth, middle, rows_low, d_mid, gain,
         gain_two_grad, index, buckets):
    count, rows, width = normed_all.shape
    cuts = halves_of(rows)
    halves = len(cuts) - 1
    head, size = wo.shape[0], index.shape[1]
    piece, owned, far = bias.shape[0] * width // size, (width, w.shape[1]), (width, far_grad.shape[0])
    all_rows, group, share = (count, rows, width), (count, FEW, width), (size, piece)
    bf, wide, dma = jnp.bfloat16, jnp.float32, pltpu.SemaphoreType.DMA
    vmem, hbm = pl.BlockSpec(memory_space=pltpu.VMEM), pl.BlockSpec(memory_space=pl.ANY)
    shape = jax.ShapeDtypeStruct
    outs = pl.pallas_call(
        functools.partial(rear_kernel, cuts),
        out_shape=[
            shape((head, width), wide), shape(owned, bf), shape(far, bf), shape(share, bf), shape((size, 128), bf),
            shape(share, bf),
        ] + [shape(all_rows, bf)] * 2,
        in_specs=[vmem] + [hbm] * 5 + [vmem] * 3 + [hbm] * 6 + [vmem] * 4,
        out_specs=[vmem] + [hbm] * 7,
        scratch_shapes=[
            pltpu.VMEM((rows, width), wide), pltpu.VMEM((rows, width), wide), pltpu.VMEM(bias.shape, wide),
            pltpu.VMEM((qkv.shape[0], head), bf), pltpu.VMEM((qkv.shape[0], 2 * head), wide),
            pltpu.VMEM((3 * head, width), wide), pltpu.VMEM(owned, bf), pltpu.VMEM(far, bf),
            pltpu.VMEM(share, bf), pltpu.VMEM(share, bf), pltpu.VMEM(share, bf), pltpu.VMEM(share, bf),
            pltpu.VMEM((size, size), bf),
        ] + scatter_bufs(rows, width, 1) * 2 + [
            pltpu.VMEM((2,) + group, bf), pltpu.VMEM((2,) + group, bf), pltpu.VMEM(group, bf),
            dma((2, 2)), dma((1,)),
        ] + [dma((count,)), dma((count,)), dma] * 5 + [
            dma((1,)), dma((1, N_GATHER_SENDS)), dma((1, 2, 32)),
        ] + scatter_sems(halves, 1) + scatter_sems(1, 1) + [
            pltpu.VMEM((size, 128), bf), dma((count,)), dma((count,)), dma,
        ] + [
            pltpu.VMEM(array.shape, array.dtype)
            for array in (attended, qkv, w, wo, near_grad, far_grad, middle, rows_low, d_mid)
        ] + [dma((9,))],
        name="rear",
        compiler_params=pltpu.CompilerParams(collective_id=4, has_side_effects=True, vmem_limit_bytes=63 * 2**20),
    )(d_rows, normed_all, attended, qkv, w, wo, bias, col, row, near_grad, far_grad, forth, middle, rows_low, d_mid, gain,
      gain_two_grad, index, buckets)
    return outs[:6]


def dot(left, right):
    return jnp.dot(left, right, preferred_element_type=jnp.float32)


def select(mask, rows):
    return dot(mask.astype(jnp.bfloat16), rows).astype(jnp.bfloat16)


def unpack_kernel(first_ref, second_ref, query_ref, key_ref, value_ref, gate_ref, up_ref):
    count = first_ref.shape[0]
    head = query_ref.shape[1] // count
    units = gate_ref.shape[1] // count
    wide = jnp.float32
    for j in range(count):
        for i, ref in enumerate((query_ref, key_ref, value_ref)):
            ref[:, j * head : (j + 1) * head] = first_ref[j, :, i * head : (i + 1) * head].astype(wide)
        gate_ref[:, j * units : j * units + head] = first_ref[j, :, 3 * head :].astype(wide)
        gate_ref[:, j * units + head : (j + 1) * units] = second_ref[j, :, : units - head].astype(wide)
        up_ref[:, j * units : (j + 1) * units] = second_ref[j, :, units - head :].astype(wide)


def unpack(first, second, width, hidden):
    rows = first.shape[1]
    widths = (width, width, width, hidden, hidden)
    return pl.pallas_call(
        unpack_kernel,
        out_shape=[jax.ShapeDtypeStruct((rows, columns), jnp.float32) for columns in widths],
        in_specs=[pl.BlockSpec(memory_space=pltpu.VMEM)] * 2,
        out_specs=[pl.BlockSpec(memory_space=pltpu.VMEM)] * 5,
        name="unpack_columns",
        compiler_params=pltpu.CompilerParams(vmem_limit_bytes=32 * 2**20),
    )(first, second)


def body(
    tokens,
    lengths,
    permutation,
    query_weight,
    key_weight,
    value_weight,
    out_weight,
    gate_weight,
    up_weight,
    down_weight,
    gain_attention,
    gain_feedforward,
    bias_table,
    cotangent,
):
    me = lax.axis_index(AXIS)
    count = tokens.shape[0]
    grain = tokens.shape[1]
    length = cotangent.shape[1]
    width = tokens.shape[2]
    shard = query_weight.shape[0]
    hidden_width = gate_weight.shape[1] // count
    head = HEAD_DIM
    total = 3 * count * length // 5
    tiles = -(-total // length)
    slots = tiles * grain

    dealt_lengths = lengths[permutation]
    ends = jnp.cumsum(dealt_lengths)
    starts = ends - dealt_lengths
    this = jnp.arange(count, dtype=jnp.int32) == me
    my_start = jnp.sum(jnp.where(this, starts, 0), keepdims=True)
    my_length = jnp.sum(jnp.where(this, dealt_lengths, 0), keepdims=True)
    place_in = jnp.arange(length, dtype=jnp.int32)
    slot_ids = jnp.arange(slots, dtype=jnp.int32)
    packed_ids = slot_ids // grain * length + me * grain + slot_ids % grain
    source_seq = jnp.sum((packed_ids[:, None] >= ends[None, :]).astype(jnp.int32), axis=1)

    few = 16
    folds = few // grain
    piece = width // folds
    share = jnp.arange(few * count, dtype=jnp.int32)
    share_row, share_fold = share // few * grain + share % grain, share % few // grain
    position = share_row - my_start % length
    position = jnp.where(position < 0, position + length, position)
    in_share = jnp.arange(few, dtype=jnp.int32)[None, :] % grain
    index = jnp.stack(
        (
            (permutation[:, None] * grain + in_share).reshape(-1),
            jnp.where(position < my_length, position, -1),
            jnp.pad(jnp.where(source_seq < count, source_seq * few + slot_ids % grain, -few), (0, few * count - slots)),
        )
    )
    small = jnp.concatenate((gain_attention, gain_feedforward, bias_table))
    small = jnp.pad(small, (0, few * 128 - small.shape[0])).reshape(few, 128)
    all_ids = jnp.arange(tiles * length, dtype=jnp.int32)
    segment = jnp.sum((all_ids[:, None] >= ends[None, :]).astype(jnp.int32), axis=1) + 1
    column, row = segment.reshape(tiles, length).T, jnp.pad(segment, (length, length))[None, :]
    relative = (
        jnp.arange(3 * length, dtype=jnp.int32)[None, :] - length - place_in[:, None]
    ).reshape(-1)
    onehot = bucket_index(relative)[None, :] == jnp.arange(BUCKETS, dtype=jnp.int32)[:, None]
    buckets = bucket_index(relative).reshape(length, -1)
    (rows_low, gain_one, rel_bias, first_columns, qkv, attended, middle, d_middle, d_low, gain_two_grad, near_grad, far_grad,
     down_grad, normed_all, forth) = front(
        tokens.reshape(length, width), cotangent[0], index, small,
        (query_weight, key_weight, value_weight, gate_weight, up_weight), down_weight, out_weight, buckets, column, row, slots,
    )
    turned = me * grain + in_share - starts[:, None] % length
    turned = starts[:, None] + jnp.where(turned < 0, turned + length, turned)
    back_slot = (turned // length * grain + in_share).reshape(-1)

    out_grad, first_grad, second_grad, out_rows, sums, token_rows = rear(
        d_low, normed_all, attended, qkv, first_columns, out_weight, rel_bias, column, row, near_grad, far_grad, forth, middle,
        rows_low, d_middle, gain_one, gain_two_grad, jnp.stack((back_slot, index[1])), buckets,
    )
    first_grad, second_grad = first_grad.reshape(count, shard, -1), second_grad.reshape(count, shard, -1)
    sums = sums.reshape(count, few, -1).astype(jnp.float32)
    gain_sums = jnp.sum(sums, axis=0)
    gain_attention_grad = gain_sums[0, :shard] + gain_sums[0, shard : 2 * shard]
    gain_feedforward_grad = gain_sums[2, :shard] + gain_sums[2, shard : 2 * shard]
    table_grad = sums[:, 1, 0] + sums[:, 1, 1]

    def whole_rows(shares):
        return shares.reshape(count, folds, grain, piece).transpose(0, 2, 1, 3).reshape(count, grain, width)

    place = place_in - my_start % length
    place = jnp.where(place < 0, place + length, place)
    turned_back = (place[None, :] == place_in[:, None]) & (place_in[:, None] < my_length)
    layer_output = select(turned_back, whole_rows(out_rows).reshape(length, width))[None]
    ids = jnp.arange(count, dtype=jnp.int32)
    dealt_slot = jnp.sum(jnp.where(permutation[None, :] == ids[:, None], ids[None, :], 0), axis=1)
    tokens_grad = whole_rows(token_rows)[dealt_slot]
    query_grad, key_grad, value_grad, gate_grad, up_grad = unpack(
        first_grad, second_grad, width, hidden_width * count
    )
    return (
        layer_output,
        tokens_grad,
        query_grad,
        key_grad,
        value_grad,
        out_grad,
        gate_grad,
        up_grad,
        down_grad,
        gain_attention_grad,
        gain_feedforward_grad,
        table_grad,
    )


def solution(mesh):
    placed = (
        P(None, "fsdp", None),
        P(),
        P(),
        P("fsdp", None),
        P("fsdp", None),
        P("fsdp", None),
        P("fsdp", None),
        P("fsdp", None),
        P("fsdp", None),
        P("fsdp", None),
        P("fsdp"),
        P("fsdp"),
        P("fsdp"),
        P("fsdp", None, None),
    )
    return jax.shard_map(
        body if mesh.shape[AXIS] == 32 else body_any,
        mesh=mesh,
        in_specs=placed,
        out_specs=(
            P("fsdp", None, None),
            P(None, "fsdp", None),
            P("fsdp", None),
            P("fsdp", None),
            P("fsdp", None),
            P("fsdp", None),
            P("fsdp", None),
            P("fsdp", None),
            P("fsdp", None),
            P("fsdp"),
            P("fsdp"),
            P("fsdp"),
        ),
        check_vma=False,
    )
```

```python
import functools

import jax
import jax.numpy as jnp
from jax import lax
from jax.experimental import pallas as pl
from jax.experimental.pallas import tpu as pltpu
from jax.sharding import PartitionSpec as P

HEADS = 32
HEAD_DIM = 64
BUCKETS = 32


EPSILON = 1e-06
masked_score = -1000000000.0
HIGHEST = lax.Precision.HIGHEST


def bucket_index(relative):
    half_buckets = BUCKETS // 2
    exact_count = half_buckets // 2
    distance = jnp.abs(relative)
    side_offset = jnp.where(relative > 0, half_buckets, 0).astype(jnp.int32)
    square = distance * distance
    far_bucket = jnp.full_like(distance, exact_count)
    for doubling in range(1, half_buckets - exact_count):
        far_bucket = far_bucket + (square >= exact_count * exact_count * 2**doubling).astype(
            jnp.int32
        )
    return side_offset + jnp.where(distance < exact_count, distance, far_bucket)


def bucket_onehot(seq_len):
    positions = jnp.arange(seq_len, dtype=jnp.int32)
    relative = (positions[None, :] - positions[:, None]).reshape(-1)
    bucket_ids = jnp.arange(BUCKETS, dtype=jnp.int32)
    return (bucket_index(relative)[None, :] == bucket_ids[:, None]).astype(jnp.float32)


def norm_scale(values):
    return lax.rsqrt(jnp.mean(values * values, axis=-1, keepdims=True) + EPSILON)


def norm_back(values, scale, gain_vec, d_norm):
    weighted = gain_vec * d_norm
    return scale * weighted - values * (scale * scale * scale) * jnp.mean(
        weighted * values, axis=-1, keepdims=True
    )


def rows_product(left, right):
    return lax.dot_general(
        left, right, (((0,), (0,)), ((), ())), preferred_element_type=jnp.float32
    )


def against_rows(left, right):
    return lax.dot_general(
        left, right, (((1,), (1,)), ((), ())), preferred_element_type=jnp.float32
    )


def masked_scores(query_heads, key_heads, rel_bias, length):
    scores = (
        jnp.einsum("qhd,khd->hqk", query_heads, key_heads, preferred_element_type=jnp.float32)
        + rel_bias
    )
    key_valid = jnp.arange(key_heads.shape[0], dtype=jnp.int32) < length
    return jnp.where(key_valid[None, None, :], scores, masked_score)


def unpack_weights(full_weights, onehot, seq_len):
    table_full = full_weights[4].astype(jnp.float32).reshape(BUCKETS, HEADS)
    rel_bias = jnp.dot(table_full.T, onehot, precision=HIGHEST).reshape(HEADS, seq_len, seq_len)
    return (
        full_weights[0],
        full_weights[1],
        full_weights[2].astype(jnp.float32),
        full_weights[3].astype(jnp.float32),
        rel_bias,
    )


def body_any(
    tokens,
    lengths,
    permutation,
    query_weight,
    key_weight,
    value_weight,
    out_weight,
    gate_weight,
    up_weight,
    down_weight,
    gain_attention,
    gain_feedforward,
    bias_table,
    cotangent,
):
    model_width = query_weight.shape[1]
    hidden_width = gate_weight.shape[1]
    packed = jnp.concatenate(
        (query_weight, key_weight, value_weight, out_weight, gate_weight, up_weight), axis=1
    )
    shards = (packed, down_weight, gain_attention, gain_feedforward, bias_table)
    full_weights = (
        lax.all_gather(shards[0], "fsdp", axis=0, tiled=True),
        lax.all_gather(shards[1], "fsdp", axis=0, tiled=True),
        lax.all_gather(shards[2], "fsdp", axis=0, tiled=True),
        lax.all_gather(shards[3], "fsdp", axis=0, tiled=True),
        lax.all_gather(shards[4], "fsdp", axis=0, tiled=True),
    )
    reordered = tokens[permutation]
    dealt = lax.all_to_all(reordered, "fsdp", split_axis=0, concat_axis=1, tiled=True)
    seq_count = dealt.shape[0]
    seq_len = dealt.shape[1]
    local_ids = lax.dynamic_slice_in_dim(permutation, lax.axis_index("fsdp") * seq_count, seq_count)
    seq_lengths = lengths[local_ids]
    positions = jnp.arange(seq_len, dtype=jnp.int32)
    row_valid = (positions[None, :] < seq_lengths[:, None]).astype(jnp.float32).reshape(-1, 1)
    onehot = bucket_onehot(seq_len)
    onehot_low = onehot.astype(jnp.bfloat16)
    full_packed, full_down, gain_one, gain_two, rel_bias = unpack_weights(
        full_weights, onehot, seq_len
    )
    head_shape = (seq_count, seq_len, HEADS, HEAD_DIM)
    rows_in = dealt.reshape(-1, model_width).astype(jnp.float32)
    scale_one = norm_scale(rows_in)
    normed = (rows_in * scale_one * gain_one).astype(jnp.bfloat16)
    projected = jnp.dot(
        normed, full_packed[:, : 3 * model_width], preferred_element_type=jnp.float32
    ).astype(jnp.bfloat16)
    query_heads = projected[:, :model_width].reshape(head_shape)
    key_heads = projected[:, model_width : 2 * model_width].reshape(head_shape)
    value_heads = projected[:, 2 * model_width :].reshape(head_shape)

    def attend_forward(pieces):
        query_one, key_one, value_one, length = pieces
        scores = masked_scores(query_one, key_one, rel_bias, length)
        row_max = jnp.max(scores, axis=-1, keepdims=True)
        exp_total = jnp.sum(jnp.exp(scores - row_max), axis=-1, keepdims=True)
        log_total = row_max + jnp.log(exp_total)
        weights_soft = jnp.exp(scores - log_total).astype(jnp.bfloat16)
        attended_one = jnp.einsum(
            "hqk,khd->qhd", weights_soft, value_one, preferred_element_type=jnp.float32
        )
        return (attended_one.astype(jnp.bfloat16), log_total)

    attended_heads, log_totals = lax.map(
        attend_forward, (query_heads, key_heads, value_heads, seq_lengths)
    )
    attended_rows = attended_heads.reshape(-1, model_width)
    middle = rows_in + jnp.dot(
        attended_rows,
        full_packed[:, 3 * model_width : 4 * model_width],
        preferred_element_type=jnp.float32,
    )
    scale_two = norm_scale(middle)
    normed_two = (middle * scale_two * gain_two).astype(jnp.bfloat16)
    gate_up = jnp.dot(
        normed_two, full_packed[:, 4 * model_width :], preferred_element_type=jnp.float32
    )

    def gelu_product(gate_part, up_part):
        return jax.nn.gelu(gate_part, approximate=True) * up_part

    hidden_full, gelu_pull = jax.vjp(
        gelu_product, gate_up[:, :hidden_width], gate_up[:, hidden_width:]
    )
    hidden = hidden_full.astype(jnp.bfloat16)
    result = middle + jnp.dot(hidden, full_down, preferred_element_type=jnp.float32)
    layer_output = (
        (result * row_valid).astype(jnp.bfloat16).reshape(seq_count, seq_len, model_width)
    )
    full_weights = (
        lax.all_gather(shards[0], "fsdp", axis=0, tiled=True),
        lax.all_gather(shards[1], "fsdp", axis=0, tiled=True),
        lax.all_gather(shards[2], "fsdp", axis=0, tiled=True),
        lax.all_gather(shards[3], "fsdp", axis=0, tiled=True),
        lax.all_gather(shards[4], "fsdp", axis=0, tiled=True),
    )
    full_packed, full_down, gain_one, gain_two, rel_bias = unpack_weights(
        full_weights, onehot, seq_len
    )
    upstream = cotangent.reshape(-1, model_width).astype(jnp.float32) * row_valid
    upstream_low = upstream.astype(jnp.bfloat16)
    d_hidden = against_rows(upstream_low, full_down)
    d_gate, d_up = gelu_pull(d_hidden)
    d_gate_up = jnp.concatenate((d_gate, d_up), axis=1).astype(jnp.bfloat16)
    d_normed_two = against_rows(d_gate_up, full_packed[:, 4 * model_width :])
    gain_two_grad = jnp.sum(d_normed_two * middle * scale_two, axis=0)
    d_middle = upstream + norm_back(middle, scale_two, gain_two, d_normed_two)
    d_branch = d_middle.astype(jnp.bfloat16)
    d_attended = against_rows(d_branch, full_packed[:, 3 * model_width : 4 * model_width]).astype(
        jnp.bfloat16
    )

    def attend_backward(pieces):
        query_one, key_one, value_one, length, log_total, d_attended_one = pieces
        scores = masked_scores(query_one, key_one, rel_bias, length)
        probs = jnp.exp(scores - log_total)
        probs_low = probs.astype(jnp.bfloat16)
        d_value = jnp.einsum(
            "hqk,qhd->khd", probs_low, d_attended_one, preferred_element_type=jnp.float32
        )
        d_probs = jnp.einsum(
            "qhd,khd->hqk", d_attended_one, value_one, preferred_element_type=jnp.float32
        )
        inner = jnp.sum(probs * d_probs, axis=-1, keepdims=True)
        d_scores = (probs * (d_probs - inner)).astype(jnp.bfloat16)
        d_query = jnp.einsum("hqk,khd->qhd", d_scores, key_one, preferred_element_type=jnp.float32)
        d_key = jnp.einsum("hqk,qhd->khd", d_scores, query_one, preferred_element_type=jnp.float32)
        d_bias = against_rows(d_scores.reshape(HEADS, -1), onehot_low)
        return (
            (
                d_query.astype(jnp.bfloat16),
                d_key.astype(jnp.bfloat16),
                d_value.astype(jnp.bfloat16),
            ),
            d_bias,
        )

    (d_query_all, d_key_all, d_value_all), d_bias_all = lax.map(
        attend_backward,
        (
            query_heads,
            key_heads,
            value_heads,
            seq_lengths,
            log_totals,
            d_attended.reshape(head_shape),
        ),
    )
    d_qkv = jnp.concatenate(
        (
            d_query_all.reshape(-1, model_width),
            d_key_all.reshape(-1, model_width),
            d_value_all.reshape(-1, model_width),
        ),
        axis=1,
    )
    d_normed = against_rows(d_qkv, full_packed[:, : 3 * model_width])
    gain_one_grad = jnp.sum(d_normed * rows_in * scale_one, axis=0)
    d_rows = d_middle + norm_back(rows_in, scale_one, gain_one, d_normed)
    d_dealt = d_rows.astype(jnp.bfloat16).reshape(seq_count, seq_len, model_width)
    returned_rows = lax.all_to_all(d_dealt, "fsdp", split_axis=1, concat_axis=0, tiled=True)
    tokens_grad = returned_rows[jnp.argsort(permutation)]
    packed_grad = lax.psum_scatter(
        jnp.concatenate(
            (
                rows_product(normed, d_qkv),
                jnp.concatenate(
                    (rows_product(attended_rows, d_branch), rows_product(normed_two, d_gate_up)),
                    axis=1,
                ),
            ),
            axis=1,
        ),
        "fsdp",
        scatter_dimension=0,
        tiled=True,
    )
    mixer_grad = packed_grad[:, : 3 * model_width]
    branch_grad = packed_grad[:, 3 * model_width :]
    down_grad = lax.psum_scatter(
        rows_product(hidden, upstream_low), "fsdp", scatter_dimension=0, tiled=True
    )
    table_sum = jnp.sum(d_bias_all, axis=0).T.reshape(-1)
    gain_attention_grad, gain_feedforward_grad, table_grad = (
        lax.psum_scatter(gain_one_grad, "fsdp", scatter_dimension=0, tiled=True),
        lax.psum_scatter(gain_two_grad, "fsdp", scatter_dimension=0, tiled=True),
        lax.psum_scatter(table_sum, "fsdp", scatter_dimension=0, tiled=True),
    )
    return (
        layer_output,
        tokens_grad,
        mixer_grad[:, :model_width],
        mixer_grad[:, model_width : 2 * model_width],
        mixer_grad[:, 2 * model_width :],
        branch_grad[:, :model_width],
        branch_grad[:, model_width : model_width + hidden_width],
        branch_grad[:, model_width + hidden_width :],
        down_grad,
        gain_attention_grad,
        gain_feedforward_grad,
        table_grad,
    )


MESH = pl.DeviceIdType.MESH
AXIS = "fsdp"


def over(left, right, left_dim=1, right_dim=0):
    return lax.dot_general(
        left, right, (((left_dim,), (right_dim,)), ((), ())), preferred_element_type=jnp.float32
    )


def low(values):
    return values.astype(jnp.bfloat16)


def tile_probs(query, key, bias, same):
    scores = jnp.where(same, over(query, key, 1, 1) + bias, masked_score)
    grown = jnp.exp(scores - jnp.max(scores, axis=-1, keepdims=True))
    return grown / jnp.sum(grown, axis=-1, keepdims=True)


class Spot:
    def __init__(self):
        me = lax.axis_index(AXIS)
        c, x, y, z = me % 2, (me // 2) % 2, (me // 4) % 2, me // 8
        self.me = me
        self.mid = (z == 1) | (z == 2)
        self.end = jnp.logical_not(self.mid)
        self.zs = (z, z + 1 - 2 * (z % 2), 2 - z // 2, 3 - 3 * (z // 2))
        self.shift = [8 * (zz - z) for zz in self.zs]
        self.core, self.x, self.y = me + 1 - 2 * c, me + 2 - 4 * x, me + 4 - 8 * y
        self.diag = self.x + self.y - me
        self.n1, self.n2 = me + self.shift[1], me + self.shift[2]

    def greet(self):
        bar = pltpu.get_barrier_semaphore()
        for peer in (self.core, self.x, self.y, self.n1):
            pl.semaphore_signal(bar, inc=1, device_id=(peer,), device_id_type=MESH)

        @pl.when(self.mid)
        def _():
            pl.semaphore_signal(bar, inc=1, device_id=(self.n2,), device_id_type=MESH)

        pl.semaphore_wait(bar, 4 + self.mid.astype(jnp.int32))

    def greet_all(self, count):
        bar = pltpu.get_barrier_semaphore()

        def signal(d, _):
            peer = (self.me + d) % count
            pl.semaphore_signal(bar, inc=1, device_id=(peer,), device_id_type=MESH)
            return _

        lax.fori_loop(1, count, signal, 0)
        pl.semaphore_wait(bar, count - 1)


class Sends:
    def __init__(self, sems):
        self.sems, self.used, self.open = sems, 0, []

    def push(self, src, dst, rsem, peer, when=None):
        ssem = self.sems.at[self.used]
        self.used += 1

        def copy():
            return pltpu.make_async_remote_copy(
                src, dst, ssem, rsem, device_id=(peer,), device_id_type=MESH
            )

        if when is None:
            copy().start()
        else:
            pl.when(when)(lambda: copy().start())
        self.open.append((lambda: copy().wait_send(), when))

    def finish(self):
        for wait, when in self.open:
            if when is None:
                wait()
            else:
                pl.when(when)(wait)
        self.open = []


def arrive(dst, rsem, spot):
    pltpu.make_async_remote_copy(
        dst, dst, rsem, rsem, device_id=(spot.core,), device_id_type=MESH
    ).wait_recv()


def gather_steps(spot, src, dst, rows, sends, rsem, own_sem, between=False):
    half = src.shape[1] // 2
    cols = (pl.ds(0, half), pl.ds(half, half))
    me, mid, shift = spot.me, spot.mid, spot.shift
    first, last = (spot.x, spot.y), (spot.y, spot.x)
    own = pltpu.make_async_copy(src.at[rows, :], dst.at[me, rows, :], own_sem)
    own.start()

    def push(part, block, peer, mine=False, when=None):
        there = dst.at[block, rows, cols[part]]
        here = src.at[rows, cols[part]] if mine else there
        sends.push(here, there, rsem.at[part, block], peer, when)

    def landed(part, block):
        arrive(dst.at[block, rows, cols[part]], rsem.at[part, block], spot)

    for part in (0, 1):
        push(part, me, spot.n1, True)
        push(part, me, spot.n2, True, mid)
        push(part, me, first[part], True)
        push(part, me, last[part], True)
    for part in (0, 1):
        push(part, me, spot.core, True)
    yield

    def from_z(part, j):
        b = me + shift[j]
        landed(part, b)
        push(part, b, spot.n2 if j == 1 else spot.n1, when=mid)
        push(part, b, first[part])
        push(part, b, last[part])
        push(part, b, spot.core)

    def from_first(part, j):
        b = first[part] + shift[j]
        landed(part, b)
        push(part, b, last[part])
        push(part, b, spot.core)

    def from_last(part, b):
        landed(part, b)
        push(part, b, spot.core)

    def from_side(part):
        b = first[part]
        landed(part, b)
        push(part, b, spot.n1)
        push(part, b, spot.n2, when=mid)
        push(part, b, last[part])
        push(part, b, spot.core)

    def along_z(part, base, j):
        b = base + shift[j]
        landed(part, b)
        push(part, b, spot.n2 if j == 1 else spot.n1, when=mid)
        push(part, b, last[part])
        push(part, b, spot.core)

    if between:
        for part in (0, 1):
            from_side(part)
            yield
        for j in range(1, 5):
            if j < 4:
                for part in (0, 1):
                    along_z(part, me, j)
                    yield
                for part in (0, 1):
                    along_z(part, first[part], j)
                    yield
            for part in (0, 1):
                from_last(part, last[part] + shift[j - 1])
                from_last(part, spot.diag + shift[j - 1])
                yield
    else:
        for j in range(4):
            if j:
                for part in (0, 1):
                    from_z(part, j)
                    yield
            for part in (0, 1):
                from_first(part, j)
                yield
            if j:
                for part in (0, 1):
                    from_last(part, last[part] + shift[j - 1])
                    yield
        for part in (0, 1):
            from_last(part, last[part] + shift[3])
            yield
        for j in range(4):
            for part in (0, 1):
                from_last(part, spot.diag + shift[j])
                yield
    for j in range(4):
        for base in (me, spot.x, spot.y, spot.diag):
            for part in (0, 1):
                landed(part, base + spot.core - me + shift[j])
    own.wait()
    yield


def scatter_steps(spot, p_refs, o_refs, rows, bufs, sems, sends):
    ring_ref, s_ref, first_ref, second_ref, za_ref, zb_ref = bufs
    lsem, csem, fsem, gsem, zasem, zbsem = sems
    given = len(p_refs)
    width = p_refs[0].shape[2]
    half = given * width // 2
    me, mid, end, zs = spot.me, spot.mid, spot.end, spot.zs
    cols, short = (pl.ds(0, half), pl.ds(half, half)), pl.ds(0, half)
    plane = (me, spot.x, spot.y, spot.diag)
    first_peer, second_peer = (spot.y, spot.x), (spot.x, spot.y)
    start, size = rows.start, rows.size

    def mine(q, j, part):
        return s_ref.at[q * 4 + zs[j], rows, cols[part]]

    def held(ref, part, slot):
        return ref.at[part, slot, rows, short]

    def chunks(count, step):
        lax.fori_loop(0, size // 16, lambda i, _: step(pl.ds(pl.multiple_of(start + i * 16, 16), 16)) or _, 0)

    def add(q, j, part, *more):
        def step(r):
            v = s_ref[q * 4 + zs[j], r, cols[part]].astype(jnp.float32)
            for ref, slot in more:
                v = v + ref[part, slot, r, short].astype(jnp.float32)
            s_ref[q * 4 + zs[j], r, cols[part]] = v.astype(s_ref.dtype)

        chunks(size, step)

    def pair_exchange(j):
        for q in (3, 2, 1, 0):
            b = plane[q] + spot.shift[j]
            slot = q * 4 + zs[j]
            for i, p_ref in enumerate(p_refs):
                own = pl.ds(i * width, width)
                sends.push(p_ref.at[b + spot.core - me, rows, :], s_ref.at[slot, rows, own], csem.at[i, slot], spot.core)
                here = ring_ref.at[j % 2 * 4 + q, rows, own]
                pltpu.make_async_copy(p_ref.at[b, rows, :], here, lsem.at[i, j % 2 * 4 + q]).start()

    def joined(q, j):
        slot, near = q * 4 + zs[j], j % 2 * 4 + q
        for i, p_ref in enumerate(p_refs):
            own = pl.ds(i * width, width)
            pltpu.make_async_copy(p_ref.at[0, rows, :], ring_ref.at[near, rows, own], lsem.at[i, near]).wait()
            arrive(s_ref.at[slot, rows, own], csem.at[i, slot], spot)
        everything = pl.ds(0, given * width)

        def step(r):
            v = ring_ref[near, r, everything].astype(jnp.float32) + s_ref[slot, r, everything].astype(jnp.float32)
            s_ref[slot, r, everything] = v.astype(s_ref.dtype)

        chunks(size, step)

    def to_first(part, q, j):
        slot = (4 if q == 3 else 0) + zs[j]
        sends.push(mine(q, j, part), held(first_ref, part, slot), fsem.at[part, slot], first_peer[part])

    def first_stage(j):
        joined(3, j)
        if j:
            pair_exchange(j - 1)
        to_first(0, 3, j)
        to_first(1, 3, j)
        yield
        joined(2, j)
        to_first(0, 2, j)
        yield
        joined(1, j)
        to_first(1, 1, j)
        joined(0, j)
        yield

    def second_stage(j):
        for part in (0, 1):
            q, slot = (1, 2)[part], 4 + zs[j]
            arrive(held(first_ref, part, slot), fsem.at[part, slot], spot)
            add(q, j, part, (first_ref, slot))
            sends.push(mine(q, j, part), held(second_ref, part, zs[j]), gsem.at[part, zs[j]], second_peer[part])
            yield

    def z_send(j):
        for part in (0, 1):
            arrive(held(first_ref, part, zs[j]), fsem.at[part, zs[j]], spot)
            arrive(held(second_ref, part, zs[j]), gsem.at[part, zs[j]], spot)
            add(0, j, part, (first_ref, zs[j]), (second_ref, zs[j]))
            if j:
                sends.push(mine(0, j, part), held(za_ref, part, 3 - j), zasem.at[part, 3 - j], spot.n1, end)
            yield

    def z_relay(j):
        if not j:
            return
        for part in (0, 1):
            came, sem, slot = (za_ref, zasem, 3 - j) if j > 1 else (zb_ref, zbsem, 0)

            @pl.when(mid)
            def _():
                arrive(held(came, part, slot), sem.at[part, slot], spot)
                add(0, j, part, (came, slot))

            slot = 3 - j if j > 1 else 0
            peer = spot.n2 if j > 1 else spot.n1
            sends.push(mine(0, j, part), held(zb_ref, part, slot), zbsem.at[part, slot], peer, mid)
            yield

    pair_exchange(3)
    yield
    stages = (first_stage, second_stage, z_send, z_relay)
    for step in range(4 + len(stages) - 1):
        for stage, what in enumerate(stages):
            j = 3 - (step - stage)
            if 0 <= j <= 3:
                yield from what(j)
    for part in (0, 1):
        o_ref, there = (o_refs[part], pl.ds(0, half)) if given == 2 else (o_refs[0], cols[part])

        def total(*more):
            def step(r):
                v = s_ref[zs[0], r, cols[part]].astype(jnp.float32)
                for ref, slot in more:
                    v = v + ref[part, slot, r, short].astype(jnp.float32)
                o_ref[r, there] = v

            chunks(size, step)

        @pl.when(mid)
        def _():
            arrive(held(za_ref, part, 2), zasem.at[part, 2], spot)
            arrive(held(zb_ref, part, 1), zbsem.at[part, 1], spot)
            total((za_ref, 2), (zb_ref, 1))

        @pl.when(end)
        def _():
            arrive(held(zb_ref, part, 0), zbsem.at[part, 0], spot)
            total((zb_ref, 0))

        yield


def swap(spot, count, src, dst, sems, what, some=None):
    begin, end = some or (1, count)
    send_sem, recv_sem, own_sem = sems
    share = src.shape[0] // count

    def part(ref, index):
        return ref.at[pl.ds(pl.multiple_of(index * share, share), share), :]

    def own():
        return pltpu.make_async_copy(part(src, spot.me), part(dst, spot.me), own_sem)

    def one(d, _):
        peer, source = (spot.me + d) % count, (spot.me + count - d) % count
        if what == "send":
            pltpu.make_async_remote_copy(
                part(src, peer), part(dst, spot.me), send_sem.at[peer], recv_sem.at[spot.me], device_id=(peer,),
                device_id_type=MESH,
            ).start()
        else:
            copy = pltpu.make_async_remote_copy(
                part(src, peer), part(dst, source), send_sem.at[peer], recv_sem.at[source], device_id=(peer,),
                device_id_type=MESH,
            )
            copy.wait_recv()
            copy.wait_send()
        return _

    if what == "send" and begin == 1:
        own().start()
    lax.fori_loop(begin, end, one, 0)
    if what == "wait" and end == count:
        own().wait()


def pack(weights, first_ref, second_ref):
    query_ref, key_ref, value_ref, gate_ref, up_ref = weights
    rows = query_ref.shape[0]
    count = first_ref.shape[0] // rows
    head, units = query_ref.shape[1] // count, gate_ref.shape[1] // count
    for j in range(count):
        there = pl.ds(j * rows, rows)
        for i, ref in enumerate((query_ref, key_ref, value_ref)):
            first_ref[there, i * head : (i + 1) * head] = ref[:, j * head : (j + 1) * head]
        first_ref[there, 3 * head :] = gate_ref[:, j * units : j * units + head]
        second_ref[there, : units - head] = gate_ref[:, j * units + head : (j + 1) * units]
        second_ref[there, units - head :] = up_ref[:, j * units : (j + 1) * units]


def weave(tasks, order):
    names = list(tasks)
    left = {name: steps for name, (_, steps) in tasks.items()}

    def advance(name):
        for other in tasks[name][0]:
            if other in left:
                advance(other)
                assert other not in left, name
        if name in left and next(left[name], left) is left:
            del left[name]

    for number, times in order:
        for _ in range(times):
            advance(names[number])
    while left:
        name = next(n for n in left if not any(other in left for other in tasks[n][0]))
        while name in left:
            advance(name)


FRONT_ORDER = (
    (0, 2), (2, 3), (0, 1), (2, 2), (0, 1), (4, 5), (2, 1), (4, 20), (1, 1), (4, 7), (6, 1), (3, 1), (6, 8),
    (1, 1), (5, 1), (6, 5), (5, 2), (7, 6), (13, 1), (7, 1), (13, 1), (7, 1), (13, 1), (5, 1), (13, 2), (7,
    4), (13, 3), (5, 1), (14, 1), (7, 1), (5, 2), (7, 1), (14, 6), (5, 1), (7, 1), (5, 1), (7, 2), (5, 1),
    (14, 1), (5, 1), (14, 1), (5, 1), (14, 3), (5, 1), (14, 1), (3, 1), (7, 1), (14, 1), (7, 4), (5, 1), (7,
    1), (5, 1), (7, 2), (5, 1), (14, 1), (5, 3), (7, 1), (5, 2), (14, 2), (5, 1), (14, 2), (5, 1), (7, 2),
    (14, 1), (7, 2), (5, 1), (14, 1), (7, 2), (14, 2), (7, 1), (14, 2), (7, 2), (14, 1), (7, 1), (14, 2), (7,
    1), (8, 1), (9, 1), (14, 6), (9, 1), (14, 1), (9, 6), (14, 1), (9, 2), (14, 1), (9, 2), (3, 1), (9, 1),
    (15, 1), (9, 15), (3, 1), (9, 4), (16, 2), (3, 1), (10, 1), (16, 3), (10, 1), (16, 4), (10, 1), (16, 2),
    (10, 1), (16, 5), (10, 1), (16, 1), (10, 1), (16, 11), (10, 1), (16, 2), (11, 1), (16, 1), (11, 1), (16,
    1), (11, 6), (17, 1), (11, 1), (17, 1), (11, 3), (17, 1), (11, 9), (17, 1), (11, 2), (17, 1), (11, 1),
    (18, 1), (11, 3), (18, 1), (11, 1), (18, 9), (11, 8), (18, 3), (11, 1), (18, 13), (12, 1), (18, 10), (19,
    1),
)
REAR_ORDER = (
    (0, 3), (1, 1), (0, 23), (4, 1), (0, 1), (1, 1), (0, 1), (1, 1), (0, 4), (5, 1), (1, 1), (5, 2), (1, 1),
    (5, 1), (1, 1), (5, 1), (1, 1), (5, 1), (1, 1), (5, 1), (1, 1), (5, 1), (1, 1), (5, 1), (1, 1), (5, 2),
    (1, 1), (5, 1), (1, 1), (5, 1), (1, 1), (5, 1), (1, 1), (5, 1), (1, 1), (5, 1), (1, 1), (5, 1), (1, 1),
    (5, 1), (1, 1), (5, 5), (1, 3), (6, 1), (7, 1), (6, 1), (1, 1), (4, 1), (1, 2), (6, 1), (1, 2), (6, 1),
    (1, 1), (6, 3), (7, 1), (6, 1), (1, 2), (6, 1), (7, 3), (1, 2), (7, 1), (1, 2), (7, 1), (1, 1), (7, 2),
    (3, 1), (1, 2), (6, 18), (8, 1), (6, 1), (8, 1), (6, 1), (8, 1), (2, 1), (8, 1), (6, 2), (8, 1), (3, 1),
    (6, 1), (8, 5), (6, 1), (8, 2), (6, 1), (8, 2), (6, 1), (8, 2), (6, 1), (2, 1), (8, 3), (6, 1), (8, 18),
    (9, 3),
)
N_GATHER_SENDS = 70
FEW = 16


def gelu_pair(gate):
    slope = 0.7978845608028654
    squared = gate * gate
    bent = jnp.tanh(slope * (gate + 0.044715 * gate * squared))
    gelu = 0.5 * gate * (1.0 + bent)
    return gelu, 0.5 * (1.0 + bent) + 0.5 * gate * (1.0 - bent * bent) * slope * (1.0 + 3.0 * 0.044715 * squared)


def scatter_sems(halves, given):
    dma = pltpu.SemaphoreType.DMA
    return [
        dma((halves, 16 * given + 36)), dma((halves, given, 8)), dma((halves, given, 16)), dma((halves, 2, 8)),
        dma((halves, 2, 4)), dma((halves, 2, 3)), dma((halves, 2, 2)),
    ]


def scatter_bufs(rows, width, given):
    half = given * width // 2
    shapes = ((8, rows, given * width), (16, rows, given * width), (2, 8, rows, half), (2, 4, rows, half))
    return [pltpu.VMEM(shape, jnp.bfloat16) for shape in shapes + ((2, 3, rows, half), (2, 2, rows, half))]


class Stage:
    def __init__(self, count, cuts, in_refs, out_refs, in_sems, out_sems):
        self.spot = Spot()
        self.count = count
        self.ranges = [pl.ds(a, b - a) for a, b in zip(cuts[:-1], cuts[1:])]
        self.cuts = cuts
        self.sends = {}
        self.in_refs, self.out_refs, self.in_sems, self.out_sems = in_refs, out_refs, in_sems, out_sems

    def gathering(self, name, at, src, dst, rows, sems, between=False):
        own_sem, ssem, rsem = sems
        self.sends[name] = Sends(ssem.at[at])
        yield from gather_steps(self.spot, src, dst, rows, self.sends[name], rsem.at[at], own_sem.at[at], between)

    def scattering(self, name, p_refs, o_refs, rows, bufs, sems, at):
        self.sends[name] = Sends(sems[0].at[at])
        yield from scatter_steps(
            self.spot, p_refs, o_refs, rows, bufs, [sem.at[at] for sem in sems[1:]], self.sends[name]
        )

    def fetch(self, group, sources, streams=None):
        streams = range(len(sources)) if streams is None else streams
        for i, source in zip(streams, sources):
            there = self.in_refs[i].at[group % 2]
            yield pltpu.make_async_copy(source.at[:, pl.ds(group * FEW, FEW), :], there, self.in_sems.at[i, group % 2])

    def store(self, group, targets):
        for i, target in enumerate(targets):
            there = target.at[:, pl.ds(group * FEW, FEW), :]
            yield pltpu.make_async_copy(self.out_refs[i], there, self.out_sems.at[i])

    def finish(self):
        for some in self.sends.values():
            some.finish()


def start_all(copies):
    for copy in copies:
        copy.start()


def wait_all(copies):
    for copy in copies:
        copy.wait()


def tile_inputs(qkv_ref, col_ref, row_ref, base, length, head):
    query = qkv_ref[pl.ds(base + length, length), :head]
    key = qkv_ref[pl.ds(base, 3 * length), head : 2 * head]
    value = qkv_ref[pl.ds(base, 3 * length), 2 * head :]
    tile = base // length
    return query, key, value, col_ref[:, tile : tile + 1] == row_ref[:, pl.ds(base, 3 * length)]


def at(shape, axis):
    return lax.broadcasted_iota(jnp.int32, shape, axis)


def marked(mask):
    return low(jnp.where(mask, 1.0, 0.0))


def packed_order(size, length, grain):
    shape = (size, size)
    row = at((size, 1), 0)
    return marked(at(shape, 1) == row % length // grain * FEW + row // length * grain + row % grain)


def front_kernel(cuts, *refs):
    tok_ref, cot_ref, index_ref, small_ref = refs[:4]
    weights = refs[4:9]
    wd_ref, wo_ref, bucket_ref, col_ref, row_ref, perm_ref = refs[9:14] + refs[-1:]
    *kept, keep_sems = refs[-17:-1]
    refs = (None,) + refs[:-17]
    (rows_ref, gain_one_ref, bias_ref, first_w_ref, qkv_ref, att_ref, middle_ref, d_mid_ref, d_ref, gain_grad_ref, near_grad_ref,
     far_grad_ref, wd_grad_ref, nx_all_ref, forth_ref) = refs[15:30]
    part_ref, up_all_ref, x_all_ref, back_ref = refs[30:34]
    branch_ref, x_ref, dn_ref, w_ref, nx_ref, up_ref, gain_ref, gate_w_ref = refs[34:42]
    one_ref, two_ref, cot_out_ref, one_in_ref, two_in_ref, cot_in_ref = refs[42:48]
    small_out_ref, all_small_ref, first_ref, second_ref = refs[48:52]
    bufs, two_total_ref, in_refs, out_refs = refs[52:58], refs[58], refs[59:61], refs[61:63]
    in_sems, out_sems = refs[63:65]
    exchanges = refs[65:83]
    one_x, two_x, cot_x, small_x, first_x, second_x = [exchanges[i : i + 3] for i in range(0, 18, 3)]
    g_sems, one_sems, two_sems = refs[83:86], refs[86:93], refs[93:100]
    loads = [
        pltpu.make_async_copy(of, to, keep_sems.at[i])
        for i, (of, to) in enumerate(zip((*weights, cot_ref, wd_ref, wo_ref), kept[:8]))
    ]
    start_all(loads)
    weights, cot_ref, wd_ref, wo_ref = kept[:5], kept[5], kept[6], kept[7]
    results = (first_w_ref, qkv_ref, att_ref, middle_ref, near_grad_ref, far_grad_ref, wd_grad_ref)
    first_w_ref, qkv_ref, att_ref, middle_ref, near_grad_ref, far_grad_ref, wd_grad_ref = kept[8:15]
    saves = [pltpu.make_async_copy(of, to, keep_sems.at[8 + i]) for i, (of, to) in enumerate(zip(kept[8:15], results))]
    two_bufs = (bufs[0], two_total_ref, *bufs[2:])
    count, slots, width = x_all_ref.shape
    stage = Stage(count, cuts, in_refs, out_refs, in_sems, out_sems)
    spot, ranges = stage.spot, stage.ranges
    units, head, length = wd_ref.shape[0], wo_ref.shape[0], bias_ref.shape[0]
    size, piece = one_ref.shape
    folds, share = width // piece, size // count
    grain = share // folds
    groups = cuts[-1] // FEW
    near = units - head
    spot.greet_all(count)
    perm_ref[...] = packed_order(size, length, grain)

    def folded(rows, sources):
        shape = (length, size)
        return low(
            sum(
                over(
                    marked((at(shape, 0) == sources) & (at(shape, 1) % share // grain == i)),
                    rows[:, i * piece : (i + 1) * piece], 0, 0,
                )
                for i in range(folds)
            )
        )

    def pick(shares, to_ref):
        source = index_ref[2:3, :slots]
        for i in range(folds):
            mask = at((size, slots), 0) == source + i * grain
            to_ref[:, i * piece : (i + 1) * piece] = low(over(marked(mask), shares, 0, 0))

    def tokens():
        for i in range(count):
            small_out_ref[i * share : (i + 1) * share, :] = small_ref[...]
        one_ref[...] = folded(tok_ref[...], index_ref[0:1, :])
        swap(spot, count, one_ref, one_in_ref, one_x, "send")
        swap(spot, count, small_out_ref, all_small_ref, small_x, "send")
        yield
        swap(spot, count, one_ref, one_in_ref, one_x, "wait")
        place = index_ref[1:2, :]
        place = jnp.where(place < 0, -1, place // grain * share + place % grain + at((1, size), 1) % share // grain * grain)
        two_ref[...] = low(over(marked(at((size, size), 0) == place), one_in_ref[...], 0, 0))
        swap(spot, count, two_ref, two_in_ref, two_x, "send")
        yield
        swap(spot, count, small_out_ref, all_small_ref, small_x, "wait")
        each = width // count
        shape = (2 * each, width)
        mine = at((size, width), 0) == at((size, width), 1) // each * share
        for i, ref in enumerate((gain_one_ref, gain_ref)):
            fold = marked(at(shape, 0) == at(shape, 1) % each + i * each)
            ref[...] = jnp.sum(jnp.where(mine, over(all_small_ref[...], fold), 0.0), axis=0, keepdims=True)
        table = jnp.where(at(all_small_ref.shape, 1) == spot.me, all_small_ref[...].astype(jnp.float32), 0.0)
        table = jnp.sum(table, axis=1, keepdims=True)
        bias_ref[...] = sum(
            jnp.where(bucket_ref[...] == b, table[b * share + 1 : b * share + 2, :], 0.0) for b in range(BUCKETS)
        )
        yield
        swap(spot, count, two_ref, two_in_ref, two_x, "wait")
        pick(two_in_ref[...], rows_ref)
        v = rows_ref[...].astype(jnp.float32)
        nx_ref[...] = (v * scale_of(v) * gain_one_ref[...]).astype(nx_ref.dtype)
        yield

    def cotangent():
        loads[5].wait()
        cot_out_ref[...] = folded(cot_ref[...], index_ref[1:2, :])
        swap(spot, count, cot_out_ref, cot_in_ref, cot_x, "send")
        yield
        swap(spot, count, cot_out_ref, cot_in_ref, cot_x, "wait")
        pick(cot_in_ref[...], up_ref)
        yield

    def columns(src, dst, sems, packs):
        if packs:
            wait_all(loads[:5])
            pack(weights, first_ref, second_ref)
            yield
        for i in range(0, count, 8):
            swap(spot, count, src, dst, sems, "send", (max(i, 1), i + 8))
            yield
        swap(spot, count, src, dst, sems, "wait")
        if packs:
            gate_w_ref[...] = dst[:, 3 * head :]
            saves[0].start()
            wait_all(loads[6:])
        yield

    def attending(first, last):
        perm = perm_ref[...]
        if first == 0:
            start_all(stage.fetch(0, (nx_all_ref,)))
            qkv_ref[:length, :] = jnp.zeros((length, 3 * head), qkv_ref.dtype)
            qkv_ref[length + groups * size :, :] = jnp.zeros((length, 3 * head), qkv_ref.dtype)
        for step in range(first, last):
            if step < groups:
                if step + 1 < groups:
                    start_all(stage.fetch(step + 1, (nx_all_ref,)))
                wait_all(stage.fetch(step, (nx_all_ref,)))
                rows = low(over(in_refs[0][step % 2].reshape(size, -1), first_w_ref[:, : 3 * head]))
                qkv_ref[length + step * size : length + (step + 1) * size, :] = low(over(perm, rows))
                yield
            if step > 0:
                attended = []
                for tile in range(size // length):
                    base = (step - 1) * size + tile * length
                    query, key, value, same = tile_inputs(qkv_ref, col_ref, row_ref, base, length, head)
                    attended.append(low(over(low(tile_probs(query, key, bias_ref[...], same)), value)))
                    if tile % 2:
                        yield
                rows = low(over(perm, jnp.concatenate(attended, axis=0), 0, 0))
                att_ref[:, (step - 1) * FEW : step * FEW, :] = rows.reshape(count, FEW, head)
                if step > max(first, 1):
                    wait_all(stage.store(step - 2, (part_ref,)))
                for i in range(2):
                    there = pl.ds(i * count // 2, count // 2)
                    piece = over(rows[i * size // 2 : (i + 1) * size // 2], wo_ref[...])
                    out_refs[0][there] = low(piece).reshape(count // 2, FEW, width)
                start_all(stage.store(step - 1, (part_ref,)))
                yield
        if last > max(first, 1):
            wait_all(stage.store(last - 2, (part_ref,)))
        if last > groups:
            start_all(saves[1:3])
        yield

    def rows_of(rows):
        return [pl.ds(rows.start + i, 16) for i in range(0, rows.size, 16)]

    def scale_of(v):
        return lax.rsqrt(jnp.sum(v * v, axis=1, keepdims=True) / width + EPSILON)

    def first_norm(rows):
        for r in rows_of(rows):
            v = rows_ref[r, :].astype(jnp.float32) + branch_ref[r, :]
            middle_ref[r, :] = v
            x_ref[r, :] = (v * scale_of(v) * gain_ref[...]).astype(x_ref.dtype)
        if rows.start + rows.size == slots:
            saves[3].start()
        yield

    def norm_back_rows(rows):
        for r in rows_of(rows):
            v, d, gain = middle_ref[r, :], dn_ref[r, :], gain_ref[...]
            scale = scale_of(v)
            gain_grad_ref[...] += jnp.sum(d * v * scale, axis=0, keepdims=True)
            w = gain * d
            mean = jnp.sum(w * v, axis=1, keepdims=True) / width
            d_mid = up_ref[r, :].astype(jnp.float32) + scale * w - v * (scale * scale * scale) * mean
            d_mid_ref[r, :] = d_mid
            d_ref[r, :] = d_mid.astype(d_ref.dtype)
        yield

    def feeding(first, last):
        sources, targets = (x_all_ref, up_all_ref), (back_ref, forth_ref)
        start_all(stage.fetch(first, sources))
        for group in range(first, last):
            if group + 1 < last:
                start_all(stage.fetch(group + 1, sources))
            wait_all(stage.fetch(group, sources))
            for i in range(2):
                blocks = slice(i * count // 2, (i + 1) * count // 2)
                x = in_refs[0][group % 2, blocks].reshape(size // 2, width)
                upstream = in_refs[1][group % 2, blocks].reshape(size // 2, width)
                both = over(x, w_ref[...])
                gate = jnp.concatenate((over(x, gate_w_ref[...]), both[:, :near]), axis=1)
                up = both[:, near:]
                d_hidden = over(upstream, wd_ref[...], 1, 1)
                gelu, d_gelu = gelu_pair(gate)
                hidden = low(gelu * up)
                d_gate, d_up = low(d_hidden * up * d_gelu), low(d_hidden * gelu)
                d_first, d_both = d_gate[:, :head], jnp.concatenate((d_gate[:, head:], d_up), axis=1)
                if i == 0 and group > first:
                    wait_all(stage.store(group - 1, targets))
                shape = (count // 2, FEW, width)
                back = over(d_both, w_ref[...], 1, 1) + over(d_first, gate_w_ref[...], 1, 1)
                out_refs[0][blocks] = low(back).reshape(shape)
                out_refs[1][blocks] = low(over(hidden, wd_ref[...])).reshape(shape)
                if i:
                    start_all(stage.store(group, targets))
                near_grad_ref[...] += over(d_first, x, 0, 0)
                far_grad_ref[...] += over(d_both, x, 0, 0)
                wd_grad_ref[...] += over(hidden, upstream, 0, 0)
                yield
        wait_all(stage.store(last - 1, targets))
        if last == groups:
            start_all(saves[4:])
        yield

    for ref in (near_grad_ref, far_grad_ref, wd_grad_ref, gain_grad_ref):
        ref[...] = jnp.zeros_like(ref)
    halves = len(ranges)
    everything = pl.ds(0, slots)
    tasks = {
        "tokens": ([], tokens()),
        "cot": ([], cotangent()),
        "first": ([], columns(first_ref, first_w_ref, first_x, True)),
        "second": (["first"], columns(second_ref, w_ref, second_x, False)),
        "gather": (["tokens"], stage.gathering("gather", 0, nx_ref, nx_all_ref, everything, g_sems)),
        "up": (["cot"], stage.gathering("up", 1, up_ref, up_all_ref, everything, g_sems, True)),
    }
    for i, rows in enumerate(ranges):
        h = str(i)
        last_step = groups + 1 if i == halves - 1 else cuts[i + 1] // FEW + 1
        first_step = cuts[i] // FEW + 1 if i else 0
        tasks |= {
            "attend" + h: ([f"attend{i - 1}"] if i else ["gather", "first"], attending(first_step, last_step)),
            "one" + h: (
                ["attend" + h], stage.scattering("one" + h, (part_ref,), (branch_ref,), rows, bufs, one_sems, i),
            ),
            "norm" + h: (["one" + h], first_norm(rows)),
            "x" + h: (["norm" + h], stage.gathering("x" + h, 2 + i, x_ref, x_all_ref, rows, g_sems)),
            "feed" + h: (
                ["x" + h, "up", "second", f"feed{i - 1}" if i else f"attend{halves - 1}"],
                feeding(cuts[i] // FEW, cuts[i + 1] // FEW),
            ),
            "two" + h: (
                ["feed" + h],
                stage.scattering("two" + h, (back_ref,), (dn_ref,), rows, two_bufs, two_sems, i),
            ),
            "back" + h: (["two" + h], norm_back_rows(rows)),
        }
    weave(tasks, FRONT_ORDER)
    wait_all(saves)
    stage.finish()


def halves_of(rows):
    return (0, 48, 80) if rows == 80 else (0, rows)


def front(tok, cot, index, small, weights, wd, wo, buckets, col, row, slots):
    size, (length, width) = index.shape[1], tok.shape
    shard = weights[0].shape[0]
    count, piece = width // shard, length * width // size
    cuts = halves_of(slots)
    halves = len(cuts) - 1
    head, units = wo.shape[0], wd.shape[0]
    low_rows, all_rows, group, share = (slots, width), (count, slots, width), (count, FEW, width), (size, piece)
    first, second = (width, 4 * head), (width, 2 * units - head)
    bf, wide, dma = jnp.bfloat16, jnp.float32, pltpu.SemaphoreType.DMA
    vmem, hbm = pl.BlockSpec(memory_space=pltpu.VMEM), pl.BlockSpec(memory_space=pl.ANY)
    shape = jax.ShapeDtypeStruct
    qkv, attended = (slots // FEW * size + 2 * length, 3 * head), (count, slots, head)
    kept = [pltpu.VMEM(array.shape, bf) for array in (*weights, cot, wd, wo)]
    kept += [pltpu.VMEM(first, bf), pltpu.VMEM(qkv, bf), pltpu.VMEM(attended, bf), pltpu.VMEM(low_rows, wide)]
    kept += [pltpu.VMEM((n, width), wide) for n in (head, second[1], units)]
    outs = pl.pallas_call(
        functools.partial(front_kernel, cuts),
        out_shape=[
            shape(low_rows, bf), shape((1, width), wide), shape(buckets.shape, wide), shape(first, bf),
            shape(qkv, bf), shape(attended, bf), shape(low_rows, wide),
            shape(low_rows, wide), shape(low_rows, bf), shape((1, width), wide), shape((head, width), wide),
            shape((second[1], width), wide), shape(wd.shape, wide),
        ] + [shape(all_rows, bf)] * 6,
        in_specs=[vmem, hbm, vmem, vmem] + [hbm] * 7 + [vmem] * 3,
        out_specs=[vmem] * 3 + [hbm] * 4 + [vmem] * 3 + [hbm] * 9,
        scratch_shapes=[
            pltpu.VMEM(low_rows, wide), pltpu.VMEM(low_rows, bf), pltpu.VMEM(low_rows, wide), pltpu.VMEM(second, bf),
            pltpu.VMEM(low_rows, bf), pltpu.VMEM(low_rows, bf), pltpu.VMEM((1, width), wide), pltpu.VMEM((width, head), bf),
        ] + [pltpu.VMEM(share, bf)] * 6 + [
            pltpu.VMEM((size, 128), bf), pltpu.VMEM((size, 128), bf), pltpu.VMEM(first, bf), pltpu.VMEM(second, bf),
        ] + scatter_bufs(slots, width, 1) + [
            pltpu.VMEM((16, slots, width), bf),
            pltpu.VMEM((2,) + group, bf), pltpu.VMEM((2,) + group, bf), pltpu.VMEM(group, bf), pltpu.VMEM(group, bf),
            dma((2, 2)), dma((2,)),
        ] + [dma((count,)), dma((count,)), dma] * 6 + [
            dma((2 + halves,)), dma((2 + halves, N_GATHER_SENDS)), dma((2 + halves, 2, 32)),
        ] + scatter_sems(halves, 1) * 2 + kept + [dma((15,)), pltpu.VMEM((size, size), bf)],
        name="front",
        compiler_params=pltpu.CompilerParams(collective_id=3, has_side_effects=True, vmem_limit_bytes=63 * 2**20),
    )(tok, cot, index, small, *weights, wd, wo, buckets, col, row)
    return outs[:15]


def rear_kernel(cuts, *refs):
    (d_ref, x_all_ref, att_ref, qkv_ref, w_ref, wo_ref, bias_ref, col_ref, row_ref, near_ref, far_ref, forth_ref, middle_ref,
     rows_ref, d_mid_ref, gain_ref, gain_two_ref, index_ref, bucket_ref) = refs[:19]
    wo_grad_ref, owned_ref, far_owned_ref, out_rows_ref, sums_ref, token_rows_ref = refs[19:25]
    d_all_ref, part_ref = refs[25:27]
    dn_ref, down_ref, bias_grad_ref, dq_ref, dkv_ref, w_grad_ref, turned_ref, far_turned_ref = refs[27:35]
    result_ref, going_ref, came_ref, last_ref, perm_ref = refs[35:40]
    sums_out_ref, *s_sems = refs[-14:-10]
    refs = refs[:-14] + refs[-10:]
    *kept, keep_sems = refs[-10:]
    large = (att_ref, qkv_ref, w_ref, wo_ref, near_ref, far_ref, middle_ref, rows_ref, d_mid_ref)
    loads = [pltpu.make_async_copy(of, to, keep_sems.at[i]) for i, (of, to) in enumerate(zip(large, kept))]
    start_all(loads)
    att_ref, qkv_ref, w_ref, wo_ref, near_ref, far_ref, middle_ref, rows_ref, d_mid_ref = kept
    bufs, other_bufs, in_refs, out_refs = refs[40:46], refs[46:52], refs[52:54], refs[54:55]
    in_sems, out_sems = refs[55:57]
    w_sems, f_sems, r_sems, t_sems, l_sems = [refs[i : i + 3] for i in range(57, 72, 3)]
    g_sems, one_sems, down_sems = refs[72:75], refs[75:82], refs[82:89]
    count, width = part_ref.shape[0], part_ref.shape[2]
    stage = Stage(count, cuts, in_refs, out_refs, in_sems, out_sems)
    spot, ranges = stage.spot, stage.ranges
    spot.greet_all(count)
    head, length, size = wo_ref.shape[0], bias_ref.shape[0], perm_ref.shape[0]
    groups = cuts[-1] // FEW
    piece, share = result_ref.shape[1], size // count
    folds = width // piece
    grain = share // folds
    perm_ref[...] = packed_order(size, length, grain)

    def owners(sources, to_ref, owner_ref, sems, load):
        load.wait()
        merged = jnp.concatenate([low(ref[...]) for ref in sources], axis=0)
        for i in range(0, width, 512):
            to_ref[i : i + 512, :] = merged[:, i : i + 512].T
        swap(spot, count, to_ref, owner_ref, sems, "send")
        yield
        swap(spot, count, to_ref, owner_ref, sems, "wait")
        yield

    def dealt_out(rows):
        shape = (rows.shape[0], size)
        return sum(
            over(
                marked((at(shape, 0) == index_ref[0:1, :]) & (at(shape, 1) % share // grain == i)),
                rows[:, i * piece : (i + 1) * piece], 0, 0,
            )
            for i in range(folds)
        )

    def output():
        loads[6].wait()
        rows = low(middle_ref[...] + down_ref[...])
        result_ref[...] = low(dealt_out(rows))
        swap(spot, count, result_ref, out_rows_ref, r_sems, "send")
        yield
        swap(spot, count, result_ref, out_rows_ref, r_sems, "wait")
        yield

    def scale_of(v):
        return lax.rsqrt(jnp.sum(v * v, axis=1, keepdims=True) / width + EPSILON)

    def shares(*values):
        shape, each = (size, width), width // count
        spread = 0.0
        for i, v in enumerate(values):
            spread += jnp.where(at(shape, 0) == at(shape, 1) // each * share + 2 * i, v, 0.0)
        fold = marked(at((width, each), 0) % each == at((width, each), 1))
        high = low(spread)
        rest = low(spread - high.astype(jnp.float32))
        return jnp.concatenate([over(p, fold) for p in (high, rest)], axis=1)

    def finals():
        wait_all(loads[7:])
        v, d, gain = rows_ref[...].astype(jnp.float32), dn_ref[...], gain_ref[...]
        scale = scale_of(v)
        w = gain * d
        mean = jnp.sum(w * v, axis=1, keepdims=True) / width
        rows = low(d_mid_ref[...] + scale * w - v * (scale * scale * scale) * mean)
        going_ref[...] = low(dealt_out(rows))
        swap(spot, count, going_ref, came_ref, t_sems, "send")
        sums = shares(jnp.sum(d * v * scale, axis=0, keepdims=True), gain_two_ref[...])
        row, lane = at(sums.shape, 0), at(sums.shape, 1)
        for b in range(BUCKETS):
            total = jnp.sum(jnp.where(bucket_ref[...] == b, bias_grad_ref[...], 0.0), axis=(0, 1), keepdims=True)
            high = low(total).astype(jnp.float32)
            sums = sums + jnp.where((row == share * b + 1) & (lane < 2), jnp.where(lane == 0, high, total - high), 0.0)
        sums_out_ref[...] = low(sums)
        swap(spot, count, sums_out_ref, sums_ref, s_sems, "send")
        shape, row, lane = (size, size), at((size, 1), 0), at((1, size), 1)
        turn = (index_ref[1:2, :] == row // share * grain + row % grain) & (row % share // grain == lane % share // grain)
        turn = marked(turn)
        yield
        swap(spot, count, going_ref, came_ref, t_sems, "wait")
        last_ref[...] = low(over(turn, came_ref[...]))
        swap(spot, count, last_ref, token_rows_ref, l_sems, "send")
        yield
        swap(spot, count, sums_out_ref, sums_ref, s_sems, "wait")
        swap(spot, count, last_ref, token_rows_ref, l_sems, "wait")
        yield

    def backing(first, last):
        perm = perm_ref[...]
        if not first:
            wait_all(loads[:4])
        for step in range(first, last):
            if step < groups:
                start_all(stage.fetch(step, (d_all_ref,)))
                start_all(stage.fetch(step, (x_all_ref,), (1,)))
                wait_all(stage.fetch(step, (d_all_ref,)))
                d_branch = in_refs[0][step % 2].reshape(size, width)
                attended = att_ref[:, step * FEW : (step + 1) * FEW, :].reshape(size, head)
                wo_grad_ref[...] += over(attended, d_branch, 0, 0)
                yield
                d_attended = low(over(perm, low(over(d_branch, wo_ref[...], 1, 1))))
                yield
                for tile in range(size // length):
                    base = step * size + tile * length
                    query, key, value, same = tile_inputs(qkv_ref, col_ref, row_ref, base, length, head)
                    probs = tile_probs(query, key, bias_ref[...], same)
                    d_out = d_attended[tile * length : (tile + 1) * length, :]
                    d_probs = over(d_out, value, 1, 1)
                    inner = jnp.sum(probs * d_probs, axis=-1, keepdims=True)
                    d_scores = low(probs * (d_probs - inner))
                    bias_grad_ref[...] += d_scores.astype(jnp.float32)
                    dq_ref[base + length : base + 2 * length, :] = low(over(d_scores, key))
                    both = jnp.concatenate((over(d_scores, query, 0, 0), over(low(probs), d_out, 0, 0)), axis=1)
                    dkv_ref[base : base + 3 * length, :] += both
                    if tile % 2:
                        yield
            if step > 0:
                at = slice(length + (step - 1) * size, length + step * size)
                rows = low(over(perm, jnp.concatenate((dq_ref[at, :], low(dkv_ref[at, :])), axis=1), 0, 0))
                wait_all(stage.fetch(step - 1, (x_all_ref,), (1,)))
                w_grad_ref[...] += over(rows, in_refs[1][(step - 1) % 2].reshape(size, width), 0, 0)
                yield
                if step > max(first, 1):
                    wait_all(stage.store(step - 2, (part_ref,)))
                for i in range(2):
                    there = pl.ds(i * count // 2, count // 2)
                    block = over(rows[i * size // 2 : (i + 1) * size // 2], w_ref[:, : 3 * head], 1, 1)
                    out_refs[0][there] = low(block).reshape(count // 2, FEW, width)
                start_all(stage.store(step - 1, (part_ref,)))
                yield
        if last > max(first, 1):
            wait_all(stage.store(last - 2, (part_ref,)))
        yield

    for ref in (wo_grad_ref, bias_grad_ref, dkv_ref, w_grad_ref):
        ref[...] = jnp.zeros_like(ref)
    halves = len(ranges)
    everything = pl.ds(0, cuts[-1])
    tasks = {
        "d": ([], stage.gathering("d", 0, d_ref, d_all_ref, everything, g_sems)),
        "down": ([], stage.scattering("down", (forth_ref,), (down_ref,), everything, other_bufs, down_sems, 0)),
        "output": (["down"], output()),
        "owners": ([f"back{halves - 1}"], owners((w_grad_ref, near_ref), turned_ref, owned_ref, w_sems, loads[4])),
        "far": ([], owners((far_ref,), far_turned_ref, far_owned_ref, f_sems, loads[5])),
    }
    for i, rows in enumerate(ranges):
        h = str(i)
        first_step = cuts[i] // FEW + 1 if i else 0
        tasks |= {
            "back" + h: ([f"back{i - 1}"] if i else ["d"], backing(first_step, cuts[i + 1] // FEW + 1)),
            "one" + h: (["back" + h], stage.scattering("one" + h, (part_ref,), (dn_ref,), rows, bufs, one_sems, i)),
        }
    tasks["finals"] = ([f"one{i}" for i in range(halves)], finals())
    weave(tasks, REAR_ORDER)
    stage.finish()


def rear(d_rows, normed_all, attended, qkv, w, wo, bias, col, row, near_grad, far_grad, forth, middle, rows_low, d_mid, gain,
         gain_two_grad, index, buckets):
    count, rows, width = normed_all.shape
    cuts = halves_of(rows)
    halves = len(cuts) - 1
    head, size = wo.shape[0], index.shape[1]
    piece, owned, far = bias.shape[0] * width // size, (width, w.shape[1]), (width, far_grad.shape[0])
    all_rows, group, share = (count, rows, width), (count, FEW, width), (size, piece)
    bf, wide, dma = jnp.bfloat16, jnp.float32, pltpu.SemaphoreType.DMA
    vmem, hbm = pl.BlockSpec(memory_space=pltpu.VMEM), pl.BlockSpec(memory_space=pl.ANY)
    shape = jax.ShapeDtypeStruct
    outs = pl.pallas_call(
        functools.partial(rear_kernel, cuts),
        out_shape=[
            shape((head, width), wide), shape(owned, bf), shape(far, bf), shape(share, bf), shape((size, 128), bf),
            shape(share, bf),
        ] + [shape(all_rows, bf)] * 2,
        in_specs=[vmem] + [hbm] * 5 + [vmem] * 3 + [hbm] * 6 + [vmem] * 4,
        out_specs=[vmem] + [hbm] * 7,
        scratch_shapes=[
            pltpu.VMEM((rows, width), wide), pltpu.VMEM((rows, width), wide), pltpu.VMEM(bias.shape, wide),
            pltpu.VMEM((qkv.shape[0], head), bf), pltpu.VMEM((qkv.shape[0], 2 * head), wide),
            pltpu.VMEM((3 * head, width), wide), pltpu.VMEM(owned, bf), pltpu.VMEM(far, bf),
            pltpu.VMEM(share, bf), pltpu.VMEM(share, bf), pltpu.VMEM(share, bf), pltpu.VMEM(share, bf),
            pltpu.VMEM((size, size), bf),
        ] + scatter_bufs(rows, width, 1) * 2 + [
            pltpu.VMEM((2,) + group, bf), pltpu.VMEM((2,) + group, bf), pltpu.VMEM(group, bf),
            dma((2, 2)), dma((1,)),
        ] + [dma((count,)), dma((count,)), dma] * 5 + [
            dma((1,)), dma((1, N_GATHER_SENDS)), dma((1, 2, 32)),
        ] + scatter_sems(halves, 1) + scatter_sems(1, 1) + [
            pltpu.VMEM((size, 128), bf), dma((count,)), dma((count,)), dma,
        ] + [
            pltpu.VMEM(array.shape, array.dtype)
            for array in (attended, qkv, w, wo, near_grad, far_grad, middle, rows_low, d_mid)
        ] + [dma((9,))],
        name="rear",
        compiler_params=pltpu.CompilerParams(collective_id=4, has_side_effects=True, vmem_limit_bytes=63 * 2**20),
    )(d_rows, normed_all, attended, qkv, w, wo, bias, col, row, near_grad, far_grad, forth, middle, rows_low, d_mid, gain,
      gain_two_grad, index, buckets)
    return outs[:6]


def dot(left, right):
    return jnp.dot(left, right, preferred_element_type=jnp.float32)


def select(mask, rows):
    return dot(mask.astype(jnp.bfloat16), rows).astype(jnp.bfloat16)


def unpack_kernel(first_ref, second_ref, out_ref, down_ref, query_ref, key_ref, value_ref, gate_ref, up_ref, *same_refs):
    for ref, same_ref in zip((out_ref, down_ref), same_refs):
        same_ref[...] = ref[...]
    count = first_ref.shape[0]
    head = query_ref.shape[1] // count
    units = gate_ref.shape[1] // count
    wide = jnp.float32
    for j in range(count):
        for i, ref in enumerate((query_ref, key_ref, value_ref)):
            ref[:, j * head : (j + 1) * head] = first_ref[j, :, i * head : (i + 1) * head].astype(wide)
        gate_ref[:, j * units : j * units + head] = first_ref[j, :, 3 * head :].astype(wide)
        gate_ref[:, j * units + head : (j + 1) * units] = second_ref[j, :, : units - head].astype(wide)
        up_ref[:, j * units : (j + 1) * units] = second_ref[j, :, units - head :].astype(wide)


def unpack(first, second, out_grad, down_grad, width, hidden):
    count, rows, _ = first.shape
    steps = 4
    widths = (width, width, width, hidden, hidden)

    def slab(array):
        return pl.BlockSpec((array.shape[0] // steps, array.shape[1]), lambda i: (i, 0))

    def deep(array):
        return pl.BlockSpec((count, rows // steps, array.shape[2]), lambda i: (0, i, 0))

    shapes = [jax.ShapeDtypeStruct((rows, columns), jnp.float32) for columns in widths]
    shapes += [jax.ShapeDtypeStruct(array.shape, jnp.float32) for array in (out_grad, down_grad)]
    return pl.pallas_call(
        unpack_kernel,
        grid=(steps,),
        out_shape=shapes,
        in_specs=[deep(first), deep(second), slab(out_grad), slab(down_grad)],
        out_specs=[slab(shape) for shape in shapes],
        name="unpack_columns",
        compiler_params=pltpu.CompilerParams(vmem_limit_bytes=63 * 2**20),
    )(first, second, out_grad, down_grad)


def body(
    tokens,
    lengths,
    permutation,
    query_weight,
    key_weight,
    value_weight,
    out_weight,
    gate_weight,
    up_weight,
    down_weight,
    gain_attention,
    gain_feedforward,
    bias_table,
    cotangent,
):
    me = lax.axis_index(AXIS)
    count = tokens.shape[0]
    grain = tokens.shape[1]
    length = cotangent.shape[1]
    width = tokens.shape[2]
    shard = query_weight.shape[0]
    hidden_width = gate_weight.shape[1] // count
    head = HEAD_DIM
    total = 3 * count * length // 5
    tiles = -(-total // length)
    slots = tiles * grain

    dealt_lengths = lengths[permutation]
    ends = jnp.cumsum(dealt_lengths)
    starts = ends - dealt_lengths
    this = jnp.arange(count, dtype=jnp.int32) == me
    my_start = jnp.sum(jnp.where(this, starts, 0), keepdims=True)
    my_length = jnp.sum(jnp.where(this, dealt_lengths, 0), keepdims=True)
    place_in = jnp.arange(length, dtype=jnp.int32)
    slot_ids = jnp.arange(slots, dtype=jnp.int32)
    packed_ids = slot_ids // grain * length + me * grain + slot_ids % grain
    source_seq = jnp.sum((packed_ids[:, None] >= ends[None, :]).astype(jnp.int32), axis=1)

    few = 16
    folds = few // grain
    piece = width // folds
    share = jnp.arange(few * count, dtype=jnp.int32)
    share_row, share_fold = share // few * grain + share % grain, share % few // grain
    position = share_row - my_start % length
    position = jnp.where(position < 0, position + length, position)
    in_share = jnp.arange(few, dtype=jnp.int32)[None, :] % grain
    index = jnp.stack(
        (
            (permutation[:, None] * grain + in_share).reshape(-1),
            jnp.where(position < my_length, position, -1),
            jnp.pad(jnp.where(source_seq < count, source_seq * few + slot_ids % grain, -few), (0, few * count - slots)),
        )
    )
    small = jnp.concatenate((gain_attention, gain_feedforward, bias_table))
    small = jnp.pad(small, (0, few * 128 - small.shape[0])).reshape(few, 128)
    all_ids = jnp.arange(tiles * length, dtype=jnp.int32)
    segment = jnp.sum((all_ids[:, None] >= ends[None, :]).astype(jnp.int32), axis=1) + 1
    column, row = segment.reshape(tiles, length).T, jnp.pad(segment, (length, length))[None, :]
    relative = (
        jnp.arange(3 * length, dtype=jnp.int32)[None, :] - length - place_in[:, None]
    ).reshape(-1)
    onehot = bucket_index(relative)[None, :] == jnp.arange(BUCKETS, dtype=jnp.int32)[:, None]
    buckets = bucket_index(relative).reshape(length, -1)
    (rows_low, gain_one, rel_bias, first_columns, qkv, attended, middle, d_middle, d_low, gain_two_grad, near_grad, far_grad,
     down_grad, normed_all, forth) = front(
        tokens.reshape(length, width), cotangent[0], index, small,
        (query_weight, key_weight, value_weight, gate_weight, up_weight), down_weight, out_weight, buckets, column, row, slots,
    )
    turned = me * grain + in_share - starts[:, None] % length
    turned = starts[:, None] + jnp.where(turned < 0, turned + length, turned)
    back_slot = (turned // length * grain + in_share).reshape(-1)

    out_grad, first_grad, second_grad, out_rows, sums, token_rows = rear(
        d_low, normed_all, attended, qkv, first_columns, out_weight, rel_bias, column, row, near_grad, far_grad, forth, middle,
        rows_low, d_middle, gain_one, gain_two_grad, jnp.stack((back_slot, index[1])), buckets,
    )
    first_grad, second_grad = first_grad.reshape(count, shard, -1), second_grad.reshape(count, shard, -1)
    sums = sums.reshape(count, few, -1).astype(jnp.float32)
    gain_sums = jnp.sum(sums, axis=0)
    gain_attention_grad = gain_sums[0, :shard] + gain_sums[0, shard : 2 * shard]
    gain_feedforward_grad = gain_sums[2, :shard] + gain_sums[2, shard : 2 * shard]
    table_grad = sums[:, 1, 0] + sums[:, 1, 1]

    def whole_rows(shares):
        return shares.reshape(count, folds, grain, piece).transpose(0, 2, 1, 3).reshape(count, grain, width)

    place = place_in - my_start % length
    place = jnp.where(place < 0, place + length, place)
    turned_back = (place[None, :] == place_in[:, None]) & (place_in[:, None] < my_length)
    layer_output = select(turned_back, whole_rows(out_rows).reshape(length, width))[None]
    ids = jnp.arange(count, dtype=jnp.int32)
    dealt_slot = jnp.sum(jnp.where(permutation[None, :] == ids[:, None], ids[None, :], 0), axis=1)
    tokens_grad = whole_rows(token_rows)[dealt_slot]
    query_grad, key_grad, value_grad, gate_grad, up_grad, out_grad, down_grad = unpack(
        first_grad, second_grad, out_grad, down_grad, width, hidden_width * count
    )
    return (
        layer_output,
        tokens_grad,
        query_grad,
        key_grad,
        value_grad,
        out_grad,
        gate_grad,
        up_grad,
        down_grad,
        gain_attention_grad,
        gain_feedforward_grad,
        table_grad,
    )


def solution(mesh):
    placed = (
        P(None, "fsdp", None),
        P(),
        P(),
        P("fsdp", None),
        P("fsdp", None),
        P("fsdp", None),
        P("fsdp", None),
        P("fsdp", None),
        P("fsdp", None),
        P("fsdp", None),
        P("fsdp"),
        P("fsdp"),
        P("fsdp"),
        P("fsdp", None, None),
    )
    return jax.shard_map(
        body if mesh.shape[AXIS] == 32 else body_any,
        mesh=mesh,
        in_specs=placed,
        out_specs=(
            P("fsdp", None, None),
            P(None, "fsdp", None),
            P("fsdp", None),
            P("fsdp", None),
            P("fsdp", None),
            P("fsdp", None),
            P("fsdp", None),
            P("fsdp", None),
            P("fsdp", None),
            P("fsdp"),
            P("fsdp"),
            P("fsdp"),
        ),
        check_vma=False,
    )
```
